32 devices in a mesh: seq: 8 (over z, y), fsdp: 4 (over x, core).
Axes of the slice: x: 2, y: 2, z: 4, core: 2. Of those that a mesh axis runs over, the one named last changes fastest.
Arguments:
- tokens: bfloat16 [4, 1024, 2304], P('fsdp', 'seq'), may hold values from -6 to 6
- doc_ids: int32 [4, 1024], P('fsdp', 'seq'), may hold values from 0 to 64, as said below
- padding: int32 [4, 1024], P('fsdp', 'seq'), may hold values from 0 to 1, as said below
- token_order: int32 [4, 1024], P('fsdp', 'seq'), may hold values from 0 to 1023, as said below
- query_code: bfloat16 [2304, 2048], P(None, 'fsdp'), may hold values from -128 to 127, as said below
- key_value_code: bfloat16 [2304, 2048], P(None, 'fsdp'), may hold values from -128 to 127, as said below
- output_code: bfloat16 [2048, 2304], P(None, 'fsdp'), may hold values from -128 to 127, as said below
- gate_up_code: bfloat16 [2304, 18432], P(None, 'fsdp'), may hold values from -128 to 127, as said below
- down_code: bfloat16 [9216, 2304], P(None, 'fsdp'), may hold values from -128 to 127, as said below
- query_scale: float32 [2048], replicated, may hold values from 0.00015 to 0.0007
- key_value_scale: float32 [2048], replicated, may hold values from 0.00015 to 0.0007
- output_scale: float32 [2304], replicated, may hold values from 0.0001 to 0.001
- gate_up_scale: float32 [18432], replicated, may hold values from 0.00012 to 0.0006
- down_scale: float32 [2304], replicated, may hold values from 5e-05 to 0.0005
- norm_gains: float32 [4, 2304], replicated, may hold values from -0.5 to 0.5
- cotangent: bfloat16 [4, 1024, 2304], P('fsdp', 'seq'), may hold values from -6 to 6
Outputs:
- block_out: bfloat16 [4, 1024, 2304], P('fsdp', 'seq')
- grad_tokens: float32 [4, 1024, 2304], P('fsdp', 'seq')
- grad_query_code: float32 [2304, 2048], P('seq', 'fsdp')
- grad_key_value_code: float32 [2304, 2048], P('seq', 'fsdp')
- grad_output_code: float32 [2048, 2304], P('seq', 'fsdp')
- grad_gate_up_code: float32 [2304, 18432], P('seq', 'fsdp')
- grad_down_code: float32 [9216, 2304], P('seq', 'fsdp')
- grad_query_scale: float32 [2048], replicated
- grad_key_value_scale: float32 [2048], replicated
- grad_output_scale: float32 [2304], replicated
- grad_gate_up_scale: float32 [18432], replicated
- grad_down_scale: float32 [2304], replicated
- grad_norm_gains: float32 [4, 2304], replicated
The draws below stay inside these ranges and needn't reach their ends.
Inputs may be any that keep to these rules, and one draw needn't show every extreme that they name: `doc_ids`: along positions (token_order) of a pack the ids never fall; equal ids mark one document. In every pack one document has rows on every device of seq, and the last document of every pack has id 128 / 2. `padding`: padding rows are the last positions of a pack. `token_order`: within each pack, a permutation of the positions 0 to 1023; runs of 64 stored rows hold runs of consecutive positions. `query_code`: whole numbers. `key_value_code`: whole numbers. `output_code`: whole numbers. `gate_up_code`: whole numbers. `down_code`: whole numbers.
All inputs are finite; a program needn't handle non-finite values.
Results may differ from the reference program's by a relative error of at most 0.02.
Values may be sent and summed in bfloat16 or wider, within the bound.
A program may use at most 256 MiB of HBM per device.

```python
import math
import jax
import jax.numpy as jnp
from jax import lax

D = 2304
HQ = 8
HK = 4
DH = 256
FF = 9216
TOK_DEV = 128
SEQ_LEN = 1024
PACKS = 4
N_SEQ = 8


def pack_layout(key):
    half = TOK_DEV // 2

    def one_pack(pack_key):
        pieces = jax.random.split(pack_key, 5)
        head = jax.random.randint(pieces[0], (), 2, half)
        tail = jax.random.randint(pieces[1], (), 3, half)
        padded = jax.random.randint(pieces[2], (), 1, tail - 1)
        position = jnp.arange(SEQ_LEN)
        breaks = (jax.random.randint(pieces[3], (SEQ_LEN,), 0, 3) == 0) & (position < head)
        starts = breaks | (position == 0) | (position == head) | (position == SEQ_LEN - tail)
        document = jnp.cumsum(starts.astype(jnp.int32)) - 1
        document = jnp.where(position >= SEQ_LEN - tail, half, document)
        genuine = (position < SEQ_LEN - padded).astype(jnp.int32)
        shuffled = jax.random.permutation(pieces[4], 2 * N_SEQ)
        place = shuffled[position // half] * half + position % half
        return (document[place].astype(jnp.int32), genuine[place], place.astype(jnp.int32))
    return jax.vmap(one_pack)(jax.random.split(key, PACKS))


def code_table(key, height, width):
    return jax.random.randint(key, (height, width), -128, 128).astype(jnp.float32).astype(jnp.bfloat16)


def draw_doc_ids(key, part):
    return pack_layout(key)[0]


def draw_padding(key, part):
    return pack_layout(key)[1]


def draw_token_order(key, part):
    return pack_layout(key)[2]


def draw_query_code(key, part):
    key = jax.random.fold_in(key, 11)
    return code_table(key, D, HQ * DH)


def draw_key_value_code(key, part):
    key = jax.random.fold_in(key, 12)
    return code_table(key, D, 2 * HK * DH)


def draw_output_code(key, part):
    key = jax.random.fold_in(key, 13)
    return code_table(key, HQ * DH, D)


def draw_gate_up_code(key, part):
    key = jax.random.fold_in(key, 14)
    return code_table(key, D, 2 * FF)


def draw_down_code(key, part):
    key = jax.random.fold_in(key, 15)
    return code_table(key, FF, D)


def level_of(key, extent, cuts, smallest, largest):
    def one(dim, blocks):
        draws = jax.random.uniform(jax.random.fold_in(jax.random.fold_in(key, 6), dim), (blocks,), jnp.float32, smallest / len(cuts), largest / len(cuts))
        return jnp.repeat(jnp.exp(draws), extent[dim] // blocks).reshape((-1,) + (1,) * (len(extent) - dim - 1))

    level = one(*cuts[0])
    for cut in cuts[1:]:
        level = level * one(*cut)
    return level


def gaussian(rng, shape, scale, reach, cuts=(), held_as=jnp.bfloat16):
    entries = jax.random.normal(rng, shape, jnp.float32) * scale
    if len(cuts) > 0:
        entries = level_of(rng, shape, cuts, -0.22, 0.18) * entries
    return jnp.clip(entries, min=-reach, max=reach).astype(held_as)


def setup_inputs(seed: int = 0) -> dict:
    seeds = jax.random.split(jax.random.key(seed), 17)
    tokens = gaussian(seeds[0], (PACKS, SEQ_LEN, D), 1.0, 6.0, ((0, 4), (1, 8)))
    doc_ids = draw_doc_ids(jax.random.fold_in(seeds[16], 71), 0)
    padding = draw_padding(jax.random.fold_in(seeds[16], 71), 0)
    token_order = draw_token_order(jax.random.fold_in(seeds[16], 71), 0)
    query_code = draw_query_code(jax.random.fold_in(seeds[16], 71), 0)
    key_value_code = draw_key_value_code(jax.random.fold_in(seeds[16], 71), 0)
    output_code = draw_output_code(jax.random.fold_in(seeds[16], 71), 0)
    gate_up_code = draw_gate_up_code(jax.random.fold_in(seeds[16], 71), 0)
    down_code = draw_down_code(jax.random.fold_in(seeds[16], 71), 0)
    query_scale = jnp.clip(jnp.exp(jax.random.uniform(seeds[9], (HQ * DH,), jnp.float32, math.log(0.00015), math.log(0.0007))), 0.00015, 0.0007)
    key_value_scale = jnp.clip(jnp.exp(jax.random.uniform(seeds[10], (2 * HK * DH,), jnp.float32, math.log(0.00015), math.log(0.0007))), 0.00015, 0.0007)
    output_scale = jnp.clip(jnp.exp(jax.random.uniform(seeds[11], (D,), jnp.float32, math.log(0.0001), math.log(0.001))), 0.0001, 0.001)
    gate_up_scale = jnp.clip(jnp.exp(jax.random.uniform(seeds[12], (2 * FF,), jnp.float32, math.log(0.00012), math.log(0.0006))), 0.00012, 0.0006)
    down_scale = jnp.clip(jnp.exp(jax.random.uniform(seeds[13], (D,), jnp.float32, math.log(4.999999873689376e-05), math.log(0.0005))), 4.999999873689376e-05, 0.0005)
    norm_gains = jnp.clip(jax.random.uniform(seeds[14], (4, D), jnp.float32, -0.5, 0.5), -0.5, 0.5)
    cotangent = gaussian(seeds[15], (PACKS, SEQ_LEN, D), 1.0, 6.0, ((0, 4), (1, 8)))
    return {"tokens": tokens, "doc_ids": doc_ids, "padding": padding, "token_order": token_order, "query_code": query_code, "key_value_code": key_value_code, "output_code": output_code, "gate_up_code": gate_up_code, "down_code": down_code, "query_scale": query_scale, "key_value_scale": key_value_scale, "output_scale": output_scale, "gate_up_scale": gate_up_scale, "down_scale": down_scale, "norm_gains": norm_gains, "cotangent": cotangent}


EPSILON = 1e-06
CAP = 50.0
BASE = 10000.0
FLOOR_SCORE = -1e+30
HIGH = lax.Precision.HIGHEST

@jax.custom_vjp
def low(v):
    return lax.optimization_barrier(v.astype(jnp.bfloat16)).astype(jnp.float32)

@jax.custom_vjp
def low_back(v):
    return v

def low_keep(v):
    return (low(v), None)

def low_pass(kept, grad):
    return (grad,)

def back_keep(v):
    return (v, None)

def back_low(kept, grad):
    return (low(grad),)
low.defvjp(low_keep, low_pass)
low_back.defvjp(back_keep, back_low)

def product(left, right):
    return jnp.dot(left, right, precision=HIGH, preferred_element_type=jnp.float32)

def scaled_product(left, codes, scale):
    return low_back(product(left, codes)) * scale[None, :]

def norm_gain(value, gain):
    return value * lax.rsqrt(lax.optimization_barrier(jnp.mean(value * value, axis=-1, keepdims=True)) + EPSILON) * (1.0 + gain)

def angles(positions):
    half = DH // 2
    rates = BASE ** (-2.0 * jnp.arange(half).astype(jnp.float32) / DH)
    turn = positions.astype(jnp.float32)[:, None] * rates[None, :]
    return (jnp.cos(turn), jnp.sin(turn))

def rotate(value, cosine, sine):
    half = DH // 2
    first = value[..., :half]
    second = value[..., half:]
    cosine = cosine[:, None, :]
    sine = sine[:, None, :]
    return jnp.concatenate([first * cosine - second * sine, second * cosine + first * sine], axis=-1)

def attend(query, keys, values, document, padded, place):
    length = query.shape[0]
    size = 512 if length % 512 == 0 else length
    count = length // size
    factor = DH ** (-0.5)
    group = HQ // HK

    def one_block(operands):
        rows, row_document, row_place = operands
        grouped = rows.reshape(size, HK, group, DH)
        raw = low_back(jnp.einsum('tagd,kad->tagk', grouped, keys, precision=HIGH))
        capped = CAP * jnp.tanh(raw * factor / CAP)
        allowed = (row_document[:, None] == document[None, :]) & (place[None, :] <= row_place[:, None]) & (padded[None, :] == 1) | (place[None, :] == row_place[:, None])
        allowed = allowed[:, None, None, :]
        capped = jnp.where(allowed, capped, FLOOR_SCORE)
        highest = lax.optimization_barrier(jnp.max(capped, axis=-1, keepdims=True))
        mass = jnp.where(allowed, jnp.exp(capped - highest), 0.0)
        share = mass / lax.optimization_barrier(jnp.sum(mass, axis=-1, keepdims=True))
        mixed = jnp.einsum('tagk,kad->tagd', low(share), values, precision=HIGH)
        return mixed.reshape(size, HQ * DH)
    outcome = lax.map(jax.checkpoint(one_block), (query.reshape(count, size, HQ, DH), document.reshape(count, size), place.reshape(count, size)))
    return outcome.reshape(length, HQ * DH)

def layer(inputs, query_codes, pair_codes, output_codes, gate_codes, down_codes, query_scale, key_value_scale, output_scale, gate_up_scale, down_scale, norm_gains, doc_ids, padding, token_order):

    def one_pack(operands):
        rows, document, padded, place = operands
        length = rows.shape[0]
        cosine, sine = angles(place)
        first_input = low(norm_gain(rows, norm_gains[0]))
        query_plain = scaled_product(first_input, query_codes, query_scale)
        pair_plain = scaled_product(first_input, pair_codes, key_value_scale)
        query = low(rotate(query_plain.reshape(length, HQ, DH), cosine, sine))
        keys = low(rotate(pair_plain[:, :HK * DH].reshape(length, HK, DH), cosine, sine))
        values = low(pair_plain[:, HK * DH:].reshape(length, HK, DH))
        mixed = low(low_back(attend(query, keys, values, document, padded, place)))
        branch = scaled_product(mixed, output_codes, output_scale)
        middle = rows + norm_gain(branch, norm_gains[1])
        second_input = low(norm_gain(middle, norm_gains[2]))
        gate_up = scaled_product(second_input, gate_codes, gate_up_scale)
        hidden = low(jax.nn.gelu(gate_up[:, :FF], approximate=True) * gate_up[:, FF:])
        down = scaled_product(hidden, down_codes, down_scale)
        return middle + norm_gain(down, norm_gains[3])
    return lax.map(one_pack, (inputs, doc_ids, padding, token_order))

def sliced(code, step):
    return jnp.floor(code / step) * step + step / 2.0

def reference(tokens, doc_ids, padding, token_order, query_code, key_value_code, output_code, gate_up_code, down_code, query_scale, key_value_scale, output_scale, gate_up_scale, down_scale, norm_gains, cotangent):
    primals = (tokens.astype(jnp.float32), query_code.astype(jnp.float32), key_value_code.astype(jnp.float32), output_code.astype(jnp.float32), sliced(gate_up_code.astype(jnp.float32), 16.0), sliced(down_code.astype(jnp.float32), 64.0), query_scale, key_value_scale, output_scale, gate_up_scale, down_scale, norm_gains)

    def forward(inputs, query_codes, pair_codes, output_codes, gate_codes, down_codes, scale_query, scale_pair, scale_output, scale_gate, scale_down, gains):
        return layer(inputs, query_codes, pair_codes, output_codes, gate_codes, down_codes, scale_query, scale_pair, scale_output, scale_gate, scale_down, gains, doc_ids, padding, token_order)
    result, pull = jax.vjp(forward, *primals)
    grads = pull(cotangent.astype(jnp.float32))
    return (result.astype(jnp.bfloat16), grads[0], grads[1], grads[2], grads[3], grads[4], grads[5], grads[6], grads[7], grads[8], grads[9], grads[10], grads[11])
```

```python
import functools
import math

import jax
import jax.numpy as jnp
from jax import lax
from jax.experimental import pallas as pl
from jax.experimental.pallas import tpu as pltpu
from jax.sharding import PartitionSpec as P

HQ = 8
HK = 4
DH = 256
FF = 9216
GROUP = 4
EPSILON = 1e-06
CAP = 50.0
BASE = 10000.0
VMEM_LIMIT = 56 * 1024 * 1024
MESH = pl.DeviceIdType.MESH
ANY = pl.BlockSpec(memory_space=pl.ANY)
VMEM = pl.BlockSpec(memory_space=pltpu.VMEM)
DMA = pltpu.SemaphoreType.DMA
F32 = jnp.float32
BF16 = jnp.bfloat16


def dot(left, right):
    return jnp.dot(left, right, preferred_element_type=F32)


def contract_last(left, right):
    return lax.dot_general(left, right, (((1,), (1,)), ((), ())), preferred_element_type=F32)


def contract_first(left, right):
    return lax.dot_general(left, right, (((0,), (0,)), ((), ())), preferred_element_type=F32)


def place_now():
    seq = lax.axis_index("seq")
    fsdp = lax.axis_index("fsdp")
    return seq, fsdp, fsdp // 2, fsdp % 2


def greet(peers):
    barrier = pltpu.get_barrier_semaphore()
    for peer in peers:
        pl.semaphore_signal(barrier, inc=1, device_id=peer, device_id_type=MESH)
    pl.semaphore_wait(barrier, len(peers))


def remote(src, dst, send, recv, peer):
    return pltpu.make_async_remote_copy(
        src_ref=src, dst_ref=dst, send_sem=send, recv_sem=recv, device_id=peer, device_id_type=MESH
    )


def comm_call(kernel, cid, out_shape, scratch, in_specs, out_specs):
    return pl.pallas_call(
        kernel,
        out_shape=out_shape,
        in_specs=in_specs,
        out_specs=out_specs,
        scratch_shapes=scratch,
        compiler_params=pltpu.CompilerParams(
            collective_id=cid, has_side_effects=True, vmem_limit_bytes=VMEM_LIMIT
        ),
    )


def group_gather_kernel(count, columns, parts, *refs):
    ins = refs[:count]
    outs = refs[count : 2 * count]
    local, xs, xr, cs, cr, fs, fr = refs[2 * count :]
    seq, me, x, c = place_now()
    across = (seq, (1 - x) * 2 + c)
    beside = (seq, x * 2 + 1 - c)
    greet([across, beside])
    waits = []
    forwards = []
    for i in range(count):
        src, out = ins[i], outs[i]
        rows = src.shape[0]
        step = rows // parts[i]

        def spot(owner, start, size, out=out, i=i):
            if columns[i]:
                width = out.shape[1] // GROUP
                return out.at[pl.ds(start, size), pl.ds(owner * width, width)]
            return out.at[owner, pl.ds(start, size)]

        own = pltpu.make_async_copy(src, spot(me, 0, rows), local.at[i])
        for k in range(parts[i]):
            part = src.at[pl.ds(k * step, step)]
            there = spot(me, k * step, step)
            copy = remote(part, there, xs.at[i, k], xr.at[i, k], across)
            copy.start()
            waits.append(copy.wait_send)
            got = spot((1 - x) * 2 + c, k * step, step)
            forwards.append((copy, remote(got, got, fs.at[i, k], fr.at[i, k], beside)))
        copy = remote(src, spot(me, 0, rows), cs.at[i], cr.at[i], beside)
        copy.start()
        own.start()
        waits += [copy.wait, own.wait]
    for copy, forward in forwards:
        copy.wait_recv()
        forward.start()
        waits.append(forward.wait)
    for wait in waits:
        wait()


def group_gather(cid, values, columns=None, parts=None):
    count = len(values)
    columns = columns or [False] * count
    parts = parts or [4] * count
    most = max(parts)
    shapes = [
        jax.ShapeDtypeStruct(
            (v.shape[0], v.shape[1] * GROUP) if col else (GROUP,) + v.shape, v.dtype
        )
        for v, col in zip(values, columns)
    ]
    return comm_call(
        functools.partial(group_gather_kernel, count, tuple(columns), tuple(parts)),
        cid,
        shapes,
        [DMA((count,)), DMA((count, most)), DMA((count, most)), DMA((count,)), DMA((count,)),
         DMA((count, most)), DMA((count, most))],
        [ANY] * count,
        [ANY] * count,
    )(*values)


def group_reduce_kernel(parts, src, out, from_core, to_x, from_x, cs, cr, xs, xr):
    seq, me, x, c = place_now()
    across = (seq, (1 - x) * 2 + c)
    beside = (seq, x * 2 + 1 - c)
    greet([across, beside])
    rows = src.shape[1]
    step = rows // parts
    order = [1 - x, x]
    cores = []
    for i in range(2):
        for k in range(parts):
            span = pl.ds(k * step, step)
            copy = remote(
                src.at[order[i] * 2 + 1 - c, span], from_core.at[i, span], cs.at[i, k], cr.at[i, k], beside
            )
            copy.start()
            cores.append(copy)
    sends = []
    for k in range(parts):
        span = pl.ds(k * step, step)
        cores[k].wait_recv()
        to_x[span, :] = (
            src[order[0] * 2 + c, span, :].astype(F32) + from_core[0, span, :].astype(F32)
        ).astype(BF16)
        copy = remote(to_x.at[span], from_x.at[span], xs.at[k], xr.at[k], across)
        copy.start()
        sends.append(copy)
    for k in range(parts):
        span = pl.ds(k * step, step)
        cores[parts + k].wait_recv()
        sends[k].wait_recv()
        out[span, :] = (
            src[order[1] * 2 + c, span, :].astype(F32)
            + from_core[1, span, :].astype(F32)
            + from_x[span, :].astype(F32)
        ).astype(out.dtype)
    for copy in cores + sends:
        copy.wait_send()


def group_reduce(cid, value, dtype, parts=4):
    rows, width = value.shape[1:]
    return comm_call(
        functools.partial(group_reduce_kernel, parts),
        cid,
        jax.ShapeDtypeStruct((rows, width), dtype),
        [pltpu.VMEM((2, rows, width), BF16), pltpu.VMEM((rows, width), BF16), pltpu.VMEM((rows, width), BF16),
         DMA((2, parts)), DMA((2, parts)), DMA((parts,)), DMA((parts,))],
        [VMEM],
        VMEM,
    )(value)


def group_exchange_kernel(src, out, local, ss, rs):
    seq, me, x, c = place_now()
    peers = [(seq, lax.rem(me + d, GROUP)) for d in range(1, GROUP)]
    greet(peers)
    copies = []
    for d in (2, 1, 3):
        peer = peers[d - 1]
        copy = remote(src.at[peer[1]], out.at[me], ss.at[d - 1], rs.at[d - 1], peer)
        copy.start()
        copies.append(copy)
    own = pltpu.make_async_copy(src.at[me], out.at[me], local)
    own.start()
    for copy in copies:
        copy.wait()
    own.wait()


def group_exchange(cid, value):
    return comm_call(
        group_exchange_kernel,
        cid,
        jax.ShapeDtypeStruct(value.shape, value.dtype),
        [DMA, DMA((GROUP - 1,)), DMA((GROUP - 1,))],
        [ANY],
        ANY,
    )(value)


def keys_gather_kernel(n, heads, meta, cot, out, metas, cots, own_sem, hs, hr, ms, mr, rs, rr, ls, lr, ys, yr,
                       local, xs, xr, cs, cr, fs, fr):
    seq, me, x, c = place_now()
    y = seq % 2
    z = seq // 2
    nz = n // 2
    across = (seq, (1 - x) * 2 + c)
    beside = (seq, x * 2 + 1 - c)
    peers = [(seq, lax.rem(me + d, GROUP)) for d in range(1, GROUP)]
    peers += [(lax.rem(seq + d, n), me) for d in range(1, n)]
    greet(peers)
    for j in range(2):
        target = c * 2 + j

        @pl.when(target == me)
        def _():
            pltpu.make_async_copy(heads.at[j], out.at[seq, x], own_sem.at[0]).start()

        @pl.when(target != me)
        def _():
            remote(heads.at[j], out.at[seq, x], hs.at[j], hr.at[x], (seq, target)).start()

    small = []
    for d in range(1, n):
        copy = remote(meta, metas.at[seq], ms.at[d - 1], mr.at[d - 1], (lax.rem(seq + d, n), me))
        copy.start()
        small.append(copy)
    own_meta = pltpu.make_async_copy(meta, metas.at[seq], own_sem.at[1])
    own_meta.start()
    for t in range(2):
        source = t * 2 + x

        @pl.when(source == me)
        def _():
            pltpu.make_async_copy(heads.at[0], out.at[seq, t], own_sem.at[0]).wait()

        @pl.when(source != me)
        def _():
            remote(heads.at[0], out.at[seq, t], hs.at[0], hr.at[t], (seq, source)).wait_recv()

    def block(owner_z, owner_y):
        return out.at[owner_z * 2 + owner_y]

    right = (seq + 2, me)
    left = (seq - 2, me)
    beyond = (z * 2 + 1 - y, me)

    def to_y(owner_z):
        remote(block(owner_z, y), block(owner_z, y), ys.at[owner_z], yr.at[owner_z], beyond).start()

    rows = cot.shape[0]
    parts = 2
    step = rows // parts

    for t in range(1, nz + 1):
        go_right = z - t + 1
        go_left = z + t - 1
        if t > 1:

            @pl.when(go_right >= 0)
            def _():
                remote(block(go_right, y), block(go_right, y), rs.at[t - 1], rr.at[t - 1], left).wait_recv()

            @pl.when(go_left < nz)
            def _():
                remote(block(go_left, y), block(go_left, y), ls.at[t - 1], lr.at[t - 1], right).wait_recv()

        if t < nz:

            @pl.when((go_right >= 0) & (z < nz - 1))
            def _():
                remote(block(go_right, y), block(go_right, y), rs.at[t], rr.at[t], right).start()

            @pl.when((go_left < nz) & (z > 0))
            def _():
                remote(block(go_left, y), block(go_left, y), ls.at[t], lr.at[t], left).start()

        @pl.when(go_right >= 0)
        def _():
            to_y(go_right)

        if t > 1:

            @pl.when(go_left < nz)
            def _():
                to_y(go_left)

        if t == 1:
            xcopies = []
            for k in range(parts):
                part = pl.ds(k * step, step)
                copy = remote(cot.at[part], cots.at[me, part], xs.at[k], xr.at[k], across)
                copy.start()
                xcopies.append(copy)
            ccopy = remote(cot, cots.at[me], cs, cr, beside)
            ccopy.start()
            own_cot = pltpu.make_async_copy(cot, cots.at[me], local)
            own_cot.start()
    forwards = []
    for k in range(parts):
        part = pl.ds(k * step, step)
        xcopies[k].wait()
        got = cots.at[(1 - x) * 2 + c, part]
        forward = remote(got, got, fs.at[k], fr.at[k], beside)
        forward.start()
        forwards.append(forward)
    for k in range(nz):
        remote(block(k, 1 - y), block(k, 1 - y), ys.at[k], yr.at[k], beyond).wait()
    for t in range(1, nz):

        @pl.when((z - t + 1 >= 0) & (z < nz - 1))
        def _():
            remote(block(z, y), block(z, y), rs.at[t], rr.at[t], right).wait_send()

        @pl.when((z + t - 1 < nz) & (z > 0))
        def _():
            remote(block(z, y), block(z, y), ls.at[t], lr.at[t], left).wait_send()

    for j in range(2):

        @pl.when(c * 2 + j != me)
        def _():
            remote(heads.at[j], out.at[seq, x], hs.at[j], hr.at[x], (seq, c * 2 + j)).wait_send()

    for copy in small + forwards + [ccopy]:
        copy.wait()
    own_meta.wait()
    own_cot.wait()


def keys_gather(cid, n, heads, meta, cot):
    nz = n // 2
    return comm_call(
        functools.partial(keys_gather_kernel, n),
        cid,
        [
            jax.ShapeDtypeStruct((n,) + heads.shape, BF16),
            jax.ShapeDtypeStruct((n,) + meta.shape, F32),
            jax.ShapeDtypeStruct((GROUP,) + cot.shape, BF16),
        ],
        [DMA((2,)), DMA((2,)), DMA((2,)), DMA((n - 1,)), DMA((n - 1,)), DMA((nz,)), DMA((nz,)), DMA((nz,)),
         DMA((nz,)), DMA((nz,)), DMA((nz,)), DMA, DMA((2,)), DMA((2,)), DMA, DMA, DMA((2,)), DMA((2,))],
        [ANY] * 3,
        [ANY] * 3,
    )(heads, meta, cot)


def keys_reduce_kernel(n, src, out, y_got, r_got, l_got, r_out, l_out, moved, ys, yr, rs, rr, ls, lr, hs, hr, local):
    seq, me, x, c = place_now()
    y = seq % 2
    z = seq // 2
    nz = n // 2
    right = (seq + 2, me)
    left = (seq - 2, me)
    beyond = (z * 2 + 1 - y, me)
    barrier = pltpu.get_barrier_semaphore()
    for d in range(1, GROUP):
        pl.semaphore_signal(barrier, inc=1, device_id=(seq, lax.rem(me + d, GROUP)), device_id_type=MESH)
    pl.semaphore_signal(barrier, inc=1, device_id=beyond, device_id_type=MESH)

    @pl.when(z > 0)
    def _():
        pl.semaphore_signal(barrier, inc=1, device_id=left, device_id_type=MESH)

    @pl.when(z < nz - 1)
    def _():
        pl.semaphore_signal(barrier, inc=1, device_id=right, device_id_type=MESH)

    chain = jnp.where(z > 0, 1, 0) + jnp.where(z < nz - 1, 1, 0)
    pl.semaphore_wait(barrier, GROUP + chain)

    def swap(k):
        return remote(src.at[k * 2 + 1 - y], y_got.at[k], ys.at[k], yr.at[k], beyond)

    for t in range(1, nz):
        go_right = z + nz - t
        go_left = z - nz + t

        @pl.when(go_right < nz)
        def _():
            swap(go_right).start()

        @pl.when(go_left >= 0)
        def _():
            swap(go_left).start()

    swap(z).start()

    def pair_sum(k, more, to):
        def body(i, carry):
            half = i // 2
            span = pl.ds(pl.multiple_of((i % 2) * 256, 256), 256)
            total = src[k * 2 + y, half, span, :].astype(F32) + y_got[k, half, span, :].astype(F32)
            for ref in more:
                total = total + ref[half, span, :].astype(F32)
            to[half, span, :] = total.astype(BF16)
            return carry

        lax.fori_loop(0, 4, body, 0)

    for t in range(1, nz):
        go_right = z + nz - t
        go_left = z - nz + t

        @pl.when(go_right < nz)
        def _():
            swap(go_right).wait_recv()
            if t == 1:
                pair_sum(go_right, [], r_out.at[t - 1])
            else:

                @pl.when(z > 0)
                def _():
                    remote(r_out.at[t - 1], r_got.at[t - 2], rs.at[t - 2], rr.at[t - 2], left).wait_recv()
                    pair_sum(go_right, [r_got.at[t - 2]], r_out.at[t - 1])

                @pl.when(z == 0)
                def _():
                    pair_sum(go_right, [], r_out.at[t - 1])

            remote(r_out.at[t - 1], r_got.at[t - 1], rs.at[t - 1], rr.at[t - 1], right).start()

        @pl.when(go_left >= 0)
        def _():
            swap(go_left).wait_recv()
            if t == 1:
                pair_sum(go_left, [], l_out.at[t - 1])
            else:

                @pl.when(z < nz - 1)
                def _():
                    remote(l_out.at[t - 1], l_got.at[t - 2], ls.at[t - 2], lr.at[t - 2], right).wait_recv()
                    pair_sum(go_left, [l_got.at[t - 2]], l_out.at[t - 1])

                @pl.when(z == nz - 1)
                def _():
                    pair_sum(go_left, [], l_out.at[t - 1])

            remote(l_out.at[t - 1], l_got.at[t - 1], ls.at[t - 1], lr.at[t - 1], left).start()

    swap(z).wait_recv()
    last = nz - 2

    def got_left():
        remote(r_out.at[last], r_got.at[last], rs.at[last], rr.at[last], left).wait_recv()

    def got_right():
        remote(l_out.at[last], l_got.at[last], ls.at[last], lr.at[last], right).wait_recv()

    @pl.when(z == 0)
    def _():
        got_right()
        pair_sum(z, [l_got.at[last]], moved)

    @pl.when(z == nz - 1)
    def _():
        got_left()
        pair_sum(z, [r_got.at[last]], moved)

    @pl.when((z > 0) & (z < nz - 1))
    def _():
        got_left()
        got_right()
        pair_sum(z, [r_got.at[last], l_got.at[last]], moved)

    for t in range(2):
        target = t * 2 + x

        @pl.when(target == me)
        def _():
            pltpu.make_async_copy(moved.at[t], out.at[c], local).start()

        @pl.when(target != me)
        def _():
            remote(moved.at[t], out.at[c], hs.at[t], hr.at[c], (seq, target)).start()

    for j in range(2):
        source = c * 2 + j

        @pl.when(source == me)
        def _():
            pltpu.make_async_copy(moved.at[0], out.at[j], local).wait()

        @pl.when(source != me)
        def _():
            remote(moved.at[0], out.at[j], hs.at[0], hr.at[j], (seq, source)).wait_recv()

    for t in range(2):

        @pl.when(t * 2 + x != me)
        def _():
            remote(moved.at[t], out.at[c], hs.at[t], hr.at[c], (seq, t * 2 + x)).wait_send()

    for k in range(nz):
        swap(k).wait_send()
    for t in range(1, nz):

        @pl.when(z + nz - t < nz)
        def _():
            remote(r_out.at[t - 1], r_got.at[t - 1], rs.at[t - 1], rr.at[t - 1], right).wait_send()

        @pl.when(z - nz + t >= 0)
        def _():
            remote(l_out.at[t - 1], l_got.at[t - 1], ls.at[t - 1], lr.at[t - 1], left).wait_send()


def keys_reduce(cid, n, value):
    nz = n // 2
    shape = value.shape[1:]
    chain = pltpu.VMEM((nz - 1,) + shape, BF16)
    return comm_call(
        functools.partial(keys_reduce_kernel, n),
        cid,
        jax.ShapeDtypeStruct(shape, BF16),
        [pltpu.VMEM((nz,) + shape, BF16), chain, chain, chain, chain, pltpu.VMEM(shape, BF16),
         DMA((nz,)), DMA((nz,)), DMA((nz - 1,)), DMA((nz - 1,)), DMA((nz - 1,)), DMA((nz - 1,)),
         DMA((2,)), DMA((2,)), DMA],
        [VMEM],
        VMEM,
    )(value)


def total_kernel(rounds, whole, part, whole_out, part_out, bufs, gots, mine, theirs, ss, rs):
    seq, me, x, c = place_now()
    across = (seq, (1 - x) * 2 + c)
    beside = (seq, x * 2 + 1 - c)
    partners = []
    for r in range(rounds):
        bit = 1 << r
        partners.append((seq + bit - 2 * bit * ((seq // bit) % 2), me))
    greet(partners + [across, beside])
    rows = whole.shape[0]
    bufs[0, :rows, :] = whole[...]
    bufs[0, rows:, :] = part[...]
    for r in range(rounds + 1):
        partner = partners[r] if r < rounds else across
        copy = remote(bufs.at[r], gots.at[r], ss.at[r], rs.at[r], partner)
        copy.start()
        copy.wait()
        if r < rounds:
            bufs[r + 1] = bufs[r] + gots[r]
    mine[0, :rows, :] = bufs[rounds, :rows, :] + gots[rounds, :rows, :]
    mine[0, rows:, :] = bufs[rounds, rows:, :]
    mine[1, rows:, :] = gots[rounds, rows:, :]
    mine[1, :rows, :] = jnp.zeros_like(whole)
    copy = remote(mine, theirs, ss.at[rounds + 1], rs.at[rounds + 1], beside)
    copy.start()
    copy.wait()
    whole_out[...] = mine[0, :rows, :] + theirs[0, :rows, :]
    part_out[x * 2 + c] = mine[0, rows:, :]
    part_out[(1 - x) * 2 + c] = mine[1, rows:, :]
    part_out[x * 2 + 1 - c] = theirs[0, rows:, :]
    part_out[(1 - x) * 2 + 1 - c] = theirs[1, rows:, :]


def totals(cid, n, whole, part):
    rounds = int(math.log2(n))
    rows = whole.shape[0] + part.shape[0]
    return comm_call(
        functools.partial(total_kernel, rounds),
        cid,
        [jax.ShapeDtypeStruct(whole.shape, F32), jax.ShapeDtypeStruct((GROUP,) + part.shape, F32)],
        [pltpu.VMEM((rounds + 1, rows, 128), F32), pltpu.VMEM((rounds + 1, rows, 128), F32),
         pltpu.VMEM((2, rows, 128), F32), pltpu.VMEM((2, rows, 128), F32),
         DMA((rounds + 2,)), DMA((rounds + 2,))],
        [VMEM, VMEM],
        [VMEM, VMEM],
    )(whole, part)


def masks(n, own_ref, meta_ref):
    def column(row):
        return jnp.broadcast_to(own_ref[0, row : row + 1, :], (128, 128)).T

    row_document = column(0)
    row_place = column(1)
    out = []
    for j in range(n):
        key_place = meta_ref[j, 0, 1:2, :]
        key_document = meta_ref[j, 0, 2:3, :]
        allowed = (row_document == key_document) & (key_place <= row_place) | (key_place == row_place)
        out.append(allowed)
    return out


def attend_kernel(n, q_ref, kv_ref, own_ref, meta_ref, low_ref, mixed_ref, total_ref):
    keys = kv_ref[:, 0].reshape(n * 128, DH)
    values = kv_ref[:, 1].reshape(n * 128, DH)
    allowed = masks(n, own_ref, meta_ref)
    for h in range(2):
        cols = slice(h * DH, (h + 1) * DH)
        raw = contract_last(q_ref[:, cols], keys)
        pieces = []
        total = jnp.zeros((128, 128), F32)
        for j in range(n):
            squash = jnp.tanh(raw[:, j * 128 : (j + 1) * 128] * (DH ** (-0.5) / CAP))
            mass = jnp.where(allowed[j], jnp.exp(CAP * squash), 0.0)
            total = total + mass
            pieces.append(mass.astype(BF16))
        row = jnp.sum(total, axis=1, keepdims=True)
        mixed = dot(jnp.concatenate(pieces, axis=1), values) / row
        mixed_ref[:, cols] = mixed
        low_ref[:, cols] = mixed.astype(BF16)
        total_ref[:, h * 128 : (h + 1) * 128] = jnp.broadcast_to(row, (128, 128))


def attend(n, query, pairs, own_meta, metas):
    return pl.pallas_call(
        functools.partial(attend_kernel, n),
        grid=(GROUP,),
        out_shape=[
            jax.ShapeDtypeStruct(query.shape, BF16),
            jax.ShapeDtypeStruct(query.shape, F32),
            jax.ShapeDtypeStruct((query.shape[0], 256), F32),
        ],
        in_specs=[
            pl.BlockSpec((128, 2 * DH), lambda p: (p, 0)),
            pl.BlockSpec((n, 2, 128, DH), lambda p: (0, 0, p, 0)),
            pl.BlockSpec((1, 8, 128), lambda p: (p, 0, 0)),
            pl.BlockSpec((n, 1, 8, 128), lambda p: (0, p, 0, 0)),
        ],
        out_specs=[
            pl.BlockSpec((128, 2 * DH), lambda p: (p, 0)),
            pl.BlockSpec((128, 2 * DH), lambda p: (p, 0)),
            pl.BlockSpec((128, 256), lambda p: (p, 0)),
        ],
        compiler_params=pltpu.CompilerParams(vmem_limit_bytes=VMEM_LIMIT),
    )(query, pairs, own_meta, metas)


def attend_back_kernel(n, q_ref, kv_ref, own_ref, meta_ref, mixed_ref, total_ref, grad_ref, dq_ref, dkv_ref):
    keys = kv_ref[:, 0].reshape(n * 128, DH)
    values = kv_ref[:, 1].reshape(n * 128, DH)
    allowed = masks(n, own_ref, meta_ref)
    grad_keys = None
    for h in range(2):
        cols = slice(h * DH, (h + 1) * DH)
        query = q_ref[:, cols]
        grad = grad_ref[:, cols]
        delta = jnp.sum(grad.astype(F32) * mixed_ref[:, cols], axis=1, keepdims=True)
        inverse = 1.0 / total_ref[:, h * 128 : (h + 1) * 128]
        raw = contract_last(query, keys)
        grad_share = contract_last(grad, values)
        shares = []
        grads = []
        for j in range(n):
            span = slice(j * 128, (j + 1) * 128)
            squash = jnp.tanh(raw[:, span] * (DH ** (-0.5) / CAP))
            share = jnp.where(allowed[j], jnp.exp(CAP * squash), 0.0) * inverse
            shares.append(share.astype(BF16))
            grads.append(
                (share * (grad_share[:, span] - delta) * ((1.0 - squash * squash) * DH ** (-0.5))).astype(BF16)
            )
        share = jnp.concatenate(shares, axis=1)
        grad_raw = jnp.concatenate(grads, axis=1)
        dq_ref[:, cols] = dot(grad_raw, keys)
        new_keys = contract_first(grad_raw, query)
        new_values = contract_first(share, grad)
        if grad_keys is None:
            grad_keys, grad_values = new_keys, new_values
        else:
            grad_keys, grad_values = grad_keys + new_keys, grad_values + new_values
    dkv_ref[:, 0] = grad_keys.astype(BF16).reshape(n, 128, DH)
    dkv_ref[:, 1] = grad_values.astype(BF16).reshape(n, 128, DH)


def attend_back(n, query, pairs, own_meta, metas, mixed, total, grad):
    rows = pl.BlockSpec((128, 2 * DH), lambda p: (p, 0))
    heads = pl.BlockSpec((n, 2, 128, DH), lambda p: (0, 0, p, 0))
    return pl.pallas_call(
        functools.partial(attend_back_kernel, n),
        grid=(GROUP,),
        out_shape=[
            jax.ShapeDtypeStruct(query.shape, F32),
            jax.ShapeDtypeStruct(pairs.shape, BF16),
        ],
        in_specs=[
            rows,
            heads,
            pl.BlockSpec((1, 8, 128), lambda p: (p, 0, 0)),
            pl.BlockSpec((n, 1, 8, 128), lambda p: (0, p, 0, 0)),
            rows,
            pl.BlockSpec((128, 256), lambda p: (p, 0)),
            rows,
        ],
        out_specs=[rows, heads],
        compiler_params=pltpu.CompilerParams(vmem_limit_bytes=VMEM_LIMIT),
    )(query, pairs, own_meta, metas, mixed, total, grad)


def rms_inverse(value):
    return lax.rsqrt(jnp.mean(value * value, axis=-1, keepdims=True) + EPSILON)


def norm_back(inverse, normed, upstream):
    return inverse * (upstream - normed * jnp.mean(upstream * normed, axis=-1, keepdims=True))


def rotate(value, cosine, sine):
    half = DH // 2
    first = value[..., :half]
    second = value[..., half:]
    return jnp.concatenate([first * cosine - second * sine, second * cosine + first * sine], axis=-1)


def code_levels(code, step):
    levels = code.astype(F32)
    return (jnp.floor(levels / step) * step + step / 2.0).astype(BF16)


def gelu_parts(gate):
    root = math.sqrt(2.0 / math.pi)
    square = gate * gate
    bend = jnp.tanh(root * gate * (1.0 + 0.044715 * square))
    value = 0.5 * gate * (1.0 + bend)
    slope = 0.5 * (1.0 + bend) + 0.5 * gate * (1.0 - bend * bend) * root * (1.0 + 3 * 0.044715 * square)
    return value, slope


def seq_swap(value, n):
    return lax.ppermute(value, "seq", [(s, s ^ 1) for s in range(n)])


def x_swap(value):
    return lax.ppermute(value, "fsdp", [(f, f ^ 2) for f in range(GROUP)])


def core_swap(value):
    return lax.ppermute(value, "fsdp", [(f, f ^ 1) for f in range(GROUP)])


def pair_rows(value, n, y):
    rows, width = value.shape
    split = value.reshape(rows, n // 2, 2, width // n)
    here = lax.dynamic_index_in_dim(split, y, 2, keepdims=False).reshape(rows, width // 2)
    there = lax.dynamic_index_in_dim(split, 1 - y, 2, keepdims=False).reshape(rows, width // 2)
    return here, seq_swap(there, n)


def chain_sum(block, n, z):
    nz = n // 2
    pick = lambda k: lax.dynamic_index_in_dim(block, jnp.clip(k, 0, nz - 1), 0, keepdims=False)
    from_left = from_right = None
    for t in range(1, nz):
        right = pick(z + nz - t)
        left = pick(z - nz + t)
        if t > 1:
            right = (right.astype(F32) + from_left.astype(F32)).astype(BF16)
            left = (left.astype(F32) + from_right.astype(F32)).astype(BF16)
        go_right = [(s, s + 2) for s in range(2 * t)]
        go_left = [(n - 1 - s, n - 3 - s) for s in range(2 * t)]
        from_left = lax.ppermute(right, "seq", go_right)
        from_right = lax.ppermute(left, "seq", go_left)
    return pick(z).astype(F32) + from_left.astype(F32) + from_right.astype(F32)


def pair_product(lefts, rights):
    return contract_first(lefts[0], rights[0]) + contract_first(lefts[1], rights[1])


def lanes(value, rows):
    flat = value.reshape(-1)
    return jnp.pad(flat, (0, rows * 128 - flat.shape[0])).reshape(rows, 128)


def per_device(
    n,
    tokens,
    doc_ids,
    padding,
    token_order,
    query_code,
    key_value_code,
    output_code,
    gate_up_code,
    down_code,
    query_scale,
    key_value_scale,
    output_scale,
    gate_up_scale,
    down_scale,
    norm_gains,
    cotangent,
):
    seq = lax.axis_index("seq")
    me = lax.axis_index("fsdp")
    is_gate = me < 2
    c = me % 2
    y = seq % 2
    z = seq // 2
    width = tokens.shape[2]
    part = width // GROUP
    rows = GROUP * tokens.shape[1]
    own = tokens.shape[1]

    def mine(vector):
        size = vector.shape[-1] // GROUP
        return lax.dynamic_slice_in_dim(vector, me * size, size, vector.ndim - 1)

    def blocks_to_rows(blocks):
        return jnp.concatenate([blocks[i] for i in range(GROUP)], axis=1)

    def own_rows(value):
        return lax.dynamic_slice_in_dim(value, me * own, own, 0)

    gain = 1.0 + norm_gains
    place = token_order[0].astype(F32)
    document = doc_ids[0].astype(F32)
    meta = jnp.stack([document, place, jnp.where(padding[0] == 1, document, -1.0)] + [document] * 5)

    token_blocks, own_meta = group_gather(1, [tokens[0], meta], parts=[4, 1])
    inputs = token_blocks.reshape(rows, width).astype(F32)
    turn = own_meta[:, 1, :].reshape(rows, 1) * (
        BASE ** (-2.0 * jnp.arange(DH // 2).astype(F32) / DH)
    )[None, :]
    cosine = jnp.cos(turn)
    sine = jnp.sin(turn)
    first_inverse = rms_inverse(inputs)
    first_input = (inputs * first_inverse * gain[0]).astype(BF16)
    query_raw = dot(first_input, query_code)
    pair_raw = dot(first_input, key_value_code)
    my_query_scale = mine(query_scale)
    my_pair_scale = mine(key_value_scale)
    pair_cosine = jnp.where(is_gate, cosine, 1.0)
    pair_sine = jnp.where(is_gate, sine, 0.0)
    query = rotate(
        (query_raw * my_query_scale).reshape(rows, 2, DH), cosine[:, None], sine[:, None]
    ).astype(BF16).reshape(rows, 2 * DH)
    pair_plain = pair_raw * my_pair_scale
    heads = jnp.stack(
        [rotate(pair_plain[:, j * DH : (j + 1) * DH], pair_cosine, pair_sine) for j in range(2)]
    ).astype(BF16)
    first_pair = pair_rows(first_input, n, y)
    pairs, metas, cot_blocks = keys_gather(2, n, heads, own_meta, cotangent[0])

    mixed_low, mixed, mass = attend(n, query, pairs, own_meta, metas)
    (mixed_rows,) = group_gather(3, [mixed_low], columns=[True])
    mixed_pair = pair_rows(mixed_rows, n, y)
    branch_own = dot(mixed_rows, output_code).astype(BF16)
    (branch_blocks,) = group_gather(4, [branch_own])
    branch_raw = blocks_to_rows(branch_blocks).astype(F32)
    branch = branch_raw * output_scale
    second_inverse = rms_inverse(branch)
    middle = inputs + branch * second_inverse * gain[1]
    third_inverse = rms_inverse(middle)
    second_input = (middle * third_inverse * gain[2]).astype(BF16)
    second_pair = pair_rows(second_input, n, y)

    gate_levels = code_levels(gate_up_code, 16.0)
    down_levels = code_levels(down_code, 64.0)
    my_gate_scale = mine(gate_up_scale)
    columns = gate_levels.shape[1]
    chunks = 4
    size = columns // chunks
    down_split = down_levels.reshape(2, columns, part)
    down_here = lax.dynamic_index_in_dim(down_split, c, 0, keepdims=False)
    down_there = lax.dynamic_index_in_dim(down_split, 1 - c, 0, keepdims=False)
    owns, others, hiddens, hiddens_core = [], [], [], []
    for k in range(chunks):
        span = slice(k * size, (k + 1) * size)
        owns.append((dot(second_input, gate_levels[:, span]) * my_gate_scale[span]).astype(BF16))
        others.append(x_swap(owns[k]))
    down_sum = 0.0
    for k in range(chunks):
        span = slice(k * size, (k + 1) * size)
        gate = jnp.where(is_gate, owns[k], others[k]).astype(F32)
        up = jnp.where(is_gate, others[k], owns[k]).astype(F32)
        hiddens.append((gelu_parts(gate)[0] * up).astype(BF16))
        hiddens_core.append(core_swap(hiddens[k]))
        down_sum = down_sum + dot(hiddens[k], down_here[span]) + dot(hiddens_core[k], down_there[span])
    down_own = down_sum.astype(BF16)
    (down_blocks,) = group_gather(5, [down_own])
    down_raw = blocks_to_rows(down_blocks).astype(F32)
    down = down_raw * down_scale
    fourth_inverse = rms_inverse(down)
    fourth = down * fourth_inverse
    result = own_rows(middle + fourth * gain[3]).astype(BF16)

    grad_result = cot_blocks.reshape(rows, width).astype(F32)
    gain_four = jnp.sum(own_rows(grad_result * fourth), axis=0)
    grad_down_full = norm_back(fourth_inverse, fourth, grad_result * gain[3])
    grad_down_own = lax.dynamic_slice_in_dim(grad_down_full, me * part, part, 1)
    scale_down = jnp.sum(down_own.astype(F32) * grad_down_own, axis=0)
    grad_down = (grad_down_own * mine(down_scale)).astype(BF16)
    grad_down_pair = (grad_down, seq_swap(grad_down, n))

    here = jnp.concatenate(hiddens, axis=1)
    there = jnp.concatenate(hiddens_core, axis=1)
    hidden_rows = jnp.concatenate([jnp.where(c == 0, here, there), jnp.where(c == 0, there, here)], axis=1)
    hidden_pair = pair_rows(hidden_rows, n, y)
    down_block = pair_product(hidden_pair, grad_down_pair).astype(BF16)
    down_grad = chain_sum(down_block.reshape(n // 2, -1, part), n, z)

    grads, gate_sums = [], []
    grad_second_sum = 0.0
    core_gots = []
    for k in range(chunks):
        span = slice(k * size, (k + 1) * size)
        core_gots.append(core_swap(contract_last(grad_down, down_there[span]).astype(BF16)))
    sums, x_gots = [], []
    for k in range(chunks):
        span = slice(k * size, (k + 1) * size)
        sums.append((contract_last(grad_down, down_here[span]) + core_gots[k].astype(F32)).astype(BF16))
        x_gots.append(x_swap(sums[k]))
    for k in range(chunks):
        span = slice(k * size, (k + 1) * size)
        grad_hidden = sums[k].astype(F32) + x_gots[k].astype(F32)
        gate = jnp.where(is_gate, owns[k], others[k]).astype(F32)
        up = jnp.where(is_gate, others[k], owns[k]).astype(F32)
        value, slope = gelu_parts(gate)
        grad_full = grad_hidden * jnp.where(is_gate, up * slope, value)
        gate_sums.append(jnp.sum(owns[k].astype(F32) * grad_full, axis=0) / my_gate_scale[span])
        grads.append((grad_full * my_gate_scale[span]).astype(BF16))
        grad_second_sum = grad_second_sum + contract_last(grads[k], gate_levels[:, span])
    scale_gate = jnp.concatenate(gate_sums)
    grad_gate_up = jnp.concatenate(grads, axis=1)
    grad_gate_pair = (grad_gate_up, seq_swap(grad_gate_up, n))

    grad_second_input = group_reduce(6, grad_second_sum.astype(BF16).reshape(GROUP, own, width), F32)
    gate_block = pair_product(second_pair, grad_gate_pair).astype(BF16)
    gate_grad = chain_sum(gate_block.reshape(n // 2, -1, columns), n, z)

    my_middle = own_rows(middle)
    third_inverse = own_rows(third_inverse)
    second_inverse = own_rows(second_inverse)
    my_branch_raw = own_rows(branch_raw)
    third = my_middle * third_inverse
    second = my_branch_raw * output_scale * second_inverse
    my_cot = cotangent[0].astype(F32)
    gain_three = jnp.sum(grad_second_input * third, axis=0)
    grad_middle = my_cot + norm_back(third_inverse, third, grad_second_input * gain[2])
    gain_two = jnp.sum(grad_middle * second, axis=0)
    grad_branch_full = norm_back(second_inverse, second, grad_middle * gain[1])
    scale_output = jnp.sum(my_branch_raw * grad_branch_full, axis=0)
    grad_branch_own = (grad_branch_full * output_scale).astype(BF16)
    grad_branch = group_exchange(
        7, grad_branch_own.reshape(own, GROUP, part).transpose(1, 0, 2)
    ).reshape(rows, part)
    grad_branch_pair = (grad_branch, seq_swap(grad_branch, n))
    output_block = pair_product(mixed_pair, grad_branch_pair).astype(BF16)
    output_grad = chain_sum(output_block.reshape(n // 2, -1, part), n, z)
    grad_mixed_sum = jnp.stack(
        [contract_last(grad_branch, output_code[i * 2 * DH : (i + 1) * 2 * DH]) for i in range(GROUP)]
    ).astype(BF16)
    grad_mixed = group_reduce(8, grad_mixed_sum, BF16)

    grad_query, grad_pairs = attend_back(n, query, pairs, own_meta, metas, mixed, mass, grad_mixed)
    grad_heads = keys_reduce(9, n, grad_pairs).astype(F32)
    grad_query_full = rotate(
        grad_query.reshape(rows, 2, DH), cosine[:, None], -sine[:, None]
    ).reshape(rows, 2 * DH)
    scale_query = jnp.sum(query_raw * grad_query_full, axis=0)
    grad_query_low = (grad_query_full * my_query_scale).astype(BF16)
    grad_pair_full = jnp.concatenate(
        [rotate(grad_heads[j], pair_cosine, -pair_sine) for j in range(2)], axis=1
    )
    scale_pair = jnp.sum(pair_raw * grad_pair_full, axis=0)
    grad_pair_low = (grad_pair_full * my_pair_scale).astype(BF16)
    joined = jnp.concatenate([grad_query_low, grad_pair_low], axis=1)
    joined_pair = (joined, seq_swap(joined, n))
    grad_first_sum = contract_last(grad_query_low, query_code) + contract_last(grad_pair_low, key_value_code)
    grad_first_input = group_reduce(10, grad_first_sum.astype(BF16).reshape(GROUP, own, width), F32)
    attention_block = pair_product(first_pair, joined_pair).astype(BF16)
    attention_grad = chain_sum(attention_block.reshape(n // 2, -1, joined.shape[1]), n, z)
    my_inputs = tokens[0].astype(F32)
    my_inverse = rms_inverse(my_inputs)
    first = my_inputs * my_inverse
    gain_one = jnp.sum(grad_first_input * first, axis=0)
    grad_inputs = grad_middle + norm_back(my_inverse, first, grad_first_input * gain[0])

    wholes = jnp.concatenate([gain_one, gain_two, gain_three, gain_four, scale_output])
    parts = [scale_query, scale_pair, scale_gate, scale_down]
    whole_total, part_total = totals(
        11, n, lanes(wholes, 96), lanes(jnp.concatenate(parts), 56)
    )
    whole_total = whole_total.reshape(-1)
    part_total = part_total.reshape(GROUP, -1)
    pieces = []
    start = 0
    for vector in parts:
        pieces.append(part_total[:, start : start + vector.shape[0]].reshape(-1))
        start += vector.shape[0]
    q_width = query_code.shape[1]
    return (
        result[None],
        grad_inputs[None],
        attention_grad[:, :q_width],
        attention_grad[:, q_width:],
        output_grad,
        gate_grad,
        down_grad,
        pieces[0],
        pieces[1],
        whole_total[4 * width : 5 * width],
        pieces[2],
        pieces[3],
        whole_total[: 4 * width].reshape(4, width),
    )


def solution(mesh):
    return jax.shard_map(
        functools.partial(per_device, mesh.shape["seq"]),
        mesh=mesh,
        in_specs=(
            P("fsdp", "seq", None),
            P("fsdp", "seq"),
            P("fsdp", "seq"),
            P("fsdp", "seq"),
            P(None, "fsdp"),
            P(None, "fsdp"),
            P(None, "fsdp"),
            P(None, "fsdp"),
            P(None, "fsdp"),
            P(),
            P(),
            P(),
            P(),
            P(),
            P(),
            P("fsdp", "seq", None),
        ),
        out_specs=(
            P("fsdp", "seq", None),
            P("fsdp", "seq", None),
            P("seq", "fsdp"),
            P("seq", "fsdp"),
            P("seq", "fsdp"),
            P("seq", "fsdp"),
            P("seq", "fsdp"),
            P(),
            P(),
            P(),
            P(),
            P(),
            P(),
        ),
        check_vma=False,
    )
```

```python
import functools
import math

import jax
import jax.numpy as jnp
from jax import lax
from jax.experimental import pallas as pl
from jax.experimental.pallas import tpu as pltpu
from jax.sharding import PartitionSpec as P

HQ = 8
HK = 4
DH = 256
FF = 9216
GROUP = 4
TILE = 384
EPSILON = 1e-06
CAP = 50.0
BASE = 10000.0
VMEM_LIMIT = 60 * 1024 * 1024
MESH = pl.DeviceIdType.MESH
ANY = pl.BlockSpec(memory_space=pl.ANY)
VMEM = pl.BlockSpec(memory_space=pltpu.VMEM)
DMA = pltpu.SemaphoreType.DMA
F32 = jnp.float32
BF16 = jnp.bfloat16


def dot(left, right):
    return jnp.dot(left, right, preferred_element_type=F32)


def contract_last(left, right):
    return lax.dot_general(left, right, (((1,), (1,)), ((), ())), preferred_element_type=F32)


def contract_first(left, right):
    return lax.dot_general(left, right, (((0,), (0,)), ((), ())), preferred_element_type=F32)


def place_now():
    seq = lax.axis_index("seq")
    fsdp = lax.axis_index("fsdp")
    return seq, fsdp, fsdp // 2, fsdp % 2


def greet(peers):
    barrier = pltpu.get_barrier_semaphore()
    for peer in peers:
        pl.semaphore_signal(barrier, inc=1, device_id=peer, device_id_type=MESH)
    pl.semaphore_wait(barrier, len(peers))


def remote(src, dst, send, recv, peer):
    return pltpu.make_async_remote_copy(
        src_ref=src, dst_ref=dst, send_sem=send, recv_sem=recv, device_id=peer, device_id_type=MESH
    )


def comm_call(kernel, cid, out_shape, scratch, in_specs, out_specs):
    return pl.pallas_call(
        kernel,
        out_shape=out_shape,
        in_specs=in_specs,
        out_specs=out_specs,
        scratch_shapes=scratch,
        compiler_params=pltpu.CompilerParams(
            collective_id=cid, has_side_effects=True, vmem_limit_bytes=VMEM_LIMIT
        ),
    )


def group_gather_kernel(count, columns, parts, *refs):
    ins = refs[:count]
    outs = refs[count : 2 * count]
    local, xs, xr, cs, cr, fs, fr = refs[2 * count :]
    seq, me, x, c = place_now()
    across = (seq, (1 - x) * 2 + c)
    beside = (seq, x * 2 + 1 - c)
    greet([across, beside])
    waits = []
    forwards = []
    for i in range(count):
        src, out = ins[i], outs[i]
        rows = src.shape[0]
        step = rows // parts[i]

        def spot(owner, start, size, out=out, i=i):
            if columns[i]:
                width = out.shape[1] // GROUP
                return out.at[pl.ds(start, size), pl.ds(owner * width, width)]
            return out.at[owner, pl.ds(start, size)]

        own = pltpu.make_async_copy(src, spot(me, 0, rows), local.at[i])
        for k in range(parts[i]):
            part = src.at[pl.ds(k * step, step)]
            there = spot(me, k * step, step)
            copy = remote(part, there, xs.at[i, k], xr.at[i, k], across)
            copy.start()
            waits.append(copy.wait_send)
            got = spot((1 - x) * 2 + c, k * step, step)
            forwards.append((copy, remote(got, got, fs.at[i, k], fr.at[i, k], beside)))
        copy = remote(src, spot(me, 0, rows), cs.at[i], cr.at[i], beside)
        copy.start()
        own.start()
        waits += [copy.wait, own.wait]
    for copy, forward in forwards:
        copy.wait_recv()
        forward.start()
        waits.append(forward.wait)
    for wait in waits:
        wait()


def group_gather(cid, values, columns=None, parts=None):
    count = len(values)
    columns = columns or [False] * count
    parts = parts or [4] * count
    most = max(parts)
    shapes = [
        jax.ShapeDtypeStruct(
            (v.shape[0], v.shape[1] * GROUP) if col else (GROUP,) + v.shape, v.dtype
        )
        for v, col in zip(values, columns)
    ]
    return comm_call(
        functools.partial(group_gather_kernel, count, tuple(columns), tuple(parts)),
        cid,
        shapes,
        [DMA((count,)), DMA((count, most)), DMA((count, most)), DMA((count,)), DMA((count,)),
         DMA((count, most)), DMA((count, most))],
        [ANY] * count,
        [ANY] * count,
    )(*values)


def group_reduce_kernel(parts, src, out, from_core, to_x, from_x, cs, cr, xs, xr):
    seq, me, x, c = place_now()
    across = (seq, (1 - x) * 2 + c)
    beside = (seq, x * 2 + 1 - c)
    greet([across, beside])
    rows = src.shape[1]
    step = rows // parts
    order = [1 - x, x]
    cores = []
    for i in range(2):
        for k in range(parts):
            span = pl.ds(k * step, step)
            copy = remote(
                src.at[order[i] * 2 + 1 - c, span], from_core.at[i, span], cs.at[i, k], cr.at[i, k], beside
            )
            copy.start()
            cores.append(copy)
    sends = []
    for k in range(parts):
        span = pl.ds(k * step, step)
        cores[k].wait_recv()
        to_x[span, :] = (
            src[order[0] * 2 + c, span, :].astype(F32) + from_core[0, span, :].astype(F32)
        ).astype(BF16)
        copy = remote(to_x.at[span], from_x.at[span], xs.at[k], xr.at[k], across)
        copy.start()
        sends.append(copy)
    for k in range(parts):
        span = pl.ds(k * step, step)
        cores[parts + k].wait_recv()
        sends[k].wait_recv()
        out[span, :] = (
            src[order[1] * 2 + c, span, :].astype(F32)
            + from_core[1, span, :].astype(F32)
            + from_x[span, :].astype(F32)
        ).astype(out.dtype)
    for copy in cores + sends:
        copy.wait_send()


def group_reduce(cid, value, dtype, parts=4):
    rows, width = value.shape[1:]
    return comm_call(
        functools.partial(group_reduce_kernel, parts),
        cid,
        jax.ShapeDtypeStruct((rows, width), dtype),
        [pltpu.VMEM((2, rows, width), BF16), pltpu.VMEM((rows, width), BF16), pltpu.VMEM((rows, width), BF16),
         DMA((2, parts)), DMA((2, parts)), DMA((parts,)), DMA((parts,))],
        [VMEM],
        VMEM,
    )(value)


def group_exchange_kernel(src, out, local, ss, rs):
    seq, me, x, c = place_now()
    peers = [(seq, lax.rem(me + d, GROUP)) for d in range(1, GROUP)]
    greet(peers)
    copies = []
    for d in (2, 1, 3):
        peer = peers[d - 1]
        copy = remote(src.at[peer[1]], out.at[me], ss.at[d - 1], rs.at[d - 1], peer)
        copy.start()
        copies.append(copy)
    own = pltpu.make_async_copy(src.at[me], out.at[me], local)
    own.start()
    for copy in copies:
        copy.wait()
    own.wait()


def group_exchange(cid, value):
    return comm_call(
        group_exchange_kernel,
        cid,
        jax.ShapeDtypeStruct(value.shape, value.dtype),
        [DMA, DMA((GROUP - 1,)), DMA((GROUP - 1,))],
        [ANY],
        ANY,
    )(value)


def keys_gather_kernel(n, heads, meta, cot, out, metas, cots, own_sem, hs, hr, ms, mr, rs, rr, ls, lr, ys, yr,
                       local, xs, xr, cs, cr, fs, fr):
    seq, me, x, c = place_now()
    y = seq % 2
    z = seq // 2
    nz = n // 2
    across = (seq, (1 - x) * 2 + c)
    beside = (seq, x * 2 + 1 - c)
    peers = [(seq, lax.rem(me + d, GROUP)) for d in range(1, GROUP)]
    peers += [(lax.rem(seq + d, n), me) for d in range(1, n)]
    greet(peers)
    for j in range(2):
        target = c * 2 + j

        @pl.when(target == me)
        def _():
            pltpu.make_async_copy(heads.at[j], out.at[seq, x], own_sem.at[0]).start()

        @pl.when(target != me)
        def _():
            remote(heads.at[j], out.at[seq, x], hs.at[j], hr.at[x], (seq, target)).start()

    small = []
    for d in range(1, n):
        copy = remote(meta, metas.at[seq], ms.at[d - 1], mr.at[d - 1], (lax.rem(seq + d, n), me))
        copy.start()
        small.append(copy)
    own_meta = pltpu.make_async_copy(meta, metas.at[seq], own_sem.at[1])
    own_meta.start()
    for t in range(2):
        source = t * 2 + x

        @pl.when(source == me)
        def _():
            pltpu.make_async_copy(heads.at[0], out.at[seq, t], own_sem.at[0]).wait()

        @pl.when(source != me)
        def _():
            remote(heads.at[0], out.at[seq, t], hs.at[0], hr.at[t], (seq, source)).wait_recv()

    def block(owner_z, owner_y):
        return out.at[owner_z * 2 + owner_y]

    right = (seq + 2, me)
    left = (seq - 2, me)
    beyond = (z * 2 + 1 - y, me)

    def to_y(owner_z):
        remote(block(owner_z, y), block(owner_z, y), ys.at[owner_z], yr.at[owner_z], beyond).start()

    rows = cot.shape[0]
    parts = 2
    step = rows // parts

    for t in range(1, nz + 1):
        go_right = z - t + 1
        go_left = z + t - 1
        if t > 1:

            @pl.when(go_right >= 0)
            def _():
                remote(block(go_right, y), block(go_right, y), rs.at[t - 1], rr.at[t - 1], left).wait_recv()

            @pl.when(go_left < nz)
            def _():
                remote(block(go_left, y), block(go_left, y), ls.at[t - 1], lr.at[t - 1], right).wait_recv()

        if t < nz:

            @pl.when((go_right >= 0) & (z < nz - 1))
            def _():
                remote(block(go_right, y), block(go_right, y), rs.at[t], rr.at[t], right).start()

            @pl.when((go_left < nz) & (z > 0))
            def _():
                remote(block(go_left, y), block(go_left, y), ls.at[t], lr.at[t], left).start()

        @pl.when(go_right >= 0)
        def _():
            to_y(go_right)

        if t > 1:

            @pl.when(go_left < nz)
            def _():
                to_y(go_left)

        if t == 1:
            xcopies = []
            for k in range(parts):
                part = pl.ds(k * step, step)
                copy = remote(cot.at[part], cots.at[me, part], xs.at[k], xr.at[k], across)
                copy.start()
                xcopies.append(copy)
            ccopy = remote(cot, cots.at[me], cs, cr, beside)
            ccopy.start()
            own_cot = pltpu.make_async_copy(cot, cots.at[me], local)
            own_cot.start()
    forwards = []
    for k in range(parts):
        part = pl.ds(k * step, step)
        xcopies[k].wait()
        got = cots.at[(1 - x) * 2 + c, part]
        forward = remote(got, got, fs.at[k], fr.at[k], beside)
        forward.start()
        forwards.append(forward)
    for k in range(nz):
        remote(block(k, 1 - y), block(k, 1 - y), ys.at[k], yr.at[k], beyond).wait()
    for t in range(1, nz):

        @pl.when((z - t + 1 >= 0) & (z < nz - 1))
        def _():
            remote(block(z, y), block(z, y), rs.at[t], rr.at[t], right).wait_send()

        @pl.when((z + t - 1 < nz) & (z > 0))
        def _():
            remote(block(z, y), block(z, y), ls.at[t], lr.at[t], left).wait_send()

    for j in range(2):

        @pl.when(c * 2 + j != me)
        def _():
            remote(heads.at[j], out.at[seq, x], hs.at[j], hr.at[x], (seq, c * 2 + j)).wait_send()

    for copy in small + forwards + [ccopy]:
        copy.wait()
    own_meta.wait()
    own_cot.wait()


def keys_gather(cid, n, heads, meta, cot):
    nz = n // 2
    return comm_call(
        functools.partial(keys_gather_kernel, n),
        cid,
        [
            jax.ShapeDtypeStruct((n,) + heads.shape, BF16),
            jax.ShapeDtypeStruct((n,) + meta.shape, F32),
            jax.ShapeDtypeStruct((GROUP,) + cot.shape, BF16),
        ],
        [DMA((2,)), DMA((2,)), DMA((2,)), DMA((n - 1,)), DMA((n - 1,)), DMA((nz,)), DMA((nz,)), DMA((nz,)),
         DMA((nz,)), DMA((nz,)), DMA((nz,)), DMA, DMA((2,)), DMA((2,)), DMA, DMA, DMA((2,)), DMA((2,))],
        [ANY] * 3,
        [ANY] * 3,
    )(heads, meta, cot)


def keys_reduce_kernel(n, src, out, y_got, r_got, l_got, r_out, l_out, moved, ys, yr, rs, rr, ls, lr, hs, hr, local):
    seq, me, x, c = place_now()
    y = seq % 2
    z = seq // 2
    nz = n // 2
    right = (seq + 2, me)
    left = (seq - 2, me)
    beyond = (z * 2 + 1 - y, me)
    barrier = pltpu.get_barrier_semaphore()
    for d in range(1, GROUP):
        pl.semaphore_signal(barrier, inc=1, device_id=(seq, lax.rem(me + d, GROUP)), device_id_type=MESH)
    pl.semaphore_signal(barrier, inc=1, device_id=beyond, device_id_type=MESH)

    @pl.when(z > 0)
    def _():
        pl.semaphore_signal(barrier, inc=1, device_id=left, device_id_type=MESH)

    @pl.when(z < nz - 1)
    def _():
        pl.semaphore_signal(barrier, inc=1, device_id=right, device_id_type=MESH)

    chain = jnp.where(z > 0, 1, 0) + jnp.where(z < nz - 1, 1, 0)
    pl.semaphore_wait(barrier, GROUP + chain)

    def swap(k):
        return remote(src.at[k * 2 + 1 - y], y_got.at[k], ys.at[k], yr.at[k], beyond)

    for t in range(1, nz):
        go_right = z + nz - t
        go_left = z - nz + t

        @pl.when(go_right < nz)
        def _():
            swap(go_right).start()

        @pl.when(go_left >= 0)
        def _():
            swap(go_left).start()

    swap(z).start()

    def pair_sum(k, more, to):
        def body(i, carry):
            half = i // 2
            span = pl.ds(pl.multiple_of((i % 2) * 256, 256), 256)
            total = src[k * 2 + y, half, span, :].astype(F32) + y_got[k, half, span, :].astype(F32)
            for ref in more:
                total = total + ref[half, span, :].astype(F32)
            to[half, span, :] = total.astype(BF16)
            return carry

        lax.fori_loop(0, 4, body, 0)

    for t in range(1, nz):
        go_right = z + nz - t
        go_left = z - nz + t

        @pl.when(go_right < nz)
        def _():
            swap(go_right).wait_recv()
            if t == 1:
                pair_sum(go_right, [], r_out.at[t - 1])
            else:

                @pl.when(z > 0)
                def _():
                    remote(r_out.at[t - 1], r_got.at[t - 2], rs.at[t - 2], rr.at[t - 2], left).wait_recv()
                    pair_sum(go_right, [r_got.at[t - 2]], r_out.at[t - 1])

                @pl.when(z == 0)
                def _():
                    pair_sum(go_right, [], r_out.at[t - 1])

            remote(r_out.at[t - 1], r_got.at[t - 1], rs.at[t - 1], rr.at[t - 1], right).start()

        @pl.when(go_left >= 0)
        def _():
            swap(go_left).wait_recv()
            if t == 1:
                pair_sum(go_left, [], l_out.at[t - 1])
            else:

                @pl.when(z < nz - 1)
                def _():
                    remote(l_out.at[t - 1], l_got.at[t - 2], ls.at[t - 2], lr.at[t - 2], right).wait_recv()
                    pair_sum(go_left, [l_got.at[t - 2]], l_out.at[t - 1])

                @pl.when(z == nz - 1)
                def _():
                    pair_sum(go_left, [], l_out.at[t - 1])

            remote(l_out.at[t - 1], l_got.at[t - 1], ls.at[t - 1], lr.at[t - 1], left).start()

    swap(z).wait_recv()
    last = nz - 2

    def got_left():
        remote(r_out.at[last], r_got.at[last], rs.at[last], rr.at[last], left).wait_recv()

    def got_right():
        remote(l_out.at[last], l_got.at[last], ls.at[last], lr.at[last], right).wait_recv()

    @pl.when(z == 0)
    def _():
        got_right()
        pair_sum(z, [l_got.at[last]], moved)

    @pl.when(z == nz - 1)
    def _():
        got_left()
        pair_sum(z, [r_got.at[last]], moved)

    @pl.when((z > 0) & (z < nz - 1))
    def _():
        got_left()
        got_right()
        pair_sum(z, [r_got.at[last], l_got.at[last]], moved)

    for t in range(2):
        target = t * 2 + x

        @pl.when(target == me)
        def _():
            pltpu.make_async_copy(moved.at[t], out.at[c], local).start()

        @pl.when(target != me)
        def _():
            remote(moved.at[t], out.at[c], hs.at[t], hr.at[c], (seq, target)).start()

    for j in range(2):
        source = c * 2 + j

        @pl.when(source == me)
        def _():
            pltpu.make_async_copy(moved.at[0], out.at[j], local).wait()

        @pl.when(source != me)
        def _():
            remote(moved.at[0], out.at[j], hs.at[0], hr.at[j], (seq, source)).wait_recv()

    for t in range(2):

        @pl.when(t * 2 + x != me)
        def _():
            remote(moved.at[t], out.at[c], hs.at[t], hr.at[c], (seq, t * 2 + x)).wait_send()

    for k in range(nz):
        swap(k).wait_send()
    for t in range(1, nz):

        @pl.when(z + nz - t < nz)
        def _():
            remote(r_out.at[t - 1], r_got.at[t - 1], rs.at[t - 1], rr.at[t - 1], right).wait_send()

        @pl.when(z - nz + t >= 0)
        def _():
            remote(l_out.at[t - 1], l_got.at[t - 1], ls.at[t - 1], lr.at[t - 1], left).wait_send()


def keys_reduce(cid, n, value):
    nz = n // 2
    shape = value.shape[1:]
    chain = pltpu.VMEM((nz - 1,) + shape, BF16)
    return comm_call(
        functools.partial(keys_reduce_kernel, n),
        cid,
        jax.ShapeDtypeStruct(shape, BF16),
        [pltpu.VMEM((nz,) + shape, BF16), chain, chain, chain, chain, pltpu.VMEM(shape, BF16),
         DMA((nz,)), DMA((nz,)), DMA((nz - 1,)), DMA((nz - 1,)), DMA((nz - 1,)), DMA((nz - 1,)),
         DMA((2,)), DMA((2,)), DMA],
        [VMEM],
        VMEM,
    )(value)


def total_kernel(rounds, whole, part, whole_out, part_out, bufs, gots, mine, theirs, ss, rs):
    seq, me, x, c = place_now()
    across = (seq, (1 - x) * 2 + c)
    beside = (seq, x * 2 + 1 - c)
    partners = []
    for r in range(rounds):
        bit = 1 << r
        partners.append((seq + bit - 2 * bit * ((seq // bit) % 2), me))
    greet(partners + [across, beside])
    rows = whole.shape[0]
    bufs[0, :rows, :] = whole[...]
    bufs[0, rows:, :] = part[...]
    for r in range(rounds + 1):
        partner = partners[r] if r < rounds else across
        copy = remote(bufs.at[r], gots.at[r], ss.at[r], rs.at[r], partner)
        copy.start()
        copy.wait()
        if r < rounds:
            bufs[r + 1] = bufs[r] + gots[r]
    mine[0, :rows, :] = bufs[rounds, :rows, :] + gots[rounds, :rows, :]
    mine[0, rows:, :] = bufs[rounds, rows:, :]
    mine[1, rows:, :] = gots[rounds, rows:, :]
    mine[1, :rows, :] = jnp.zeros_like(whole)
    copy = remote(mine, theirs, ss.at[rounds + 1], rs.at[rounds + 1], beside)
    copy.start()
    copy.wait()
    whole_out[...] = mine[0, :rows, :] + theirs[0, :rows, :]
    part_out[x * 2 + c] = mine[0, rows:, :]
    part_out[(1 - x) * 2 + c] = mine[1, rows:, :]
    part_out[x * 2 + 1 - c] = theirs[0, rows:, :]
    part_out[(1 - x) * 2 + 1 - c] = theirs[1, rows:, :]


def totals(cid, n, whole, part):
    rounds = int(math.log2(n))
    rows = whole.shape[0] + part.shape[0]
    return comm_call(
        functools.partial(total_kernel, rounds),
        cid,
        [jax.ShapeDtypeStruct(whole.shape, F32), jax.ShapeDtypeStruct((GROUP,) + part.shape, F32)],
        [pltpu.VMEM((rounds + 1, rows, 128), F32), pltpu.VMEM((rounds + 1, rows, 128), F32),
         pltpu.VMEM((2, rows, 128), F32), pltpu.VMEM((2, rows, 128), F32),
         DMA((rounds + 2,)), DMA((rounds + 2,))],
        [VMEM, VMEM],
        [VMEM, VMEM],
    )(whole, part)


def masks(n, own_ref, meta_ref):
    def column(row):
        return jnp.broadcast_to(own_ref[0, row : row + 1, :], (128, 128)).T

    row_document = column(0)
    row_place = column(1)
    out = []
    for j in range(n):
        key_place = meta_ref[j, 0, 1:2, :]
        key_document = meta_ref[j, 0, 2:3, :]
        allowed = (row_document == key_document) & (key_place <= row_place) | (key_place == row_place)
        out.append(allowed)
    return out


def attend_kernel(n, q_ref, kv_ref, own_ref, meta_ref, low_ref, mixed_ref, total_ref):
    keys = kv_ref[:, 0].reshape(n * 128, DH)
    values = kv_ref[:, 1].reshape(n * 128, DH)
    allowed = masks(n, own_ref, meta_ref)
    for h in range(2):
        cols = slice(h * DH, (h + 1) * DH)
        raw = contract_last(q_ref[:, cols], keys)
        pieces = []
        total = jnp.zeros((128, 128), F32)
        for j in range(n):
            squash = jnp.tanh(raw[:, j * 128 : (j + 1) * 128] * (DH ** (-0.5) / CAP))
            mass = jnp.where(allowed[j], jnp.exp(CAP * squash), 0.0)
            total = total + mass
            pieces.append(mass.astype(BF16))
        row = jnp.sum(total, axis=1, keepdims=True)
        mixed = dot(jnp.concatenate(pieces, axis=1), values) / row
        mixed_ref[:, cols] = mixed
        low_ref[:, cols] = mixed.astype(BF16)
        total_ref[:, h * 128 : (h + 1) * 128] = jnp.broadcast_to(row, (128, 128))


def attend(n, query, pairs, own_meta, metas):
    return pl.pallas_call(
        functools.partial(attend_kernel, n),
        grid=(GROUP,),
        out_shape=[
            jax.ShapeDtypeStruct(query.shape, BF16),
            jax.ShapeDtypeStruct(query.shape, F32),
            jax.ShapeDtypeStruct((query.shape[0], 256), F32),
        ],
        in_specs=[
            pl.BlockSpec((128, 2 * DH), lambda p: (p, 0)),
            pl.BlockSpec((n, 2, 128, DH), lambda p: (0, 0, p, 0)),
            pl.BlockSpec((1, 8, 128), lambda p: (p, 0, 0)),
            pl.BlockSpec((n, 1, 8, 128), lambda p: (0, p, 0, 0)),
        ],
        out_specs=[
            pl.BlockSpec((128, 2 * DH), lambda p: (p, 0)),
            pl.BlockSpec((128, 2 * DH), lambda p: (p, 0)),
            pl.BlockSpec((128, 256), lambda p: (p, 0)),
        ],
        compiler_params=pltpu.CompilerParams(vmem_limit_bytes=VMEM_LIMIT),
    )(query, pairs, own_meta, metas)


def attend_back_kernel(n, q_ref, kv_ref, own_ref, meta_ref, mixed_ref, total_ref, grad_ref, dq_ref, dkv_ref):
    keys = kv_ref[:, 0].reshape(n * 128, DH)
    values = kv_ref[:, 1].reshape(n * 128, DH)
    allowed = masks(n, own_ref, meta_ref)
    grad_keys = None
    for h in range(2):
        cols = slice(h * DH, (h + 1) * DH)
        query = q_ref[:, cols]
        grad = grad_ref[:, cols]
        delta = jnp.sum(grad.astype(F32) * mixed_ref[:, cols], axis=1, keepdims=True)
        inverse = 1.0 / total_ref[:, h * 128 : (h + 1) * 128]
        raw = contract_last(query, keys)
        grad_share = contract_last(grad, values)
        shares = []
        grads = []
        for j in range(n):
            span = slice(j * 128, (j + 1) * 128)
            squash = jnp.tanh(raw[:, span] * (DH ** (-0.5) / CAP))
            share = jnp.where(allowed[j], jnp.exp(CAP * squash), 0.0) * inverse
            shares.append(share.astype(BF16))
            grads.append(
                (share * (grad_share[:, span] - delta) * ((1.0 - squash * squash) * DH ** (-0.5))).astype(BF16)
            )
        share = jnp.concatenate(shares, axis=1)
        grad_raw = jnp.concatenate(grads, axis=1)
        dq_ref[:, cols] = dot(grad_raw, keys)
        new_keys = contract_first(grad_raw, query)
        new_values = contract_first(share, grad)
        if grad_keys is None:
            grad_keys, grad_values = new_keys, new_values
        else:
            grad_keys, grad_values = grad_keys + new_keys, grad_values + new_values
    dkv_ref[:, 0] = grad_keys.astype(BF16).reshape(n, 128, DH)
    dkv_ref[:, 1] = grad_values.astype(BF16).reshape(n, 128, DH)


def attend_back(n, query, pairs, own_meta, metas, mixed, total, grad):
    rows = pl.BlockSpec((128, 2 * DH), lambda p: (p, 0))
    heads = pl.BlockSpec((n, 2, 128, DH), lambda p: (0, 0, p, 0))
    return pl.pallas_call(
        functools.partial(attend_back_kernel, n),
        grid=(GROUP,),
        out_shape=[
            jax.ShapeDtypeStruct(query.shape, F32),
            jax.ShapeDtypeStruct(pairs.shape, BF16),
        ],
        in_specs=[
            rows,
            heads,
            pl.BlockSpec((1, 8, 128), lambda p: (p, 0, 0)),
            pl.BlockSpec((n, 1, 8, 128), lambda p: (0, p, 0, 0)),
            rows,
            pl.BlockSpec((128, 256), lambda p: (p, 0)),
            rows,
        ],
        out_specs=[rows, heads],
        compiler_params=pltpu.CompilerParams(vmem_limit_bytes=VMEM_LIMIT),
    )(query, pairs, own_meta, metas, mixed, total, grad)


def levels(code, step):
    return (jnp.floor(code.astype(F32) * (1.0 / step)) * step + step / 2.0).astype(BF16)


def gelu_parts(gate):
    root = math.sqrt(2.0 / math.pi)
    square = gate * gate
    bend = jnp.tanh(root * gate * (1.0 + 0.044715 * square))
    value = 0.5 * gate * (1.0 + bend)
    slope = 0.5 * (1.0 + bend) + 0.5 * gate * (1.0 - bend * bend) * root * (1.0 + 3 * 0.044715 * square)
    return value, slope


def strips(count, size, body):
    def step(i, carry):
        body(pl.ds(pl.multiple_of(i * size, size), size))
        return carry

    lax.fori_loop(0, count, step, 0)


def ffn_forward_kernel(tiles, riders, *refs):
    b, wgu, gs, wd, cots, g3, ds = refs[:7]
    refs = refs[7:]
    rider_in, refs = refs[:riders], refs[riders:]
    gu_o, hid_o, hidy_o, down_o, gf_o, sums_o = refs[:6]
    refs = refs[6:]
    rider_out, refs = refs[:riders], refs[riders:]
    (gu, hid, hidy, wbuf, wlev, dbuf, dlev, acc, downs, wsem, dsem, xs, xr, hs, hr, ys, yr, fs, fr,
     gxs, gxr, gcs, gcr, gfs, gfr, rs, rr, ks, outs) = refs
    seq, me, x, c = place_now()
    y = seq % 2
    across = (seq, (1 - x) * 2 + c)
    beside = (seq, x * 2 + 1 - c)
    beyond = (seq + 1 - 2 * y, me)
    rows, tw = gu.shape[2:]
    deep = b.shape[1]
    per = tiles // 4

    def load_up(t):
        return pltpu.make_async_copy(wgu.at[:, pl.ds(pl.multiple_of(t * tw, 128), tw)], wbuf.at[t % 2], wsem.at[t % 2])

    def load_down(t, half):
        start = ((c + half) % 2 * tiles + t) * tw
        return pltpu.make_async_copy(
            wd.at[pl.ds(pl.multiple_of(start, 128), tw)], dbuf.at[t % 2, half], dsem.at[t % 2, half]
        )

    load_up(0).start()
    load_up(1).start()
    for t in range(2):
        for half in range(2):
            load_down(t, half).start()
    greet([across, beside, beyond])
    travellers = []
    for i in range(riders):
        copy = remote(rider_in[i], rider_out[i], rs.at[i], rr.at[i], beyond)
        copy.start()
        travellers.append(copy)
    acc[...] = jnp.zeros_like(acc)

    def to_x(t):
        return remote(gu.at[x, t], gu.at[x, t], xs.at[t], xr.at[t], across)

    def to_core(t):
        return remote(hid.at[c * tiles + t], hid.at[c * tiles + t], hs.at[t], hr.at[t], beside)

    def slot(t, core):
        return (2 * core + t // (2 * per)) * per + t % per

    def to_y(t):
        return remote(hid.at[c * tiles + t], hidy.at[slot(t, c)], ys.at[t], yr.at[t], beyond)

    def keep(t, i, core):
        return pltpu.make_async_copy(hid.at[core * tiles + t], hid_o.at[slot(t, core)], ks.at[i, t])

    def wide(t):
        load_up(t).wait()

        def level(span):
            wlev[span, :] = levels(wbuf[t % 2, span, :], 16.0)

        strips(deep // 128, 128, level)

        @pl.when(t + 2 < tiles)
        def _():
            load_up(t + 2).start()

        scale = gs[t]

        def product(span):
            gu[x, t, span, :] = (dot(b[span, :], wlev[...]) * scale).astype(BF16)

        strips(rows // 256, 256, product)
        to_x(t).start()

    def middle(t):
        to_x(t).wait_recv()

        def body(span):
            gate = gu[0, t, span, :].astype(F32)
            up = gu[1, t, span, :].astype(F32)
            hid[c * tiles + t, span, :] = (gelu_parts(gate)[0] * up).astype(BF16)

        strips(rows // 64, 64, body)
        to_core(t).start()

        @pl.when((t // per) % 2 != y)
        def _():
            to_y(t).start()

        @pl.when((t // per) % 2 == y)
        def _():
            keep(t, 0, c).start()

    def narrow(t):
        for half in range(2):
            load_down(t, half).wait()

            def level(span):
                dlev[half, span, :] = levels(dbuf[t % 2, half, span, :], 64.0)

            strips(tw // 128, 128, level)

        @pl.when(t + 2 < tiles)
        def _():
            for half in range(2):
                load_down(t + 2, half).start()

        to_core(t).wait_recv()

        def product(span):
            acc[span, :] += dot(hid[c * tiles + t, span, :], dlev[0]) + dot(
                hid[(1 - c) * tiles + t, span, :], dlev[1]
            )

        strips(rows // 256, 256, product)

        @pl.when((t // per) % 2 == y)
        def _():
            keep(t, 1, 1 - c).start()

    def step(i, carry):
        @pl.when(i < tiles)
        def _():
            wide(i)

        @pl.when((i >= 1) & (i < tiles + 1))
        def _():
            middle(i - 1)

        @pl.when(i >= 2)
        def _():
            narrow(i - 2)

        return carry

    lax.fori_loop(0, tiles + 2, step, 0)
    gu_out = pltpu.make_async_copy(gu, gu_o, outs.at[0])
    gu_out.start()

    parts = 4
    size = rows // parts
    sends = []
    own_sends = []
    for k in range(parts):
        span = pl.ds(k * size, size)
        downs[me, span, :] = acc[span, :].astype(BF16)
        part = downs.at[me, span]
        copy = remote(part, part, gxs.at[k], gxr.at[k], across)
        copy.start()
        sends.append(copy)
        copy = remote(part, part, gcs.at[k], gcr.at[k], beside)
        copy.start()
        own_sends.append(copy)

    def pass_on(t, carry):
        @pl.when((t // per) % 2 == y)
        def _():
            remote(hid.at[0], hidy.at[slot(t, c)], ys.at[t], yr.at[t], beyond).wait_recv()
            got = hidy.at[slot(t, c)]
            remote(got, got, fs.at[t], fr.at[t], beside).start()

        return carry

    lax.fori_loop(0, tiles, pass_on, 0)
    forwards = []
    for k in range(parts):
        sends[k].wait_recv()
        got = downs.at[(1 - x) * 2 + c, pl.ds(k * size, size)]
        copy = remote(got, got, gfs.at[k], gfr.at[k], beside)
        copy.start()
        forwards.append(copy)
    for copy in own_sends + forwards:
        copy.wait_recv()
    down_out = pltpu.make_async_copy(downs, down_o, outs.at[3])
    down_out.start()
    sums_o[...] = jnp.zeros_like(sums_o)
    width = GROUP * acc.shape[1]

    def last_norm(i, carry):
        pack = i // 2
        span = pl.ds(pl.multiple_of(i * 64, 64), 64)
        inner = (i % 2) * 64

        def cot_of(j):
            return cots[pack, pl.ds(pl.multiple_of(j * 128 + inner, 64), 64), :].astype(F32)

        square = jnp.zeros((64, 1), F32)
        cross = jnp.zeros((64, 1), F32)
        for j in range(GROUP):
            value = downs[j, span, :].astype(F32) * ds[j]
            square = square + jnp.sum(value * value, axis=1, keepdims=True)
            cross = cross + jnp.sum(value * (cot_of(j) * g3[j]), axis=1, keepdims=True)
        inverse = lax.rsqrt(square * (1.0 / width) + EPSILON)
        raw = downs[me, span, :].astype(F32)
        normed = raw * ds[me] * inverse
        cot = cot_of(me)
        grad = inverse * (cot * g3[me] - normed * (cross * inverse * (1.0 / width)))
        gf_o[span, :] = (grad * ds[me]).astype(BF16)
        sums_o[0:1, :] += jnp.sum(raw * grad, axis=0, keepdims=True)
        sums_o[1:2, :] += jnp.sum(cot * normed, axis=0, keepdims=True)
        return carry

    lax.fori_loop(0, rows // 64, last_norm, 0)

    def drain(t, carry):
        to_x(t).wait_send()
        to_core(t).wait_send()

        @pl.when((t // per) % 2 != y)
        def _():
            to_y(t).wait_send()

        @pl.when((t // per) % 2 == y)
        def _():
            keep(t, 0, c).wait()
            keep(t, 1, 1 - c).wait()
            got = hidy.at[slot(t, c)]
            remote(got, got, fs.at[t], fr.at[t], beside).wait_send()
            got = hidy.at[slot(t, 1 - c)]
            remote(got, got, fs.at[t], fr.at[t], beside).wait_recv()

        return carry

    lax.fori_loop(0, tiles, drain, 0)
    hidy_out = pltpu.make_async_copy(hidy, hidy_o, outs.at[4])
    hidy_out.start()
    for copy in sends + own_sends + forwards:
        copy.wait_send()
    for copy in travellers:
        copy.wait()
    gu_out.wait()
    down_out.wait()
    hidy_out.wait()


def ffn_forward(cid, b, wgu, gs, wd, cots, g3, ds, riders):
    rows, deep = b.shape
    tiles, _, tw = gs.shape
    part = wd.shape[1]
    count = len(riders)
    lone = max(count, 1)
    return comm_call(
        functools.partial(ffn_forward_kernel, tiles, count),
        cid,
        [
            jax.ShapeDtypeStruct((2, tiles, rows, tw), BF16),
            jax.ShapeDtypeStruct((tiles, rows, tw), BF16),
            jax.ShapeDtypeStruct((tiles, rows, tw), BF16),
            jax.ShapeDtypeStruct((GROUP, rows, part), BF16),
            jax.ShapeDtypeStruct((rows, part), BF16),
            jax.ShapeDtypeStruct((8, part), F32),
        ]
        + [jax.ShapeDtypeStruct(r.shape, r.dtype) for r in riders],
        [
            pltpu.VMEM((2, tiles, rows, tw), BF16),
            pltpu.VMEM((2 * tiles, rows, tw), BF16),
            pltpu.VMEM((tiles, rows, tw), BF16),
            pltpu.VMEM((2, deep, tw), BF16),
            pltpu.VMEM((deep, tw), BF16),
            pltpu.VMEM((2, 2, tw, part), BF16),
            pltpu.VMEM((2, tw, part), BF16),
            pltpu.VMEM((rows, part), F32),
            pltpu.VMEM((GROUP, rows, part), BF16),
            DMA((2,)), DMA((2, 2)), DMA((tiles,)), DMA((tiles,)), DMA((tiles,)), DMA((tiles,)), DMA((tiles,)),
            DMA((tiles,)), DMA((tiles,)), DMA((tiles,)), DMA((4,)), DMA((4,)), DMA((4,)), DMA((4,)), DMA((4,)),
            DMA((4,)), DMA((lone,)), DMA((lone,)), DMA((2, tiles)), DMA((5,)),
        ],
        [VMEM, ANY, VMEM, ANY, VMEM, VMEM, VMEM] + [ANY] * count,
        [ANY, ANY, ANY, ANY, VMEM, VMEM] + [ANY] * count,
    )(b, wgu, gs, wd, cots, g3, ds, *riders)


def ffn_backward_kernel(tiles, nz, chained, *refs):
    gf, wd, wgu, gs, gu, hid, hidy = refs[:7]
    dg_o, dgy_o, gsum_o, out, ddown_o = refs[7:12]
    (hh, hy, gfy, wbuf, wlev, dbuf, dlev, pair, co, cgot, near, sx, xgot, dg, acc, low, from_core, to_xb, from_x,
     r_out, l_out, r_got, l_got,
     hsem, wsem, dsem, psem, cs, cr, xs, xr, ys, yr, os, gys, gyr, ccs, ccr, cxs, cxr, rs, rr, ls, lr) = refs[12:]
    seq, me, x, c = place_now()
    y = seq % 2
    z = seq // 2
    across = (seq, (1 - x) * 2 + c)
    beside = (seq, x * 2 + 1 - c)
    beyond = (seq + 1 - 2 * y, me)
    right = (seq + 2, me)
    left = (seq - 2, me)
    rows, tw = dg.shape[1:]
    deep = acc.shape[1]
    per = hid.shape[0] // 4 if chained else 0
    ring = dg.shape[0]

    def load_up(t):
        return pltpu.make_async_copy(wgu.at[:, pl.ds(pl.multiple_of(t * tw, 128), tw)], wbuf.at[t % 2], wsem.at[t % 2])

    def load_down(t, half):
        start = ((c + half) % 2 * tiles + t) * tw
        return pltpu.make_async_copy(
            wd.at[pl.ds(pl.multiple_of(start, 128), tw)], dbuf.at[t % 2, half], dsem.at[t % 2, half]
        )

    def load_pair(t):
        return pltpu.make_async_copy(gu.at[:, t], pair.at[t % 2], psem.at[t % 2])

    for t in range(2):
        for half in range(2):
            load_down(t, half).start()
        load_pair(t).start()
        load_up(t).start()
    if chained:
        load_hid = pltpu.make_async_copy(hid, hh, hsem.at[0])
        load_hidy = pltpu.make_async_copy(hidy, hy, hsem.at[1])
        load_hid.start()
        load_hidy.start()
    barrier = pltpu.get_barrier_semaphore()
    for peer in (across, beside, beyond):
        pl.semaphore_signal(barrier, inc=1, device_id=peer, device_id_type=MESH)
    if chained:

        @pl.when(z > 0)
        def _():
            pl.semaphore_signal(barrier, inc=1, device_id=left, device_id_type=MESH)

        @pl.when(z < nz - 1)
        def _():
            pl.semaphore_signal(barrier, inc=1, device_id=right, device_id_type=MESH)

        pl.semaphore_wait(barrier, 3 + jnp.where(z > 0, 1, 0) + jnp.where(z < nz - 1, 1, 0))
        gf_swap = remote(gf, gfy, gys, gyr, beyond)
        gf_swap.start()
    else:
        pl.semaphore_wait(barrier, 3)
    acc[...] = jnp.zeros_like(acc)

    def to_core(t):
        return remote(co.at[t % 2], cgot.at[t], cs.at[t], cr.at[t], beside)

    def to_x(t):
        return remote(sx.at[t % 4], xgot.at[t], xs.at[t], xr.at[t], across)

    def columns(ref, t):
        return ref.at[:, pl.ds(pl.multiple_of(t * tw, 128), tw)]

    def to_y(t):
        return remote(dg.at[t % ring], columns(dgy_o, t), ys.at[t], yr.at[t], beyond)

    def keep(t):
        return pltpu.make_async_copy(dg.at[t % ring], columns(dg_o, t), os.at[t])

    def hidden(t):
        for half in range(2):
            load_down(t, half).wait()

            def level(span):
                dlev[half, span, :] = levels(dbuf[t % 2, half, span, :], 64.0)

            strips(tw // 128, 128, level)

        @pl.when(t + 2 < tiles)
        def _():
            for half in range(2):
                load_down(t + 2, half).start()

        @pl.when(t >= 2)
        def _():
            to_core(t - 2).wait_send()

        def product(span):
            co[t % 2, span, :] = contract_last(gf[span, :], dlev[1]).astype(BF16)

        strips(rows // 256, 256, product)
        to_core(t).start()

        def product_near(span):
            near[t % 2, span, :] = contract_last(gf[span, :], dlev[0])

        strips(rows // 256, 256, product_near)

    def chip(t):
        @pl.when(t >= 4)
        def _():
            to_x(t - 4).wait_send()

        to_core(t).wait_recv()

        def body(span):
            sx[t % 4, span, :] = (near[t % 2, span, :] + cgot[t, span, :].astype(F32)).astype(BF16)

        strips(rows // 64, 64, body)
        to_x(t).start()

    is_gate = jnp.where(x == 0, 1.0, 0.0).astype(F32)

    def own(t):
        load_pair(t).wait()

        @pl.when(t >= ring)
        def _():
            to_y(t - ring).wait_send()
            keep(t - ring).wait()

        to_x(t).wait_recv()
        scale = gs[t]
        gsum_o[t] = jnp.zeros((8, tw), F32)

        def body(span):
            grad = sx[t % 4, span, :].astype(F32) + xgot[t, span, :].astype(F32)
            gate = pair[t % 2, 0, span, :].astype(F32)
            up = pair[t % 2, 1, span, :].astype(F32)
            value, slope = gelu_parts(gate)
            full = grad * (is_gate * (up * slope) + (1.0 - is_gate) * value)
            gsum_o[t, 0:1, :] += jnp.sum(pair[t % 2, x, span, :].astype(F32) * full, axis=0, keepdims=True)
            dg[t % ring, span, :] = (full * scale).astype(BF16)

        strips(rows // 64, 64, body)

        @pl.when(t + 2 < tiles)
        def _():
            load_pair(t + 2).start()

        to_y(t).start()
        keep(t).start()

    def back(t):
        load_up(t).wait()

        def level(span):
            wlev[span, :] = levels(wbuf[t % 2, span, :], 16.0)

        strips(deep // 128, 128, level)

        @pl.when(t + 2 < tiles)
        def _():
            load_up(t + 2).start()

        def product(span):
            acc[span, :] += contract_last(dg[t % ring, span, :], wlev[...])

        strips(rows // 128, 128, product)

    def partial(k, j):
        return contract_first(hh[k * per + j], gf[...]) + contract_first(hy[k * per + j], gfy[...])

    def chain(j, s):
        go_right = z + nz - s
        go_left = z - nz + s

        def one(go, got, out_buf, ss, sr, to, source, first):
            @pl.when(j > 0)
            def _():
                remote(out_buf.at[s - 1], got.at[j - 1, s - 1], ss.at[j - 1, s - 1], sr.at[j - 1, s - 1], to).wait_send()

            total = partial(go, j)
            more = (s > 1) & jnp.logical_not(first)

            @pl.when(more)
            def _():
                remote(out_buf.at[0], got.at[j, s - 2], ss.at[j, s - 2], sr.at[j, s - 2], source).wait_recv()
                out_buf[s - 1] = (total + got[j, s - 2].astype(F32)).astype(BF16)

            @pl.when(jnp.logical_not(more))
            def _():
                out_buf[s - 1] = total.astype(BF16)

            remote(out_buf.at[s - 1], got.at[j, s - 1], ss.at[j, s - 1], sr.at[j, s - 1], to).start()

        @pl.when(go_right < nz)
        def _():
            one(go_right, r_got, r_out, rs, rr, right, left, z == 0)

        @pl.when(go_left >= 0)
        def _():
            one(go_left, l_got, l_out, ls, lr, left, right, z == nz - 1)

    def chain_end(j):
        ddown_o[j] = partial(z, j)

        @pl.when(z > 0)
        def _():
            remote(r_out.at[0], r_got.at[j, nz - 2], rs.at[j, nz - 2], rr.at[j, nz - 2], left).wait_recv()
            ddown_o[j] += r_got[j, nz - 2].astype(F32)

        @pl.when(z < nz - 1)
        def _():
            remote(l_out.at[0], l_got.at[j, nz - 2], ls.at[j, nz - 2], lr.at[j, nz - 2], right).wait_recv()
            ddown_o[j] += l_got[j, nz - 2].astype(F32)

    hops = nz - 1

    def step(i, carry):
        @pl.when(i < tiles)
        def _():
            hidden(i)

        @pl.when((i >= 1) & (i < tiles + 1))
        def _():
            chip(i - 1)

        if chained:

            @pl.when(i == 1)
            def _():
                gf_swap.wait_recv()
                load_hid.wait()
                load_hidy.wait()

            @pl.when((i >= 1) & (i < 1 + per * hops))
            def _():
                chain((i - 1) // hops, (i - 1) % hops + 1)

        @pl.when(i >= 2)
        def _():
            own(i - 2)
            back(i - 2)

        return carry

    lax.fori_loop(0, tiles + 2, step, 0)

    parts = 4
    block = rows // GROUP
    size = block // parts
    order = [1 - x, x]
    cores = []
    for i in range(2):
        for k in range(parts):
            owner = order[i] * 2 + 1 - c
            span = pl.ds(k * size, size)
            low[i, span, :] = acc[pl.ds(pl.multiple_of(owner * block + k * size, 16), size), :].astype(BF16)
            copy = remote(low.at[i, span], from_core.at[i, span], ccs.at[i, k], ccr.at[i, k], beside)
            copy.start()
            cores.append(copy)
    sends = []
    for k in range(parts):
        span = pl.ds(k * size, size)
        here = pl.ds(pl.multiple_of((order[0] * 2 + c) * block + k * size, 16), size)
        cores[k].wait_recv()
        to_xb[span, :] = (acc[here, :] + from_core[0, span, :].astype(F32)).astype(BF16)
        copy = remote(to_xb.at[span], from_x.at[span], cxs.at[k], cxr.at[k], across)
        copy.start()
        sends.append(copy)
    if chained:
        for j in range(per):
            chain_end(j)
    for k in range(parts):
        span = pl.ds(k * size, size)
        here = pl.ds(pl.multiple_of((order[1] * 2 + c) * block + k * size, 16), size)
        cores[parts + k].wait_recv()
        sends[k].wait_recv()
        out[span, :] = acc[here, :] + from_core[1, span, :].astype(F32) + from_x[span, :].astype(F32)

    for copy in cores + sends:
        copy.wait_send()
    for t in range(tiles - 2, tiles):
        to_core(t).wait_send()
    for t in range(tiles - 4, tiles):
        to_x(t).wait_send()
    for t in range(tiles - ring, tiles):
        to_y(t).wait_send()
        keep(t).wait()

    def drain(t, carry):
        to_y(t).wait_recv()
        return carry

    lax.fori_loop(0, tiles, drain, 0)
    if chained:
        gf_swap.wait_send()
        j = per - 1
        for s in range(1, nz):

            @pl.when(z + nz - s < nz)
            def _():
                remote(r_out.at[s - 1], r_got.at[j, s - 1], rs.at[j, s - 1], rr.at[j, s - 1], right).wait_send()

            @pl.when(z - nz + s >= 0)
            def _():
                remote(l_out.at[s - 1], l_got.at[j, s - 1], ls.at[j, s - 1], lr.at[j, s - 1], left).wait_send()


def ffn_backward(cid, n, gf, wd, wgu, gs, gu, hid, hidy):
    rows, part = gf.shape
    deep = wgu.shape[0]
    tiles, _, tw = gs.shape
    nz = n // 2
    chained = nz == 4
    per = tiles // nz if chained else 1
    hops = nz - 1 if chained else 1
    block = rows // GROUP
    half = (tiles, rows, tw) if chained else (1, 16, 128)
    message = (tw, part) if chained else (16, 128)
    ring = 4
    return comm_call(
        functools.partial(ffn_backward_kernel, tiles, nz, chained),
        cid,
        [
            jax.ShapeDtypeStruct((rows, tiles * tw), BF16),
            jax.ShapeDtypeStruct((rows, tiles * tw), BF16),
            jax.ShapeDtypeStruct((tiles, 8, tw), F32),
            jax.ShapeDtypeStruct((block, deep), F32),
            jax.ShapeDtypeStruct((per,) + message, F32),
        ],
        [
            pltpu.VMEM(half, BF16),
            pltpu.VMEM(half, BF16),
            pltpu.VMEM((rows, part), BF16),
            pltpu.VMEM((2, deep, tw), BF16),
            pltpu.VMEM((deep, tw), BF16),
            pltpu.VMEM((2, 2, tw, part), BF16),
            pltpu.VMEM((2, tw, part), BF16),
            pltpu.VMEM((2, 2, rows, tw), BF16),
            pltpu.VMEM((2, rows, tw), BF16),
            pltpu.VMEM((tiles, rows, tw), BF16),
            pltpu.VMEM((2, rows, tw), F32),
            pltpu.VMEM((4, rows, tw), BF16),
            pltpu.VMEM((tiles, rows, tw), BF16),
            pltpu.VMEM((ring, rows, tw), BF16),
            pltpu.VMEM((rows, deep), F32),
            pltpu.VMEM((2, block, deep), BF16),
            pltpu.VMEM((2, block, deep), BF16),
            pltpu.VMEM((block, deep), BF16),
            pltpu.VMEM((block, deep), BF16),
            pltpu.VMEM((hops,) + message, BF16),
            pltpu.VMEM((hops,) + message, BF16),
            pltpu.VMEM((per, hops) + message, BF16),
            pltpu.VMEM((per, hops) + message, BF16),
            DMA((2,)), DMA((2,)), DMA((2, 2)), DMA((2,)), DMA((tiles,)), DMA((tiles,)), DMA((tiles,)), DMA((tiles,)),
            DMA((tiles,)), DMA((tiles,)), DMA((tiles,)), DMA, DMA, DMA((2, 4)), DMA((2, 4)), DMA((4,)), DMA((4,)),
            DMA((per, hops)), DMA((per, hops)), DMA((per, hops)), DMA((per, hops)),
        ],
        [VMEM, ANY, ANY, VMEM, ANY, ANY, ANY],
        [ANY, ANY, VMEM, VMEM, VMEM],
    )(gf, wd, wgu, gs, gu, hid, hidy)


def rms_inverse(value):
    return lax.rsqrt(jnp.mean(value * value, axis=-1, keepdims=True) + EPSILON)


def norm_back(inverse, normed, upstream):
    return inverse * (upstream - normed * jnp.mean(upstream * normed, axis=-1, keepdims=True))


def rotate(value, cosine, sine):
    half = DH // 2
    first = value[..., :half]
    second = value[..., half:]
    return jnp.concatenate([first * cosine - second * sine, second * cosine + first * sine], axis=-1)


def seq_swap(value, n):
    return lax.ppermute(value, "seq", [(s, s ^ 1) for s in range(n)])


def core_swap(value):
    return lax.ppermute(value, "fsdp", [(f, f ^ 1) for f in range(GROUP)])


def slice_halves(value, n, y):
    rows, width = value.shape
    turned = value.T.reshape(n // 2, 2, width // n, rows)
    here = lax.dynamic_index_in_dim(turned, y, 1, keepdims=False).reshape(width // 2, rows)
    there = lax.dynamic_index_in_dim(turned, 1 - y, 1, keepdims=False).reshape(width // 2, rows)
    return here, there


class ChainSum:
    def __init__(self, block, n, z):
        self.block, self.n, self.z, self.t = block, n, z, 1
        self.got = None

    def pick(self, k):
        return lax.dynamic_index_in_dim(self.block, jnp.clip(k, 0, self.n // 2 - 1), 0, keepdims=False)

    def hop(self):
        n, z, t = self.n, self.z, self.t
        right = self.pick(z + n // 2 - t)
        left = self.pick(z - n // 2 + t)
        if t > 1:
            right = (right.astype(F32) + self.got[0].astype(F32)).astype(BF16)
            left = (left.astype(F32) + self.got[1].astype(F32)).astype(BF16)
        self.got = (
            lax.ppermute(right, "seq", [(s, s + 2) for s in range(2 * t)]),
            lax.ppermute(left, "seq", [(n - 1 - s, n - 3 - s) for s in range(2 * t)]),
        )
        self.t += 1

    def after(self, value):
        self.got, value = lax.optimization_barrier((self.got, value))
        return value

    def end(self):
        while self.t < self.n // 2:
            self.hop()
        return self.pick(self.z).astype(F32) + self.got[0].astype(F32) + self.got[1].astype(F32)


def pair_product(lefts, rights):
    return dot(lefts[0], rights[0]) + dot(lefts[1], rights[1])


def lanes(value, rows):
    flat = value.reshape(-1)
    return jnp.pad(flat, (0, rows * 128 - flat.shape[0])).reshape(rows, 128)


def per_device(
    n,
    tokens,
    doc_ids,
    padding,
    token_order,
    query_code,
    key_value_code,
    output_code,
    gate_up_code,
    down_code,
    query_scale,
    key_value_scale,
    output_scale,
    gate_up_scale,
    down_scale,
    norm_gains,
    cotangent,
):
    seq = lax.axis_index("seq")
    me = lax.axis_index("fsdp")
    is_gate = me < 2
    c = me % 2
    y = seq % 2
    z = seq // 2
    width = tokens.shape[2]
    part = width // GROUP
    rows = GROUP * tokens.shape[1]
    own = tokens.shape[1]

    def mine(vector):
        size = vector.shape[-1] // GROUP
        return lax.dynamic_slice_in_dim(vector, me * size, size, vector.ndim - 1)

    def blocks_to_rows(blocks):
        return jnp.concatenate([blocks[i] for i in range(GROUP)], axis=1)

    def own_rows(value):
        return lax.dynamic_slice_in_dim(value, me * own, own, 0)

    gain = 1.0 + norm_gains
    place = token_order[0].astype(F32)
    document = doc_ids[0].astype(F32)
    meta = jnp.stack([document, place, jnp.where(padding[0] == 1, document, -1.0)] + [document] * 5)

    token_blocks, own_meta = group_gather(1, [tokens[0], meta], parts=[4, 1])
    inputs = token_blocks.reshape(rows, width).astype(F32)
    turn = own_meta[:, 1, :].reshape(rows, 1) * (
        BASE ** (-2.0 * jnp.arange(DH // 2).astype(F32) / DH)
    )[None, :]
    cosine = jnp.cos(turn)
    sine = jnp.sin(turn)
    first_inverse = rms_inverse(inputs)
    first_input = (inputs * first_inverse * gain[0]).astype(BF16)
    query_raw = dot(first_input, query_code)
    pair_raw = dot(first_input, key_value_code)
    my_query_scale = mine(query_scale)
    my_pair_scale = mine(key_value_scale)
    pair_cosine = jnp.where(is_gate, cosine, 1.0)
    pair_sine = jnp.where(is_gate, sine, 0.0)
    query = rotate(
        (query_raw * my_query_scale).reshape(rows, 2, DH), cosine[:, None], sine[:, None]
    ).astype(BF16).reshape(rows, 2 * DH)
    pair_plain = pair_raw * my_pair_scale
    heads = jnp.stack(
        [rotate(pair_plain[:, j * DH : (j + 1) * DH], pair_cosine, pair_sine) for j in range(2)]
    ).astype(BF16)
    cot_columns = cotangent[0].reshape(own, GROUP, part).transpose(1, 0, 2).reshape(rows, part)
    pairs, metas, cot_blocks = keys_gather(2, n, heads, own_meta, cot_columns)

    mixed_low, mixed, mass = attend(n, query, pairs, own_meta, metas)
    (mixed_rows,) = group_gather(3, [mixed_low], columns=[True])
    branch_own = dot(mixed_rows, output_code).astype(BF16)
    (branch_blocks,) = group_gather(4, [branch_own])
    branch_raw = blocks_to_rows(branch_blocks).astype(F32)
    branch = branch_raw * output_scale
    second_inverse = rms_inverse(branch)
    middle = inputs + branch * second_inverse * gain[1]
    third_inverse = rms_inverse(middle)
    second_input = (middle * third_inverse * gain[2]).astype(BF16)

    halves = [slice_halves(v, n, y) for v in (first_input, mixed_rows, second_input)]
    my_gate_scale = mine(gate_up_scale)
    columns = gate_up_code.shape[1]
    tiles = columns // TILE
    gate_scales = my_gate_scale.reshape(tiles, 1, TILE)
    gate_up, hidden, hidden_y, down_blocks, grad_down, down_sums, *riders = ffn_forward(
        5,
        second_input,
        gate_up_code,
        gate_scales,
        down_code,
        cot_blocks,
        gain[3].reshape(GROUP, 1, part),
        down_scale.reshape(GROUP, 1, part),
        [half[1] for half in halves],
    )
    first_pair, mixed_pair, second_pair = [(half[0], rider) for half, rider in zip(halves, riders)]
    my_middle = own_rows(middle)
    my_down = blocks_to_rows(lax.dynamic_slice_in_dim(down_blocks, me * own, own, 1)).astype(F32) * down_scale
    result = (my_middle + my_down * rms_inverse(my_down) * gain[3]).astype(BF16)
    grad_gate_up, grad_gate_up_y, gate_sums, grad_second_input, down_grad = ffn_backward(
        6, n, grad_down, down_code, gate_up_code, gate_scales, gate_up, hidden, hidden_y
    )
    if n == 8:
        down_grad = down_grad.reshape(-1, part)
    else:
        hidden_own = jnp.concatenate(
            [
                (jax.nn.gelu(gate_up[0, t].astype(F32)) * gate_up[1, t].astype(F32)).astype(BF16)
                for t in range(tiles)
            ],
            axis=1,
        )
        hidden_core = core_swap(hidden_own)
        hidden_rows = jnp.concatenate(
            [jnp.where(c == 0, hidden_own, hidden_core), jnp.where(c == 0, hidden_core, hidden_own)], axis=1
        )
        down_grad = lax.psum_scatter(
            contract_first(hidden_rows, grad_down), "seq", scatter_dimension=0, tiled=True
        )
    scale_down = down_sums[0]
    gain_four = down_sums[1]
    scale_gate = gate_sums[:, 0, :].reshape(columns) / my_gate_scale
    gate_block = pair_product(second_pair, (grad_gate_up, grad_gate_up_y)).astype(BF16)
    gate_chain = ChainSum(gate_block.reshape(n // 2, -1, columns), n, z)
    gate_chain.hop()

    third_inverse = own_rows(third_inverse)
    second_inverse = own_rows(second_inverse)
    my_branch_raw = own_rows(branch_raw)
    third = my_middle * third_inverse
    second = my_branch_raw * output_scale * second_inverse
    my_cot = cotangent[0].astype(F32)
    gain_three = jnp.sum(grad_second_input * third, axis=0)
    grad_middle = my_cot + norm_back(third_inverse, third, grad_second_input * gain[2])
    gain_two = jnp.sum(grad_middle * second, axis=0)
    grad_branch_full = norm_back(second_inverse, second, grad_middle * gain[1])
    scale_output = jnp.sum(my_branch_raw * grad_branch_full, axis=0)
    grad_branch_own = (grad_branch_full * output_scale).astype(BF16)
    grad_branch = group_exchange(
        7, grad_branch_own.reshape(own, GROUP, part).transpose(1, 0, 2)
    ).reshape(rows, part)
    grad_branch_pair = (grad_branch, seq_swap(grad_branch, n))
    output_block = pair_product(mixed_pair, grad_branch_pair).astype(BF16)
    output_chain = ChainSum(output_block.reshape(n // 2, -1, part), n, z)
    grad_mixed_sum = jnp.stack(
        [contract_last(grad_branch, output_code[i * 2 * DH : (i + 1) * 2 * DH]) for i in range(GROUP)]
    ).astype(BF16)
    grad_mixed = group_reduce(8, grad_mixed_sum, BF16)

    grad_query, grad_pairs = attend_back(n, query, pairs, own_meta, metas, mixed, mass, grad_mixed)
    grad_pairs = gate_chain.after(grad_pairs)
    gate_chain.hop()
    grad_heads = keys_reduce(9, n, grad_pairs).astype(F32)
    grad_query_full = rotate(
        grad_query.reshape(rows, 2, DH), cosine[:, None], -sine[:, None]
    ).reshape(rows, 2 * DH)
    scale_query = jnp.sum(query_raw * grad_query_full, axis=0)
    grad_query_low = (grad_query_full * my_query_scale).astype(BF16)
    grad_pair_full = jnp.concatenate(
        [rotate(grad_heads[j], pair_cosine, -pair_sine) for j in range(2)], axis=1
    )
    scale_pair = jnp.sum(pair_raw * grad_pair_full, axis=0)
    grad_pair_low = (grad_pair_full * my_pair_scale).astype(BF16)
    joined = jnp.concatenate([grad_query_low, grad_pair_low], axis=1)
    joined_pair = (joined, seq_swap(joined, n))
    grad_first_sum = contract_last(grad_query_low, query_code) + contract_last(grad_pair_low, key_value_code)
    grad_first_input = group_reduce(10, grad_first_sum.astype(BF16).reshape(GROUP, own, width), F32)
    attention_block = pair_product(first_pair, joined_pair).astype(BF16)
    attention_chain = ChainSum(attention_block.reshape(n // 2, -1, joined.shape[1]), n, z)
    grad_first_input = gate_chain.after(grad_first_input)
    gate_chain.hop()
    my_inputs = tokens[0].astype(F32)
    my_inverse = rms_inverse(my_inputs)
    first = my_inputs * my_inverse
    gain_one = jnp.sum(grad_first_input * first, axis=0)
    grad_inputs = grad_middle + norm_back(my_inverse, first, grad_first_input * gain[0])

    wholes = jnp.concatenate([gain_one, gain_two, gain_three, scale_output])
    parts = [scale_query, scale_pair, scale_gate, scale_down, gain_four]
    whole_total, part_total = totals(
        11, n, lanes(wholes, 72), lanes(jnp.concatenate(parts), 56)
    )
    whole_total = whole_total.reshape(-1)
    part_total = part_total.reshape(GROUP, -1)
    pieces = []
    start = 0
    for vector in parts:
        pieces.append(part_total[:, start : start + vector.shape[0]].reshape(-1))
        start += vector.shape[0]
    q_width = query_code.shape[1]
    attention_grad = attention_chain.end()
    return (
        result[None],
        grad_inputs[None],
        attention_grad[:, :q_width],
        attention_grad[:, q_width:],
        output_chain.end(),
        gate_chain.end(),
        down_grad,
        pieces[0],
        pieces[1],
        whole_total[3 * width :],
        pieces[2],
        pieces[3],
        jnp.concatenate([whole_total[: 3 * width], pieces[4]]).reshape(4, width),
    )


def solution(mesh):
    return jax.shard_map(
        functools.partial(per_device, mesh.shape["seq"]),
        mesh=mesh,
        in_specs=(
            P("fsdp", "seq", None),
            P("fsdp", "seq"),
            P("fsdp", "seq"),
            P("fsdp", "seq"),
            P(None, "fsdp"),
            P(None, "fsdp"),
            P(None, "fsdp"),
            P(None, "fsdp"),
            P(None, "fsdp"),
            P(),
            P(),
            P(),
            P(),
            P(),
            P(),
            P("fsdp", "seq", None),
        ),
        out_specs=(
            P("fsdp", "seq", None),
            P("fsdp", "seq", None),
            P("seq", "fsdp"),
            P("seq", "fsdp"),
            P("seq", "fsdp"),
            P("seq", "fsdp"),
            P("seq", "fsdp"),
            P(),
            P(),
            P(),
            P(),
            P(),
            P(),
        ),
        check_vma=False,
    )
```

```python
import functools
import math

import jax
import jax.numpy as jnp
from jax import lax
from jax.experimental import pallas as pl
from jax.experimental.pallas import tpu as pltpu
from jax.sharding import PartitionSpec as P

HQ = 8
HK = 4
DH = 256
FF = 9216
GROUP = 4
TILE = 384
EPSILON = 1e-06
CAP = 50.0
BASE = 10000.0
VMEM_LIMIT = 60 * 1024 * 1024
MESH = pl.DeviceIdType.MESH
ANY = pl.BlockSpec(memory_space=pl.ANY)
VMEM = pl.BlockSpec(memory_space=pltpu.VMEM)
DMA = pltpu.SemaphoreType.DMA
F32 = jnp.float32
BF16 = jnp.bfloat16


def dot(left, right):
    return jnp.dot(left, right, preferred_element_type=F32)


def contract_last(left, right):
    return lax.dot_general(left, right, (((1,), (1,)), ((), ())), preferred_element_type=F32)


def contract_first(left, right):
    return lax.dot_general(left, right, (((0,), (0,)), ((), ())), preferred_element_type=F32)


def place_now():
    seq = lax.axis_index("seq")
    fsdp = lax.axis_index("fsdp")
    return seq, fsdp, fsdp // 2, fsdp % 2


def greet(peers):
    barrier = pltpu.get_barrier_semaphore()
    for peer in peers:
        pl.semaphore_signal(barrier, inc=1, device_id=peer, device_id_type=MESH)
    pl.semaphore_wait(barrier, len(peers))


def remote(src, dst, send, recv, peer):
    return pltpu.make_async_remote_copy(
        src_ref=src, dst_ref=dst, send_sem=send, recv_sem=recv, device_id=peer, device_id_type=MESH
    )


def comm_call(kernel, cid, out_shape, scratch, in_specs, out_specs):
    return pl.pallas_call(
        kernel,
        out_shape=out_shape,
        in_specs=in_specs,
        out_specs=out_specs,
        scratch_shapes=scratch,
        compiler_params=pltpu.CompilerParams(
            collective_id=cid, has_side_effects=True, vmem_limit_bytes=VMEM_LIMIT
        ),
    )


def group_gather_kernel(count, columns, parts, *refs):
    ins = refs[:count]
    outs = refs[count : 2 * count]
    local, xs, xr, cs, cr, fs, fr = refs[2 * count :]
    seq, me, x, c = place_now()
    across = (seq, (1 - x) * 2 + c)
    beside = (seq, x * 2 + 1 - c)
    greet([across, beside])
    waits = []
    forwards = []
    for i in range(count):
        src, out = ins[i], outs[i]
        rows = src.shape[0]
        step = rows // parts[i]

        def spot(owner, start, size, out=out, i=i):
            if columns[i]:
                width = out.shape[1] // GROUP
                return out.at[pl.ds(start, size), pl.ds(owner * width, width)]
            return out.at[owner, pl.ds(start, size)]

        own = pltpu.make_async_copy(src, spot(me, 0, rows), local.at[i])
        for k in range(parts[i]):
            part = src.at[pl.ds(k * step, step)]
            there = spot(me, k * step, step)
            copy = remote(part, there, xs.at[i, k], xr.at[i, k], across)
            copy.start()
            waits.append(copy.wait_send)
            got = spot((1 - x) * 2 + c, k * step, step)
            forwards.append((copy, remote(got, got, fs.at[i, k], fr.at[i, k], beside)))
        copy = remote(src, spot(me, 0, rows), cs.at[i], cr.at[i], beside)
        copy.start()
        own.start()
        waits += [copy.wait, own.wait]
    for copy, forward in forwards:
        copy.wait_recv()
        forward.start()
        waits.append(forward.wait)
    for wait in waits:
        wait()


def group_gather(cid, values, columns=None, parts=None):
    count = len(values)
    columns = columns or [False] * count
    parts = parts or [4] * count
    most = max(parts)
    shapes = [
        jax.ShapeDtypeStruct(
            (v.shape[0], v.shape[1] * GROUP) if col else (GROUP,) + v.shape, v.dtype
        )
        for v, col in zip(values, columns)
    ]
    return comm_call(
        functools.partial(group_gather_kernel, count, tuple(columns), tuple(parts)),
        cid,
        shapes,
        [DMA((count,)), DMA((count, most)), DMA((count, most)), DMA((count,)), DMA((count,)),
         DMA((count, most)), DMA((count, most))],
        [ANY] * count,
        [ANY] * count,
    )(*values)


def group_reduce_kernel(parts, src, out, from_core, to_x, from_x, cs, cr, xs, xr):
    seq, me, x, c = place_now()
    across = (seq, (1 - x) * 2 + c)
    beside = (seq, x * 2 + 1 - c)
    greet([across, beside])
    rows = src.shape[1]
    step = rows // parts
    order = [1 - x, x]
    cores = []
    for i in range(2):
        for k in range(parts):
            span = pl.ds(k * step, step)
            copy = remote(
                src.at[order[i] * 2 + 1 - c, span], from_core.at[i, span], cs.at[i, k], cr.at[i, k], beside
            )
            copy.start()
            cores.append(copy)
    sends = []
    for k in range(parts):
        span = pl.ds(k * step, step)
        cores[k].wait_recv()
        to_x[span, :] = (
            src[order[0] * 2 + c, span, :].astype(F32) + from_core[0, span, :].astype(F32)
        ).astype(BF16)
        copy = remote(to_x.at[span], from_x.at[span], xs.at[k], xr.at[k], across)
        copy.start()
        sends.append(copy)
    for k in range(parts):
        span = pl.ds(k * step, step)
        cores[parts + k].wait_recv()
        sends[k].wait_recv()
        out[span, :] = (
            src[order[1] * 2 + c, span, :].astype(F32)
            + from_core[1, span, :].astype(F32)
            + from_x[span, :].astype(F32)
        ).astype(out.dtype)
    for copy in cores + sends:
        copy.wait_send()


def group_reduce(cid, value, dtype, parts=4):
    rows, width = value.shape[1:]
    return comm_call(
        functools.partial(group_reduce_kernel, parts),
        cid,
        jax.ShapeDtypeStruct((rows, width), dtype),
        [pltpu.VMEM((2, rows, width), BF16), pltpu.VMEM((rows, width), BF16), pltpu.VMEM((rows, width), BF16),
         DMA((2, parts)), DMA((2, parts)), DMA((parts,)), DMA((parts,))],
        [VMEM],
        VMEM,
    )(value)


def keys_gather_kernel(n, heads, meta, cot, out, metas, cots, own_sem, hs, hr, ms, mr, rs, rr, ls, lr, ys, yr,
                       local, xs, xr, cs, cr, fs, fr):
    seq, me, x, c = place_now()
    y = seq % 2
    z = seq // 2
    nz = n // 2
    across = (seq, (1 - x) * 2 + c)
    beside = (seq, x * 2 + 1 - c)
    peers = [(seq, lax.rem(me + d, GROUP)) for d in range(1, GROUP)]
    peers += [(lax.rem(seq + d, n), me) for d in range(1, n)]
    greet(peers)
    for j in range(2):
        target = c * 2 + j

        @pl.when(target == me)
        def _():
            pltpu.make_async_copy(heads.at[j], out.at[seq, x], own_sem.at[0]).start()

        @pl.when(target != me)
        def _():
            remote(heads.at[j], out.at[seq, x], hs.at[j], hr.at[x], (seq, target)).start()

    small = []
    for d in range(1, n):
        copy = remote(meta, metas.at[seq], ms.at[d - 1], mr.at[d - 1], (lax.rem(seq + d, n), me))
        copy.start()
        small.append(copy)
    own_meta = pltpu.make_async_copy(meta, metas.at[seq], own_sem.at[1])
    own_meta.start()
    for t in range(2):
        source = t * 2 + x

        @pl.when(source == me)
        def _():
            pltpu.make_async_copy(heads.at[0], out.at[seq, t], own_sem.at[0]).wait()

        @pl.when(source != me)
        def _():
            remote(heads.at[0], out.at[seq, t], hs.at[0], hr.at[t], (seq, source)).wait_recv()

    def block(owner_z, owner_y):
        return out.at[owner_z * 2 + owner_y]

    right = (seq + 2, me)
    left = (seq - 2, me)
    beyond = (z * 2 + 1 - y, me)

    def to_y(owner_z):
        remote(block(owner_z, y), block(owner_z, y), ys.at[owner_z], yr.at[owner_z], beyond).start()

    rows = cot.shape[0]
    parts = 2
    step = rows // parts

    for t in range(1, nz + 1):
        go_right = z - t + 1
        go_left = z + t - 1
        if t > 1:

            @pl.when(go_right >= 0)
            def _():
                remote(block(go_right, y), block(go_right, y), rs.at[t - 1], rr.at[t - 1], left).wait_recv()

            @pl.when(go_left < nz)
            def _():
                remote(block(go_left, y), block(go_left, y), ls.at[t - 1], lr.at[t - 1], right).wait_recv()

        if t < nz:

            @pl.when((go_right >= 0) & (z < nz - 1))
            def _():
                remote(block(go_right, y), block(go_right, y), rs.at[t], rr.at[t], right).start()

            @pl.when((go_left < nz) & (z > 0))
            def _():
                remote(block(go_left, y), block(go_left, y), ls.at[t], lr.at[t], left).start()

        @pl.when(go_right >= 0)
        def _():
            to_y(go_right)

        if t > 1:

            @pl.when(go_left < nz)
            def _():
                to_y(go_left)

        if t == 1:
            xcopies = []
            for k in range(parts):
                part = pl.ds(k * step, step)
                copy = remote(cot.at[part], cots.at[me, part], xs.at[k], xr.at[k], across)
                copy.start()
                xcopies.append(copy)
            ccopy = remote(cot, cots.at[me], cs, cr, beside)
            ccopy.start()
            own_cot = pltpu.make_async_copy(cot, cots.at[me], local)
            own_cot.start()
    forwards = []
    for k in range(parts):
        part = pl.ds(k * step, step)
        xcopies[k].wait()
        got = cots.at[(1 - x) * 2 + c, part]
        forward = remote(got, got, fs.at[k], fr.at[k], beside)
        forward.start()
        forwards.append(forward)
    for k in range(nz):
        remote(block(k, 1 - y), block(k, 1 - y), ys.at[k], yr.at[k], beyond).wait()
    for t in range(1, nz):

        @pl.when((z - t + 1 >= 0) & (z < nz - 1))
        def _():
            remote(block(z, y), block(z, y), rs.at[t], rr.at[t], right).wait_send()

        @pl.when((z + t - 1 < nz) & (z > 0))
        def _():
            remote(block(z, y), block(z, y), ls.at[t], lr.at[t], left).wait_send()

    for j in range(2):

        @pl.when(c * 2 + j != me)
        def _():
            remote(heads.at[j], out.at[seq, x], hs.at[j], hr.at[x], (seq, c * 2 + j)).wait_send()

    for copy in small + forwards + [ccopy]:
        copy.wait()
    own_meta.wait()
    own_cot.wait()


def keys_gather(cid, n, heads, meta, cot):
    nz = n // 2
    return comm_call(
        functools.partial(keys_gather_kernel, n),
        cid,
        [
            jax.ShapeDtypeStruct((n,) + heads.shape, BF16),
            jax.ShapeDtypeStruct((n,) + meta.shape, F32),
            jax.ShapeDtypeStruct((GROUP,) + cot.shape, BF16),
        ],
        [DMA((2,)), DMA((2,)), DMA((2,)), DMA((n - 1,)), DMA((n - 1,)), DMA((nz,)), DMA((nz,)), DMA((nz,)),
         DMA((nz,)), DMA((nz,)), DMA((nz,)), DMA, DMA((2,)), DMA((2,)), DMA, DMA, DMA((2,)), DMA((2,))],
        [ANY] * 3,
        [ANY] * 3,
    )(heads, meta, cot)


def keys_reduce_kernel(n, src, out, y_got, r_got, l_got, r_out, l_out, moved, ys, yr, rs, rr, ls, lr, hs, hr, local):
    seq, me, x, c = place_now()
    y = seq % 2
    z = seq // 2
    nz = n // 2
    right = (seq + 2, me)
    left = (seq - 2, me)
    beyond = (z * 2 + 1 - y, me)
    barrier = pltpu.get_barrier_semaphore()
    for d in range(1, GROUP):
        pl.semaphore_signal(barrier, inc=1, device_id=(seq, lax.rem(me + d, GROUP)), device_id_type=MESH)
    pl.semaphore_signal(barrier, inc=1, device_id=beyond, device_id_type=MESH)

    @pl.when(z > 0)
    def _():
        pl.semaphore_signal(barrier, inc=1, device_id=left, device_id_type=MESH)

    @pl.when(z < nz - 1)
    def _():
        pl.semaphore_signal(barrier, inc=1, device_id=right, device_id_type=MESH)

    chain = jnp.where(z > 0, 1, 0) + jnp.where(z < nz - 1, 1, 0)
    pl.semaphore_wait(barrier, GROUP + chain)

    def swap(k):
        return remote(src.at[k * 2 + 1 - y], y_got.at[k], ys.at[k], yr.at[k], beyond)

    for t in range(1, nz):
        go_right = z + nz - t
        go_left = z - nz + t

        @pl.when(go_right < nz)
        def _():
            swap(go_right).start()

        @pl.when(go_left >= 0)
        def _():
            swap(go_left).start()

    swap(z).start()

    def pair_sum(k, more, to):
        def body(i, carry):
            half = i // 2
            span = pl.ds(pl.multiple_of((i % 2) * 256, 256), 256)
            total = src[k * 2 + y, half, span, :].astype(F32) + y_got[k, half, span, :].astype(F32)
            for ref in more:
                total = total + ref[half, span, :].astype(F32)
            to[half, span, :] = total.astype(BF16)
            return carry

        lax.fori_loop(0, 4, body, 0)

    for t in range(1, nz):
        go_right = z + nz - t
        go_left = z - nz + t

        @pl.when(go_right < nz)
        def _():
            swap(go_right).wait_recv()
            if t == 1:
                pair_sum(go_right, [], r_out.at[t - 1])
            else:

                @pl.when(z > 0)
                def _():
                    remote(r_out.at[t - 1], r_got.at[t - 2], rs.at[t - 2], rr.at[t - 2], left).wait_recv()
                    pair_sum(go_right, [r_got.at[t - 2]], r_out.at[t - 1])

                @pl.when(z == 0)
                def _():
                    pair_sum(go_right, [], r_out.at[t - 1])

            remote(r_out.at[t - 1], r_got.at[t - 1], rs.at[t - 1], rr.at[t - 1], right).start()

        @pl.when(go_left >= 0)
        def _():
            swap(go_left).wait_recv()
            if t == 1:
                pair_sum(go_left, [], l_out.at[t - 1])
            else:

                @pl.when(z < nz - 1)
                def _():
                    remote(l_out.at[t - 1], l_got.at[t - 2], ls.at[t - 2], lr.at[t - 2], right).wait_recv()
                    pair_sum(go_left, [l_got.at[t - 2]], l_out.at[t - 1])

                @pl.when(z == nz - 1)
                def _():
                    pair_sum(go_left, [], l_out.at[t - 1])

            remote(l_out.at[t - 1], l_got.at[t - 1], ls.at[t - 1], lr.at[t - 1], left).start()

    swap(z).wait_recv()
    last = nz - 2

    def got_left():
        remote(r_out.at[last], r_got.at[last], rs.at[last], rr.at[last], left).wait_recv()

    def got_right():
        remote(l_out.at[last], l_got.at[last], ls.at[last], lr.at[last], right).wait_recv()

    @pl.when(z == 0)
    def _():
        got_right()
        pair_sum(z, [l_got.at[last]], moved)

    @pl.when(z == nz - 1)
    def _():
        got_left()
        pair_sum(z, [r_got.at[last]], moved)

    @pl.when((z > 0) & (z < nz - 1))
    def _():
        got_left()
        got_right()
        pair_sum(z, [r_got.at[last], l_got.at[last]], moved)

    for t in range(2):
        target = t * 2 + x

        @pl.when(target == me)
        def _():
            pltpu.make_async_copy(moved.at[t], out.at[c], local).start()

        @pl.when(target != me)
        def _():
            remote(moved.at[t], out.at[c], hs.at[t], hr.at[c], (seq, target)).start()

    for j in range(2):
        source = c * 2 + j

        @pl.when(source == me)
        def _():
            pltpu.make_async_copy(moved.at[0], out.at[j], local).wait()

        @pl.when(source != me)
        def _():
            remote(moved.at[0], out.at[j], hs.at[0], hr.at[j], (seq, source)).wait_recv()

    for t in range(2):

        @pl.when(t * 2 + x != me)
        def _():
            remote(moved.at[t], out.at[c], hs.at[t], hr.at[c], (seq, t * 2 + x)).wait_send()

    for k in range(nz):
        swap(k).wait_send()
    for t in range(1, nz):

        @pl.when(z + nz - t < nz)
        def _():
            remote(r_out.at[t - 1], r_got.at[t - 1], rs.at[t - 1], rr.at[t - 1], right).wait_send()

        @pl.when(z - nz + t >= 0)
        def _():
            remote(l_out.at[t - 1], l_got.at[t - 1], ls.at[t - 1], lr.at[t - 1], left).wait_send()


def keys_reduce(cid, n, value):
    nz = n // 2
    shape = value.shape[1:]
    chain = pltpu.VMEM((nz - 1,) + shape, BF16)
    return comm_call(
        functools.partial(keys_reduce_kernel, n),
        cid,
        jax.ShapeDtypeStruct(shape, BF16),
        [pltpu.VMEM((nz,) + shape, BF16), chain, chain, chain, chain, pltpu.VMEM(shape, BF16),
         DMA((nz,)), DMA((nz,)), DMA((nz - 1,)), DMA((nz - 1,)), DMA((nz - 1,)), DMA((nz - 1,)),
         DMA((2,)), DMA((2,)), DMA],
        [VMEM],
        VMEM,
    )(value)


def total_kernel(rounds, whole, part, whole_out, part_out, bufs, gots, mine, theirs, ss, rs):
    seq, me, x, c = place_now()
    across = (seq, (1 - x) * 2 + c)
    beside = (seq, x * 2 + 1 - c)
    partners = []
    for r in range(rounds):
        bit = 1 << r
        partners.append((seq + bit - 2 * bit * ((seq // bit) % 2), me))
    greet(partners + [across, beside])
    rows = whole.shape[0]
    bufs[0, :rows, :] = whole[...]
    bufs[0, rows:, :] = part[...]
    for r in range(rounds + 1):
        partner = partners[r] if r < rounds else across
        copy = remote(bufs.at[r], gots.at[r], ss.at[r], rs.at[r], partner)
        copy.start()
        copy.wait()
        if r < rounds:
            bufs[r + 1] = bufs[r] + gots[r]
    mine[0, :rows, :] = bufs[rounds, :rows, :] + gots[rounds, :rows, :]
    mine[0, rows:, :] = bufs[rounds, rows:, :]
    mine[1, rows:, :] = gots[rounds, rows:, :]
    mine[1, :rows, :] = jnp.zeros_like(whole)
    copy = remote(mine, theirs, ss.at[rounds + 1], rs.at[rounds + 1], beside)
    copy.start()
    copy.wait()
    whole_out[...] = mine[0, :rows, :] + theirs[0, :rows, :]
    part_out[x * 2 + c] = mine[0, rows:, :]
    part_out[(1 - x) * 2 + c] = mine[1, rows:, :]
    part_out[x * 2 + 1 - c] = theirs[0, rows:, :]
    part_out[(1 - x) * 2 + 1 - c] = theirs[1, rows:, :]


def totals(cid, n, whole, part):
    rounds = int(math.log2(n))
    rows = whole.shape[0] + part.shape[0]
    return comm_call(
        functools.partial(total_kernel, rounds),
        cid,
        [jax.ShapeDtypeStruct(whole.shape, F32), jax.ShapeDtypeStruct((GROUP,) + part.shape, F32)],
        [pltpu.VMEM((rounds + 1, rows, 128), F32), pltpu.VMEM((rounds + 1, rows, 128), F32),
         pltpu.VMEM((2, rows, 128), F32), pltpu.VMEM((2, rows, 128), F32),
         DMA((rounds + 2,)), DMA((rounds + 2,))],
        [VMEM, VMEM],
        [VMEM, VMEM],
    )(whole, part)


def masks(n, own_ref, meta_ref):
    def column(row):
        return jnp.broadcast_to(own_ref[0, row : row + 1, :], (128, 128)).T

    row_document = column(0)
    row_place = column(1)
    out = []
    for j in range(n):
        key_place = meta_ref[j, 0, 1:2, :]
        key_document = meta_ref[j, 0, 2:3, :]
        allowed = (row_document == key_document) & (key_place <= row_place) | (key_place == row_place)
        out.append(allowed)
    return out


def attend_kernel(n, q_ref, kv_ref, own_ref, meta_ref, low_ref, mixed_ref, total_ref):
    keys = kv_ref[:, 0].reshape(n * 128, DH)
    values = kv_ref[:, 1].reshape(n * 128, DH)
    allowed = masks(n, own_ref, meta_ref)
    for h in range(2):
        cols = slice(h * DH, (h + 1) * DH)
        raw = contract_last(q_ref[:, cols], keys)
        pieces = []
        total = jnp.zeros((128, 128), F32)
        for j in range(n):
            squash = jnp.tanh(raw[:, j * 128 : (j + 1) * 128] * (DH ** (-0.5) / CAP))
            mass = jnp.where(allowed[j], jnp.exp(CAP * squash), 0.0)
            total = total + mass
            pieces.append(mass.astype(BF16))
        row = jnp.sum(total, axis=1, keepdims=True)
        mixed = dot(jnp.concatenate(pieces, axis=1), values) / row
        mixed_ref[:, cols] = mixed
        low_ref[:, cols] = mixed.astype(BF16)
        total_ref[:, h * 128 : (h + 1) * 128] = jnp.broadcast_to(row, (128, 128))


def attend(n, query, pairs, own_meta, metas):
    return pl.pallas_call(
        functools.partial(attend_kernel, n),
        grid=(GROUP,),
        out_shape=[
            jax.ShapeDtypeStruct(query.shape, BF16),
            jax.ShapeDtypeStruct(query.shape, F32),
            jax.ShapeDtypeStruct((query.shape[0], 256), F32),
        ],
        in_specs=[
            pl.BlockSpec((128, 2 * DH), lambda p: (p, 0)),
            pl.BlockSpec((n, 2, 128, DH), lambda p: (0, 0, p, 0)),
            pl.BlockSpec((1, 8, 128), lambda p: (p, 0, 0)),
            pl.BlockSpec((n, 1, 8, 128), lambda p: (0, p, 0, 0)),
        ],
        out_specs=[
            pl.BlockSpec((128, 2 * DH), lambda p: (p, 0)),
            pl.BlockSpec((128, 2 * DH), lambda p: (p, 0)),
            pl.BlockSpec((128, 256), lambda p: (p, 0)),
        ],
        compiler_params=pltpu.CompilerParams(vmem_limit_bytes=VMEM_LIMIT),
    )(query, pairs, own_meta, metas)


def back_pack(n, keys, values, allowed, q_ref, grad_ref, mixed_ref, total_ref, dq_ref, dkv_ref):
    grad_keys = None
    for h in range(2):
        cols = slice(h * DH, (h + 1) * DH)
        query = q_ref[:, cols]
        grad = grad_ref[:, cols]
        delta = jnp.sum(grad.astype(F32) * mixed_ref[:, cols], axis=1, keepdims=True)
        inverse = 1.0 / total_ref[:, h * 128 : (h + 1) * 128]
        raw = contract_last(query, keys)
        grad_share = contract_last(grad, values)
        shares = []
        grads = []
        for j in range(n):
            span = slice(j * 128, (j + 1) * 128)
            squash = jnp.tanh(raw[:, span] * (DH ** (-0.5) / CAP))
            share = jnp.where(allowed[j], jnp.exp(CAP * squash), 0.0) * inverse
            shares.append(share.astype(BF16))
            grads.append(
                (share * (grad_share[:, span] - delta) * ((1.0 - squash * squash) * DH ** (-0.5))).astype(BF16)
            )
        share = jnp.concatenate(shares, axis=1)
        grad_raw = jnp.concatenate(grads, axis=1)
        dq_ref[:, cols] = dot(grad_raw, keys)
        new_keys = contract_first(grad_raw, query)
        new_values = contract_first(share, grad)
        if grad_keys is None:
            grad_keys, grad_values = new_keys, new_values
        else:
            grad_keys, grad_values = grad_keys + new_keys, grad_values + new_values
    dkv_ref[:, 0] = grad_keys.astype(BF16).reshape(n, 128, DH)
    dkv_ref[:, 1] = grad_values.astype(BF16).reshape(n, 128, DH)


class Chain:
    def __init__(self, nz, count, seq, me, partial, keep, scratch):
        self.nz, self.count, self.partial, self.keep = nz, count, partial, keep
        self.z = seq // 2
        self.right, self.left = (seq + 2, me), (seq - 2, me)
        (self.out_r, self.out_l, self.got_r, self.got_l, self.stage, self.ss_r, self.sr_r, self.ss_l, self.sr_l,
         self.keep_sem) = scratch

    @staticmethod
    def scratch(nz, count, rows, width):
        hops = nz - 1
        message = (rows, width)
        sems = DMA((count, hops))
        return [
            pltpu.VMEM((hops,) + message, BF16), pltpu.VMEM((hops,) + message, BF16),
            pltpu.VMEM((count, hops) + message, BF16), pltpu.VMEM((count, hops) + message, BF16),
            pltpu.VMEM((2,) + message, F32), sems, sems, sems, sems, DMA((2,)),
        ]

    def copy_right(self, j, s, peer):
        return remote(
            self.out_r.at[s - 1], self.got_r.at[j, s - 1], self.ss_r.at[j, s - 1], self.sr_r.at[j, s - 1], peer
        )

    def copy_left(self, j, s, peer):
        return remote(
            self.out_l.at[s - 1], self.got_l.at[j, s - 1], self.ss_l.at[j, s - 1], self.sr_l.at[j, s - 1], peer
        )

    def step(self, j, s):
        z, nz = self.z, self.nz

        def one(go, copy, out, got, to, source, first):
            @pl.when(j > 0)
            def _():
                copy(j - 1, s, to).wait_send()

            total = self.partial(go, j)
            more = (s > 1) & jnp.logical_not(first)

            @pl.when(more)
            def _():
                copy(j, s - 1, source).wait_recv()
                out[s - 1] = (total + got[j, s - 2].astype(F32)).astype(BF16)

            @pl.when(jnp.logical_not(more))
            def _():
                out[s - 1] = total.astype(BF16)

            copy(j, s, to).start()

        go_right = z + nz - s
        go_left = z - nz + s

        @pl.when(go_right < nz)
        def _():
            one(go_right, self.copy_right, self.out_r, self.got_r, self.right, self.left, z == 0)

        @pl.when(go_left >= 0)
        def _():
            one(go_left, self.copy_left, self.out_l, self.got_l, self.left, self.right, z == nz - 1)

    def end(self, j):
        z, nz = self.z, self.nz
        k = j % 2

        @pl.when(j >= 2)
        def _():
            self.keep(j - 2, self.stage.at[k], self.keep_sem.at[k]).wait()

        self.stage[k] = self.partial(z, j)

        @pl.when(z > 0)
        def _():
            self.copy_right(j, nz - 1, self.left).wait_recv()
            self.stage[k] += self.got_r[j, nz - 2].astype(F32)

        @pl.when(z < nz - 1)
        def _():
            self.copy_left(j, nz - 1, self.right).wait_recv()
            self.stage[k] += self.got_l[j, nz - 2].astype(F32)

        self.keep(j, self.stage.at[k], self.keep_sem.at[k]).start()

    def run(self, first, last):
        hops = self.nz - 1

        def unit(u, carry):
            j = u // hops
            s = u % hops + 1
            self.step(j, s)

            @pl.when((s == hops) & (j > 0))
            def _():
                self.end(j - 1)

            return carry

        lax.fori_loop(first, last, unit, 0)

    def units(self):
        return self.count * (self.nz - 1)

    def finish(self):
        z, nz = self.z, self.nz
        last = self.count - 1
        self.end(jnp.int32(last))
        for j in range(max(0, last - 1), last + 1):
            self.keep(j, self.stage.at[j % 2], self.keep_sem.at[j % 2]).wait()
        for s in range(1, nz):

            @pl.when(z + nz - s < nz)
            def _():
                self.copy_right(last, s, self.right).wait_send()

            @pl.when(z - nz + s >= 0)
            def _():
                self.copy_left(last, s, self.left).wait_send()


def greet_all(seq, me, nz, others):
    z = seq // 2
    barrier = pltpu.get_barrier_semaphore()
    for peer in others + [(seq + 1 - 2 * (seq % 2), me)]:
        pl.semaphore_signal(barrier, inc=1, device_id=peer, device_id_type=MESH)

    @pl.when(z > 0)
    def _():
        pl.semaphore_signal(barrier, inc=1, device_id=(seq - 2, me), device_id_type=MESH)

    @pl.when(z < nz - 1)
    def _():
        pl.semaphore_signal(barrier, inc=1, device_id=(seq + 2, me), device_id_type=MESH)

    pl.semaphore_wait(barrier, len(others) + 1 + jnp.where(z > 0, 1, 0) + jnp.where(z < nz - 1, 1, 0))


def levels(code, step):
    return (jnp.floor(code.astype(F32) * (1.0 / step)) * step + step / 2.0).astype(BF16)


def gelu_parts(gate):
    root = math.sqrt(2.0 / math.pi)
    square = gate * gate
    bend = jnp.tanh(root * gate * (1.0 + 0.044715 * square))
    value = 0.5 * gate * (1.0 + bend)
    slope = 0.5 * (1.0 + bend) + 0.5 * gate * (1.0 - bend * bend) * root * (1.0 + 3 * 0.044715 * square)
    return value, slope


def strips(count, size, body):
    def step(i, carry):
        body(pl.ds(pl.multiple_of(i * size, size), size))
        return carry

    lax.fori_loop(0, count, step, 0)


def ffn_forward_kernel(tiles, riders, *refs):
    b, wgu, gs, wd, cots, g3, ds = refs[:7]
    refs = refs[7:]
    rider_in, refs = refs[:riders], refs[riders:]
    gu_o, hid_o, hidy_o, down_o, gf_o, sums_o = refs[:6]
    refs = refs[6:]
    rider_out, refs = refs[:riders], refs[riders:]
    (gu, hid, hidy, wbuf, wlev, dbuf, dlev, acc, downs, wsem, dsem, xs, xr, hs, hr, ys, yr, fs, fr,
     gxs, gxr, gcs, gcr, gfs, gfr, rs, rr, ks, outs) = refs
    seq, me, x, c = place_now()
    y = seq % 2
    across = (seq, (1 - x) * 2 + c)
    beside = (seq, x * 2 + 1 - c)
    beyond = (seq + 1 - 2 * y, me)
    rows, tw = gu.shape[2:]
    deep = b.shape[1]
    per = tiles // 4

    def load_up(t):
        return pltpu.make_async_copy(wgu.at[:, pl.ds(pl.multiple_of(t * tw, 128), tw)], wbuf.at[t % 2], wsem.at[t % 2])

    def load_down(t, half):
        start = ((c + half) % 2 * tiles + t) * tw
        return pltpu.make_async_copy(
            wd.at[:, pl.ds(pl.multiple_of(start, 128), tw)], dbuf.at[t % 2, half], dsem.at[t % 2, half]
        )

    load_up(0).start()
    load_up(1).start()
    for t in range(2):
        for half in range(2):
            load_down(t, half).start()
    greet([across, beside, beyond])
    travellers = []
    for i in range(riders):
        copy = remote(rider_in[i], rider_out[i], rs.at[i], rr.at[i], beyond)
        copy.start()
        travellers.append(copy)
    acc[...] = jnp.zeros_like(acc)

    def to_x(t):
        return remote(gu.at[x, t], gu.at[x, t], xs.at[t], xr.at[t], across)

    def to_core(t):
        return remote(hid.at[c * tiles + t], hid.at[c * tiles + t], hs.at[t], hr.at[t], beside)

    def slot(t, core):
        return (2 * core + t // (2 * per)) * per + t % per

    def to_y(t):
        return remote(hid.at[c * tiles + t], hidy.at[slot(t, c)], ys.at[t], yr.at[t], beyond)

    def keep(t, i, core):
        return pltpu.make_async_copy(hid.at[core * tiles + t], hid_o.at[slot(t, core)], ks.at[i, t])

    def wide(t):
        load_up(t).wait()

        def level(span):
            wlev[span, :] = levels(wbuf[t % 2, span, :], 16.0)

        strips(deep // 128, 128, level)

        @pl.when(t + 2 < tiles)
        def _():
            load_up(t + 2).start()

        scale = gs[t]

        def product(span):
            gu[x, t, span, :] = (dot(b[span, :], wlev[...]) * scale).astype(BF16)

        strips(rows // 256, 256, product)
        to_x(t).start()

    def middle(t):
        to_x(t).wait_recv()

        def body(span):
            gate = gu[0, t, span, :].astype(F32)
            up = gu[1, t, span, :].astype(F32)
            hid[c * tiles + t, span, :] = (gelu_parts(gate)[0] * up).astype(BF16)

        strips(rows // 64, 64, body)
        to_core(t).start()

        @pl.when((t // per) % 2 != y)
        def _():
            to_y(t).start()

        @pl.when((t // per) % 2 == y)
        def _():
            keep(t, 0, c).start()

    def narrow(t):
        for half in range(2):
            load_down(t, half).wait()

            def level(span):
                dlev[half, span, :] = levels(dbuf[t % 2, half, span, :], 64.0)

            strips(dlev.shape[1] // 64, 64, level)

        @pl.when(t + 2 < tiles)
        def _():
            for half in range(2):
                load_down(t + 2, half).start()

        to_core(t).wait_recv()

        def product(span):
            acc[span, :] += contract_last(hid[c * tiles + t, span, :], dlev[0]) + contract_last(
                hid[(1 - c) * tiles + t, span, :], dlev[1]
            )

        strips(rows // 256, 256, product)

        @pl.when((t // per) % 2 == y)
        def _():
            keep(t, 1, 1 - c).start()

    def step(i, carry):
        @pl.when(i < tiles)
        def _():
            wide(i)

        @pl.when((i >= 1) & (i < tiles + 1))
        def _():
            middle(i - 1)

        @pl.when(i >= 2)
        def _():
            narrow(i - 2)

        return carry

    lax.fori_loop(0, tiles + 2, step, 0)
    gu_out = pltpu.make_async_copy(gu, gu_o, outs.at[0])
    gu_out.start()

    parts = 4
    size = rows // parts
    sends = []
    own_sends = []
    for k in range(parts):
        span = pl.ds(k * size, size)
        downs[me, span, :] = acc[span, :].astype(BF16)
        part = downs.at[me, span]
        copy = remote(part, part, gxs.at[k], gxr.at[k], across)
        copy.start()
        sends.append(copy)
        copy = remote(part, part, gcs.at[k], gcr.at[k], beside)
        copy.start()
        own_sends.append(copy)

    def pass_on(t, carry):
        @pl.when((t // per) % 2 == y)
        def _():
            remote(hid.at[0], hidy.at[slot(t, c)], ys.at[t], yr.at[t], beyond).wait_recv()
            got = hidy.at[slot(t, c)]
            remote(got, got, fs.at[t], fr.at[t], beside).start()

        return carry

    lax.fori_loop(0, tiles, pass_on, 0)
    forwards = []
    for k in range(parts):
        sends[k].wait_recv()
        got = downs.at[(1 - x) * 2 + c, pl.ds(k * size, size)]
        copy = remote(got, got, gfs.at[k], gfr.at[k], beside)
        copy.start()
        forwards.append(copy)
    for copy in own_sends + forwards:
        copy.wait_recv()
    down_out = pltpu.make_async_copy(downs, down_o, outs.at[3])
    down_out.start()
    sums_o[...] = jnp.zeros_like(sums_o)
    width = GROUP * acc.shape[1]

    def last_norm(i, carry):
        pack = i // 2
        span = pl.ds(pl.multiple_of(i * 64, 64), 64)
        inner = (i % 2) * 64

        def cot_of(j):
            return cots[pack, pl.ds(pl.multiple_of(j * 128 + inner, 64), 64), :].astype(F32)

        square = jnp.zeros((64, 1), F32)
        cross = jnp.zeros((64, 1), F32)
        for j in range(GROUP):
            value = downs[j, span, :].astype(F32) * ds[j]
            square = square + jnp.sum(value * value, axis=1, keepdims=True)
            cross = cross + jnp.sum(value * (cot_of(j) * g3[j]), axis=1, keepdims=True)
        inverse = lax.rsqrt(square * (1.0 / width) + EPSILON)
        raw = downs[me, span, :].astype(F32)
        normed = raw * ds[me] * inverse
        cot = cot_of(me)
        grad = inverse * (cot * g3[me] - normed * (cross * inverse * (1.0 / width)))
        gf_o[span, :] = (grad * ds[me]).astype(BF16)
        sums_o[0:1, :] += jnp.sum(raw * grad, axis=0, keepdims=True)
        sums_o[1:2, :] += jnp.sum(cot * normed, axis=0, keepdims=True)
        return carry

    lax.fori_loop(0, rows // 64, last_norm, 0)

    def drain(t, carry):
        to_x(t).wait_send()
        to_core(t).wait_send()

        @pl.when((t // per) % 2 != y)
        def _():
            to_y(t).wait_send()

        @pl.when((t // per) % 2 == y)
        def _():
            keep(t, 0, c).wait()
            keep(t, 1, 1 - c).wait()
            got = hidy.at[slot(t, c)]
            remote(got, got, fs.at[t], fr.at[t], beside).wait_send()
            got = hidy.at[slot(t, 1 - c)]
            remote(got, got, fs.at[t], fr.at[t], beside).wait_recv()

        return carry

    lax.fori_loop(0, tiles, drain, 0)
    hidy_out = pltpu.make_async_copy(hidy, hidy_o, outs.at[4])
    hidy_out.start()
    for copy in sends + own_sends + forwards:
        copy.wait_send()
    for copy in travellers:
        copy.wait()
    gu_out.wait()
    down_out.wait()
    hidy_out.wait()


def ffn_forward(cid, b, wgu, gs, wd, cots, g3, ds, riders):
    rows, deep = b.shape
    tiles, _, tw = gs.shape
    part = wd.shape[0]
    count = len(riders)
    lone = max(count, 1)
    return comm_call(
        functools.partial(ffn_forward_kernel, tiles, count),
        cid,
        [
            jax.ShapeDtypeStruct((2, tiles, rows, tw), BF16),
            jax.ShapeDtypeStruct((tiles, rows, tw), BF16),
            jax.ShapeDtypeStruct((tiles, rows, tw), BF16),
            jax.ShapeDtypeStruct((GROUP, rows, part), BF16),
            jax.ShapeDtypeStruct((rows, part), BF16),
            jax.ShapeDtypeStruct((8, part), F32),
        ]
        + [jax.ShapeDtypeStruct(r.shape, r.dtype) for r in riders],
        [
            pltpu.VMEM((2, tiles, rows, tw), BF16),
            pltpu.VMEM((2 * tiles, rows, tw), BF16),
            pltpu.VMEM((tiles, rows, tw), BF16),
            pltpu.VMEM((2, deep, tw), BF16),
            pltpu.VMEM((deep, tw), BF16),
            pltpu.VMEM((2, 2, part, tw), BF16),
            pltpu.VMEM((2, part, tw), BF16),
            pltpu.VMEM((rows, part), F32),
            pltpu.VMEM((GROUP, rows, part), BF16),
            DMA((2,)), DMA((2, 2)), DMA((tiles,)), DMA((tiles,)), DMA((tiles,)), DMA((tiles,)), DMA((tiles,)),
            DMA((tiles,)), DMA((tiles,)), DMA((tiles,)), DMA((4,)), DMA((4,)), DMA((4,)), DMA((4,)), DMA((4,)),
            DMA((4,)), DMA((lone,)), DMA((lone,)), DMA((2, tiles)), DMA((5,)),
        ],
        [VMEM, ANY, VMEM, ANY, VMEM, VMEM, VMEM] + [ANY] * count,
        [ANY, ANY, ANY, ANY, VMEM, VMEM] + [ANY] * count,
    )(b, wgu, gs, wd, cots, g3, ds, *riders)


def ffn_backward_kernel(tiles, nz, chained, *refs):
    gf, wd, wgu, gs, gu, hid, hidy = refs[:7]
    dg_o, dgy_o, gsum_o, out, ddown_o = refs[7:12]
    (hh, hy, gfy, wbuf, wlev, dbuf, dlev, pair, co, cgot, near, sx, xgot, dg, acc, low, from_core, to_xb, from_x,
     hsem, wsem, dsem, psem, cs, cr, xs, xr, ys, yr, os, gys, gyr, ccs, ccr, cxs, cxr) = refs[12:48]
    chain_refs = refs[48:]
    seq, me, x, c = place_now()
    y = seq % 2
    z = seq // 2
    across = (seq, (1 - x) * 2 + c)
    beside = (seq, x * 2 + 1 - c)
    beyond = (seq + 1 - 2 * y, me)
    rows, tw = dg.shape[1:]
    part = acc.shape[2]
    deep = GROUP * part
    per = hid.shape[0] // 4 if chained else 0
    ring = dg.shape[0]

    def load_up(t):
        return pltpu.make_async_copy(wgu.at[:, pl.ds(pl.multiple_of(t * tw, 128), tw)], wbuf.at[t % 2], wsem.at[t % 2])

    def load_down(t, half):
        start = ((c + half) % 2 * tiles + t) * tw
        return pltpu.make_async_copy(
            wd.at[:, pl.ds(pl.multiple_of(start, 128), tw)], dbuf.at[t % 2, half], dsem.at[t % 2, half]
        )

    def load_pair(t):
        return pltpu.make_async_copy(gu.at[:, t], pair.at[t % 2], psem.at[t % 2])

    for t in range(2):
        for half in range(2):
            load_down(t, half).start()
        load_pair(t).start()
        load_up(t).start()
    if chained:
        load_hid = pltpu.make_async_copy(hid, hh, hsem.at[0])
        load_hidy = pltpu.make_async_copy(hidy, hy, hsem.at[1])
        load_hid.start()
        load_hidy.start()
    if chained:
        greet_all(seq, me, nz, [across, beside])
        gf_swap = remote(gf, gfy, gys, gyr, beyond)
        gf_swap.start()
    else:
        greet([across, beside, beyond])
    acc[...] = jnp.zeros_like(acc)

    def to_core(t):
        return remote(co.at[t % 2], cgot.at[t], cs.at[t], cr.at[t], beside)

    def to_x(t):
        return remote(sx.at[t % 4], xgot.at[t], xs.at[t], xr.at[t], across)

    def columns(ref, t):
        return ref.at[:, pl.ds(pl.multiple_of(t * tw, 128), tw)]

    def to_y(t):
        return remote(dg.at[t % ring], columns(dgy_o, t), ys.at[t], yr.at[t], beyond)

    def keep(t):
        return pltpu.make_async_copy(dg.at[t % ring], columns(dg_o, t), os.at[t])

    def hidden(t):
        for half in range(2):
            load_down(t, half).wait()

            def level(span):
                dlev[half, span, :] = levels(dbuf[t % 2, half, span, :], 64.0)

            strips(dlev.shape[1] // 64, 64, level)

        @pl.when(t + 2 < tiles)
        def _():
            for half in range(2):
                load_down(t + 2, half).start()

        @pl.when(t >= 2)
        def _():
            to_core(t - 2).wait_send()

        def product(span):
            co[t % 2, span, :] = dot(gf[span, :], dlev[1]).astype(BF16)

        strips(rows // 256, 256, product)
        to_core(t).start()

        def product_near(span):
            near[t % 2, span, :] = dot(gf[span, :], dlev[0])

        strips(rows // 256, 256, product_near)

    def chip(t):
        @pl.when(t >= 4)
        def _():
            to_x(t - 4).wait_send()

        to_core(t).wait_recv()

        def body(span):
            sx[t % 4, span, :] = (near[t % 2, span, :] + cgot[t, span, :].astype(F32)).astype(BF16)

        strips(rows // 64, 64, body)
        to_x(t).start()

    is_gate = jnp.where(x == 0, 1.0, 0.0).astype(F32)

    def own(t):
        load_pair(t).wait()

        @pl.when(t >= ring)
        def _():
            to_y(t - ring).wait_send()
            keep(t - ring).wait()

        to_x(t).wait_recv()
        scale = gs[t]
        gsum_o[t] = jnp.zeros((8, tw), F32)

        def body(span):
            grad = sx[t % 4, span, :].astype(F32) + xgot[t, span, :].astype(F32)
            gate = pair[t % 2, 0, span, :].astype(F32)
            up = pair[t % 2, 1, span, :].astype(F32)
            value, slope = gelu_parts(gate)
            full = grad * (is_gate * (up * slope) + (1.0 - is_gate) * value)
            gsum_o[t, 0:1, :] += jnp.sum(pair[t % 2, x, span, :].astype(F32) * full, axis=0, keepdims=True)
            dg[t % ring, span, :] = (full * scale).astype(BF16)

        strips(rows // 64, 64, body)

        @pl.when(t + 2 < tiles)
        def _():
            load_pair(t + 2).start()

        to_y(t).start()
        keep(t).start()

    def back(t):
        load_up(t).wait()

        def level(span):
            wlev[span, :] = levels(wbuf[t % 2, span, :], 16.0)

        strips(deep // 128, 128, level)

        @pl.when(t + 2 < tiles)
        def _():
            load_up(t + 2).start()

        def product(span):
            for j in range(GROUP):
                acc[j, span, :] += contract_last(dg[t % ring, span, :], wlev[j * part : (j + 1) * part, :])

        strips(rows // 128, 128, product)

    if chained:

        def partial(k, j):
            return contract_first(hh[k * per + j], gf[...]) + contract_first(hy[k * per + j], gfy[...])

        downs = Chain(
            nz, per, seq, me, partial, lambda j, stage, sem: pltpu.make_async_copy(stage, ddown_o.at[j], sem), chain_refs
        )
    hops = nz - 1

    def step(i, carry):
        @pl.when(i < tiles)
        def _():
            hidden(i)

        @pl.when((i >= 1) & (i < tiles + 1))
        def _():
            chip(i - 1)

        if chained:

            @pl.when(i == 1)
            def _():
                gf_swap.wait_recv()
                load_hid.wait()
                load_hidy.wait()

            @pl.when((i >= 1) & (i < 1 + per * hops))
            def _():
                downs.run(i - 1, i)

        @pl.when(i >= 2)
        def _():
            own(i - 2)
            back(i - 2)

        return carry

    lax.fori_loop(0, tiles + 2, step, 0)

    parts = 4
    block = rows // GROUP
    size = block // parts
    order = [1 - x, x]
    js = range(GROUP)
    cores = []
    for i in range(2):
        for k in range(parts):
            owner = order[i] * 2 + 1 - c
            span = pl.ds(k * size, size)
            for j in js:
                low[i, j, span, :] = acc[j, pl.ds(pl.multiple_of(owner * block + k * size, 16), size), :].astype(BF16)
            copy = remote(low.at[i, :, span], from_core.at[i, :, span], ccs.at[i, k], ccr.at[i, k], beside)
            copy.start()
            cores.append(copy)
    sends = []
    for k in range(parts):
        span = pl.ds(k * size, size)
        here = pl.ds(pl.multiple_of((order[0] * 2 + c) * block + k * size, 16), size)
        cores[k].wait_recv()
        for j in js:
            to_xb[j, span, :] = (acc[j, here, :] + from_core[0, j, span, :].astype(F32)).astype(BF16)
        copy = remote(to_xb.at[:, span], from_x.at[:, span], cxs.at[k], cxr.at[k], across)
        copy.start()
        sends.append(copy)
    if chained:
        downs.finish()
    for k in range(parts):
        span = pl.ds(k * size, size)
        here = pl.ds(pl.multiple_of((order[1] * 2 + c) * block + k * size, 16), size)
        cores[parts + k].wait_recv()
        sends[k].wait_recv()
        for j in js:
            out[j, span, :] = acc[j, here, :] + from_core[1, j, span, :].astype(F32) + from_x[j, span, :].astype(F32)

    for copy in cores + sends:
        copy.wait_send()
    for t in range(tiles - 2, tiles):
        to_core(t).wait_send()
    for t in range(tiles - 4, tiles):
        to_x(t).wait_send()
    for t in range(tiles - ring, tiles):
        to_y(t).wait_send()
        keep(t).wait()

    def drain(t, carry):
        to_y(t).wait_recv()
        return carry

    lax.fori_loop(0, tiles, drain, 0)
    if chained:
        gf_swap.wait_send()


def ffn_backward(cid, n, gf, wd, wgu, gs, gu, hid, hidy):
    rows, part = gf.shape
    deep = wgu.shape[0]
    tiles, _, tw = gs.shape
    nz = n // 2
    chained = nz == 4
    per = tiles // nz if chained else 1
    hops = nz - 1 if chained else 1
    block = rows // GROUP
    half = (tiles, rows, tw) if chained else (1, 16, 128)
    message = (tw, part) if chained else (16, 128)
    ring = 4
    return comm_call(
        functools.partial(ffn_backward_kernel, tiles, nz, chained),
        cid,
        [
            jax.ShapeDtypeStruct((rows, tiles * tw), BF16),
            jax.ShapeDtypeStruct((rows, tiles * tw), BF16),
            jax.ShapeDtypeStruct((tiles, 8, tw), F32),
            jax.ShapeDtypeStruct((GROUP, block, part), F32),
            jax.ShapeDtypeStruct((per,) + message, F32),
        ],
        [
            pltpu.VMEM(half, BF16),
            pltpu.VMEM(half, BF16),
            pltpu.VMEM((rows, part), BF16),
            pltpu.VMEM((2, deep, tw), BF16),
            pltpu.VMEM((deep, tw), BF16),
            pltpu.VMEM((2, 2, part, tw), BF16),
            pltpu.VMEM((2, part, tw), BF16),
            pltpu.VMEM((2, 2, rows, tw), BF16),
            pltpu.VMEM((2, rows, tw), BF16),
            pltpu.VMEM((tiles, rows, tw), BF16),
            pltpu.VMEM((2, rows, tw), F32),
            pltpu.VMEM((4, rows, tw), BF16),
            pltpu.VMEM((tiles, rows, tw), BF16),
            pltpu.VMEM((ring, rows, tw), BF16),
            pltpu.VMEM((GROUP, rows, part), F32),
            pltpu.VMEM((2, GROUP, block, part), BF16),
            pltpu.VMEM((2, GROUP, block, part), BF16),
            pltpu.VMEM((GROUP, block, part), BF16),
            pltpu.VMEM((GROUP, block, part), BF16),
            DMA((2,)), DMA((2,)), DMA((2, 2)), DMA((2,)), DMA((tiles,)), DMA((tiles,)), DMA((tiles,)), DMA((tiles,)),
            DMA((tiles,)), DMA((tiles,)), DMA((tiles,)), DMA, DMA, DMA((2, 4)), DMA((2, 4)), DMA((4,)), DMA((4,)),
        ]
        + (Chain.scratch(nz, per, *message) if chained else []),
        [VMEM, ANY, ANY, VMEM, ANY, ANY, ANY],
        [ANY, ANY, VMEM, VMEM, ANY],
    )(gf, wd, wgu, gs, gu, hid, hidy)


def gate_chain(nz, first, count, seq, me, bt, bty, dg, dgy, out, slabs, slab_sem, scratch):
    size = bt.shape[0] // nz
    loads = []
    for i, ref in enumerate((dg, dgy)):
        copy = pltpu.make_async_copy(ref.at[:, pl.ds(first * TILE, count * TILE)], slabs.at[i], slab_sem.at[i])
        copy.start()
        loads.append(copy)

    def partial(k, j):
        rows = pl.ds(pl.multiple_of(k * size, 16), size)
        cols = pl.ds(pl.multiple_of(j * TILE, 128), TILE)
        return dot(bt[rows, :], slabs[0, :, cols]) + dot(bty[rows, :], slabs[1, :, cols])

    def keep(j, stage, sem):
        return pltpu.make_async_copy(stage, out.at[:, pl.ds(pl.multiple_of(j * TILE, 128), TILE)], sem)

    return Chain(nz, count, seq, me, partial, keep, scratch), loads


def gate_scratch(nz, count, bt):
    rows = bt.shape[1]
    return [pltpu.VMEM((2, rows, count * TILE), BF16), DMA((2,))] + Chain.scratch(
        nz, count, bt.shape[0] // nz, TILE
    )


def branch_back_kernel(n, tiles, *refs):
    (gsi, mid, raw, cot, g2, g3, scale, wo, q, mixed, mass, own_meta, metas, kv, bt, bty, dg, dgy) = refs[:18]
    dmid, sums, gy, gyy, dq, dkv, gate_o = refs[18:25]
    (low, gys, gy_all, part, from_core, to_x, from_x, grad, kvs, dkvs, es, er, el, cs, cr, xs, xr, ks, ds, yss, ysr,
     ows) = refs[25:47]
    rest = refs[47:]
    seq, me, x, c = place_now()
    nz = n // 2
    across = (seq, (1 - x) * 2 + c)
    beside = (seq, x * 2 + 1 - c)
    beyond = (seq + 1 - 2 * (seq % 2), me)
    peers = [(seq, lax.rem(me + d, GROUP)) for d in range(1, GROUP)]
    chain = None
    if tiles:
        chain, loads = gate_chain(nz, 0, tiles, seq, me, bt, bty, dg, dgy, gate_o, rest[0], rest[1], rest[2:])
        greet_all(seq, me, nz, peers)
    else:
        greet(peers + [beyond])
    width = GROUP * raw.shape[2]
    mean = 1.0 / width
    sums[...] = jnp.zeros_like(sums)
    js = range(GROUP)

    def rowsum(values):
        total = values[0]
        for value in values[1:]:
            total = total + value
        return jnp.sum(total, axis=1, keepdims=True) * mean

    def norms(span):
        middle = [mid[j, span, :] for j in js]
        up = [gsi[j, span, :] for j in js]
        inverse = lax.rsqrt(rowsum([v * v for v in middle]) + EPSILON)
        third = [v * inverse for v in middle]
        scaled = [up[j] * g3[j] for j in js]
        cross = rowsum([scaled[j] * third[j] for j in js])
        grad_middle = [
            cot[j, span, :].astype(F32) + inverse * (scaled[j] - third[j] * cross) for j in js
        ]
        plain = [raw[j, span, :].astype(F32) for j in js]
        branch = [plain[j] * scale[j] for j in js]
        inverse = lax.rsqrt(rowsum([v * v for v in branch]) + EPSILON)
        second = [v * inverse for v in branch]
        scaled = [grad_middle[j] * g2[j] for j in js]
        cross = rowsum([scaled[j] * second[j] for j in js])
        for j in js:
            full = inverse * (scaled[j] - second[j] * cross)
            gys[j, span, :] = (full * scale[j]).astype(BF16)
            dmid[j, span, :] = grad_middle[j]
            sums[j, 0:1, :] += jnp.sum(grad_middle[j] * second[j], axis=0, keepdims=True)
            sums[j, 1:2, :] += jnp.sum(up[j] * third[j], axis=0, keepdims=True)
            sums[j, 2:3, :] += jnp.sum(plain[j] * full, axis=0, keepdims=True)

    strips(raw.shape[1] // 16, 16, norms)

    copies = []
    for d in (2, 1, 3):
        peer = peers[d - 1]
        copy = remote(gys.at[peer[1]], gy_all.at[me], es.at[d - 1], er.at[d - 1], peer)
        copy.start()
        copies.append(copy)
    own = pltpu.make_async_copy(gys.at[me], gy_all.at[me], el)
    own.start()
    for p in range(2):
        pltpu.make_async_copy(kv.at[:, :, pl.ds(p * 128, 128)], kvs.at[p], ks.at[p]).start()
    units = chain.units() if chain else 0
    at = [0]

    def beside_work(count):
        if chain:
            last = min(units, at[0] + count)
            chain.run(at[0], last)
            at[0] = last

    if chain:
        for load in loads:
            load.wait()
    beside_work(3)
    for copy in copies:
        copy.wait_recv()
    own.wait()
    gy_out = pltpu.make_async_copy(gy_all, gy, ows)
    gy_out.start()
    swap = remote(gy_all, gyy, yss, ysr, beyond)
    swap.start()

    heads = part.shape[3]
    rows = part.shape[2]
    order = [1 - x, x]

    def product(i, k, to):
        grad_branch = gy_all[...].reshape(rows, raw.shape[2])
        start = (order[i] * 2 + k) * heads
        to[...] = dot(grad_branch, wo[:, pl.ds(pl.multiple_of(start, 128), heads)]).astype(BF16)

    cores = []
    for i in range(2):
        product(i, 1 - c, part.at[i, 0])
        copy = remote(part.at[i, 0], from_core.at[i], cs.at[i], cr.at[i], beside)
        copy.start()
        cores.append(copy)
    for i in range(2):
        product(i, c, part.at[i, 1])
    cores[0].wait_recv()

    def add_core(span):
        to_x[span, :] = (part[0, 1, span, :].astype(F32) + from_core[0, span, :].astype(F32)).astype(BF16)

    strips(rows // 64, 64, add_core)
    over = remote(to_x, from_x, xs, xr, across)
    over.start()
    beside_work(4)
    cores[1].wait_recv()
    over.wait_recv()

    def add_all(span):
        grad[span, :] = (
            part[1, 1, span, :].astype(F32) + from_core[1, span, :].astype(F32) + from_x[span, :].astype(F32)
        ).astype(BF16)

    strips(rows // 64, 64, add_all)

    def load_pack(p):
        return pltpu.make_async_copy(
            kv.at[:, :, pl.ds(pl.multiple_of(p * 128, 128), 128)], kvs.at[p % 2], ks.at[p % 2]
        )

    def store_pack(p):
        return pltpu.make_async_copy(
            dkvs.at[p % 2], dkv.at[:, :, pl.ds(pl.multiple_of(p * 128, 128), 128)], ds.at[p % 2]
        )

    base = at[0]
    each = max(0, units - base) // GROUP

    def one_pack(p, carry):
        load_pack(p).wait()

        @pl.when(p >= 2)
        def _():
            store_pack(p - 2).wait()

        span = pl.ds(pl.multiple_of(p * 128, 128), 128)
        keys = kvs[p % 2, :, 0].reshape(n * 128, DH)
        values = kvs[p % 2, :, 1].reshape(n * 128, DH)
        allowed = masks(n, own_meta.at[pl.ds(p, 1)], metas.at[:, pl.ds(p, 1)])
        back_pack(
            n, keys, values, allowed, q.at[span], grad.at[span], mixed.at[span], mass.at[span], dq.at[span],
            dkvs.at[p % 2],
        )
        store_pack(p).start()

        @pl.when(p + 2 < GROUP)
        def _():
            load_pack(p + 2).start()

        if each:
            chain.run(base + p * each, base + (p + 1) * each)
        return carry

    lax.fori_loop(0, GROUP, one_pack, 0)
    at[0] = base + GROUP * each
    beside_work(units)
    if chain:
        chain.finish()
    for copy in copies + cores + [over]:
        copy.wait_send()
    store_pack(2).wait()
    store_pack(3).wait()
    swap.wait()
    gy_out.wait()


def branch_back(cid, n, tiles, gsi, mid, raw, cot, g2, g3, scale, wo, q, mixed, mass, own_meta, metas, kv, pairs):
    bt, bty, dg, dgy = pairs
    own, part = raw.shape[1:]
    rows = q.shape[0]
    heads = q.shape[1]
    block = lambda kind: jax.ShapeDtypeStruct((GROUP, own, part), kind)
    gate_rows = bt.shape[0] // (n // 2)
    pack = (2, n, 2, own, DH)
    return comm_call(
        functools.partial(branch_back_kernel, n, tiles),
        cid,
        [
            block(F32),
            jax.ShapeDtypeStruct((GROUP, 8, part), F32),
            block(BF16),
            block(BF16),
            jax.ShapeDtypeStruct(q.shape, F32),
            jax.ShapeDtypeStruct(kv.shape, BF16),
            jax.ShapeDtypeStruct((gate_rows, max(tiles, 1) * TILE), F32),
        ],
        [
            pltpu.VMEM((8, 128), BF16),
            pltpu.VMEM((GROUP, own, part), BF16),
            pltpu.VMEM((GROUP, own, part), BF16),
            pltpu.VMEM((2, 2, rows, heads), BF16),
            pltpu.VMEM((2, rows, heads), BF16),
            pltpu.VMEM((rows, heads), BF16),
            pltpu.VMEM((rows, heads), BF16),
            pltpu.VMEM((rows, heads), BF16),
            pltpu.VMEM(pack, BF16),
            pltpu.VMEM(pack, BF16),
            DMA((3,)), DMA((3,)), DMA, DMA((2,)), DMA((2,)), DMA, DMA, DMA((2,)), DMA((2,)), DMA, DMA, DMA,
        ]
        + (gate_scratch(n // 2, tiles, bt) if tiles else []),
        [VMEM] * 13 + [ANY] + [VMEM] * 2 + [ANY] * 2,
        [VMEM, VMEM, ANY, ANY, VMEM, ANY, ANY],
    )(gsi, mid, raw, cot, g2, g3, scale, wo, q, mixed, mass, own_meta, metas, kv, bt, bty, dg, dgy)


def keys_back_kernel(n, first, tiles, *refs):
    (src, dq, q_raw, p_raw, cosine, sine, q_scale, p_scale, wq, wkv, bt, bty, dg, dgy) = refs[:14]
    joined, joined_y, out, sums, gate_o = refs[14:19]
    (y_got, r_got, l_got, r_out, l_out, moved, back, acc, low, from_core, to_xb, from_x,
     ys, yr, rs, rr, ls, lr, hs, hr, local, jys, jyr, ccs, ccr, cxs, cxr) = refs[19:46]
    slabs, slab_sem, *rest = refs[46:]
    seq, me, x, c = place_now()
    y = seq % 2
    z = seq // 2
    nz = n // 2
    right = (seq + 2, me)
    left = (seq - 2, me)
    beyond = (z * 2 + 1 - y, me)
    across = (seq, (1 - x) * 2 + c)
    beside = (seq, x * 2 + 1 - c)
    chain, loads = gate_chain(nz, first, tiles, seq, me, bt, bty, dg, dgy, gate_o, slabs, slab_sem, rest)
    greet_all(seq, me, nz, [(seq, lax.rem(me + d, GROUP)) for d in range(1, GROUP)])
    rows, width = dq.shape
    deep = acc.shape[1]
    half = DH // 2

    def swap(k):
        return remote(src.at[k * 2 + 1 - y], y_got.at[k], ys.at[k], yr.at[k], beyond)

    for t in range(1, nz):
        go_right = z + nz - t
        go_left = z - nz + t

        @pl.when(go_right < nz)
        def _():
            swap(go_right).start()

        @pl.when(go_left >= 0)
        def _():
            swap(go_left).start()

    swap(z).start()
    sums[...] = jnp.zeros_like(sums)

    def turn_queries(span):
        cos = cosine[span, :]
        sin = sine[span, :]
        for h in range(2):
            a = slice(h * DH, h * DH + half)
            b = slice(h * DH + half, (h + 1) * DH)
            one = dq[span, a]
            two = dq[span, b]
            for cols, full in ((a, one * cos + two * sin), (b, two * cos - one * sin)):
                sums[0:1, cols] += jnp.sum(q_raw[span, cols] * full, axis=0, keepdims=True)
                joined[span, cols] = (full * q_scale[:, cols]).astype(BF16)

    strips(rows // 64, 64, turn_queries)

    def query_part(span):
        acc[span, :] = contract_last(joined[span, :width], wq[...])

    strips(rows // 128, 128, query_part)

    def pair_sum(k, more, to):
        def body(i, carry):
            part = i // 4
            span = pl.ds(pl.multiple_of((i % 4) * 128, 128), 128)
            total = src[k * 2 + y, part, span, :].astype(F32) + y_got[k, part, span, :].astype(F32)
            for ref in more:
                total = total + ref[part, span, :].astype(F32)
            to[part, span, :] = total.astype(BF16)
            return carry

        lax.fori_loop(0, 8, body, 0)

    for load in loads:
        load.wait()
    units = chain.units()
    at = [0]

    def beside_work(count):
        last = min(units, at[0] + count)
        chain.run(at[0], last)
        at[0] = last

    for t in range(1, nz):
        go_right = z + nz - t
        go_left = z - nz + t

        def hop(go, at_end, got, send, ss, sr, to, source):
            swap(go).wait_recv()
            if t == 1:
                pair_sum(go, [], send.at[t - 1])
            else:

                @pl.when(jnp.logical_not(at_end))
                def _():
                    remote(send.at[t - 1], got.at[t - 2], ss.at[t - 2], sr.at[t - 2], source).wait_recv()
                    pair_sum(go, [got.at[t - 2]], send.at[t - 1])

                @pl.when(at_end)
                def _():
                    pair_sum(go, [], send.at[t - 1])

            remote(send.at[t - 1], got.at[t - 1], ss.at[t - 1], sr.at[t - 1], to).start()

        @pl.when(go_right < nz)
        def _():
            hop(go_right, z == 0, r_got, r_out, rs, rr, right, left)

        @pl.when(go_left >= 0)
        def _():
            hop(go_left, z == nz - 1, l_got, l_out, ls, lr, left, right)

        beside_work(1)

    swap(z).wait_recv()
    last = nz - 2

    def got_left():
        remote(r_out.at[last], r_got.at[last], rs.at[last], rr.at[last], left).wait_recv()

    def got_right():
        remote(l_out.at[last], l_got.at[last], ls.at[last], lr.at[last], right).wait_recv()

    @pl.when(z == 0)
    def _():
        got_right()
        pair_sum(z, [l_got.at[last]], moved)

    @pl.when(z == nz - 1)
    def _():
        got_left()
        pair_sum(z, [r_got.at[last]], moved)

    @pl.when((z > 0) & (z < nz - 1))
    def _():
        got_left()
        got_right()
        pair_sum(z, [r_got.at[last], l_got.at[last]], moved)

    for t in range(2):
        target = t * 2 + x

        @pl.when(target == me)
        def _():
            pltpu.make_async_copy(moved.at[t], back.at[c], local).start()

        @pl.when(target != me)
        def _():
            remote(moved.at[t], back.at[c], hs.at[t], hr.at[c], (seq, target)).start()

    beside_work(1)
    for j in range(2):
        source = c * 2 + j

        @pl.when(source == me)
        def _():
            pltpu.make_async_copy(moved.at[0], back.at[j], local).wait()

        @pl.when(source != me)
        def _():
            remote(moved.at[0], back.at[j], hs.at[0], hr.at[j], (seq, source)).wait_recv()

    is_key = jnp.where(x == 0, 1.0, 0.0).astype(F32)

    def turn_pairs(span):
        cos = is_key * cosine[span, :] + (1.0 - is_key)
        sin = is_key * sine[span, :]
        for h in range(2):
            a = slice(h * DH, h * DH + half)
            b = slice(h * DH + half, (h + 1) * DH)
            one = back[h, span, :half].astype(F32)
            two = back[h, span, half:].astype(F32)
            for cols, full in ((a, one * cos + two * sin), (b, two * cos - one * sin)):
                sums[1:2, cols] += jnp.sum(p_raw[span, cols] * full, axis=0, keepdims=True)
                joined[span, width + cols.start : width + cols.stop] = (full * p_scale[:, cols]).astype(BF16)

    strips(rows // 64, 64, turn_pairs)
    joined_swap = remote(joined, joined_y, jys, jyr, beyond)
    joined_swap.start()

    def pair_part(span):
        acc[span, :] += contract_last(joined[span, width:], wkv[...])

    strips(rows // 128, 128, pair_part)

    parts = 4
    block = rows // GROUP
    size = block // parts
    order = [1 - x, x]
    cores = []
    for i in range(2):
        for k in range(parts):
            owner = order[i] * 2 + 1 - c
            span = pl.ds(k * size, size)
            low[i, span, :] = acc[pl.ds(pl.multiple_of(owner * block + k * size, 16), size), :].astype(BF16)
            copy = remote(low.at[i, span], from_core.at[i, span], ccs.at[i, k], ccr.at[i, k], beside)
            copy.start()
            cores.append(copy)
    sends = []
    for k in range(parts):
        span = pl.ds(k * size, size)
        here = pl.ds(pl.multiple_of((order[0] * 2 + c) * block + k * size, 16), size)
        cores[k].wait_recv()
        to_xb[span, :] = (acc[here, :] + from_core[0, span, :].astype(F32)).astype(BF16)
        copy = remote(to_xb.at[span], from_x.at[span], cxs.at[k], cxr.at[k], across)
        copy.start()
        sends.append(copy)
    beside_work(units)
    chain.finish()
    for k in range(parts):
        span = pl.ds(k * size, size)
        here = pl.ds(pl.multiple_of((order[1] * 2 + c) * block + k * size, 16), size)
        cores[parts + k].wait_recv()
        sends[k].wait_recv()
        out[span, :] = acc[here, :] + from_core[1, span, :].astype(F32) + from_x[span, :].astype(F32)

    for t in range(2):

        @pl.when(t * 2 + x != me)
        def _():
            remote(moved.at[t], back.at[c], hs.at[t], hr.at[c], (seq, t * 2 + x)).wait_send()

    for k in range(nz):
        swap(k).wait_send()
    for t in range(1, nz):

        @pl.when(z + nz - t < nz)
        def _():
            remote(r_out.at[t - 1], r_got.at[t - 1], rs.at[t - 1], rr.at[t - 1], right).wait_send()

        @pl.when(z - nz + t >= 0)
        def _():
            remote(l_out.at[t - 1], l_got.at[t - 1], ls.at[t - 1], lr.at[t - 1], left).wait_send()

    for copy in cores + sends:
        copy.wait_send()
    joined_swap.wait()


def keys_back(cid, n, first, tiles, src, dq, q_raw, p_raw, cosine, sine, q_scale, p_scale, wq, wkv, pairs):
    bt, bty, dg, dgy = pairs
    nz = n // 2
    rows, width = dq.shape
    deep = wq.shape[0]
    block = rows // GROUP
    shape = src.shape[1:]
    chain = pltpu.VMEM((nz - 1,) + shape, BF16)
    joined = jax.ShapeDtypeStruct((rows, 2 * width), BF16)
    return comm_call(
        functools.partial(keys_back_kernel, n, first, tiles),
        cid,
        [
            joined,
            joined,
            jax.ShapeDtypeStruct((block, deep), F32),
            jax.ShapeDtypeStruct((8, width), F32),
            jax.ShapeDtypeStruct((bt.shape[0] // nz, tiles * TILE), F32),
        ],
        [
            pltpu.VMEM((nz,) + shape, BF16), chain, chain, chain, chain, pltpu.VMEM(shape, BF16), pltpu.VMEM(shape, BF16),
            pltpu.VMEM((rows, deep), F32),
            pltpu.VMEM((2, block, deep), BF16),
            pltpu.VMEM((2, block, deep), BF16),
            pltpu.VMEM((block, deep), BF16),
            pltpu.VMEM((block, deep), BF16),
            DMA((nz,)), DMA((nz,)), DMA((nz - 1,)), DMA((nz - 1,)), DMA((nz - 1,)), DMA((nz - 1,)),
            DMA((2,)), DMA((2,)), DMA, DMA, DMA, DMA((2, 4)), DMA((2, 4)), DMA((4,)), DMA((4,)),
        ]
        + gate_scratch(nz, tiles, bt),
        [VMEM] * 12 + [ANY] * 2,
        [VMEM, ANY, VMEM, VMEM, ANY],
    )(src, dq, q_raw, p_raw, cosine, sine, q_scale, p_scale, wq, wkv, bt, bty, dg, dgy)


def finish_kernel(n, rounds, first, tiles, *refs):
    (whole, part, bt, bty, dg, dgy, ot, oty, gy, gyy, at, aty, joined, joined_y) = refs[:14]
    whole_out, part_out, gate_o, output_o, attention_o = refs[14:19]
    bufs, gots, mine, theirs, ss, rs = refs[19:25]
    slabs, slab_sem = refs[25:27]
    gate_refs, output_refs, attention_refs = refs[27:37], refs[37:47], refs[47:57]
    seq, me, x, c = place_now()
    nz = n // 2
    across = (seq, (1 - x) * 2 + c)
    beside = (seq, x * 2 + 1 - c)
    gates, loads = gate_chain(nz, first, tiles, seq, me, bt, bty, dg, dgy, gate_o, slabs, slab_sem, gate_refs)
    output_rows = ot.shape[0] // nz
    attention_rows = at.shape[0] // nz
    wide = joined.shape[1] // 2

    def output_partial(k, j):
        rows = pl.ds(pl.multiple_of(k * output_rows, 16), output_rows)
        return dot(ot[rows, :], gy[...]) + dot(oty[rows, :], gyy[...])

    def attention_partial(k, j):
        rows = pl.ds(pl.multiple_of(k * attention_rows, 16), attention_rows)
        cols = pl.ds(pl.multiple_of(j * wide, 128), wide)
        return dot(at[rows, :], joined[:, cols]) + dot(aty[rows, :], joined_y[:, cols])

    outputs = Chain(
        nz, 1, seq, me, output_partial, lambda j, stage, sem: pltpu.make_async_copy(stage, output_o, sem), output_refs
    )
    attentions = Chain(
        nz,
        2,
        seq,
        me,
        attention_partial,
        lambda j, stage, sem: pltpu.make_async_copy(
            stage, attention_o.at[:, pl.ds(pl.multiple_of(j * wide, 128), wide)], sem
        ),
        attention_refs,
    )
    partners = []
    for r in range(rounds):
        bit = 1 << r
        partners.append((seq + bit - 2 * bit * ((seq // bit) % 2), me))
    greet([(lax.rem(seq + d, n), me) for d in range(1, n)] + [across, beside])
    for load in loads:
        load.wait()
    rows = whole.shape[0]
    bufs[0, :rows, :] = whole[...]
    bufs[0, rows:, :] = part[...]
    work = [(gates, u) for u in range(0, gates.units(), 3)]
    work += [(outputs, 0), (attentions, 0), (attentions, 3)]
    at_work = [0]

    def beside_work(count):
        todo = work[at_work[0] : at_work[0] + count]
        at_work[0] += count
        start = None
        for i, (chain, u) in enumerate(todo):
            if start is None:
                start = u
            if i + 1 == len(todo) or todo[i + 1][0] is not chain:
                chain.run(start, u + 3)
                start = None

    for r in range(rounds + 1):
        partner = partners[r] if r < rounds else across
        copy = remote(bufs.at[r], gots.at[r], ss.at[r], rs.at[r], partner)
        copy.start()
        beside_work(1)
        copy.wait()
        if r < rounds:
            bufs[r + 1] = bufs[r] + gots[r]
    mine[0, :rows, :] = bufs[rounds, :rows, :] + gots[rounds, :rows, :]
    mine[0, rows:, :] = bufs[rounds, rows:, :]
    mine[1, rows:, :] = gots[rounds, rows:, :]
    mine[1, :rows, :] = jnp.zeros((rows, 128), F32)
    copy = remote(mine, theirs, ss.at[rounds + 1], rs.at[rounds + 1], beside)
    copy.start()
    beside_work(len(work))
    copy.wait()
    whole_out[...] = mine[0, :rows, :] + theirs[0, :rows, :]
    part_out[x * 2 + c] = mine[0, rows:, :]
    part_out[(1 - x) * 2 + c] = mine[1, rows:, :]
    part_out[x * 2 + 1 - c] = theirs[0, rows:, :]
    part_out[(1 - x) * 2 + 1 - c] = theirs[1, rows:, :]
    gates.finish()
    outputs.finish()
    attentions.finish()


def finish(cid, n, first, tiles, whole, part, pairs, output_pairs, attention_pairs):
    bt, bty, dg, dgy = pairs
    ot, oty, gy, gyy = output_pairs
    at, aty, joined, joined_y = attention_pairs
    nz = n // 2
    rounds = int(math.log2(n))
    rows = whole.shape[0] + part.shape[0]
    output_rows = ot.shape[0] // nz
    attention_rows = at.shape[0] // nz
    return comm_call(
        functools.partial(finish_kernel, n, rounds, first, tiles),
        cid,
        [
            jax.ShapeDtypeStruct(whole.shape, F32),
            jax.ShapeDtypeStruct((GROUP,) + part.shape, F32),
            jax.ShapeDtypeStruct((bt.shape[0] // nz, tiles * TILE), F32),
            jax.ShapeDtypeStruct((output_rows, gy.shape[1]), F32),
            jax.ShapeDtypeStruct((attention_rows, joined.shape[1]), F32),
        ],
        [
            pltpu.VMEM((rounds + 1, rows, 128), F32),
            pltpu.VMEM((rounds + 1, rows, 128), F32),
            pltpu.VMEM((2, rows, 128), F32),
            pltpu.VMEM((2, rows, 128), F32),
            DMA((rounds + 2,)),
            DMA((rounds + 2,)),
        ]
        + gate_scratch(nz, tiles, bt)
        + Chain.scratch(nz, 1, output_rows, gy.shape[1])
        + Chain.scratch(nz, 2, attention_rows, joined.shape[1] // 2),
        [VMEM] * 4 + [ANY] * 2 + [VMEM] * 8,
        [VMEM, VMEM, ANY, ANY, ANY],
    )(whole, part, bt, bty, dg, dgy, ot, oty, gy, gyy, at, aty, joined, joined_y)


def rms_inverse(value):
    return lax.rsqrt(jnp.mean(value * value, axis=-1, keepdims=True) + EPSILON)


def norm_back(inverse, normed, upstream):
    return inverse * (upstream - normed * jnp.mean(upstream * normed, axis=-1, keepdims=True))


def rotate(value, cosine, sine):
    half = DH // 2
    first = value[..., :half]
    second = value[..., half:]
    return jnp.concatenate([first * cosine - second * sine, second * cosine + first * sine], axis=-1)


def core_swap(value):
    return lax.ppermute(value, "fsdp", [(f, f ^ 1) for f in range(GROUP)])


def slice_halves(value, n, y):
    rows, width = value.shape
    turned = value.T.reshape(n // 2, 2, width // n, rows)
    here = lax.dynamic_index_in_dim(turned, y, 1, keepdims=False).reshape(width // 2, rows)
    there = lax.dynamic_index_in_dim(turned, 1 - y, 1, keepdims=False).reshape(width // 2, rows)
    return here, there


def lanes(value, rows):
    flat = value.reshape(-1)
    return jnp.pad(flat, (0, rows * 128 - flat.shape[0])).reshape(rows, 128)


def per_device(
    n,
    tokens,
    doc_ids,
    padding,
    token_order,
    query_code,
    key_value_code,
    output_code,
    gate_up_code,
    down_code,
    query_scale,
    key_value_scale,
    output_scale,
    gate_up_scale,
    down_scale,
    norm_gains,
    cotangent,
):
    seq = lax.axis_index("seq")
    me = lax.axis_index("fsdp")
    is_gate = me < 2
    c = me % 2
    y = seq % 2
    width = tokens.shape[2]
    part = width // GROUP
    rows = GROUP * tokens.shape[1]
    own = tokens.shape[1]

    def mine(vector):
        size = vector.shape[-1] // GROUP
        return lax.dynamic_slice_in_dim(vector, me * size, size, vector.ndim - 1)

    def blocks_to_rows(blocks):
        return jnp.concatenate([blocks[i] for i in range(GROUP)], axis=1)

    def own_rows(value):
        return lax.dynamic_slice_in_dim(value, me * own, own, 0)

    gain = 1.0 + norm_gains
    place = token_order[0].astype(F32)
    document = doc_ids[0].astype(F32)
    meta = jnp.stack([document, place, jnp.where(padding[0] == 1, document, -1.0)] + [document] * 5)

    token_blocks, own_meta = group_gather(1, [tokens[0], meta], parts=[4, 1])
    inputs = token_blocks.reshape(rows, width).astype(F32)
    turn = own_meta[:, 1, :].reshape(rows, 1) * (
        BASE ** (-2.0 * jnp.arange(DH // 2).astype(F32) / DH)
    )[None, :]
    cosine = jnp.cos(turn)
    sine = jnp.sin(turn)
    first_inverse = rms_inverse(inputs)
    first_input = (inputs * first_inverse * gain[0]).astype(BF16)
    query_raw = dot(first_input, query_code)
    pair_raw = dot(first_input, key_value_code)
    my_query_scale = mine(query_scale)
    my_pair_scale = mine(key_value_scale)
    pair_cosine = jnp.where(is_gate, cosine, 1.0)
    pair_sine = jnp.where(is_gate, sine, 0.0)
    query = rotate(
        (query_raw * my_query_scale).reshape(rows, 2, DH), cosine[:, None], sine[:, None]
    ).astype(BF16).reshape(rows, 2 * DH)
    pair_plain = pair_raw * my_pair_scale
    heads = jnp.stack(
        [rotate(pair_plain[:, j * DH : (j + 1) * DH], pair_cosine, pair_sine) for j in range(2)]
    ).astype(BF16)
    cot_columns = cotangent[0].reshape(own, GROUP, part).transpose(1, 0, 2).reshape(rows, part)
    pairs, metas, cot_blocks = keys_gather(2, n, heads, own_meta, cot_columns)

    mixed_low, mixed, mass = attend(n, query, pairs, own_meta, metas)
    (mixed_rows,) = group_gather(3, [mixed_low], columns=[True])
    branch_own = dot(mixed_rows, output_code).astype(BF16)
    (branch_blocks,) = group_gather(4, [branch_own])
    branch_raw = blocks_to_rows(branch_blocks).astype(F32)
    branch = branch_raw * output_scale
    second_inverse = rms_inverse(branch)
    middle = inputs + branch * second_inverse * gain[1]
    third_inverse = rms_inverse(middle)
    second_input = (middle * third_inverse * gain[2]).astype(BF16)

    halves = [slice_halves(v, n, y) for v in (second_input, mixed_rows, first_input)]
    my_gate_scale = mine(gate_up_scale)
    columns = gate_up_code.shape[1]
    tiles = columns // TILE
    gate_scales = my_gate_scale.reshape(tiles, 1, TILE)
    gate_up, hidden, hidden_y, down_blocks, grad_down, down_sums, *riders = ffn_forward(
        5,
        second_input,
        gate_up_code,
        gate_scales,
        down_code.T,
        cot_blocks,
        gain[3].reshape(GROUP, 1, part),
        down_scale.reshape(GROUP, 1, part),
        [half[1] for half in halves],
    )
    second_pair, mixed_pair, first_pair = [(half[0], rider) for half, rider in zip(halves, riders)]
    my_middle = own_rows(middle)
    my_down = blocks_to_rows(lax.dynamic_slice_in_dim(down_blocks, me * own, own, 1)).astype(F32) * down_scale
    result = (my_middle + my_down * rms_inverse(my_down) * gain[3]).astype(BF16)
    grad_gate_up, grad_gate_up_y, gate_sums, grad_second_input, down_grad = ffn_backward(
        6, n, grad_down, down_code.T, gate_up_code, gate_scales, gate_up, hidden, hidden_y
    )
    if n == 8:
        down_grad = down_grad.reshape(-1, part)
    else:
        hidden_own = jnp.concatenate(
            [
                (jax.nn.gelu(gate_up[0, t].astype(F32)) * gate_up[1, t].astype(F32)).astype(BF16)
                for t in range(tiles)
            ],
            axis=1,
        )
        hidden_core = core_swap(hidden_own)
        hidden_rows = jnp.concatenate(
            [jnp.where(c == 0, hidden_own, hidden_core), jnp.where(c == 0, hidden_core, hidden_own)], axis=1
        )
        down_grad = lax.psum_scatter(
            contract_first(hidden_rows, grad_down), "seq", scatter_dimension=0, tiled=True
        )
    scale_down = down_sums[0]
    gain_four = down_sums[1]
    scale_gate = gate_sums[:, 0, :].reshape(columns) / my_gate_scale
    gate_pairs = second_pair + (grad_gate_up, grad_gate_up_y)
    tiles_one, tiles_two = (4, 3) if n == 8 else (0, 0)
    tiles_three = tiles - tiles_one - tiles_two

    def to_blocks(value):
        return value.reshape(own, GROUP, part).transpose(1, 0, 2)

    grad_middle, branch_sums, grad_branch, grad_branch_y, grad_query, grad_pairs, gate_one = branch_back(
        7,
        n,
        tiles_one,
        grad_second_input,
        to_blocks(my_middle),
        lax.dynamic_slice_in_dim(branch_blocks, me * own, own, 1),
        to_blocks(cotangent[0]),
        gain[1].reshape(GROUP, 1, part),
        gain[2].reshape(GROUP, 1, part),
        output_scale.reshape(GROUP, 1, part),
        output_code.T,
        query,
        mixed,
        mass,
        own_meta,
        metas,
        pairs,
        gate_pairs,
    )
    grad_middle = blocks_to_rows(grad_middle)
    gain_two = branch_sums[:, 0].reshape(width)
    gain_three = branch_sums[:, 1].reshape(width)
    scale_output = branch_sums[:, 2].reshape(width)
    grad_branch = grad_branch.reshape(rows, part)
    grad_branch_y = grad_branch_y.reshape(rows, part)

    if n == 8:
        joined, joined_y, grad_first_input, key_sums, gate_two = keys_back(
            9,
            n,
            tiles_one,
            tiles_two,
            grad_pairs,
            grad_query,
            query_raw,
            pair_raw,
            cosine,
            sine,
            my_query_scale[None],
            my_pair_scale[None],
            query_code,
            key_value_code,
            gate_pairs,
        )
        scale_query = key_sums[0]
        scale_pair = key_sums[1]
    else:
        grad_heads = keys_reduce(9, n, grad_pairs).astype(F32)
        grad_query_full = rotate(
            grad_query.reshape(rows, 2, DH), cosine[:, None], -sine[:, None]
        ).reshape(rows, 2 * DH)
        scale_query = jnp.sum(query_raw * grad_query_full, axis=0)
        grad_query_low = (grad_query_full * my_query_scale).astype(BF16)
        grad_pair_full = jnp.concatenate(
            [rotate(grad_heads[j], pair_cosine, -pair_sine) for j in range(2)], axis=1
        )
        scale_pair = jnp.sum(pair_raw * grad_pair_full, axis=0)
        grad_pair_low = (grad_pair_full * my_pair_scale).astype(BF16)
        joined = jnp.concatenate([grad_query_low, grad_pair_low], axis=1)
        grad_first_sum = contract_last(grad_query_low, query_code) + contract_last(grad_pair_low, key_value_code)
        grad_first_input = group_reduce(10, grad_first_sum.astype(BF16).reshape(GROUP, own, width), F32)
    my_inputs = tokens[0].astype(F32)
    my_inverse = rms_inverse(my_inputs)
    first = my_inputs * my_inverse
    gain_one = jnp.sum(grad_first_input * first, axis=0)
    grad_inputs = grad_middle + norm_back(my_inverse, first, grad_first_input * gain[0])

    wholes = lanes(jnp.concatenate([gain_one, gain_two, gain_three, scale_output]), 72)
    parts = [scale_query, scale_pair, scale_gate, scale_down, gain_four]
    part_rows = lanes(jnp.concatenate(parts), 56)
    if n == 8:
        whole_total, part_total, gate_three, output_grad, attention_grad = finish(
            11,
            n,
            tiles_one + tiles_two,
            tiles_three,
            wholes,
            part_rows,
            gate_pairs,
            mixed_pair + (grad_branch, grad_branch_y),
            first_pair + (joined, joined_y),
        )
        gate_grad = jnp.concatenate([gate_one, gate_two, gate_three], axis=1)
    else:
        whole_total, part_total = totals(11, n, wholes, part_rows)

        def weight_sum(left, right):
            return lax.psum_scatter(contract_first(left, right), "seq", scatter_dimension=0, tiled=True)

        gate_grad = weight_sum(second_input, grad_gate_up)
        output_grad = weight_sum(mixed_rows, grad_branch)
        attention_grad = weight_sum(first_input, joined)
    whole_total = whole_total.reshape(-1)
    part_total = part_total.reshape(GROUP, -1)
    pieces = []
    start = 0
    for vector in parts:
        pieces.append(part_total[:, start : start + vector.shape[0]].reshape(-1))
        start += vector.shape[0]
    q_width = query_code.shape[1]
    return (
        result[None],
        grad_inputs[None],
        attention_grad[:, :q_width],
        attention_grad[:, q_width:],
        output_grad,
        gate_grad,
        down_grad,
        pieces[0],
        pieces[1],
        whole_total[3 * width :],
        pieces[2],
        pieces[3],
        jnp.concatenate([whole_total[: 3 * width], pieces[4]]).reshape(4, width),
    )


def solution(mesh):
    return jax.shard_map(
        functools.partial(per_device, mesh.shape["seq"]),
        mesh=mesh,
        in_specs=(
            P("fsdp", "seq", None),
            P("fsdp", "seq"),
            P("fsdp", "seq"),
            P("fsdp", "seq"),
            P(None, "fsdp"),
            P(None, "fsdp"),
            P(None, "fsdp"),
            P(None, "fsdp"),
            P(None, "fsdp"),
            P(),
            P(),
            P(),
            P(),
            P(),
            P(),
            P("fsdp", "seq", None),
        ),
        out_specs=(
            P("fsdp", "seq", None),
            P("fsdp", "seq", None),
            P("seq", "fsdp"),
            P("seq", "fsdp"),
            P("seq", "fsdp"),
            P("seq", "fsdp"),
            P("seq", "fsdp"),
            P(),
            P(),
            P(),
            P(),
            P(),
            P(),
        ),
        check_vma=False,
    )
```

```python
import functools
import math

import jax
import jax.numpy as jnp
from jax import lax
from jax.experimental import pallas as pl
from jax.experimental.pallas import tpu as pltpu
from jax.sharding import PartitionSpec as P

HQ = 8
HK = 4
DH = 256
FF = 9216
GROUP = 4
TILE = 384
EPSILON = 1e-06
CAP = 50.0
BASE = 10000.0
VMEM_LIMIT = 60 * 1024 * 1024
MESH = pl.DeviceIdType.MESH
ANY = pl.BlockSpec(memory_space=pl.ANY)
VMEM = pl.BlockSpec(memory_space=pltpu.VMEM)
DMA = pltpu.SemaphoreType.DMA
F32 = jnp.float32
BF16 = jnp.bfloat16


def dot(left, right):
    return jnp.dot(left, right, preferred_element_type=F32)


def contract_last(left, right):
    return lax.dot_general(left, right, (((1,), (1,)), ((), ())), preferred_element_type=F32)


def contract_first(left, right):
    return lax.dot_general(left, right, (((0,), (0,)), ((), ())), preferred_element_type=F32)


def place_now():
    seq = lax.axis_index("seq")
    fsdp = lax.axis_index("fsdp")
    return seq, fsdp, fsdp // 2, fsdp % 2


def greet(peers):
    barrier = pltpu.get_barrier_semaphore()
    for peer in peers:
        pl.semaphore_signal(barrier, inc=1, device_id=peer, device_id_type=MESH)
    pl.semaphore_wait(barrier, len(peers))


def remote(src, dst, send, recv, peer):
    return pltpu.make_async_remote_copy(
        src_ref=src, dst_ref=dst, send_sem=send, recv_sem=recv, device_id=peer, device_id_type=MESH
    )


def comm_call(kernel, cid, out_shape, scratch, in_specs, out_specs):
    return pl.pallas_call(
        kernel,
        out_shape=out_shape,
        in_specs=in_specs,
        out_specs=out_specs,
        scratch_shapes=scratch,
        compiler_params=pltpu.CompilerParams(
            collective_id=cid, has_side_effects=True, vmem_limit_bytes=VMEM_LIMIT
        ),
    )


def group_reduce_kernel(parts, src, out, from_core, to_x, from_x, cs, cr, xs, xr):
    seq, me, x, c = place_now()
    across = (seq, (1 - x) * 2 + c)
    beside = (seq, x * 2 + 1 - c)
    greet([across, beside])
    rows = src.shape[1]
    step = rows // parts
    order = [1 - x, x]
    cores = []
    for i in range(2):
        for k in range(parts):
            span = pl.ds(k * step, step)
            copy = remote(
                src.at[order[i] * 2 + 1 - c, span], from_core.at[i, span], cs.at[i, k], cr.at[i, k], beside
            )
            copy.start()
            cores.append(copy)
    sends = []
    for k in range(parts):
        span = pl.ds(k * step, step)
        cores[k].wait_recv()
        to_x[span, :] = (
            src[order[0] * 2 + c, span, :].astype(F32) + from_core[0, span, :].astype(F32)
        ).astype(BF16)
        copy = remote(to_x.at[span], from_x.at[span], xs.at[k], xr.at[k], across)
        copy.start()
        sends.append(copy)
    for k in range(parts):
        span = pl.ds(k * step, step)
        cores[parts + k].wait_recv()
        sends[k].wait_recv()
        out[span, :] = (
            src[order[1] * 2 + c, span, :].astype(F32)
            + from_core[1, span, :].astype(F32)
            + from_x[span, :].astype(F32)
        ).astype(out.dtype)
    for copy in cores + sends:
        copy.wait_send()


def group_reduce(cid, value, dtype, parts=4):
    rows, width = value.shape[1:]
    return comm_call(
        functools.partial(group_reduce_kernel, parts),
        cid,
        jax.ShapeDtypeStruct((rows, width), dtype),
        [pltpu.VMEM((2, rows, width), BF16), pltpu.VMEM((rows, width), BF16), pltpu.VMEM((rows, width), BF16),
         DMA((2, parts)), DMA((2, parts)), DMA((parts,)), DMA((parts,))],
        [VMEM],
        VMEM,
    )(value)


def keys_reduce_kernel(n, src, out, y_got, r_got, l_got, r_out, l_out, moved, ys, yr, rs, rr, ls, lr, hs, hr, local):
    seq, me, x, c = place_now()
    y = seq % 2
    z = seq // 2
    nz = n // 2
    right = (seq + 2, me)
    left = (seq - 2, me)
    beyond = (z * 2 + 1 - y, me)
    barrier = pltpu.get_barrier_semaphore()
    for d in range(1, GROUP):
        pl.semaphore_signal(barrier, inc=1, device_id=(seq, lax.rem(me + d, GROUP)), device_id_type=MESH)
    pl.semaphore_signal(barrier, inc=1, device_id=beyond, device_id_type=MESH)

    @pl.when(z > 0)
    def _():
        pl.semaphore_signal(barrier, inc=1, device_id=left, device_id_type=MESH)

    @pl.when(z < nz - 1)
    def _():
        pl.semaphore_signal(barrier, inc=1, device_id=right, device_id_type=MESH)

    chain = jnp.where(z > 0, 1, 0) + jnp.where(z < nz - 1, 1, 0)
    pl.semaphore_wait(barrier, GROUP + chain)

    def swap(k):
        return remote(src.at[k * 2 + 1 - y], y_got.at[k], ys.at[k], yr.at[k], beyond)

    for t in range(1, nz):
        go_right = z + nz - t
        go_left = z - nz + t

        @pl.when(go_right < nz)
        def _():
            swap(go_right).start()

        @pl.when(go_left >= 0)
        def _():
            swap(go_left).start()

    swap(z).start()

    def pair_sum(k, more, to):
        def body(i, carry):
            half = i // 2
            span = pl.ds(pl.multiple_of((i % 2) * 256, 256), 256)
            total = src[k * 2 + y, half, span, :].astype(F32) + y_got[k, half, span, :].astype(F32)
            for ref in more:
                total = total + ref[half, span, :].astype(F32)
            to[half, span, :] = total.astype(BF16)
            return carry

        lax.fori_loop(0, 4, body, 0)

    for t in range(1, nz):
        go_right = z + nz - t
        go_left = z - nz + t

        @pl.when(go_right < nz)
        def _():
            swap(go_right).wait_recv()
            if t == 1:
                pair_sum(go_right, [], r_out.at[t - 1])
            else:

                @pl.when(z > 0)
                def _():
                    remote(r_out.at[t - 1], r_got.at[t - 2], rs.at[t - 2], rr.at[t - 2], left).wait_recv()
                    pair_sum(go_right, [r_got.at[t - 2]], r_out.at[t - 1])

                @pl.when(z == 0)
                def _():
                    pair_sum(go_right, [], r_out.at[t - 1])

            remote(r_out.at[t - 1], r_got.at[t - 1], rs.at[t - 1], rr.at[t - 1], right).start()

        @pl.when(go_left >= 0)
        def _():
            swap(go_left).wait_recv()
            if t == 1:
                pair_sum(go_left, [], l_out.at[t - 1])
            else:

                @pl.when(z < nz - 1)
                def _():
                    remote(l_out.at[t - 1], l_got.at[t - 2], ls.at[t - 2], lr.at[t - 2], right).wait_recv()
                    pair_sum(go_left, [l_got.at[t - 2]], l_out.at[t - 1])

                @pl.when(z == nz - 1)
                def _():
                    pair_sum(go_left, [], l_out.at[t - 1])

            remote(l_out.at[t - 1], l_got.at[t - 1], ls.at[t - 1], lr.at[t - 1], left).start()

    swap(z).wait_recv()
    last = nz - 2

    def got_left():
        remote(r_out.at[last], r_got.at[last], rs.at[last], rr.at[last], left).wait_recv()

    def got_right():
        remote(l_out.at[last], l_got.at[last], ls.at[last], lr.at[last], right).wait_recv()

    @pl.when(z == 0)
    def _():
        got_right()
        pair_sum(z, [l_got.at[last]], moved)

    @pl.when(z == nz - 1)
    def _():
        got_left()
        pair_sum(z, [r_got.at[last]], moved)

    @pl.when((z > 0) & (z < nz - 1))
    def _():
        got_left()
        got_right()
        pair_sum(z, [r_got.at[last], l_got.at[last]], moved)

    for t in range(2):
        target = t * 2 + x

        @pl.when(target == me)
        def _():
            pltpu.make_async_copy(moved.at[t], out.at[c], local).start()

        @pl.when(target != me)
        def _():
            remote(moved.at[t], out.at[c], hs.at[t], hr.at[c], (seq, target)).start()

    for j in range(2):
        source = c * 2 + j

        @pl.when(source == me)
        def _():
            pltpu.make_async_copy(moved.at[0], out.at[j], local).wait()

        @pl.when(source != me)
        def _():
            remote(moved.at[0], out.at[j], hs.at[0], hr.at[j], (seq, source)).wait_recv()

    for t in range(2):

        @pl.when(t * 2 + x != me)
        def _():
            remote(moved.at[t], out.at[c], hs.at[t], hr.at[c], (seq, t * 2 + x)).wait_send()

    for k in range(nz):
        swap(k).wait_send()
    for t in range(1, nz):

        @pl.when(z + nz - t < nz)
        def _():
            remote(r_out.at[t - 1], r_got.at[t - 1], rs.at[t - 1], rr.at[t - 1], right).wait_send()

        @pl.when(z - nz + t >= 0)
        def _():
            remote(l_out.at[t - 1], l_got.at[t - 1], ls.at[t - 1], lr.at[t - 1], left).wait_send()


def keys_reduce(cid, n, value):
    nz = n // 2
    shape = value.shape[1:]
    chain = pltpu.VMEM((nz - 1,) + shape, BF16)
    return comm_call(
        functools.partial(keys_reduce_kernel, n),
        cid,
        jax.ShapeDtypeStruct(shape, BF16),
        [pltpu.VMEM((nz,) + shape, BF16), chain, chain, chain, chain, pltpu.VMEM(shape, BF16),
         DMA((nz,)), DMA((nz,)), DMA((nz - 1,)), DMA((nz - 1,)), DMA((nz - 1,)), DMA((nz - 1,)),
         DMA((2,)), DMA((2,)), DMA],
        [VMEM],
        VMEM,
    )(value)


def total_kernel(rounds, whole, part, whole_out, part_out, bufs, gots, mine, theirs, ss, rs):
    seq, me, x, c = place_now()
    across = (seq, (1 - x) * 2 + c)
    beside = (seq, x * 2 + 1 - c)
    partners = []
    for r in range(rounds):
        bit = 1 << r
        partners.append((seq + bit - 2 * bit * ((seq // bit) % 2), me))
    greet(partners + [across, beside])
    rows = whole.shape[0]
    bufs[0, :rows, :] = whole[...]
    bufs[0, rows:, :] = part[...]
    for r in range(rounds + 1):
        partner = partners[r] if r < rounds else across
        copy = remote(bufs.at[r], gots.at[r], ss.at[r], rs.at[r], partner)
        copy.start()
        copy.wait()
        if r < rounds:
            bufs[r + 1] = bufs[r] + gots[r]
    mine[0, :rows, :] = bufs[rounds, :rows, :] + gots[rounds, :rows, :]
    mine[0, rows:, :] = bufs[rounds, rows:, :]
    mine[1, rows:, :] = gots[rounds, rows:, :]
    mine[1, :rows, :] = jnp.zeros_like(whole)
    copy = remote(mine, theirs, ss.at[rounds + 1], rs.at[rounds + 1], beside)
    copy.start()
    copy.wait()
    whole_out[...] = mine[0, :rows, :] + theirs[0, :rows, :]
    part_out[x * 2 + c] = mine[0, rows:, :]
    part_out[(1 - x) * 2 + c] = mine[1, rows:, :]
    part_out[x * 2 + 1 - c] = theirs[0, rows:, :]
    part_out[(1 - x) * 2 + 1 - c] = theirs[1, rows:, :]


def totals(cid, n, whole, part):
    rounds = int(math.log2(n))
    rows = whole.shape[0] + part.shape[0]
    return comm_call(
        functools.partial(total_kernel, rounds),
        cid,
        [jax.ShapeDtypeStruct(whole.shape, F32), jax.ShapeDtypeStruct((GROUP,) + part.shape, F32)],
        [pltpu.VMEM((rounds + 1, rows, 128), F32), pltpu.VMEM((rounds + 1, rows, 128), F32),
         pltpu.VMEM((2, rows, 128), F32), pltpu.VMEM((2, rows, 128), F32),
         DMA((rounds + 2,)), DMA((rounds + 2,))],
        [VMEM, VMEM],
        [VMEM, VMEM],
    )(whole, part)


def turned(block, unit, to):
    half = to.shape[1]
    flat = contract_first(block, unit[...])
    to[0] = flat[:half].astype(BF16)
    to[1] = flat[half:].astype(BF16)


def fill_unit(unit):
    shape = unit.shape
    unit[...] = jnp.where(
        lax.broadcasted_iota(jnp.int32, shape, 0) == lax.broadcasted_iota(jnp.int32, shape, 1), 1.0, 0.0
    ).astype(BF16)


def front_kernel(n, *refs):
    tok, cot, meta, g1, rates, q_scale, p_scale, wq, wkv = refs[:9]
    toks, cots, own_meta, metas, out, q, q_raw, p_raw, cosine, sine, turned_o = refs[9:20]
    (tb, ab, wqs, wkvs, heads, om, unit, at,
     ws, txs, txr, tcs, tcr, tfs, tfr, gms, gmr, own_sem, hs, hr, ms, mr, rs, rr, ls, lr, ys, yr,
     xs, xr, cs, cr, fs, fr, os) = refs[20:]
    seq, me, x, c = place_now()
    y = seq % 2
    z = seq // 2
    nz = n // 2
    across = (seq, (1 - x) * 2 + c)
    beside = (seq, x * 2 + 1 - c)
    group = [(seq, lax.rem(me + d, GROUP)) for d in range(1, GROUP)]
    load_q = pltpu.make_async_copy(wq, wqs, ws.at[0])
    load_kv = pltpu.make_async_copy(wkv, wkvs, ws.at[1])
    load_q.start()
    load_kv.start()
    greet(group + [(lax.rem(seq + d, n), me) for d in range(1, n)])
    blk = tok.shape[0] // GROUP
    part = tok.shape[1]
    own = blk

    sends = []
    for k in range(GROUP):
        rows = pl.ds(k * blk, blk)
        copy = remote(tok.at[rows], tb.at[me, rows], txs.at[k], txr.at[k], across)
        copy.start()
        sends.append(copy)
    to_core = remote(tok, tb.at[me], tcs, tcr, beside)
    to_core.start()
    group_meta = []
    for d in range(1, GROUP):
        copy = remote(meta, om.at[me], gms.at[d - 1], gmr.at[d - 1], group[d - 1])
        copy.start()
        group_meta.append(copy)
    own_tok = pltpu.make_async_copy(tok, tb.at[me], own_sem.at[0])
    own_tok.start()
    own_row = pltpu.make_async_copy(meta, om.at[me], own_sem.at[1])
    own_row.start()
    fill_unit(unit)
    for copy in group_meta:
        copy.wait()
    own_row.wait()
    width = GROUP * part
    half = DH // 2
    js = range(GROUP)
    is_key = jnp.where(x == 0, 1.0, 0.0).astype(F32)

    def process(p):
        def norm(i, carry):
            span = lambda j: pl.ds(pl.multiple_of(j * blk + i * 32, 32), 32)
            values = [tb[p, span(j), :].astype(F32) for j in js]
            total = values[0] * values[0]
            for value in values[1:]:
                total = total + value * value
            inverse = lax.rsqrt(jnp.sum(total, axis=1, keepdims=True) * (1.0 / width) + EPSILON)
            to = pl.ds(pl.multiple_of(p * own + i * 32, 32), 32)
            for j in js:
                ab[j, to, :] = (values[j] * inverse * g1[j]).astype(BF16)
            return carry

        lax.fori_loop(0, blk // 32, norm, 0)
        rows = pl.ds(pl.multiple_of(p * own, 128), own)
        turn = jnp.broadcast_to(om[p, 1:2, :], (128, 128)).T * rates[...]
        cos = jnp.cos(turn)
        sin = jnp.sin(turn)
        cosine[rows, :] = cos
        sine[rows, :] = sin

        def product(weights):
            total = dot(ab[0, rows, :], weights[0:part, :])
            for j in range(1, GROUP):
                total = total + dot(ab[j, rows, :], weights[j * part : (j + 1) * part, :])
            return total

        plain = product(wqs)
        q_raw[rows, :] = plain
        plain = plain * q_scale[...]
        for h in range(2):
            one = plain[:, h * DH : h * DH + half]
            two = plain[:, h * DH + half : (h + 1) * DH]
            q[rows, h * DH : h * DH + half] = (one * cos - two * sin).astype(BF16)
            q[rows, h * DH + half : (h + 1) * DH] = (two * cos + one * sin).astype(BF16)
        cos = is_key * cos + (1.0 - is_key)
        sin = is_key * sin
        plain = product(wkvs)
        p_raw[rows, :] = plain
        plain = plain * p_scale[...]
        for h in range(2):
            one = plain[:, h * DH : h * DH + half]
            two = plain[:, h * DH + half : (h + 1) * DH]
            heads[h, rows, :half] = (one * cos - two * sin).astype(BF16)
            heads[h, rows, half:] = (two * cos + one * sin).astype(BF16)

    own_tok.wait()
    load_q.wait()
    load_kv.wait()
    process(me)
    to_core.wait_recv()
    process(x * 2 + 1 - c)
    forwards = []
    for k in range(GROUP):
        sends[k].wait_recv()
        got = tb.at[(1 - x) * 2 + c, pl.ds(k * blk, blk)]
        forward = remote(got, got, tfs.at[k], tfr.at[k], beside)
        forward.start()
        forwards.append(forward)
    process((1 - x) * 2 + c)
    for forward in forwards:
        forward.wait_recv()
    process((1 - x) * 2 + 1 - c)

    for j in range(2):
        target = c * 2 + j

        @pl.when(target == me)
        def _():
            pltpu.make_async_copy(heads.at[j], out.at[seq, x], own_sem.at[0]).start()

        @pl.when(target != me)
        def _():
            remote(heads.at[j], out.at[seq, x], hs.at[j], hr.at[x], (seq, target)).start()

    small = []
    for d in range(1, n):
        copy = remote(om, metas.at[seq], ms.at[d - 1], mr.at[d - 1], (lax.rem(seq + d, n), me))
        copy.start()
        small.append(copy)
    outs = [
        pltpu.make_async_copy(om, metas.at[seq], os.at[0]),
        pltpu.make_async_copy(om, own_meta, os.at[1]),
        pltpu.make_async_copy(tb, toks, os.at[2]),
    ]
    for copy in outs:
        copy.start()
    for t in range(2):
        source = t * 2 + x

        @pl.when(source == me)
        def _():
            pltpu.make_async_copy(heads.at[0], out.at[seq, t], own_sem.at[0]).wait()

        @pl.when(source != me)
        def _():
            remote(heads.at[0], out.at[seq, t], hs.at[0], hr.at[t], (seq, source)).wait_recv()

    def block(owner_z, owner_y):
        return out.at[owner_z * 2 + owner_y]

    right = (seq + 2, me)
    left = (seq - 2, me)
    beyond = (z * 2 + 1 - y, me)

    def to_y(owner_z):
        remote(block(owner_z, y), block(owner_z, y), ys.at[owner_z], yr.at[owner_z], beyond).start()

    parts = 2
    step = cot.shape[0] // parts
    for t in range(1, nz + 1):
        go_right = z - t + 1
        go_left = z + t - 1
        if t > 1:

            @pl.when(go_right >= 0)
            def _():
                remote(block(go_right, y), block(go_right, y), rs.at[t - 1], rr.at[t - 1], left).wait_recv()

            @pl.when(go_left < nz)
            def _():
                remote(block(go_left, y), block(go_left, y), ls.at[t - 1], lr.at[t - 1], right).wait_recv()

        if t < nz:

            @pl.when((go_right >= 0) & (z < nz - 1))
            def _():
                remote(block(go_right, y), block(go_right, y), rs.at[t], rr.at[t], right).start()

            @pl.when((go_left < nz) & (z > 0))
            def _():
                remote(block(go_left, y), block(go_left, y), ls.at[t], lr.at[t], left).start()

        @pl.when(go_right >= 0)
        def _():
            to_y(go_right)

        if t > 1:

            @pl.when(go_left < nz)
            def _():
                to_y(go_left)

        if t == 1:
            xcopies = []
            for k in range(parts):
                rows = pl.ds(k * step, step)
                copy = remote(cot.at[rows], cots.at[me, rows], xs.at[k], xr.at[k], across)
                copy.start()
                xcopies.append(copy)
            ccopy = remote(cot, cots.at[me], cs, cr, beside)
            ccopy.start()
            own_cot = pltpu.make_async_copy(cot, cots.at[me], os.at[3])
            own_cot.start()
            for j in js:
                turned(ab[j], unit, at.at[j])
            turned_out = pltpu.make_async_copy(at, turned_o, os.at[4])
            turned_out.start()
    later = []
    for k in range(parts):
        rows = pl.ds(k * step, step)
        xcopies[k].wait()
        got = cots.at[(1 - x) * 2 + c, rows]
        forward = remote(got, got, fs.at[k], fr.at[k], beside)
        forward.start()
        later.append(forward)
    for k in range(nz):
        remote(block(k, 1 - y), block(k, 1 - y), ys.at[k], yr.at[k], beyond).wait()
    for t in range(1, nz):

        @pl.when((z - t + 1 >= 0) & (z < nz - 1))
        def _():
            remote(block(z, y), block(z, y), rs.at[t], rr.at[t], right).wait_send()

        @pl.when((z + t - 1 < nz) & (z > 0))
        def _():
            remote(block(z, y), block(z, y), ls.at[t], lr.at[t], left).wait_send()

    for j in range(2):

        @pl.when(c * 2 + j != me)
        def _():
            remote(heads.at[j], out.at[seq, x], hs.at[j], hr.at[x], (seq, c * 2 + j)).wait_send()

    for copy in small + later + [ccopy]:
        copy.wait()
    for copy in sends + forwards + [to_core]:
        copy.wait_send()
    for copy in outs + [own_cot, turned_out]:
        copy.wait()


def front(cid, n, tok, cot, meta, g1, rates, q_scale, p_scale, wq, wkv):
    nz = n // 2
    rows, part = tok.shape
    own = rows // GROUP
    deep, wide = wq.shape
    blocks = jax.ShapeDtypeStruct((GROUP, rows, part), BF16)
    table = jax.ShapeDtypeStruct((rows, DH // 2), F32)
    raw = jax.ShapeDtypeStruct((rows, wide), F32)
    turned_shape = (GROUP, 2, part // 2, rows)
    return comm_call(
        functools.partial(front_kernel, n),
        cid,
        [
            blocks,
            blocks,
            jax.ShapeDtypeStruct((GROUP,) + meta.shape, F32),
            jax.ShapeDtypeStruct((n, GROUP) + meta.shape, F32),
            jax.ShapeDtypeStruct((n, 2, rows, DH), BF16),
            jax.ShapeDtypeStruct((rows, wide), BF16),
            raw,
            raw,
            table,
            table,
            jax.ShapeDtypeStruct(turned_shape, BF16),
        ],
        [
            pltpu.VMEM((GROUP, rows, part), BF16),
            pltpu.VMEM((GROUP, rows, part), BF16),
            pltpu.VMEM((deep, wide), BF16),
            pltpu.VMEM((deep, wide), BF16),
            pltpu.VMEM((2, rows, DH), BF16),
            pltpu.VMEM((GROUP,) + meta.shape, F32),
            pltpu.VMEM((rows, rows), BF16),
            pltpu.VMEM(turned_shape, BF16),
            DMA((2,)), DMA((GROUP,)), DMA((GROUP,)), DMA, DMA, DMA((GROUP,)), DMA((GROUP,)), DMA((GROUP - 1,)),
            DMA((GROUP - 1,)), DMA((2,)), DMA((2,)), DMA((2,)), DMA((n - 1,)), DMA((n - 1,)), DMA((nz,)), DMA((nz,)),
            DMA((nz,)), DMA((nz,)), DMA((nz,)), DMA((nz,)), DMA((2,)), DMA((2,)), DMA, DMA, DMA((2,)), DMA((2,)),
            DMA((5,)),
        ],
        [VMEM, ANY, VMEM, VMEM, VMEM, VMEM, VMEM, ANY, ANY],
        [ANY, ANY, ANY, ANY, ANY, VMEM, VMEM, VMEM, VMEM, VMEM, ANY],
    )(tok, cot, meta, g1, rates, q_scale, p_scale, wq, wkv)


def branch_kernel(low, wo, toks, scale, g2, g3, b_o, raw_o, mid_o, ot_o, bt_o, ob, pb, bb, acc, unit, ot, bt,
                  xs, xr, cs, cr, fs, fr, gxs, gxr, gcs, gcr, gfs, gfr, local, os):
    seq, me, x, c = place_now()
    across = (seq, (1 - x) * 2 + c)
    beside = (seq, x * 2 + 1 - c)
    greet([across, beside])
    rows, heads = low.shape
    part = pb.shape[2]
    parts = 4
    size = rows // parts
    own = rows // GROUP
    js = range(GROUP)

    def spot(owner, k):
        return ob.at[pl.ds(k * size, size), pl.ds(pl.multiple_of(owner * heads, 128), heads)]

    sends = []
    for k in range(parts):
        copy = remote(low.at[pl.ds(k * size, size)], spot(me, k), xs.at[k], xr.at[k], across)
        copy.start()
        sends.append(copy)
    mine = ob.at[:, pl.ds(pl.multiple_of(me * heads, 128), heads)]
    to_core = remote(low, mine, cs, cr, beside)
    to_core.start()
    own_copy = pltpu.make_async_copy(low, mine, local)
    own_copy.start()
    fill_unit(unit)

    def add(owner, start):
        cols = pl.ds(pl.multiple_of(owner * heads, 128), heads)
        more = contract_last(ob[:, cols], wo[:, cols])
        acc[...] = more if start else acc[...] + more

    own_copy.wait()
    add(me, True)
    to_core.wait_recv()
    add(x * 2 + 1 - c, False)
    forwards = []
    for k in range(parts):
        sends[k].wait_recv()
        got = spot((1 - x) * 2 + c, k)
        forward = remote(got, got, fs.at[k], fr.at[k], beside)
        forward.start()
        forwards.append(forward)
    add((1 - x) * 2 + c, False)
    for forward in forwards:
        forward.wait_recv()
    add((1 - x) * 2 + 1 - c, False)

    over = []
    core = []
    for k in range(parts):
        span = pl.ds(k * size, size)
        pb[me, span, :] = acc[span, :].astype(BF16)
        piece = pb.at[me, span]
        copy = remote(piece, piece, gxs.at[k], gxr.at[k], across)
        copy.start()
        over.append(copy)
        copy = remote(piece, piece, gcs.at[k], gcr.at[k], beside)
        copy.start()
        core.append(copy)
    for j in js:
        turned(ob[:, j * heads : (j + 1) * heads], unit, ot.at[j])
    ot_out = pltpu.make_async_copy(ot, ot_o, os.at[0])
    ot_out.start()
    passed = []
    for k in range(parts):
        over[k].wait_recv()
        got = pb.at[(1 - x) * 2 + c, pl.ds(k * size, size)]
        forward = remote(got, got, gfs.at[k], gfr.at[k], beside)
        forward.start()
        passed.append(forward)
    for copy in core + passed:
        copy.wait_recv()
    mean = 1.0 / (GROUP * part)

    def rowsum(values):
        total = values[0] * values[0]
        for value in values[1:]:
            total = total + value * value
        return jnp.sum(total, axis=1, keepdims=True) * mean

    def norms(i, carry):
        pack = i // (own // 16)
        inner = i % (own // 16) * 16
        span = pl.ds(pl.multiple_of(i * 16, 16), 16)
        branch = [pb[j, span, :].astype(F32) * scale[j] for j in js]
        inverse = lax.rsqrt(rowsum(branch) + EPSILON)
        middle = [
            toks[pack, pl.ds(pl.multiple_of(j * own + inner, 16), 16), :].astype(F32) + branch[j] * inverse * g2[j]
            for j in js
        ]
        inverse = lax.rsqrt(rowsum(middle) + EPSILON)
        for j in js:
            bb[j, span, :] = (middle[j] * inverse * g3[j]).astype(BF16)

        @pl.when(pack == me)
        def _():
            for j in js:
                mid_o[j, pl.ds(pl.multiple_of(inner, 16), 16), :] = middle[j]

        return carry

    lax.fori_loop(0, rows // 16, norms, 0)
    b_out = pltpu.make_async_copy(bb, b_o, os.at[1])
    b_out.start()
    raw_out = pltpu.make_async_copy(pb.at[:, pl.ds(pl.multiple_of(me * own, 128), own)], raw_o, os.at[2])
    raw_out.start()
    for j in js:
        turned(bb[j], unit, bt.at[j])
    bt_out = pltpu.make_async_copy(bt, bt_o, os.at[3])
    bt_out.start()
    for copy in sends + forwards + over + core + passed + [to_core]:
        copy.wait_send()
    for copy in (ot_out, b_out, raw_out, bt_out):
        copy.wait()


def branch_forward(cid, low, wo, toks, scale, g2, g3):
    rows, heads = low.shape
    part = wo.shape[0]
    own = rows // GROUP
    turned_b = (GROUP, 2, part // 2, rows)
    turned_o = (GROUP, 2, heads // 2, rows)
    four = DMA((4,))
    return comm_call(
        branch_kernel,
        cid,
        [
            jax.ShapeDtypeStruct((GROUP, rows, part), BF16),
            jax.ShapeDtypeStruct((GROUP, own, part), BF16),
            jax.ShapeDtypeStruct((GROUP, own, part), F32),
            jax.ShapeDtypeStruct(turned_o, BF16),
            jax.ShapeDtypeStruct(turned_b, BF16),
        ],
        [
            pltpu.VMEM((rows, GROUP * heads), BF16),
            pltpu.VMEM((GROUP, rows, part), BF16),
            pltpu.VMEM((GROUP, rows, part), BF16),
            pltpu.VMEM((rows, part), F32),
            pltpu.VMEM((rows, rows), BF16),
            pltpu.VMEM(turned_o, BF16),
            pltpu.VMEM(turned_b, BF16),
            four, four, DMA, DMA, four, four, four, four, four, four, four, four, DMA, four,
        ],
        [VMEM] * 6,
        [ANY, ANY, VMEM, ANY, ANY],
    )(low, wo, toks, scale, g2, g3)


def masks(n, own_ref, meta_ref):
    def column(row):
        return jnp.broadcast_to(own_ref[0, row : row + 1, :], (128, 128)).T

    row_document = column(0)
    row_place = column(1)
    out = []
    for j in range(n):
        key_place = meta_ref[j, 0, 1:2, :]
        key_document = meta_ref[j, 0, 2:3, :]
        allowed = (row_document == key_document) & (key_place <= row_place) | (key_place == row_place)
        out.append(allowed)
    return out


def attend_kernel(n, q_ref, kv_ref, own_ref, meta_ref, low_ref, mixed_ref, total_ref):
    keys = kv_ref[:, 0].reshape(n * 128, DH)
    values = kv_ref[:, 1].reshape(n * 128, DH)
    allowed = masks(n, own_ref, meta_ref)
    for h in range(2):
        cols = slice(h * DH, (h + 1) * DH)
        raw = contract_last(q_ref[:, cols], keys)
        pieces = []
        total = jnp.zeros((128, 128), F32)
        for j in range(n):
            squash = jnp.tanh(raw[:, j * 128 : (j + 1) * 128] * (DH ** (-0.5) / CAP))
            mass = jnp.where(allowed[j], jnp.exp(CAP * squash), 0.0)
            total = total + mass
            pieces.append(mass.astype(BF16))
        row = jnp.sum(total, axis=1, keepdims=True)
        mixed = dot(jnp.concatenate(pieces, axis=1), values) / row
        mixed_ref[:, cols] = mixed
        low_ref[:, cols] = mixed.astype(BF16)
        total_ref[:, h * 128 : (h + 1) * 128] = jnp.broadcast_to(row, (128, 128))


def attend(n, query, pairs, own_meta, metas):
    return pl.pallas_call(
        functools.partial(attend_kernel, n),
        grid=(GROUP,),
        out_shape=[
            jax.ShapeDtypeStruct(query.shape, BF16),
            jax.ShapeDtypeStruct(query.shape, F32),
            jax.ShapeDtypeStruct((query.shape[0], 256), F32),
        ],
        in_specs=[
            pl.BlockSpec((128, 2 * DH), lambda p: (p, 0)),
            pl.BlockSpec((n, 2, 128, DH), lambda p: (0, 0, p, 0)),
            pl.BlockSpec((1, 8, 128), lambda p: (p, 0, 0)),
            pl.BlockSpec((n, 1, 8, 128), lambda p: (0, p, 0, 0)),
        ],
        out_specs=[
            pl.BlockSpec((128, 2 * DH), lambda p: (p, 0)),
            pl.BlockSpec((128, 2 * DH), lambda p: (p, 0)),
            pl.BlockSpec((128, 256), lambda p: (p, 0)),
        ],
        compiler_params=pltpu.CompilerParams(vmem_limit_bytes=VMEM_LIMIT),
    )(query, pairs, own_meta, metas)


def back_pack(n, keys, values, allowed, q_ref, grad_ref, mixed_ref, total_ref, dq_ref, dkv_ref):
    grad_keys = None
    for h in range(2):
        cols = slice(h * DH, (h + 1) * DH)
        query = q_ref[:, cols]
        grad = grad_ref[:, cols]
        delta = jnp.sum(grad.astype(F32) * mixed_ref[:, cols], axis=1, keepdims=True)
        inverse = 1.0 / total_ref[:, h * 128 : (h + 1) * 128]
        raw = contract_last(query, keys)
        grad_share = contract_last(grad, values)
        shares = []
        grads = []
        for j in range(n):
            span = slice(j * 128, (j + 1) * 128)
            squash = jnp.tanh(raw[:, span] * (DH ** (-0.5) / CAP))
            share = jnp.where(allowed[j], jnp.exp(CAP * squash), 0.0) * inverse
            shares.append(share.astype(BF16))
            grads.append(
                (share * (grad_share[:, span] - delta) * ((1.0 - squash * squash) * DH ** (-0.5))).astype(BF16)
            )
        share = jnp.concatenate(shares, axis=1)
        grad_raw = jnp.concatenate(grads, axis=1)
        dq_ref[:, cols] = dot(grad_raw, keys)
        new_keys = contract_first(grad_raw, query)
        new_values = contract_first(share, grad)
        if grad_keys is None:
            grad_keys, grad_values = new_keys, new_values
        else:
            grad_keys, grad_values = grad_keys + new_keys, grad_values + new_values
    dkv_ref[:, 0] = grad_keys.astype(BF16).reshape(n, 128, DH)
    dkv_ref[:, 1] = grad_values.astype(BF16).reshape(n, 128, DH)


class Chain:
    def __init__(self, nz, count, seq, me, partial, keep, scratch):
        self.nz, self.count, self.partial, self.keep = nz, count, partial, keep
        self.z = seq // 2
        self.right, self.left = (seq + 2, me), (seq - 2, me)
        (self.out_r, self.out_l, self.got_r, self.got_l, self.stage, self.ss_r, self.sr_r, self.ss_l, self.sr_l,
         self.keep_sem) = scratch

    @staticmethod
    def scratch(nz, count, rows, width):
        hops = nz - 1
        message = (rows, width)
        sems = DMA((count, hops))
        return [
            pltpu.VMEM((hops,) + message, BF16), pltpu.VMEM((hops,) + message, BF16),
            pltpu.VMEM((count, hops) + message, BF16), pltpu.VMEM((count, hops) + message, BF16),
            pltpu.VMEM((2,) + message, F32), sems, sems, sems, sems, DMA((2,)),
        ]

    def copy_right(self, j, s, peer):
        return remote(
            self.out_r.at[s - 1], self.got_r.at[j, s - 1], self.ss_r.at[j, s - 1], self.sr_r.at[j, s - 1], peer
        )

    def copy_left(self, j, s, peer):
        return remote(
            self.out_l.at[s - 1], self.got_l.at[j, s - 1], self.ss_l.at[j, s - 1], self.sr_l.at[j, s - 1], peer
        )

    def step(self, j, s):
        z, nz = self.z, self.nz

        def one(go, copy, out, got, to, source, first):
            @pl.when(j > 0)
            def _():
                copy(j - 1, s, to).wait_send()

            total = self.partial(go, j)
            more = (s > 1) & jnp.logical_not(first)

            @pl.when(more)
            def _():
                copy(j, s - 1, source).wait_recv()
                out[s - 1] = (total + got[j, s - 2].astype(F32)).astype(BF16)

            @pl.when(jnp.logical_not(more))
            def _():
                out[s - 1] = total.astype(BF16)

            copy(j, s, to).start()

        go_right = z + nz - s
        go_left = z - nz + s

        @pl.when(go_right < nz)
        def _():
            one(go_right, self.copy_right, self.out_r, self.got_r, self.right, self.left, z == 0)

        @pl.when(go_left >= 0)
        def _():
            one(go_left, self.copy_left, self.out_l, self.got_l, self.left, self.right, z == nz - 1)

    def end(self, j):
        z, nz = self.z, self.nz
        k = j % 2

        @pl.when(j >= 2)
        def _():
            self.keep(j - 2, self.stage.at[k], self.keep_sem.at[k]).wait()

        self.stage[k] = self.partial(z, j)

        @pl.when(z > 0)
        def _():
            self.copy_right(j, nz - 1, self.left).wait_recv()
            self.stage[k] += self.got_r[j, nz - 2].astype(F32)

        @pl.when(z < nz - 1)
        def _():
            self.copy_left(j, nz - 1, self.right).wait_recv()
            self.stage[k] += self.got_l[j, nz - 2].astype(F32)

        self.keep(j, self.stage.at[k], self.keep_sem.at[k]).start()

    def run(self, first, last):
        hops = self.nz - 1

        def unit(u, carry):
            j = u // hops
            s = u % hops + 1
            self.step(j, s)

            @pl.when((s == hops) & (j > 0))
            def _():
                self.end(j - 1)

            return carry

        lax.fori_loop(first, last, unit, 0)

    def units(self):
        return self.count * (self.nz - 1)

    def finish(self):
        z, nz = self.z, self.nz
        last = self.count - 1
        self.end(jnp.int32(last))
        for j in range(max(0, last - 1), last + 1):
            self.keep(j, self.stage.at[j % 2], self.keep_sem.at[j % 2]).wait()
        for s in range(1, nz):

            @pl.when(z + nz - s < nz)
            def _():
                self.copy_right(last, s, self.right).wait_send()

            @pl.when(z - nz + s >= 0)
            def _():
                self.copy_left(last, s, self.left).wait_send()


def greet_all(seq, me, nz, others):
    z = seq // 2
    barrier = pltpu.get_barrier_semaphore()
    for peer in others + [(seq + 1 - 2 * (seq % 2), me)]:
        pl.semaphore_signal(barrier, inc=1, device_id=peer, device_id_type=MESH)

    @pl.when(z > 0)
    def _():
        pl.semaphore_signal(barrier, inc=1, device_id=(seq - 2, me), device_id_type=MESH)

    @pl.when(z < nz - 1)
    def _():
        pl.semaphore_signal(barrier, inc=1, device_id=(seq + 2, me), device_id_type=MESH)

    pl.semaphore_wait(barrier, len(others) + 1 + jnp.where(z > 0, 1, 0) + jnp.where(z < nz - 1, 1, 0))


def levels(code, step):
    return (jnp.floor(code.astype(F32) * (1.0 / step)) * step + step / 2.0).astype(BF16)


def gelu_parts(gate):
    root = math.sqrt(2.0 / math.pi)
    square = gate * gate
    bend = jnp.tanh(root * gate * (1.0 + 0.044715 * square))
    value = 0.5 * gate * (1.0 + bend)
    slope = 0.5 * (1.0 + bend) + 0.5 * gate * (1.0 - bend * bend) * root * (1.0 + 3 * 0.044715 * square)
    return value, slope


def strips(count, size, body):
    def step(i, carry):
        body(pl.ds(pl.multiple_of(i * size, size), size))
        return carry

    lax.fori_loop(0, count, step, 0)


def ffn_forward_kernel(tiles, riders, *refs):
    b, wgu, gs, wd, cots, g3, ds = refs[:7]
    refs = refs[7:]
    rider_in, refs = refs[:riders], refs[riders:]
    gu_o, hid_o, hidy_o, down_o, gf_o, sums_o = refs[:6]
    refs = refs[6:]
    rider_out, refs = refs[:riders], refs[riders:]
    (gu, hid, hidy, wbuf, wlev, dbuf, dlev, acc, downs, wsem, dsem, xs, xr, hs, hr, ys, yr, fs, fr,
     gxs, gxr, gcs, gcr, gfs, gfr, rs, rr, ks, outs) = refs
    seq, me, x, c = place_now()
    y = seq % 2
    across = (seq, (1 - x) * 2 + c)
    beside = (seq, x * 2 + 1 - c)
    beyond = (seq + 1 - 2 * y, me)
    rows, tw = gu.shape[2:]
    part = b.shape[2]
    deep = GROUP * part
    per = tiles // 4

    def load_up(t):
        return pltpu.make_async_copy(wgu.at[:, pl.ds(pl.multiple_of(t * tw, 128), tw)], wbuf.at[t % 2], wsem.at[t % 2])

    def load_down(t, half):
        start = ((c + half) % 2 * tiles + t) * tw
        return pltpu.make_async_copy(
            wd.at[:, pl.ds(pl.multiple_of(start, 128), tw)], dbuf.at[t % 2, half], dsem.at[t % 2, half]
        )

    load_up(0).start()
    load_up(1).start()
    for t in range(2):
        for half in range(2):
            load_down(t, half).start()
    greet([across, beside, beyond])
    travellers = []
    for i in range(riders):
        copy = remote(rider_in[i].at[:, 1 - y], rider_out[i], rs.at[i], rr.at[i], beyond)
        copy.start()
        travellers.append(copy)
    acc[...] = jnp.zeros_like(acc)

    def to_x(t):
        return remote(gu.at[x, t], gu.at[x, t], xs.at[t], xr.at[t], across)

    def to_core(t):
        return remote(hid.at[c * tiles + t], hid.at[c * tiles + t], hs.at[t], hr.at[t], beside)

    def slot(t, core):
        return (2 * core + t // (2 * per)) * per + t % per

    def to_y(t):
        return remote(hid.at[c * tiles + t], hidy.at[slot(t, c)], ys.at[t], yr.at[t], beyond)

    def keep(t, i, core):
        return pltpu.make_async_copy(hid.at[core * tiles + t], hid_o.at[slot(t, core)], ks.at[i, t])

    def wide(t):
        load_up(t).wait()

        def level(span):
            wlev[span, :] = levels(wbuf[t % 2, span, :], 16.0)

        strips(deep // 128, 128, level)

        @pl.when(t + 2 < tiles)
        def _():
            load_up(t + 2).start()

        scale = gs[t]

        def product(span):
            total = dot(b[0, span, :], wlev[0:part, :])
            for j in range(1, GROUP):
                total = total + dot(b[j, span, :], wlev[j * part : (j + 1) * part, :])
            gu[x, t, span, :] = (total * scale).astype(BF16)

        strips(rows // 256, 256, product)
        to_x(t).start()

    def middle(t):
        to_x(t).wait_recv()

        def body(span):
            gate = gu[0, t, span, :].astype(F32)
            up = gu[1, t, span, :].astype(F32)
            hid[c * tiles + t, span, :] = (gelu_parts(gate)[0] * up).astype(BF16)

        strips(rows // 64, 64, body)
        to_core(t).start()

        @pl.when((t // per) % 2 != y)
        def _():
            to_y(t).start()

        @pl.when((t // per) % 2 == y)
        def _():
            keep(t, 0, c).start()

    def narrow(t):
        for half in range(2):
            load_down(t, half).wait()

            def level(span):
                dlev[half, span, :] = levels(dbuf[t % 2, half, span, :], 64.0)

            strips(dlev.shape[1] // 64, 64, level)

        @pl.when(t + 2 < tiles)
        def _():
            for half in range(2):
                load_down(t + 2, half).start()

        to_core(t).wait_recv()

        def product(span):
            acc[span, :] += contract_last(hid[c * tiles + t, span, :], dlev[0]) + contract_last(
                hid[(1 - c) * tiles + t, span, :], dlev[1]
            )

        strips(rows // 256, 256, product)

        @pl.when((t // per) % 2 == y)
        def _():
            keep(t, 1, 1 - c).start()

    def step(i, carry):
        @pl.when(i < tiles)
        def _():
            wide(i)

        @pl.when((i >= 1) & (i < tiles + 1))
        def _():
            middle(i - 1)

        @pl.when(i >= 2)
        def _():
            narrow(i - 2)

        return carry

    lax.fori_loop(0, tiles + 2, step, 0)
    gu_out = pltpu.make_async_copy(gu, gu_o, outs.at[0])
    gu_out.start()

    parts = 4
    size = rows // parts
    sends = []
    own_sends = []
    for k in range(parts):
        span = pl.ds(k * size, size)
        downs[me, span, :] = acc[span, :].astype(BF16)
        part = downs.at[me, span]
        copy = remote(part, part, gxs.at[k], gxr.at[k], across)
        copy.start()
        sends.append(copy)
        copy = remote(part, part, gcs.at[k], gcr.at[k], beside)
        copy.start()
        own_sends.append(copy)

    def pass_on(t, carry):
        @pl.when((t // per) % 2 == y)
        def _():
            remote(hid.at[0], hidy.at[slot(t, c)], ys.at[t], yr.at[t], beyond).wait_recv()
            got = hidy.at[slot(t, c)]
            remote(got, got, fs.at[t], fr.at[t], beside).start()

        return carry

    lax.fori_loop(0, tiles, pass_on, 0)
    forwards = []
    for k in range(parts):
        sends[k].wait_recv()
        got = downs.at[(1 - x) * 2 + c, pl.ds(k * size, size)]
        copy = remote(got, got, gfs.at[k], gfr.at[k], beside)
        copy.start()
        forwards.append(copy)
    for copy in own_sends + forwards:
        copy.wait_recv()
    down_out = pltpu.make_async_copy(downs, down_o, outs.at[3])
    down_out.start()
    sums_o[...] = jnp.zeros_like(sums_o)
    width = GROUP * acc.shape[1]

    def last_norm(i, carry):
        pack = i // 2
        span = pl.ds(pl.multiple_of(i * 64, 64), 64)
        inner = (i % 2) * 64

        def cot_of(j):
            return cots[pack, pl.ds(pl.multiple_of(j * 128 + inner, 64), 64), :].astype(F32)

        square = jnp.zeros((64, 1), F32)
        cross = jnp.zeros((64, 1), F32)
        for j in range(GROUP):
            value = downs[j, span, :].astype(F32) * ds[j]
            square = square + jnp.sum(value * value, axis=1, keepdims=True)
            cross = cross + jnp.sum(value * (cot_of(j) * g3[j]), axis=1, keepdims=True)
        inverse = lax.rsqrt(square * (1.0 / width) + EPSILON)
        raw = downs[me, span, :].astype(F32)
        normed = raw * ds[me] * inverse
        cot = cot_of(me)
        grad = inverse * (cot * g3[me] - normed * (cross * inverse * (1.0 / width)))
        gf_o[span, :] = (grad * ds[me]).astype(BF16)
        sums_o[0:1, :] += jnp.sum(raw * grad, axis=0, keepdims=True)
        sums_o[1:2, :] += jnp.sum(cot * normed, axis=0, keepdims=True)
        return carry

    lax.fori_loop(0, rows // 64, last_norm, 0)

    def drain(t, carry):
        to_x(t).wait_send()
        to_core(t).wait_send()

        @pl.when((t // per) % 2 != y)
        def _():
            to_y(t).wait_send()

        @pl.when((t // per) % 2 == y)
        def _():
            keep(t, 0, c).wait()
            keep(t, 1, 1 - c).wait()
            got = hidy.at[slot(t, c)]
            remote(got, got, fs.at[t], fr.at[t], beside).wait_send()
            got = hidy.at[slot(t, 1 - c)]
            remote(got, got, fs.at[t], fr.at[t], beside).wait_recv()

        return carry

    lax.fori_loop(0, tiles, drain, 0)
    hidy_out = pltpu.make_async_copy(hidy, hidy_o, outs.at[4])
    hidy_out.start()
    for copy in sends + own_sends + forwards:
        copy.wait_send()
    for copy in travellers:
        copy.wait()
    gu_out.wait()
    down_out.wait()
    hidy_out.wait()


def ffn_forward(cid, b, wgu, gs, wd, cots, g3, ds, riders):
    rows, part = b.shape[1:]
    deep = GROUP * part
    tiles, _, tw = gs.shape
    count = len(riders)
    lone = max(count, 1)
    return comm_call(
        functools.partial(ffn_forward_kernel, tiles, count),
        cid,
        [
            jax.ShapeDtypeStruct((2, tiles, rows, tw), BF16),
            jax.ShapeDtypeStruct((tiles, rows, tw), BF16),
            jax.ShapeDtypeStruct((tiles, rows, tw), BF16),
            jax.ShapeDtypeStruct((GROUP, rows, part), BF16),
            jax.ShapeDtypeStruct((rows, part), BF16),
            jax.ShapeDtypeStruct((8, part), F32),
        ]
        + [jax.ShapeDtypeStruct(r.shape[:1] + r.shape[2:], r.dtype) for r in riders],
        [
            pltpu.VMEM((2, tiles, rows, tw), BF16),
            pltpu.VMEM((2 * tiles, rows, tw), BF16),
            pltpu.VMEM((tiles, rows, tw), BF16),
            pltpu.VMEM((2, deep, tw), BF16),
            pltpu.VMEM((deep, tw), BF16),
            pltpu.VMEM((2, 2, part, tw), BF16),
            pltpu.VMEM((2, part, tw), BF16),
            pltpu.VMEM((rows, part), F32),
            pltpu.VMEM((GROUP, rows, part), BF16),
            DMA((2,)), DMA((2, 2)), DMA((tiles,)), DMA((tiles,)), DMA((tiles,)), DMA((tiles,)), DMA((tiles,)),
            DMA((tiles,)), DMA((tiles,)), DMA((tiles,)), DMA((4,)), DMA((4,)), DMA((4,)), DMA((4,)), DMA((4,)),
            DMA((4,)), DMA((lone,)), DMA((lone,)), DMA((2, tiles)), DMA((5,)),
        ],
        [VMEM, ANY, VMEM, ANY, VMEM, VMEM, VMEM] + [ANY] * count,
        [ANY, ANY, ANY, ANY, VMEM, VMEM] + [ANY] * count,
    )(b, wgu, gs, wd, cots, g3, ds, *riders)


def ffn_backward_kernel(tiles, nz, chained, *refs):
    gf, wd, wgu, gs, gu, hid, hidy = refs[:7]
    dg_o, dgy_o, gsum_o, out, ddown_o = refs[7:12]
    (hh, hy, gfy, wbuf, wlev, dbuf, dlev, pair, co, cgot, near, sx, xgot, dg, acc, low, from_core, to_xb, from_x,
     hsem, wsem, dsem, psem, cs, cr, xs, xr, ys, yr, os, gys, gyr, ccs, ccr, cxs, cxr) = refs[12:48]
    chain_refs = refs[48:]
    seq, me, x, c = place_now()
    y = seq % 2
    z = seq // 2
    across = (seq, (1 - x) * 2 + c)
    beside = (seq, x * 2 + 1 - c)
    beyond = (seq + 1 - 2 * y, me)
    rows, tw = dg.shape[1:]
    part = acc.shape[2]
    deep = GROUP * part
    per = hid.shape[0] // 4 if chained else 0
    ring = dg.shape[0]

    def load_up(t):
        return pltpu.make_async_copy(wgu.at[:, pl.ds(pl.multiple_of(t * tw, 128), tw)], wbuf.at[t % 2], wsem.at[t % 2])

    def load_down(t, half):
        start = ((c + half) % 2 * tiles + t) * tw
        return pltpu.make_async_copy(
            wd.at[:, pl.ds(pl.multiple_of(start, 128), tw)], dbuf.at[t % 2, half], dsem.at[t % 2, half]
        )

    def load_pair(t):
        return pltpu.make_async_copy(gu.at[:, t], pair.at[t % 2], psem.at[t % 2])

    for t in range(2):
        for half in range(2):
            load_down(t, half).start()
        load_pair(t).start()
        load_up(t).start()
    if chained:
        load_hid = pltpu.make_async_copy(hid, hh, hsem.at[0])
        load_hidy = pltpu.make_async_copy(hidy, hy, hsem.at[1])
        load_hid.start()
        load_hidy.start()
    if chained:
        greet_all(seq, me, nz, [across, beside])
        gf_swap = remote(gf, gfy, gys, gyr, beyond)
        gf_swap.start()
    else:
        greet([across, beside, beyond])
    acc[...] = jnp.zeros_like(acc)

    def to_core(t):
        return remote(co.at[t % 2], cgot.at[t], cs.at[t], cr.at[t], beside)

    def to_x(t):
        return remote(sx.at[t % 4], xgot.at[t], xs.at[t], xr.at[t], across)

    def columns(ref, t):
        return ref.at[:, pl.ds(pl.multiple_of(t * tw, 128), tw)]

    def to_y(t):
        return remote(dg.at[t % ring], columns(dgy_o, t), ys.at[t], yr.at[t], beyond)

    def keep(t):
        return pltpu.make_async_copy(dg.at[t % ring], columns(dg_o, t), os.at[t])

    def hidden(t):
        for half in range(2):
            load_down(t, half).wait()

            def level(span):
                dlev[half, span, :] = levels(dbuf[t % 2, half, span, :], 64.0)

            strips(dlev.shape[1] // 64, 64, level)

        @pl.when(t + 2 < tiles)
        def _():
            for half in range(2):
                load_down(t + 2, half).start()

        @pl.when(t >= 2)
        def _():
            to_core(t - 2).wait_send()

        def product(span):
            co[t % 2, span, :] = dot(gf[span, :], dlev[1]).astype(BF16)

        strips(rows // 256, 256, product)
        to_core(t).start()

        def product_near(span):
            near[t % 2, span, :] = dot(gf[span, :], dlev[0])

        strips(rows // 256, 256, product_near)

    def chip(t):
        @pl.when(t >= 4)
        def _():
            to_x(t - 4).wait_send()

        to_core(t).wait_recv()

        def body(span):
            sx[t % 4, span, :] = (near[t % 2, span, :] + cgot[t, span, :].astype(F32)).astype(BF16)

        strips(rows // 64, 64, body)
        to_x(t).start()

    is_gate = jnp.where(x == 0, 1.0, 0.0).astype(F32)

    def own(t):
        load_pair(t).wait()

        @pl.when(t >= ring)
        def _():
            to_y(t - ring).wait_send()
            keep(t - ring).wait()

        to_x(t).wait_recv()
        scale = gs[t]
        gsum_o[t] = jnp.zeros((8, tw), F32)

        def body(span):
            grad = sx[t % 4, span, :].astype(F32) + xgot[t, span, :].astype(F32)
            gate = pair[t % 2, 0, span, :].astype(F32)
            up = pair[t % 2, 1, span, :].astype(F32)
            value, slope = gelu_parts(gate)
            full = grad * (is_gate * (up * slope) + (1.0 - is_gate) * value)
            gsum_o[t, 0:1, :] += jnp.sum(pair[t % 2, x, span, :].astype(F32) * full, axis=0, keepdims=True)
            dg[t % ring, span, :] = (full * scale).astype(BF16)

        strips(rows // 64, 64, body)

        @pl.when(t + 2 < tiles)
        def _():
            load_pair(t + 2).start()

        to_y(t).start()
        keep(t).start()

    def back(t):
        load_up(t).wait()

        def level(span):
            wlev[span, :] = levels(wbuf[t % 2, span, :], 16.0)

        strips(deep // 128, 128, level)

        @pl.when(t + 2 < tiles)
        def _():
            load_up(t + 2).start()

        def product(span):
            for j in range(GROUP):
                acc[j, span, :] += contract_last(dg[t % ring, span, :], wlev[j * part : (j + 1) * part, :])

        strips(rows // 128, 128, product)

    if chained:

        def partial(k, j):
            return contract_first(hh[k * per + j], gf[...]) + contract_first(hy[k * per + j], gfy[...])

        downs = Chain(
            nz, per, seq, me, partial, lambda j, stage, sem: pltpu.make_async_copy(stage, ddown_o.at[j], sem), chain_refs
        )
    hops = nz - 1

    def step(i, carry):
        @pl.when(i < tiles)
        def _():
            hidden(i)

        @pl.when((i >= 1) & (i < tiles + 1))
        def _():
            chip(i - 1)

        if chained:

            @pl.when(i == 1)
            def _():
                gf_swap.wait_recv()
                load_hid.wait()
                load_hidy.wait()

            @pl.when((i >= 1) & (i < 1 + per * hops))
            def _():
                downs.run(i - 1, i)

        @pl.when(i >= 2)
        def _():
            own(i - 2)
            back(i - 2)

        return carry

    lax.fori_loop(0, tiles + 2, step, 0)

    parts = 4
    block = rows // GROUP
    size = block // parts
    order = [1 - x, x]
    js = range(GROUP)
    cores = []
    for i in range(2):
        for k in range(parts):
            owner = order[i] * 2 + 1 - c
            span = pl.ds(k * size, size)
            for j in js:
                low[i, j, span, :] = acc[j, pl.ds(pl.multiple_of(owner * block + k * size, 16), size), :].astype(BF16)
            copy = remote(low.at[i, :, span], from_core.at[i, :, span], ccs.at[i, k], ccr.at[i, k], beside)
            copy.start()
            cores.append(copy)
    sends = []
    for k in range(parts):
        span = pl.ds(k * size, size)
        here = pl.ds(pl.multiple_of((order[0] * 2 + c) * block + k * size, 16), size)
        cores[k].wait_recv()
        for j in js:
            to_xb[j, span, :] = (acc[j, here, :] + from_core[0, j, span, :].astype(F32)).astype(BF16)
        copy = remote(to_xb.at[:, span], from_x.at[:, span], cxs.at[k], cxr.at[k], across)
        copy.start()
        sends.append(copy)
    if chained:
        downs.finish()
    for k in range(parts):
        span = pl.ds(k * size, size)
        here = pl.ds(pl.multiple_of((order[1] * 2 + c) * block + k * size, 16), size)
        cores[parts + k].wait_recv()
        sends[k].wait_recv()
        for j in js:
            out[j, span, :] = acc[j, here, :] + from_core[1, j, span, :].astype(F32) + from_x[j, span, :].astype(F32)

    for copy in cores + sends:
        copy.wait_send()
    for t in range(tiles - 2, tiles):
        to_core(t).wait_send()
    for t in range(tiles - 4, tiles):
        to_x(t).wait_send()
    for t in range(tiles - ring, tiles):
        to_y(t).wait_send()
        keep(t).wait()

    def drain(t, carry):
        to_y(t).wait_recv()
        return carry

    lax.fori_loop(0, tiles, drain, 0)
    if chained:
        gf_swap.wait_send()


def ffn_backward(cid, n, gf, wd, wgu, gs, gu, hid, hidy):
    rows, part = gf.shape
    deep = wgu.shape[0]
    tiles, _, tw = gs.shape
    nz = n // 2
    chained = nz == 4
    per = tiles // nz if chained else 1
    hops = nz - 1 if chained else 1
    block = rows // GROUP
    half = (tiles, rows, tw) if chained else (1, 16, 128)
    message = (tw, part) if chained else (16, 128)
    ring = 4
    return comm_call(
        functools.partial(ffn_backward_kernel, tiles, nz, chained),
        cid,
        [
            jax.ShapeDtypeStruct((rows, tiles * tw), BF16),
            jax.ShapeDtypeStruct((rows, tiles * tw), BF16),
            jax.ShapeDtypeStruct((tiles, 8, tw), F32),
            jax.ShapeDtypeStruct((GROUP, block, part), F32),
            jax.ShapeDtypeStruct((per,) + message, F32),
        ],
        [
            pltpu.VMEM(half, BF16),
            pltpu.VMEM(half, BF16),
            pltpu.VMEM((rows, part), BF16),
            pltpu.VMEM((2, deep, tw), BF16),
            pltpu.VMEM((deep, tw), BF16),
            pltpu.VMEM((2, 2, part, tw), BF16),
            pltpu.VMEM((2, part, tw), BF16),
            pltpu.VMEM((2, 2, rows, tw), BF16),
            pltpu.VMEM((2, rows, tw), BF16),
            pltpu.VMEM((tiles, rows, tw), BF16),
            pltpu.VMEM((2, rows, tw), F32),
            pltpu.VMEM((4, rows, tw), BF16),
            pltpu.VMEM((tiles, rows, tw), BF16),
            pltpu.VMEM((ring, rows, tw), BF16),
            pltpu.VMEM((GROUP, rows, part), F32),
            pltpu.VMEM((2, GROUP, block, part), BF16),
            pltpu.VMEM((2, GROUP, block, part), BF16),
            pltpu.VMEM((GROUP, block, part), BF16),
            pltpu.VMEM((GROUP, block, part), BF16),
            DMA((2,)), DMA((2,)), DMA((2, 2)), DMA((2,)), DMA((tiles,)), DMA((tiles,)), DMA((tiles,)), DMA((tiles,)),
            DMA((tiles,)), DMA((tiles,)), DMA((tiles,)), DMA, DMA, DMA((2, 4)), DMA((2, 4)), DMA((4,)), DMA((4,)),
        ]
        + (Chain.scratch(nz, per, *message) if chained else []),
        [VMEM, ANY, ANY, VMEM, ANY, ANY, ANY],
        [ANY, ANY, VMEM, VMEM, ANY],
    )(gf, wd, wgu, gs, gu, hid, hidy)


def gate_chain(nz, first, count, seq, me, bt, bty, dg, dgy, out, slabs, halves, slab_sem, scratch):
    loads = [pltpu.make_async_copy(bt.at[:, seq % 2], halves.at[0], slab_sem.at[2])]
    loads.append(pltpu.make_async_copy(bty, halves.at[1], slab_sem.at[3]))
    for i, ref in enumerate((dg, dgy)):
        loads.append(
            pltpu.make_async_copy(ref.at[:, pl.ds(first * TILE, count * TILE)], slabs.at[i], slab_sem.at[i])
        )
    for copy in loads:
        copy.start()

    def partial(k, j):
        cols = pl.ds(pl.multiple_of(j * TILE, 128), TILE)
        return dot(halves[0, k], slabs[0, :, cols]) + dot(halves[1, k], slabs[1, :, cols])

    def keep(j, stage, sem):
        return pltpu.make_async_copy(stage, out.at[:, pl.ds(pl.multiple_of(j * TILE, 128), TILE)], sem)

    return Chain(nz, count, seq, me, partial, keep, scratch), loads


def gate_scratch(nz, count, bt):
    rows = bt.shape[3]
    return [
        pltpu.VMEM((2, rows, count * TILE), BF16), pltpu.VMEM((2, nz) + bt.shape[2:], BF16), DMA((4,))
    ] + Chain.scratch(nz, count, bt.shape[2], TILE)


def branch_back_kernel(n, tiles, *refs):
    (gsi, mid, raw, cot, g2, g3, scale, wo, q, mixed, mass, own_meta, metas, kv, bt, bty, dg, dgy) = refs[:18]
    dmid, sums, gy, gyy, dq, dkv, gate_o = refs[18:25]
    (low, gys, gy_all, part, from_core, to_x, from_x, grad, kvs, dkvs, es, er, el, cs, cr, xs, xr, ks, ds, yss, ysr,
     ows) = refs[25:47]
    rest = refs[47:]
    seq, me, x, c = place_now()
    nz = n // 2
    across = (seq, (1 - x) * 2 + c)
    beside = (seq, x * 2 + 1 - c)
    beyond = (seq + 1 - 2 * (seq % 2), me)
    peers = [(seq, lax.rem(me + d, GROUP)) for d in range(1, GROUP)]
    chain = None
    if tiles:
        chain, loads = gate_chain(nz, 0, tiles, seq, me, bt, bty, dg, dgy, gate_o, *rest[:3], rest[3:])
        greet_all(seq, me, nz, peers)
    else:
        greet(peers + [beyond])
    width = GROUP * raw.shape[2]
    mean = 1.0 / width
    sums[...] = jnp.zeros_like(sums)
    js = range(GROUP)

    def rowsum(values):
        total = values[0]
        for value in values[1:]:
            total = total + value
        return jnp.sum(total, axis=1, keepdims=True) * mean

    def norms(span):
        middle = [mid[j, span, :] for j in js]
        up = [gsi[j, span, :] for j in js]
        inverse = lax.rsqrt(rowsum([v * v for v in middle]) + EPSILON)
        third = [v * inverse for v in middle]
        scaled = [up[j] * g3[j] for j in js]
        cross = rowsum([scaled[j] * third[j] for j in js])
        grad_middle = [
            cot[j, span, :].astype(F32) + inverse * (scaled[j] - third[j] * cross) for j in js
        ]
        plain = [raw[j, span, :].astype(F32) for j in js]
        branch = [plain[j] * scale[j] for j in js]
        inverse = lax.rsqrt(rowsum([v * v for v in branch]) + EPSILON)
        second = [v * inverse for v in branch]
        scaled = [grad_middle[j] * g2[j] for j in js]
        cross = rowsum([scaled[j] * second[j] for j in js])
        for j in js:
            full = inverse * (scaled[j] - second[j] * cross)
            gys[j, span, :] = (full * scale[j]).astype(BF16)
            dmid[j, span, :] = grad_middle[j]
            sums[j, 0:1, :] += jnp.sum(grad_middle[j] * second[j], axis=0, keepdims=True)
            sums[j, 1:2, :] += jnp.sum(up[j] * third[j], axis=0, keepdims=True)
            sums[j, 2:3, :] += jnp.sum(plain[j] * full, axis=0, keepdims=True)

    strips(raw.shape[1] // 16, 16, norms)

    copies = []
    for d in (2, 1, 3):
        peer = peers[d - 1]
        copy = remote(gys.at[peer[1]], gy_all.at[me], es.at[d - 1], er.at[d - 1], peer)
        copy.start()
        copies.append(copy)
    own = pltpu.make_async_copy(gys.at[me], gy_all.at[me], el)
    own.start()
    for p in range(2):
        pltpu.make_async_copy(kv.at[:, :, pl.ds(p * 128, 128)], kvs.at[p], ks.at[p]).start()
    units = chain.units() if chain else 0
    at = [0]

    def beside_work(count):
        if chain:
            last = min(units, at[0] + count)
            chain.run(at[0], last)
            at[0] = last

    if chain:
        for load in loads:
            load.wait()
    beside_work(3)
    for copy in copies:
        copy.wait_recv()
    own.wait()
    gy_out = pltpu.make_async_copy(gy_all, gy, ows)
    gy_out.start()
    swap = remote(gy_all, gyy, yss, ysr, beyond)
    swap.start()

    heads = part.shape[3]
    rows = part.shape[2]
    order = [1 - x, x]

    def product(i, k, to):
        grad_branch = gy_all[...].reshape(rows, raw.shape[2])
        start = (order[i] * 2 + k) * heads
        to[...] = dot(grad_branch, wo[:, pl.ds(pl.multiple_of(start, 128), heads)]).astype(BF16)

    cores = []
    for i in range(2):
        product(i, 1 - c, part.at[i, 0])
        copy = remote(part.at[i, 0], from_core.at[i], cs.at[i], cr.at[i], beside)
        copy.start()
        cores.append(copy)
    for i in range(2):
        product(i, c, part.at[i, 1])
    cores[0].wait_recv()

    def add_core(span):
        to_x[span, :] = (part[0, 1, span, :].astype(F32) + from_core[0, span, :].astype(F32)).astype(BF16)

    strips(rows // 64, 64, add_core)
    over = remote(to_x, from_x, xs, xr, across)
    over.start()
    beside_work(4)
    cores[1].wait_recv()
    over.wait_recv()

    def add_all(span):
        grad[span, :] = (
            part[1, 1, span, :].astype(F32) + from_core[1, span, :].astype(F32) + from_x[span, :].astype(F32)
        ).astype(BF16)

    strips(rows // 64, 64, add_all)

    def load_pack(p):
        return pltpu.make_async_copy(
            kv.at[:, :, pl.ds(pl.multiple_of(p * 128, 128), 128)], kvs.at[p % 2], ks.at[p % 2]
        )

    def store_pack(p):
        return pltpu.make_async_copy(
            dkvs.at[p % 2], dkv.at[:, :, pl.ds(pl.multiple_of(p * 128, 128), 128)], ds.at[p % 2]
        )

    base = at[0]
    each = max(0, units - base) // GROUP

    def one_pack(p, carry):
        load_pack(p).wait()

        @pl.when(p >= 2)
        def _():
            store_pack(p - 2).wait()

        span = pl.ds(pl.multiple_of(p * 128, 128), 128)
        keys = kvs[p % 2, :, 0].reshape(n * 128, DH)
        values = kvs[p % 2, :, 1].reshape(n * 128, DH)
        allowed = masks(n, own_meta.at[pl.ds(p, 1)], metas.at[:, pl.ds(p, 1)])
        back_pack(
            n, keys, values, allowed, q.at[span], grad.at[span], mixed.at[span], mass.at[span], dq.at[span],
            dkvs.at[p % 2],
        )
        store_pack(p).start()

        @pl.when(p + 2 < GROUP)
        def _():
            load_pack(p + 2).start()

        if each:
            chain.run(base + p * each, base + (p + 1) * each)
        return carry

    lax.fori_loop(0, GROUP, one_pack, 0)
    at[0] = base + GROUP * each
    beside_work(units)
    if chain:
        chain.finish()
    for copy in copies + cores + [over]:
        copy.wait_send()
    store_pack(2).wait()
    store_pack(3).wait()
    swap.wait()
    gy_out.wait()


def branch_back(cid, n, tiles, gsi, mid, raw, cot, g2, g3, scale, wo, q, mixed, mass, own_meta, metas, kv, pairs):
    bt, bty, dg, dgy = pairs
    own, part = raw.shape[1:]
    rows = q.shape[0]
    heads = q.shape[1]
    block = lambda kind: jax.ShapeDtypeStruct((GROUP, own, part), kind)
    gate_rows = bt.shape[2]
    pack = (2, n, 2, own, DH)
    return comm_call(
        functools.partial(branch_back_kernel, n, tiles),
        cid,
        [
            block(F32),
            jax.ShapeDtypeStruct((GROUP, 8, part), F32),
            block(BF16),
            block(BF16),
            jax.ShapeDtypeStruct(q.shape, F32),
            jax.ShapeDtypeStruct(kv.shape, BF16),
            jax.ShapeDtypeStruct((gate_rows, max(tiles, 1) * TILE), F32),
        ],
        [
            pltpu.VMEM((8, 128), BF16),
            pltpu.VMEM((GROUP, own, part), BF16),
            pltpu.VMEM((GROUP, own, part), BF16),
            pltpu.VMEM((2, 2, rows, heads), BF16),
            pltpu.VMEM((2, rows, heads), BF16),
            pltpu.VMEM((rows, heads), BF16),
            pltpu.VMEM((rows, heads), BF16),
            pltpu.VMEM((rows, heads), BF16),
            pltpu.VMEM(pack, BF16),
            pltpu.VMEM(pack, BF16),
            DMA((3,)), DMA((3,)), DMA, DMA((2,)), DMA((2,)), DMA, DMA, DMA((2,)), DMA((2,)), DMA, DMA, DMA,
        ]
        + (gate_scratch(n // 2, tiles, bt) if tiles else []),
        [VMEM] * 13 + [ANY] * 5,
        [VMEM, VMEM, ANY, ANY, VMEM, ANY, ANY],
    )(gsi, mid, raw, cot, g2, g3, scale, wo, q, mixed, mass, own_meta, metas, kv, bt, bty, dg, dgy)


def keys_back_kernel(n, first, tiles, *refs):
    (src, dq, q_raw, p_raw, cosine, sine, q_scale, p_scale, wq, wkv, bt, bty, dg, dgy) = refs[:14]
    joined, joined_y, out, sums, gate_o = refs[14:19]
    (y_got, r_got, l_got, r_out, l_out, moved, back, acc, low, from_core, to_xb, from_x,
     ys, yr, rs, rr, ls, lr, hs, hr, local, jys, jyr, ccs, ccr, cxs, cxr) = refs[19:46]
    slabs, halves, slab_sem, *rest = refs[46:]
    seq, me, x, c = place_now()
    y = seq % 2
    z = seq // 2
    nz = n // 2
    right = (seq + 2, me)
    left = (seq - 2, me)
    beyond = (z * 2 + 1 - y, me)
    across = (seq, (1 - x) * 2 + c)
    beside = (seq, x * 2 + 1 - c)
    chain, loads = gate_chain(nz, first, tiles, seq, me, bt, bty, dg, dgy, gate_o, slabs, halves, slab_sem, rest)
    greet_all(seq, me, nz, [(seq, lax.rem(me + d, GROUP)) for d in range(1, GROUP)])
    rows, width = dq.shape
    deep = acc.shape[1]
    half = DH // 2

    def swap(k):
        return remote(src.at[k * 2 + 1 - y], y_got.at[k], ys.at[k], yr.at[k], beyond)

    for t in range(1, nz):
        go_right = z + nz - t
        go_left = z - nz + t

        @pl.when(go_right < nz)
        def _():
            swap(go_right).start()

        @pl.when(go_left >= 0)
        def _():
            swap(go_left).start()

    swap(z).start()
    sums[...] = jnp.zeros_like(sums)

    def turn_queries(span):
        cos = cosine[span, :]
        sin = sine[span, :]
        for h in range(2):
            a = slice(h * DH, h * DH + half)
            b = slice(h * DH + half, (h + 1) * DH)
            one = dq[span, a]
            two = dq[span, b]
            for cols, full in ((a, one * cos + two * sin), (b, two * cos - one * sin)):
                sums[0:1, cols] += jnp.sum(q_raw[span, cols] * full, axis=0, keepdims=True)
                joined[span, cols] = (full * q_scale[:, cols]).astype(BF16)

    strips(rows // 64, 64, turn_queries)

    def query_part(span):
        acc[span, :] = contract_last(joined[span, :width], wq[...])

    strips(rows // 128, 128, query_part)

    def pair_sum(k, more, to):
        def body(i, carry):
            part = i // 4
            span = pl.ds(pl.multiple_of((i % 4) * 128, 128), 128)
            total = src[k * 2 + y, part, span, :].astype(F32) + y_got[k, part, span, :].astype(F32)
            for ref in more:
                total = total + ref[part, span, :].astype(F32)
            to[part, span, :] = total.astype(BF16)
            return carry

        lax.fori_loop(0, 8, body, 0)

    for load in loads:
        load.wait()
    units = chain.units()
    at = [0]

    def beside_work(count):
        last = min(units, at[0] + count)
        chain.run(at[0], last)
        at[0] = last

    for t in range(1, nz):
        go_right = z + nz - t
        go_left = z - nz + t

        def hop(go, at_end, got, send, ss, sr, to, source):
            swap(go).wait_recv()
            if t == 1:
                pair_sum(go, [], send.at[t - 1])
            else:

                @pl.when(jnp.logical_not(at_end))
                def _():
                    remote(send.at[t - 1], got.at[t - 2], ss.at[t - 2], sr.at[t - 2], source).wait_recv()
                    pair_sum(go, [got.at[t - 2]], send.at[t - 1])

                @pl.when(at_end)
                def _():
                    pair_sum(go, [], send.at[t - 1])

            remote(send.at[t - 1], got.at[t - 1], ss.at[t - 1], sr.at[t - 1], to).start()

        @pl.when(go_right < nz)
        def _():
            hop(go_right, z == 0, r_got, r_out, rs, rr, right, left)

        @pl.when(go_left >= 0)
        def _():
            hop(go_left, z == nz - 1, l_got, l_out, ls, lr, left, right)

        beside_work(1)

    swap(z).wait_recv()
    last = nz - 2

    def got_left():
        remote(r_out.at[last], r_got.at[last], rs.at[last], rr.at[last], left).wait_recv()

    def got_right():
        remote(l_out.at[last], l_got.at[last], ls.at[last], lr.at[last], right).wait_recv()

    @pl.when(z == 0)
    def _():
        got_right()
        pair_sum(z, [l_got.at[last]], moved)

    @pl.when(z == nz - 1)
    def _():
        got_left()
        pair_sum(z, [r_got.at[last]], moved)

    @pl.when((z > 0) & (z < nz - 1))
    def _():
        got_left()
        got_right()
        pair_sum(z, [r_got.at[last], l_got.at[last]], moved)

    for t in range(2):
        target = t * 2 + x

        @pl.when(target == me)
        def _():
            pltpu.make_async_copy(moved.at[t], back.at[c], local).start()

        @pl.when(target != me)
        def _():
            remote(moved.at[t], back.at[c], hs.at[t], hr.at[c], (seq, target)).start()

    beside_work(1)
    for j in range(2):
        source = c * 2 + j

        @pl.when(source == me)
        def _():
            pltpu.make_async_copy(moved.at[0], back.at[j], local).wait()

        @pl.when(source != me)
        def _():
            remote(moved.at[0], back.at[j], hs.at[0], hr.at[j], (seq, source)).wait_recv()

    is_key = jnp.where(x == 0, 1.0, 0.0).astype(F32)

    def turn_pairs(span):
        cos = is_key * cosine[span, :] + (1.0 - is_key)
        sin = is_key * sine[span, :]
        for h in range(2):
            a = slice(h * DH, h * DH + half)
            b = slice(h * DH + half, (h + 1) * DH)
            one = back[h, span, :half].astype(F32)
            two = back[h, span, half:].astype(F32)
            for cols, full in ((a, one * cos + two * sin), (b, two * cos - one * sin)):
                sums[1:2, cols] += jnp.sum(p_raw[span, cols] * full, axis=0, keepdims=True)
                joined[span, width + cols.start : width + cols.stop] = (full * p_scale[:, cols]).astype(BF16)

    strips(rows // 64, 64, turn_pairs)
    joined_swap = remote(joined, joined_y, jys, jyr, beyond)
    joined_swap.start()

    def pair_part(span):
        acc[span, :] += contract_last(joined[span, width:], wkv[...])

    strips(rows // 128, 128, pair_part)

    parts = 4
    block = rows // GROUP
    size = block // parts
    order = [1 - x, x]
    cores = []
    for i in range(2):
        for k in range(parts):
            owner = order[i] * 2 + 1 - c
            span = pl.ds(k * size, size)
            low[i, span, :] = acc[pl.ds(pl.multiple_of(owner * block + k * size, 16), size), :].astype(BF16)
            copy = remote(low.at[i, span], from_core.at[i, span], ccs.at[i, k], ccr.at[i, k], beside)
            copy.start()
            cores.append(copy)
    sends = []
    for k in range(parts):
        span = pl.ds(k * size, size)
        here = pl.ds(pl.multiple_of((order[0] * 2 + c) * block + k * size, 16), size)
        cores[k].wait_recv()
        to_xb[span, :] = (acc[here, :] + from_core[0, span, :].astype(F32)).astype(BF16)
        copy = remote(to_xb.at[span], from_x.at[span], cxs.at[k], cxr.at[k], across)
        copy.start()
        sends.append(copy)
    beside_work(units)
    chain.finish()
    for k in range(parts):
        span = pl.ds(k * size, size)
        here = pl.ds(pl.multiple_of((order[1] * 2 + c) * block + k * size, 16), size)
        cores[parts + k].wait_recv()
        sends[k].wait_recv()
        out[span, :] = acc[here, :] + from_core[1, span, :].astype(F32) + from_x[span, :].astype(F32)

    for t in range(2):

        @pl.when(t * 2 + x != me)
        def _():
            remote(moved.at[t], back.at[c], hs.at[t], hr.at[c], (seq, t * 2 + x)).wait_send()

    for k in range(nz):
        swap(k).wait_send()
    for t in range(1, nz):

        @pl.when(z + nz - t < nz)
        def _():
            remote(r_out.at[t - 1], r_got.at[t - 1], rs.at[t - 1], rr.at[t - 1], right).wait_send()

        @pl.when(z - nz + t >= 0)
        def _():
            remote(l_out.at[t - 1], l_got.at[t - 1], ls.at[t - 1], lr.at[t - 1], left).wait_send()

    for copy in cores + sends:
        copy.wait_send()
    joined_swap.wait()


def keys_back(cid, n, first, tiles, src, dq, q_raw, p_raw, cosine, sine, q_scale, p_scale, wq, wkv, pairs):
    bt, bty, dg, dgy = pairs
    nz = n // 2
    rows, width = dq.shape
    deep = wq.shape[0]
    block = rows // GROUP
    shape = src.shape[1:]
    chain = pltpu.VMEM((nz - 1,) + shape, BF16)
    joined = jax.ShapeDtypeStruct((rows, 2 * width), BF16)
    return comm_call(
        functools.partial(keys_back_kernel, n, first, tiles),
        cid,
        [
            joined,
            joined,
            jax.ShapeDtypeStruct((block, deep), F32),
            jax.ShapeDtypeStruct((8, width), F32),
            jax.ShapeDtypeStruct((bt.shape[2], tiles * TILE), F32),
        ],
        [
            pltpu.VMEM((nz,) + shape, BF16), chain, chain, chain, chain, pltpu.VMEM(shape, BF16), pltpu.VMEM(shape, BF16),
            pltpu.VMEM((rows, deep), F32),
            pltpu.VMEM((2, block, deep), BF16),
            pltpu.VMEM((2, block, deep), BF16),
            pltpu.VMEM((block, deep), BF16),
            pltpu.VMEM((block, deep), BF16),
            DMA((nz,)), DMA((nz,)), DMA((nz - 1,)), DMA((nz - 1,)), DMA((nz - 1,)), DMA((nz - 1,)),
            DMA((2,)), DMA((2,)), DMA, DMA, DMA, DMA((2, 4)), DMA((2, 4)), DMA((4,)), DMA((4,)),
        ]
        + gate_scratch(nz, tiles, bt),
        [VMEM] * 10 + [ANY] * 4,
        [VMEM, ANY, VMEM, VMEM, ANY],
    )(src, dq, q_raw, p_raw, cosine, sine, q_scale, p_scale, wq, wkv, bt, bty, dg, dgy)


def finish_kernel(n, rounds, first, tiles, *refs):
    (whole, part, bt, bty, dg, dgy, ot, oty, gy, gyy, at, aty, joined, joined_y) = refs[:14]
    whole_out, part_out, gate_o, output_o, attention_o = refs[14:19]
    bufs, gots, mine, theirs, ss, rs = refs[19:25]
    slabs, halves, slab_sem = refs[25:28]
    gate_refs, output_refs, attention_refs = refs[28:38], refs[38:48], refs[48:58]
    output_halves, attention_halves, half_sem = refs[58:]
    seq, me, x, c = place_now()
    nz = n // 2
    across = (seq, (1 - x) * 2 + c)
    beside = (seq, x * 2 + 1 - c)
    gates, loads = gate_chain(nz, first, tiles, seq, me, bt, bty, dg, dgy, gate_o, slabs, halves, slab_sem, gate_refs)
    for i, (ref, to) in enumerate(
        ((ot.at[:, seq % 2], output_halves.at[0]), (oty, output_halves.at[1]),
         (at.at[:, seq % 2], attention_halves.at[0]), (aty, attention_halves.at[1]))
    ):
        load = pltpu.make_async_copy(ref, to, half_sem.at[i])
        load.start()
        loads.append(load)
    wide = joined.shape[1] // 2

    def output_partial(k, j):
        return dot(output_halves[0, k], gy[...]) + dot(output_halves[1, k], gyy[...])

    def attention_partial(k, j):
        cols = pl.ds(pl.multiple_of(j * wide, 128), wide)
        return dot(attention_halves[0, k], joined[:, cols]) + dot(attention_halves[1, k], joined_y[:, cols])

    outputs = Chain(
        nz, 1, seq, me, output_partial, lambda j, stage, sem: pltpu.make_async_copy(stage, output_o, sem), output_refs
    )
    attentions = Chain(
        nz,
        2,
        seq,
        me,
        attention_partial,
        lambda j, stage, sem: pltpu.make_async_copy(
            stage, attention_o.at[:, pl.ds(pl.multiple_of(j * wide, 128), wide)], sem
        ),
        attention_refs,
    )
    partners = []
    for r in range(rounds):
        bit = 1 << r
        partners.append((seq + bit - 2 * bit * ((seq // bit) % 2), me))
    greet([(lax.rem(seq + d, n), me) for d in range(1, n)] + [across, beside])
    for load in loads:
        load.wait()
    rows = whole.shape[0]
    bufs[0, :rows, :] = whole[...]
    bufs[0, rows:, :] = part[...]
    work = [(gates, u) for u in range(0, gates.units(), 3)]
    work += [(outputs, 0), (attentions, 0), (attentions, 3)]
    at_work = [0]

    def beside_work(count):
        todo = work[at_work[0] : at_work[0] + count]
        at_work[0] += count
        start = None
        for i, (chain, u) in enumerate(todo):
            if start is None:
                start = u
            if i + 1 == len(todo) or todo[i + 1][0] is not chain:
                chain.run(start, u + 3)
                start = None

    for r in range(rounds + 1):
        partner = partners[r] if r < rounds else across
        copy = remote(bufs.at[r], gots.at[r], ss.at[r], rs.at[r], partner)
        copy.start()
        beside_work(1)
        copy.wait()
        if r < rounds:
            bufs[r + 1] = bufs[r] + gots[r]
    mine[0, :rows, :] = bufs[rounds, :rows, :] + gots[rounds, :rows, :]
    mine[0, rows:, :] = bufs[rounds, rows:, :]
    mine[1, rows:, :] = gots[rounds, rows:, :]
    mine[1, :rows, :] = jnp.zeros((rows, 128), F32)
    copy = remote(mine, theirs, ss.at[rounds + 1], rs.at[rounds + 1], beside)
    copy.start()
    beside_work(len(work))
    copy.wait()
    whole_out[...] = mine[0, :rows, :] + theirs[0, :rows, :]
    part_out[x * 2 + c] = mine[0, rows:, :]
    part_out[(1 - x) * 2 + c] = mine[1, rows:, :]
    part_out[x * 2 + 1 - c] = theirs[0, rows:, :]
    part_out[(1 - x) * 2 + 1 - c] = theirs[1, rows:, :]
    gates.finish()
    outputs.finish()
    attentions.finish()


def finish(cid, n, first, tiles, whole, part, pairs, output_pairs, attention_pairs):
    bt, bty, dg, dgy = pairs
    ot, oty, gy, gyy = output_pairs
    at, aty, joined, joined_y = attention_pairs
    nz = n // 2
    rounds = int(math.log2(n))
    rows = whole.shape[0] + part.shape[0]
    output_rows = ot.shape[2]
    attention_rows = at.shape[2]
    return comm_call(
        functools.partial(finish_kernel, n, rounds, first, tiles),
        cid,
        [
            jax.ShapeDtypeStruct(whole.shape, F32),
            jax.ShapeDtypeStruct((GROUP,) + part.shape, F32),
            jax.ShapeDtypeStruct((bt.shape[2], tiles * TILE), F32),
            jax.ShapeDtypeStruct((output_rows, gy.shape[1]), F32),
            jax.ShapeDtypeStruct((attention_rows, joined.shape[1]), F32),
        ],
        [
            pltpu.VMEM((rounds + 1, rows, 128), F32),
            pltpu.VMEM((rounds + 1, rows, 128), F32),
            pltpu.VMEM((2, rows, 128), F32),
            pltpu.VMEM((2, rows, 128), F32),
            DMA((rounds + 2,)),
            DMA((rounds + 2,)),
        ]
        + gate_scratch(nz, tiles, bt)
        + Chain.scratch(nz, 1, output_rows, gy.shape[1])
        + Chain.scratch(nz, 2, attention_rows, joined.shape[1] // 2)
        + [
            pltpu.VMEM((2, nz) + ot.shape[2:], BF16),
            pltpu.VMEM((2, nz) + at.shape[2:], BF16),
            DMA((4,)),
        ],
        [VMEM] * 2 + [ANY] * 6 + [VMEM] * 2 + [ANY] * 2 + [VMEM] * 2,
        [VMEM, VMEM, ANY, ANY, ANY],
    )(whole, part, bt, bty, dg, dgy, ot, oty, gy, gyy, at, aty, joined, joined_y)


def rms_inverse(value):
    return lax.rsqrt(jnp.mean(value * value, axis=-1, keepdims=True) + EPSILON)


def norm_back(inverse, normed, upstream):
    return inverse * (upstream - normed * jnp.mean(upstream * normed, axis=-1, keepdims=True))


def rotate(value, cosine, sine):
    half = DH // 2
    first = value[..., :half]
    second = value[..., half:]
    return jnp.concatenate([first * cosine - second * sine, second * cosine + first * sine], axis=-1)


def core_swap(value):
    return lax.ppermute(value, "fsdp", [(f, f ^ 1) for f in range(GROUP)])


def lanes(value, rows):
    flat = value.reshape(-1)
    return jnp.pad(flat, (0, rows * 128 - flat.shape[0])).reshape(rows, 128)


def per_device(
    n,
    tokens,
    doc_ids,
    padding,
    token_order,
    query_code,
    key_value_code,
    output_code,
    gate_up_code,
    down_code,
    query_scale,
    key_value_scale,
    output_scale,
    gate_up_scale,
    down_scale,
    norm_gains,
    cotangent,
):
    me = lax.axis_index("fsdp")
    c = me % 2
    width = tokens.shape[2]
    part = width // GROUP
    rows = GROUP * tokens.shape[1]
    own = tokens.shape[1]

    def mine(vector):
        size = vector.shape[-1] // GROUP
        return lax.dynamic_slice_in_dim(vector, me * size, size, vector.ndim - 1)

    def blocks_to_rows(blocks):
        return jnp.concatenate([blocks[i] for i in range(GROUP)], axis=1)

    gain = 1.0 + norm_gains
    place = token_order[0].astype(F32)
    document = doc_ids[0].astype(F32)
    meta = jnp.stack([document, place, jnp.where(padding[0] == 1, document, -1.0)] + [document] * 5)

    def to_blocks(value):
        return value.reshape(own, GROUP, part).transpose(1, 0, 2)

    my_query_scale = mine(query_scale)
    my_pair_scale = mine(key_value_scale)
    token_cols = to_blocks(tokens[0])
    cot_cols = to_blocks(cotangent[0])
    rates = BASE ** (-2.0 * jnp.arange(DH // 2).astype(F32) / DH)
    (
        token_blocks, cot_blocks, own_meta, metas, pairs, query, query_raw, pair_raw, cosine, sine, first_turned
    ) = front(
        1,
        n,
        token_cols.reshape(rows, part),
        cot_cols.reshape(rows, part),
        meta,
        gain[0].reshape(GROUP, 1, part),
        rates[None],
        my_query_scale[None],
        my_pair_scale[None],
        query_code,
        key_value_code,
    )

    mixed_low, mixed, mass = attend(n, query, pairs, own_meta, metas)
    second_input, branch_own, my_middle, mixed_turned, second_turned = branch_forward(
        3,
        mixed_low,
        output_code.T,
        token_blocks,
        output_scale.reshape(GROUP, 1, part),
        gain[1].reshape(GROUP, 1, part),
        gain[2].reshape(GROUP, 1, part),
    )

    my_gate_scale = mine(gate_up_scale)
    columns = gate_up_code.shape[1]
    tiles = columns // TILE
    gate_scales = my_gate_scale.reshape(tiles, 1, TILE)
    gate_up, hidden, hidden_y, down_blocks, grad_down, down_sums, *riders = ffn_forward(
        5,
        second_input,
        gate_up_code,
        gate_scales,
        down_code.T,
        cot_blocks,
        gain[3].reshape(GROUP, 1, part),
        down_scale.reshape(GROUP, 1, part),
        [second_turned, mixed_turned, first_turned],
    )
    second_pair, mixed_pair, first_pair = zip((second_turned, mixed_turned, first_turned), riders)
    my_down = lax.dynamic_slice_in_dim(down_blocks, me * own, own, 1).astype(F32) * down_scale.reshape(GROUP, 1, part)
    down_inverse = lax.rsqrt(jnp.mean(my_down * my_down, axis=(0, 2), keepdims=True) + EPSILON)
    result = blocks_to_rows((my_middle + my_down * down_inverse * gain[3].reshape(GROUP, 1, part)).astype(BF16))
    grad_gate_up, grad_gate_up_y, gate_sums, grad_second_input, down_grad = ffn_backward(
        6, n, grad_down, down_code.T, gate_up_code, gate_scales, gate_up, hidden, hidden_y
    )
    if n == 8:
        down_grad = down_grad.reshape(-1, part)
    else:
        hidden_own = jnp.concatenate(
            [
                (jax.nn.gelu(gate_up[0, t].astype(F32)) * gate_up[1, t].astype(F32)).astype(BF16)
                for t in range(tiles)
            ],
            axis=1,
        )
        hidden_core = core_swap(hidden_own)
        hidden_rows = jnp.concatenate(
            [jnp.where(c == 0, hidden_own, hidden_core), jnp.where(c == 0, hidden_core, hidden_own)], axis=1
        )
        down_grad = lax.psum_scatter(
            contract_first(hidden_rows, grad_down), "seq", scatter_dimension=0, tiled=True
        )
    scale_down = down_sums[0]
    gain_four = down_sums[1]
    scale_gate = gate_sums[:, 0, :].reshape(columns) / my_gate_scale
    gate_pairs = second_pair + (grad_gate_up, grad_gate_up_y)
    tiles_one, tiles_two = (4, 3) if n == 8 else (0, 0)
    tiles_three = tiles - tiles_one - tiles_two
    grad_middle, branch_sums, grad_branch, grad_branch_y, grad_query, grad_pairs, gate_one = branch_back(
        7,
        n,
        tiles_one,
        grad_second_input,
        my_middle,
        branch_own,
        cot_cols,
        gain[1].reshape(GROUP, 1, part),
        gain[2].reshape(GROUP, 1, part),
        output_scale.reshape(GROUP, 1, part),
        output_code.T,
        query,
        mixed,
        mass,
        own_meta,
        metas,
        pairs,
        gate_pairs,
    )
    grad_middle = blocks_to_rows(grad_middle)
    gain_two = branch_sums[:, 0].reshape(width)
    gain_three = branch_sums[:, 1].reshape(width)
    scale_output = branch_sums[:, 2].reshape(width)
    grad_branch = grad_branch.reshape(rows, part)
    grad_branch_y = grad_branch_y.reshape(rows, part)

    if n == 8:
        joined, joined_y, grad_first_input, key_sums, gate_two = keys_back(
            9,
            n,
            tiles_one,
            tiles_two,
            grad_pairs,
            grad_query,
            query_raw,
            pair_raw,
            cosine,
            sine,
            my_query_scale[None],
            my_pair_scale[None],
            query_code,
            key_value_code,
            gate_pairs,
        )
        scale_query = key_sums[0]
        scale_pair = key_sums[1]
    else:
        is_key = me < 2
        pair_cosine = jnp.where(is_key, cosine, 1.0)
        pair_sine = jnp.where(is_key, sine, 0.0)
        grad_heads = keys_reduce(9, n, grad_pairs).astype(F32)
        grad_query_full = rotate(
            grad_query.reshape(rows, 2, DH), cosine[:, None], -sine[:, None]
        ).reshape(rows, 2 * DH)
        scale_query = jnp.sum(query_raw * grad_query_full, axis=0)
        grad_query_low = (grad_query_full * my_query_scale).astype(BF16)
        grad_pair_full = jnp.concatenate(
            [rotate(grad_heads[j], pair_cosine, -pair_sine) for j in range(2)], axis=1
        )
        scale_pair = jnp.sum(pair_raw * grad_pair_full, axis=0)
        grad_pair_low = (grad_pair_full * my_pair_scale).astype(BF16)
        joined = jnp.concatenate([grad_query_low, grad_pair_low], axis=1)
        grad_first_sum = contract_last(grad_query_low, query_code) + contract_last(grad_pair_low, key_value_code)
        grad_first_input = group_reduce(10, grad_first_sum.astype(BF16).reshape(GROUP, own, width), F32)
    my_inputs = tokens[0].astype(F32)
    my_inverse = rms_inverse(my_inputs)
    first = my_inputs * my_inverse
    gain_one = jnp.sum(grad_first_input * first, axis=0)
    grad_inputs = grad_middle + norm_back(my_inverse, first, grad_first_input * gain[0])

    wholes = lanes(jnp.concatenate([gain_one, gain_two, gain_three, scale_output]), 72)
    parts = [scale_query, scale_pair, scale_gate, scale_down, gain_four]
    part_rows = lanes(jnp.concatenate(parts), 56)
    if n == 8:
        whole_total, part_total, gate_three, output_grad, attention_grad = finish(
            11,
            n,
            tiles_one + tiles_two,
            tiles_three,
            wholes,
            part_rows,
            gate_pairs,
            mixed_pair + (grad_branch, grad_branch_y),
            first_pair + (joined, joined_y),
        )
        gate_grad = jnp.concatenate([gate_one, gate_two, gate_three], axis=1)
    else:
        whole_total, part_total = totals(11, n, wholes, part_rows)

        def weight_sum(left, right):
            return lax.psum_scatter(dot(left.reshape(-1, rows), right), "seq", scatter_dimension=0, tiled=True)

        gate_grad = weight_sum(second_turned, grad_gate_up)
        output_grad = weight_sum(mixed_turned, grad_branch)
        attention_grad = weight_sum(first_turned, joined)
    whole_total = whole_total.reshape(-1)
    part_total = part_total.reshape(GROUP, -1)
    pieces = []
    start = 0
    for vector in parts:
        pieces.append(part_total[:, start : start + vector.shape[0]].reshape(-1))
        start += vector.shape[0]
    q_width = query_code.shape[1]
    return (
        result[None],
        grad_inputs[None],
        attention_grad[:, :q_width],
        attention_grad[:, q_width:],
        output_grad,
        gate_grad,
        down_grad,
        pieces[0],
        pieces[1],
        whole_total[3 * width :],
        pieces[2],
        pieces[3],
        jnp.concatenate([whole_total[: 3 * width], pieces[4]]).reshape(4, width),
    )


def solution(mesh):
    return jax.shard_map(
        functools.partial(per_device, mesh.shape["seq"]),
        mesh=mesh,
        in_specs=(
            P("fsdp", "seq", None),
            P("fsdp", "seq"),
            P("fsdp", "seq"),
            P("fsdp", "seq"),
            P(None, "fsdp"),
            P(None, "fsdp"),
            P(None, "fsdp"),
            P(None, "fsdp"),
            P(None, "fsdp"),
            P(),
            P(),
            P(),
            P(),
            P(),
            P(),
            P("fsdp", "seq", None),
        ),
        out_specs=(
            P("fsdp", "seq", None),
            P("fsdp", "seq", None),
            P("seq", "fsdp"),
            P("seq", "fsdp"),
            P("seq", "fsdp"),
            P("seq", "fsdp"),
            P("seq", "fsdp"),
            P(),
            P(),
            P(),
            P(),
            P(),
            P(),
        ),
        check_vma=False,
    )
```

```python
import functools
import math

import jax
import jax.numpy as jnp
from jax import lax
from jax.experimental import pallas as pl
from jax.experimental.pallas import tpu as pltpu
from jax.sharding import PartitionSpec as P

HQ = 8
HK = 4
DH = 256
FF = 9216
GROUP = 4
TILE = 384
EPSILON = 1e-06
CAP = 50.0
BASE = 10000.0
VMEM_LIMIT = 60 * 1024 * 1024
MESH = pl.DeviceIdType.MESH
ANY = pl.BlockSpec(memory_space=pl.ANY)
VMEM = pl.BlockSpec(memory_space=pltpu.VMEM)
DMA = pltpu.SemaphoreType.DMA
F32 = jnp.float32
BF16 = jnp.bfloat16


def dot(left, right):
    return jnp.dot(left, right, preferred_element_type=F32)


def contract_last(left, right):
    return lax.dot_general(left, right, (((1,), (1,)), ((), ())), preferred_element_type=F32)


def contract_first(left, right):
    return lax.dot_general(left, right, (((0,), (0,)), ((), ())), preferred_element_type=F32)


def place_now():
    seq = lax.axis_index("seq")
    fsdp = lax.axis_index("fsdp")
    return seq, fsdp, fsdp // 2, fsdp % 2


def greet(peers):
    barrier = pltpu.get_barrier_semaphore()
    for peer in peers:
        pl.semaphore_signal(barrier, inc=1, device_id=peer, device_id_type=MESH)
    pl.semaphore_wait(barrier, len(peers))


def remote(src, dst, send, recv, peer):
    return pltpu.make_async_remote_copy(
        src_ref=src, dst_ref=dst, send_sem=send, recv_sem=recv, device_id=peer, device_id_type=MESH
    )


def comm_call(kernel, cid, out_shape, scratch, in_specs, out_specs):
    return pl.pallas_call(
        kernel,
        out_shape=out_shape,
        in_specs=in_specs,
        out_specs=out_specs,
        scratch_shapes=scratch,
        compiler_params=pltpu.CompilerParams(
            collective_id=cid, has_side_effects=True, vmem_limit_bytes=VMEM_LIMIT
        ),
    )


def group_reduce_kernel(parts, src, out, from_core, to_x, from_x, cs, cr, xs, xr):
    seq, me, x, c = place_now()
    across = (seq, (1 - x) * 2 + c)
    beside = (seq, x * 2 + 1 - c)
    greet([across, beside])
    rows = src.shape[1]
    step = rows // parts
    order = [1 - x, x]
    cores = []
    for i in range(2):
        for k in range(parts):
            span = pl.ds(k * step, step)
            copy = remote(
                src.at[order[i] * 2 + 1 - c, span], from_core.at[i, span], cs.at[i, k], cr.at[i, k], beside
            )
            copy.start()
            cores.append(copy)
    sends = []
    for k in range(parts):
        span = pl.ds(k * step, step)
        cores[k].wait_recv()
        to_x[span, :] = (
            src[order[0] * 2 + c, span, :].astype(F32) + from_core[0, span, :].astype(F32)
        ).astype(BF16)
        copy = remote(to_x.at[span], from_x.at[span], xs.at[k], xr.at[k], across)
        copy.start()
        sends.append(copy)
    for k in range(parts):
        span = pl.ds(k * step, step)
        cores[parts + k].wait_recv()
        sends[k].wait_recv()
        out[span, :] = (
            src[order[1] * 2 + c, span, :].astype(F32)
            + from_core[1, span, :].astype(F32)
            + from_x[span, :].astype(F32)
        ).astype(out.dtype)
    for copy in cores + sends:
        copy.wait_send()


def group_reduce(cid, value, dtype, parts=4):
    rows, width = value.shape[1:]
    return comm_call(
        functools.partial(group_reduce_kernel, parts),
        cid,
        jax.ShapeDtypeStruct((rows, width), dtype),
        [pltpu.VMEM((2, rows, width), BF16), pltpu.VMEM((rows, width), BF16), pltpu.VMEM((rows, width), BF16),
         DMA((2, parts)), DMA((2, parts)), DMA((parts,)), DMA((parts,))],
        [VMEM],
        VMEM,
    )(value)


def keys_reduce_kernel(n, src, out, y_got, r_got, l_got, r_out, l_out, moved, ys, yr, rs, rr, ls, lr, hs, hr, local):
    seq, me, x, c = place_now()
    y = seq % 2
    z = seq // 2
    nz = n // 2
    right = (seq + 2, me)
    left = (seq - 2, me)
    beyond = (z * 2 + 1 - y, me)
    barrier = pltpu.get_barrier_semaphore()
    for d in range(1, GROUP):
        pl.semaphore_signal(barrier, inc=1, device_id=(seq, lax.rem(me + d, GROUP)), device_id_type=MESH)
    pl.semaphore_signal(barrier, inc=1, device_id=beyond, device_id_type=MESH)

    @pl.when(z > 0)
    def _():
        pl.semaphore_signal(barrier, inc=1, device_id=left, device_id_type=MESH)

    @pl.when(z < nz - 1)
    def _():
        pl.semaphore_signal(barrier, inc=1, device_id=right, device_id_type=MESH)

    chain = jnp.where(z > 0, 1, 0) + jnp.where(z < nz - 1, 1, 0)
    pl.semaphore_wait(barrier, GROUP + chain)

    def swap(k):
        return remote(src.at[k * 2 + 1 - y], y_got.at[k], ys.at[k], yr.at[k], beyond)

    for t in range(1, nz):
        go_right = z + nz - t
        go_left = z - nz + t

        @pl.when(go_right < nz)
        def _():
            swap(go_right).start()

        @pl.when(go_left >= 0)
        def _():
            swap(go_left).start()

    swap(z).start()

    def pair_sum(k, more, to):
        def body(i, carry):
            half = i // 2
            span = pl.ds(pl.multiple_of((i % 2) * 256, 256), 256)
            total = src[k * 2 + y, half, span, :].astype(F32) + y_got[k, half, span, :].astype(F32)
            for ref in more:
                total = total + ref[half, span, :].astype(F32)
            to[half, span, :] = total.astype(BF16)
            return carry

        lax.fori_loop(0, 4, body, 0)

    for t in range(1, nz):
        go_right = z + nz - t
        go_left = z - nz + t

        @pl.when(go_right < nz)
        def _():
            swap(go_right).wait_recv()
            if t == 1:
                pair_sum(go_right, [], r_out.at[t - 1])
            else:

                @pl.when(z > 0)
                def _():
                    remote(r_out.at[t - 1], r_got.at[t - 2], rs.at[t - 2], rr.at[t - 2], left).wait_recv()
                    pair_sum(go_right, [r_got.at[t - 2]], r_out.at[t - 1])

                @pl.when(z == 0)
                def _():
                    pair_sum(go_right, [], r_out.at[t - 1])

            remote(r_out.at[t - 1], r_got.at[t - 1], rs.at[t - 1], rr.at[t - 1], right).start()

        @pl.when(go_left >= 0)
        def _():
            swap(go_left).wait_recv()
            if t == 1:
                pair_sum(go_left, [], l_out.at[t - 1])
            else:

                @pl.when(z < nz - 1)
                def _():
                    remote(l_out.at[t - 1], l_got.at[t - 2], ls.at[t - 2], lr.at[t - 2], right).wait_recv()
                    pair_sum(go_left, [l_got.at[t - 2]], l_out.at[t - 1])

                @pl.when(z == nz - 1)
                def _():
                    pair_sum(go_left, [], l_out.at[t - 1])

            remote(l_out.at[t - 1], l_got.at[t - 1], ls.at[t - 1], lr.at[t - 1], left).start()

    swap(z).wait_recv()
    last = nz - 2

    def got_left():
        remote(r_out.at[last], r_got.at[last], rs.at[last], rr.at[last], left).wait_recv()

    def got_right():
        remote(l_out.at[last], l_got.at[last], ls.at[last], lr.at[last], right).wait_recv()

    @pl.when(z == 0)
    def _():
        got_right()
        pair_sum(z, [l_got.at[last]], moved)

    @pl.when(z == nz - 1)
    def _():
        got_left()
        pair_sum(z, [r_got.at[last]], moved)

    @pl.when((z > 0) & (z < nz - 1))
    def _():
        got_left()
        got_right()
        pair_sum(z, [r_got.at[last], l_got.at[last]], moved)

    for t in range(2):
        target = t * 2 + x

        @pl.when(target == me)
        def _():
            pltpu.make_async_copy(moved.at[t], out.at[c], local).start()

        @pl.when(target != me)
        def _():
            remote(moved.at[t], out.at[c], hs.at[t], hr.at[c], (seq, target)).start()

    for j in range(2):
        source = c * 2 + j

        @pl.when(source == me)
        def _():
            pltpu.make_async_copy(moved.at[0], out.at[j], local).wait()

        @pl.when(source != me)
        def _():
            remote(moved.at[0], out.at[j], hs.at[0], hr.at[j], (seq, source)).wait_recv()

    for t in range(2):

        @pl.when(t * 2 + x != me)
        def _():
            remote(moved.at[t], out.at[c], hs.at[t], hr.at[c], (seq, t * 2 + x)).wait_send()

    for k in range(nz):
        swap(k).wait_send()
    for t in range(1, nz):

        @pl.when(z + nz - t < nz)
        def _():
            remote(r_out.at[t - 1], r_got.at[t - 1], rs.at[t - 1], rr.at[t - 1], right).wait_send()

        @pl.when(z - nz + t >= 0)
        def _():
            remote(l_out.at[t - 1], l_got.at[t - 1], ls.at[t - 1], lr.at[t - 1], left).wait_send()


def keys_reduce(cid, n, value):
    nz = n // 2
    shape = value.shape[1:]
    chain = pltpu.VMEM((nz - 1,) + shape, BF16)
    return comm_call(
        functools.partial(keys_reduce_kernel, n),
        cid,
        jax.ShapeDtypeStruct(shape, BF16),
        [pltpu.VMEM((nz,) + shape, BF16), chain, chain, chain, chain, pltpu.VMEM(shape, BF16),
         DMA((nz,)), DMA((nz,)), DMA((nz - 1,)), DMA((nz - 1,)), DMA((nz - 1,)), DMA((nz - 1,)),
         DMA((2,)), DMA((2,)), DMA],
        [VMEM],
        VMEM,
    )(value)


def total_kernel(rounds, whole, part, whole_out, part_out, bufs, gots, mine, theirs, ss, rs):
    seq, me, x, c = place_now()
    across = (seq, (1 - x) * 2 + c)
    beside = (seq, x * 2 + 1 - c)
    partners = []
    for r in range(rounds):
        bit = 1 << r
        partners.append((seq + bit - 2 * bit * ((seq // bit) % 2), me))
    greet(partners + [across, beside])
    rows = whole.shape[0]
    bufs[0, :rows, :] = whole[...]
    bufs[0, rows:, :] = part[...]
    for r in range(rounds + 1):
        partner = partners[r] if r < rounds else across
        copy = remote(bufs.at[r], gots.at[r], ss.at[r], rs.at[r], partner)
        copy.start()
        copy.wait()
        if r < rounds:
            bufs[r + 1] = bufs[r] + gots[r]
    mine[0, :rows, :] = bufs[rounds, :rows, :] + gots[rounds, :rows, :]
    mine[0, rows:, :] = bufs[rounds, rows:, :]
    mine[1, rows:, :] = gots[rounds, rows:, :]
    mine[1, :rows, :] = jnp.zeros_like(whole)
    copy = remote(mine, theirs, ss.at[rounds + 1], rs.at[rounds + 1], beside)
    copy.start()
    copy.wait()
    whole_out[...] = mine[0, :rows, :] + theirs[0, :rows, :]
    part_out[x * 2 + c] = mine[0, rows:, :]
    part_out[(1 - x) * 2 + c] = mine[1, rows:, :]
    part_out[x * 2 + 1 - c] = theirs[0, rows:, :]
    part_out[(1 - x) * 2 + 1 - c] = theirs[1, rows:, :]


def totals(cid, n, whole, part):
    rounds = int(math.log2(n))
    rows = whole.shape[0] + part.shape[0]
    return comm_call(
        functools.partial(total_kernel, rounds),
        cid,
        [jax.ShapeDtypeStruct(whole.shape, F32), jax.ShapeDtypeStruct((GROUP,) + part.shape, F32)],
        [pltpu.VMEM((rounds + 1, rows, 128), F32), pltpu.VMEM((rounds + 1, rows, 128), F32),
         pltpu.VMEM((2, rows, 128), F32), pltpu.VMEM((2, rows, 128), F32),
         DMA((rounds + 2,)), DMA((rounds + 2,))],
        [VMEM, VMEM],
        [VMEM, VMEM],
    )(whole, part)


def turned(block, unit, to):
    half = to.shape[1]
    flat = contract_last(unit[...], block)
    to[0] = flat[:half].astype(BF16)
    to[1] = flat[half:].astype(BF16)


def fill_unit(unit):
    shape = unit.shape
    unit[...] = jnp.where(
        lax.broadcasted_iota(jnp.int32, shape, 0) == lax.broadcasted_iota(jnp.int32, shape, 1), 1.0, 0.0
    ).astype(BF16)


def front_kernel(n, *refs):
    tok, cot, meta, g1, rates, q_scale, p_scale, wq, wkv = refs[:9]
    toks, cots, own_meta, metas, out, q, q_raw, p_raw, cosine, sine, turned_o = refs[9:20]
    (tb, ab, wqs, wkvs, heads, om, unit, at,
     ws, txs, txr, tcs, tcr, tfs, tfr, gms, gmr, own_sem, hs, hr, ms, mr, rs, rr, ls, lr, ys, yr,
     xs, xr, cs, cr, fs, fr, os) = refs[20:]
    seq, me, x, c = place_now()
    y = seq % 2
    z = seq // 2
    nz = n // 2
    across = (seq, (1 - x) * 2 + c)
    beside = (seq, x * 2 + 1 - c)
    group = [(seq, lax.rem(me + d, GROUP)) for d in range(1, GROUP)]
    load_q = pltpu.make_async_copy(wq, wqs, ws.at[0])
    load_kv = pltpu.make_async_copy(wkv, wkvs, ws.at[1])
    load_q.start()
    load_kv.start()
    greet(group + [(lax.rem(seq + d, n), me) for d in range(1, n)])
    blk = tok.shape[0] // GROUP
    part = tok.shape[1]
    own = blk

    sends = []
    for k in range(GROUP):
        rows = pl.ds(k * blk, blk)
        copy = remote(tok.at[rows], tb.at[me, rows], txs.at[k], txr.at[k], across)
        copy.start()
        sends.append(copy)
    to_core = remote(tok, tb.at[me], tcs, tcr, beside)
    to_core.start()
    group_meta = []
    for d in range(1, GROUP):
        copy = remote(meta, om.at[me], gms.at[d - 1], gmr.at[d - 1], group[d - 1])
        copy.start()
        group_meta.append(copy)
    own_tok = pltpu.make_async_copy(tok, tb.at[me], own_sem.at[0])
    own_tok.start()
    own_row = pltpu.make_async_copy(meta, om.at[me], own_sem.at[1])
    own_row.start()
    fill_unit(unit)
    for copy in group_meta:
        copy.wait()
    own_row.wait()
    width = GROUP * part
    half = DH // 2
    js = range(GROUP)
    is_key = jnp.where(x == 0, 1.0, 0.0).astype(F32)

    def process(p):
        def norm(i, carry):
            span = lambda j: pl.ds(pl.multiple_of(j * blk + i * 32, 32), 32)
            values = [tb[p, span(j), :].astype(F32) for j in js]
            total = values[0] * values[0]
            for value in values[1:]:
                total = total + value * value
            inverse = lax.rsqrt(jnp.sum(total, axis=1, keepdims=True) * (1.0 / width) + EPSILON)
            to = pl.ds(pl.multiple_of(p * own + i * 32, 32), 32)
            for j in js:
                ab[j, to, :] = (values[j] * inverse * g1[j]).astype(BF16)
            return carry

        lax.fori_loop(0, blk // 32, norm, 0)
        rows = pl.ds(pl.multiple_of(p * own, 128), own)
        turn = jnp.broadcast_to(om[p, 1:2, :], (128, 128)).T * rates[...]
        cos = jnp.cos(turn)
        sin = jnp.sin(turn)
        cosine[rows, :] = cos
        sine[rows, :] = sin

        def product(weights):
            total = dot(ab[0, rows, :], weights[0:part, :])
            for j in range(1, GROUP):
                total = total + dot(ab[j, rows, :], weights[j * part : (j + 1) * part, :])
            return total

        plain = product(wqs)
        q_raw[rows, :] = plain
        plain = plain * q_scale[...]
        for h in range(2):
            one = plain[:, h * DH : h * DH + half]
            two = plain[:, h * DH + half : (h + 1) * DH]
            q[rows, h * DH : h * DH + half] = (one * cos - two * sin).astype(BF16)
            q[rows, h * DH + half : (h + 1) * DH] = (two * cos + one * sin).astype(BF16)
        cos = is_key * cos + (1.0 - is_key)
        sin = is_key * sin
        plain = product(wkvs)
        p_raw[rows, :] = plain
        plain = plain * p_scale[...]
        for h in range(2):
            one = plain[:, h * DH : h * DH + half]
            two = plain[:, h * DH + half : (h + 1) * DH]
            heads[h, rows, :half] = (one * cos - two * sin).astype(BF16)
            heads[h, rows, half:] = (two * cos + one * sin).astype(BF16)

    own_tok.wait()
    load_q.wait()
    load_kv.wait()
    process(me)
    to_core.wait_recv()
    process(x * 2 + 1 - c)
    forwards = []
    for k in range(GROUP):
        sends[k].wait_recv()
        got = tb.at[(1 - x) * 2 + c, pl.ds(k * blk, blk)]
        forward = remote(got, got, tfs.at[k], tfr.at[k], beside)
        forward.start()
        forwards.append(forward)
    process((1 - x) * 2 + c)
    for forward in forwards:
        forward.wait_recv()
    process((1 - x) * 2 + 1 - c)

    for j in range(2):
        target = c * 2 + j

        @pl.when(target == me)
        def _():
            pltpu.make_async_copy(heads.at[j], out.at[seq, x], own_sem.at[0]).start()

        @pl.when(target != me)
        def _():
            remote(heads.at[j], out.at[seq, x], hs.at[j], hr.at[x], (seq, target)).start()

    small = []
    for d in range(1, n):
        copy = remote(om, metas.at[seq], ms.at[d - 1], mr.at[d - 1], (lax.rem(seq + d, n), me))
        copy.start()
        small.append(copy)
    outs = [
        pltpu.make_async_copy(om, metas.at[seq], os.at[0]),
        pltpu.make_async_copy(om, own_meta, os.at[1]),
        pltpu.make_async_copy(tb, toks, os.at[2]),
    ]
    for copy in outs:
        copy.start()
    for t in range(2):
        source = t * 2 + x

        @pl.when(source == me)
        def _():
            pltpu.make_async_copy(heads.at[0], out.at[seq, t], own_sem.at[0]).wait()

        @pl.when(source != me)
        def _():
            remote(heads.at[0], out.at[seq, t], hs.at[0], hr.at[t], (seq, source)).wait_recv()

    def block(owner_z, owner_y):
        return out.at[owner_z * 2 + owner_y]

    right = (seq + 2, me)
    left = (seq - 2, me)
    beyond = (z * 2 + 1 - y, me)

    def to_y(owner_z):
        remote(block(owner_z, y), block(owner_z, y), ys.at[owner_z], yr.at[owner_z], beyond).start()

    parts = 2
    step = cot.shape[0] // parts
    for t in range(1, nz + 1):
        go_right = z - t + 1
        go_left = z + t - 1
        if t > 1:

            @pl.when(go_right >= 0)
            def _():
                remote(block(go_right, y), block(go_right, y), rs.at[t - 1], rr.at[t - 1], left).wait_recv()

            @pl.when(go_left < nz)
            def _():
                remote(block(go_left, y), block(go_left, y), ls.at[t - 1], lr.at[t - 1], right).wait_recv()

        if t < nz:

            @pl.when((go_right >= 0) & (z < nz - 1))
            def _():
                remote(block(go_right, y), block(go_right, y), rs.at[t], rr.at[t], right).start()

            @pl.when((go_left < nz) & (z > 0))
            def _():
                remote(block(go_left, y), block(go_left, y), ls.at[t], lr.at[t], left).start()

        @pl.when(go_right >= 0)
        def _():
            to_y(go_right)

        if t > 1:

            @pl.when(go_left < nz)
            def _():
                to_y(go_left)

        if t == 1:
            xcopies = []
            for k in range(parts):
                rows = pl.ds(k * step, step)
                copy = remote(cot.at[rows], cots.at[me, rows], xs.at[k], xr.at[k], across)
                copy.start()
                xcopies.append(copy)
            ccopy = remote(cot, cots.at[me], cs, cr, beside)
            ccopy.start()
            own_cot = pltpu.make_async_copy(cot, cots.at[me], os.at[3])
            own_cot.start()
            for j in js:
                turned(ab[j], unit, at.at[j])
            turned_out = pltpu.make_async_copy(at, turned_o, os.at[4])
            turned_out.start()
    later = []
    for k in range(parts):
        rows = pl.ds(k * step, step)
        xcopies[k].wait()
        got = cots.at[(1 - x) * 2 + c, rows]
        forward = remote(got, got, fs.at[k], fr.at[k], beside)
        forward.start()
        later.append(forward)
    for k in range(nz):
        remote(block(k, 1 - y), block(k, 1 - y), ys.at[k], yr.at[k], beyond).wait()
    for t in range(1, nz):

        @pl.when((z - t + 1 >= 0) & (z < nz - 1))
        def _():
            remote(block(z, y), block(z, y), rs.at[t], rr.at[t], right).wait_send()

        @pl.when((z + t - 1 < nz) & (z > 0))
        def _():
            remote(block(z, y), block(z, y), ls.at[t], lr.at[t], left).wait_send()

    for j in range(2):

        @pl.when(c * 2 + j != me)
        def _():
            remote(heads.at[j], out.at[seq, x], hs.at[j], hr.at[x], (seq, c * 2 + j)).wait_send()

    for copy in small + later + [ccopy]:
        copy.wait()
    for copy in sends + forwards + [to_core]:
        copy.wait_send()
    for copy in outs + [own_cot, turned_out]:
        copy.wait()


def front(cid, n, tok, cot, meta, g1, rates, q_scale, p_scale, wq, wkv):
    nz = n // 2
    rows, part = tok.shape
    own = rows // GROUP
    deep, wide = wq.shape
    blocks = jax.ShapeDtypeStruct((GROUP, rows, part), BF16)
    table = jax.ShapeDtypeStruct((rows, DH // 2), F32)
    raw = jax.ShapeDtypeStruct((rows, wide), F32)
    turned_shape = (GROUP, 2, part // 2, rows)
    return comm_call(
        functools.partial(front_kernel, n),
        cid,
        [
            blocks,
            blocks,
            jax.ShapeDtypeStruct((GROUP,) + meta.shape, F32),
            jax.ShapeDtypeStruct((n, GROUP) + meta.shape, F32),
            jax.ShapeDtypeStruct((n, 2, rows, DH), BF16),
            jax.ShapeDtypeStruct((rows, wide), BF16),
            raw,
            raw,
            table,
            table,
            jax.ShapeDtypeStruct(turned_shape, BF16),
        ],
        [
            pltpu.VMEM((GROUP, rows, part), BF16),
            pltpu.VMEM((GROUP, rows, part), BF16),
            pltpu.VMEM((deep, wide), BF16),
            pltpu.VMEM((deep, wide), BF16),
            pltpu.VMEM((2, rows, DH), BF16),
            pltpu.VMEM((GROUP,) + meta.shape, F32),
            pltpu.VMEM((part, part), BF16),
            pltpu.VMEM(turned_shape, BF16),
            DMA((2,)), DMA((GROUP,)), DMA((GROUP,)), DMA, DMA, DMA((GROUP,)), DMA((GROUP,)), DMA((GROUP - 1,)),
            DMA((GROUP - 1,)), DMA((2,)), DMA((2,)), DMA((2,)), DMA((n - 1,)), DMA((n - 1,)), DMA((nz,)), DMA((nz,)),
            DMA((nz,)), DMA((nz,)), DMA((nz,)), DMA((nz,)), DMA((2,)), DMA((2,)), DMA, DMA, DMA((2,)), DMA((2,)),
            DMA((5,)),
        ],
        [VMEM, ANY, VMEM, VMEM, VMEM, VMEM, VMEM, ANY, ANY],
        [ANY, ANY, ANY, ANY, ANY, VMEM, VMEM, VMEM, VMEM, VMEM, ANY],
    )(tok, cot, meta, g1, rates, q_scale, p_scale, wq, wkv)


def branch_kernel(low, wo, toks, scale, g2, g3, b_o, raw_o, mid_o, ot_o, bt_o, ob, pb, bb, acc, unit, bt,
                  xs, xr, cs, cr, fs, fr, gxs, gxr, gcs, gcr, gfs, gfr, local, os, hos):
    seq, me, x, c = place_now()
    across = (seq, (1 - x) * 2 + c)
    beside = (seq, x * 2 + 1 - c)
    greet([across, beside])
    rows, heads = low.shape
    part = pb.shape[2]
    parts = 4
    size = rows // parts
    own = rows // GROUP
    js = range(GROUP)

    def spot(owner, k):
        return ob.at[pl.ds(k * size, size), pl.ds(pl.multiple_of(owner * heads, 128), heads)]

    sends = []
    for k in range(parts):
        copy = remote(low.at[pl.ds(k * size, size)], spot(me, k), xs.at[k], xr.at[k], across)
        copy.start()
        sends.append(copy)
    mine = ob.at[:, pl.ds(pl.multiple_of(me * heads, 128), heads)]
    to_core = remote(low, mine, cs, cr, beside)
    to_core.start()
    own_copy = pltpu.make_async_copy(low, mine, local)
    own_copy.start()
    fill_unit(unit)

    def add(owner, start):
        cols = pl.ds(pl.multiple_of(owner * heads, 128), heads)
        more = contract_last(ob[:, cols], wo[:, cols])
        acc[...] = more if start else acc[...] + more

    own_copy.wait()
    add(me, True)
    to_core.wait_recv()
    add(x * 2 + 1 - c, False)
    forwards = []
    for k in range(parts):
        sends[k].wait_recv()
        got = spot((1 - x) * 2 + c, k)
        forward = remote(got, got, fs.at[k], fr.at[k], beside)
        forward.start()
        forwards.append(forward)
    add((1 - x) * 2 + c, False)
    for forward in forwards:
        forward.wait_recv()
    add((1 - x) * 2 + 1 - c, False)

    over = []
    core = []
    for k in range(parts):
        span = pl.ds(k * size, size)
        pb[me, span, :] = acc[span, :].astype(BF16)
        piece = pb.at[me, span]
        copy = remote(piece, piece, gxs.at[k], gxr.at[k], across)
        copy.start()
        over.append(copy)
        copy = remote(piece, piece, gcs.at[k], gcr.at[k], beside)
        copy.start()
        core.append(copy)
    head_outs = []
    for j in js:
        for i in range(2):
            cols = pl.ds(j * heads + i * (heads // 2), heads // 2)
            copy = pltpu.make_async_copy(ob.at[:, cols], ot_o.at[j, i], hos.at[j, i])
            copy.start()
            head_outs.append(copy)
    passed = []
    for k in range(parts):
        over[k].wait_recv()
        got = pb.at[(1 - x) * 2 + c, pl.ds(k * size, size)]
        forward = remote(got, got, gfs.at[k], gfr.at[k], beside)
        forward.start()
        passed.append(forward)
    for copy in core + passed:
        copy.wait_recv()
    mean = 1.0 / (GROUP * part)

    def rowsum(values):
        total = values[0] * values[0]
        for value in values[1:]:
            total = total + value * value
        return jnp.sum(total, axis=1, keepdims=True) * mean

    def norms(i, carry):
        pack = i // (own // 16)
        inner = i % (own // 16) * 16
        span = pl.ds(pl.multiple_of(i * 16, 16), 16)
        branch = [pb[j, span, :].astype(F32) * scale[j] for j in js]
        inverse = lax.rsqrt(rowsum(branch) + EPSILON)
        middle = [
            toks[pack, pl.ds(pl.multiple_of(j * own + inner, 16), 16), :].astype(F32) + branch[j] * inverse * g2[j]
            for j in js
        ]
        inverse = lax.rsqrt(rowsum(middle) + EPSILON)
        for j in js:
            bb[j, span, :] = (middle[j] * inverse * g3[j]).astype(BF16)

        @pl.when(pack == me)
        def _():
            for j in js:
                mid_o[j, pl.ds(pl.multiple_of(inner, 16), 16), :] = middle[j]

        return carry

    lax.fori_loop(0, rows // 16, norms, 0)
    b_out = pltpu.make_async_copy(bb, b_o, os.at[1])
    b_out.start()
    raw_out = pltpu.make_async_copy(pb.at[:, pl.ds(pl.multiple_of(me * own, 128), own)], raw_o, os.at[2])
    raw_out.start()
    for j in js:
        turned(bb[j], unit, bt.at[j])
    bt_out = pltpu.make_async_copy(bt, bt_o, os.at[3])
    bt_out.start()
    for copy in sends + forwards + over + core + passed + [to_core]:
        copy.wait_send()
    for copy in head_outs + [b_out, raw_out, bt_out]:
        copy.wait()


def branch_forward(cid, low, wo, toks, scale, g2, g3):
    rows, heads = low.shape
    part = wo.shape[0]
    own = rows // GROUP
    turned_b = (GROUP, 2, part // 2, rows)
    slices = (GROUP, 2, rows, heads // 2)
    four = DMA((4,))
    return comm_call(
        branch_kernel,
        cid,
        [
            jax.ShapeDtypeStruct((GROUP, rows, part), BF16),
            jax.ShapeDtypeStruct((GROUP, own, part), BF16),
            jax.ShapeDtypeStruct((GROUP, own, part), F32),
            jax.ShapeDtypeStruct(slices, BF16),
            jax.ShapeDtypeStruct(turned_b, BF16),
        ],
        [
            pltpu.VMEM((rows, GROUP * heads), BF16),
            pltpu.VMEM((GROUP, rows, part), BF16),
            pltpu.VMEM((GROUP, rows, part), BF16),
            pltpu.VMEM((rows, part), F32),
            pltpu.VMEM((part, part), BF16),
            pltpu.VMEM(turned_b, BF16),
            four, four, DMA, DMA, four, four, four, four, four, four, four, four, DMA, four, DMA((GROUP, 2)),
        ],
        [VMEM] * 6,
        [ANY, ANY, VMEM, ANY, ANY],
    )(low, wo, toks, scale, g2, g3)


def masks(n, own_ref, meta_ref):
    def column(row):
        return jnp.broadcast_to(own_ref[0, row : row + 1, :], (128, 128)).T

    row_document = column(0)
    row_place = column(1)
    out = []
    for j in range(n):
        key_place = meta_ref[j, 0, 1:2, :]
        key_document = meta_ref[j, 0, 2:3, :]
        allowed = (row_document == key_document) & (key_place <= row_place) | (key_place == row_place)
        out.append(allowed)
    return out


def attend_kernel(n, q_ref, kv_ref, own_ref, meta_ref, low_ref, mixed_ref, total_ref):
    keys = kv_ref[:, 0].reshape(n * 128, DH)
    values = kv_ref[:, 1].reshape(n * 128, DH)
    allowed = masks(n, own_ref, meta_ref)
    for h in range(2):
        cols = slice(h * DH, (h + 1) * DH)
        raw = contract_last(q_ref[:, cols], keys)
        pieces = []
        total = jnp.zeros((128, 128), F32)
        for j in range(n):
            squash = jnp.tanh(raw[:, j * 128 : (j + 1) * 128] * (DH ** (-0.5) / CAP))
            mass = jnp.where(allowed[j], jnp.exp(CAP * squash), 0.0)
            total = total + mass
            pieces.append(mass.astype(BF16))
        row = jnp.sum(total, axis=1, keepdims=True)
        mixed = dot(jnp.concatenate(pieces, axis=1), values) / row
        mixed_ref[:, cols] = mixed
        low_ref[:, cols] = mixed.astype(BF16)
        total_ref[:, h * 128 : (h + 1) * 128] = jnp.broadcast_to(row, (128, 128))


def attend(n, query, pairs, own_meta, metas):
    return pl.pallas_call(
        functools.partial(attend_kernel, n),
        grid=(GROUP,),
        out_shape=[
            jax.ShapeDtypeStruct(query.shape, BF16),
            jax.ShapeDtypeStruct(query.shape, F32),
            jax.ShapeDtypeStruct((query.shape[0], 256), F32),
        ],
        in_specs=[
            pl.BlockSpec((128, 2 * DH), lambda p: (p, 0)),
            pl.BlockSpec((n, 2, 128, DH), lambda p: (0, 0, p, 0)),
            pl.BlockSpec((1, 8, 128), lambda p: (p, 0, 0)),
            pl.BlockSpec((n, 1, 8, 128), lambda p: (0, p, 0, 0)),
        ],
        out_specs=[
            pl.BlockSpec((128, 2 * DH), lambda p: (p, 0)),
            pl.BlockSpec((128, 2 * DH), lambda p: (p, 0)),
            pl.BlockSpec((128, 256), lambda p: (p, 0)),
        ],
        compiler_params=pltpu.CompilerParams(vmem_limit_bytes=VMEM_LIMIT),
    )(query, pairs, own_meta, metas)


def back_pack(n, keys, values, allowed, q_ref, grad_ref, mixed_ref, total_ref, dq_ref, dkv_ref):
    grad_keys = None
    for h in range(2):
        cols = slice(h * DH, (h + 1) * DH)
        query = q_ref[:, cols]
        grad = grad_ref[:, cols]
        delta = jnp.sum(grad.astype(F32) * mixed_ref[:, cols], axis=1, keepdims=True)
        inverse = 1.0 / total_ref[:, h * 128 : (h + 1) * 128]
        raw = contract_last(query, keys)
        grad_share = contract_last(grad, values)
        shares = []
        grads = []
        for j in range(n):
            span = slice(j * 128, (j + 1) * 128)
            squash = jnp.tanh(raw[:, span] * (DH ** (-0.5) / CAP))
            share = jnp.where(allowed[j], jnp.exp(CAP * squash), 0.0) * inverse
            shares.append(share.astype(BF16))
            grads.append(
                (share * (grad_share[:, span] - delta) * ((1.0 - squash * squash) * DH ** (-0.5))).astype(BF16)
            )
        share = jnp.concatenate(shares, axis=1)
        grad_raw = jnp.concatenate(grads, axis=1)
        dq_ref[:, cols] = dot(grad_raw, keys)
        new_keys = contract_first(grad_raw, query)
        new_values = contract_first(share, grad)
        if grad_keys is None:
            grad_keys, grad_values = new_keys, new_values
        else:
            grad_keys, grad_values = grad_keys + new_keys, grad_values + new_values
    dkv_ref[:, 0] = grad_keys.astype(BF16).reshape(n, 128, DH)
    dkv_ref[:, 1] = grad_values.astype(BF16).reshape(n, 128, DH)


class Chain:
    def __init__(self, nz, count, seq, me, partial, keep, landing, scratch):
        self.nz, self.count, self.partial, self.keep = nz, count, partial, keep
        self.z = seq // 2
        self.right, self.left = (seq + 2, me), (seq - 2, me)
        self.got_r, self.got_l = landing
        (self.out_r, self.out_l, self.in_r, self.in_l, self.stage, self.ss_r, self.sr_r, self.ss_l, self.sr_l,
         self.keep_sem, self.load_sem) = scratch

    @staticmethod
    def landing(nz, count, rows, width):
        return [jax.ShapeDtypeStruct((count, nz - 1, rows, width), BF16)] * 2

    @staticmethod
    def scratch(nz, count, rows, width):
        hops = nz - 1
        message = (rows, width)
        sems = DMA((count, hops))
        return [
            pltpu.VMEM((hops,) + message, BF16), pltpu.VMEM((hops,) + message, BF16),
            pltpu.VMEM(message, BF16), pltpu.VMEM(message, BF16),
            pltpu.VMEM((2,) + message, F32), sems, sems, sems, sems, DMA((2,)), DMA((2,)),
        ]

    def copy_right(self, j, s, peer):
        return remote(
            self.out_r.at[s - 1], self.got_r.at[j, s - 1], self.ss_r.at[j, s - 1], self.sr_r.at[j, s - 1], peer
        )

    def copy_left(self, j, s, peer):
        return remote(
            self.out_l.at[s - 1], self.got_l.at[j, s - 1], self.ss_l.at[j, s - 1], self.sr_l.at[j, s - 1], peer
        )

    def load_right(self, j, s):
        return pltpu.make_async_copy(self.got_r.at[j, s - 1], self.in_r, self.load_sem.at[0])

    def load_left(self, j, s):
        return pltpu.make_async_copy(self.got_l.at[j, s - 1], self.in_l, self.load_sem.at[1])

    def step(self, j, s):
        z, nz = self.z, self.nz

        def one(go, copy, load, out, into, to, source, first):
            more = (s > 1) & jnp.logical_not(first)

            @pl.when(more)
            def _():
                copy(j, s - 1, source).wait_recv()
                load(j, s - 1).start()

            @pl.when(j > 0)
            def _():
                copy(j - 1, s, to).wait_send()

            total = self.partial(go, j)

            @pl.when(more)
            def _():
                load(j, s - 1).wait()
                out[s - 1] = (total + into[...].astype(F32)).astype(BF16)

            @pl.when(jnp.logical_not(more))
            def _():
                out[s - 1] = total.astype(BF16)

            copy(j, s, to).start()

        go_right = z + nz - s
        go_left = z - nz + s

        @pl.when(go_right < nz)
        def _():
            one(go_right, self.copy_right, self.load_right, self.out_r, self.in_r, self.right, self.left, z == 0)

        @pl.when(go_left >= 0)
        def _():
            one(go_left, self.copy_left, self.load_left, self.out_l, self.in_l, self.left, self.right, z == nz - 1)

    def end(self, j):
        z, nz = self.z, self.nz
        k = j % 2

        @pl.when(j >= 2)
        def _():
            self.keep(j - 2, self.stage.at[k], self.keep_sem.at[k]).wait()

        @pl.when(z > 0)
        def _():
            self.copy_right(j, nz - 1, self.left).wait_recv()
            self.load_right(j, nz - 1).start()

        @pl.when(z < nz - 1)
        def _():
            self.copy_left(j, nz - 1, self.right).wait_recv()
            self.load_left(j, nz - 1).start()

        self.stage[k] = self.partial(z, j)

        @pl.when(z > 0)
        def _():
            self.load_right(j, nz - 1).wait()
            self.stage[k] += self.in_r[...].astype(F32)

        @pl.when(z < nz - 1)
        def _():
            self.load_left(j, nz - 1).wait()
            self.stage[k] += self.in_l[...].astype(F32)

        self.keep(j, self.stage.at[k], self.keep_sem.at[k]).start()

    def run(self, first, last):
        hops = self.nz - 1

        def unit(u, carry):
            slot = u // hops
            s = u % hops + 1
            j = slot - (s - 1)

            @pl.when((j >= 0) & (j < self.count))
            def _():
                self.step(j, s)

            @pl.when((s == hops) & (slot >= hops))
            def _():
                self.end(slot - hops)

            return carry

        lax.fori_loop(first, last, unit, 0)

    def units(self):
        return (self.count + self.nz - 1) * (self.nz - 1)

    def finish(self):
        z, nz = self.z, self.nz
        last = self.count - 1
        for j in range(max(0, last - 1), last + 1):
            self.keep(j, self.stage.at[j % 2], self.keep_sem.at[j % 2]).wait()
        for s in range(1, nz):

            @pl.when(z + nz - s < nz)
            def _():
                self.copy_right(last, s, self.right).wait_send()

            @pl.when(z - nz + s >= 0)
            def _():
                self.copy_left(last, s, self.left).wait_send()


def greet_all(seq, me, nz, others):
    z = seq // 2
    barrier = pltpu.get_barrier_semaphore()
    for peer in others + [(seq + 1 - 2 * (seq % 2), me)]:
        pl.semaphore_signal(barrier, inc=1, device_id=peer, device_id_type=MESH)

    @pl.when(z > 0)
    def _():
        pl.semaphore_signal(barrier, inc=1, device_id=(seq - 2, me), device_id_type=MESH)

    @pl.when(z < nz - 1)
    def _():
        pl.semaphore_signal(barrier, inc=1, device_id=(seq + 2, me), device_id_type=MESH)

    pl.semaphore_wait(barrier, len(others) + 1 + jnp.where(z > 0, 1, 0) + jnp.where(z < nz - 1, 1, 0))


def gate_chain(nz, first, count, seq, me, bt, bty, dg, dgy, out, landing, slabs, halves, slab_sem, scratch):
    loads = [pltpu.make_async_copy(bt.at[:, seq % 2], halves.at[0], slab_sem.at[2])]
    loads.append(pltpu.make_async_copy(bty, halves.at[1], slab_sem.at[3]))
    for i, ref in enumerate((dg, dgy)):
        loads.append(
            pltpu.make_async_copy(ref.at[:, pl.ds(first * TILE, count * TILE)], slabs.at[i], slab_sem.at[i])
        )

    def partial(k, j):
        cols = pl.ds(pl.multiple_of(j * TILE, 128), TILE)
        return dot(halves[0, k], slabs[0, :, cols]) + dot(halves[1, k], slabs[1, :, cols])

    def keep(j, stage, sem):
        return pltpu.make_async_copy(stage, out.at[:, pl.ds(pl.multiple_of(j * TILE, 128), TILE)], sem)

    return Chain(nz, count, seq, me, partial, keep, landing, scratch), loads


def gate_landing(nz, count, bt):
    return Chain.landing(nz, count, bt.shape[2], TILE)


def gate_scratch(nz, count, bt):
    rows = bt.shape[3]
    return [
        pltpu.VMEM((2, rows, count * TILE), BF16), pltpu.VMEM((2, nz) + bt.shape[2:], BF16), DMA((4,))
    ] + Chain.scratch(nz, count, bt.shape[2], TILE)


def levels(code, step):
    return (jnp.floor(code.astype(F32) * (1.0 / step)) * step + step / 2.0).astype(BF16)


def gelu_parts(gate):
    root = math.sqrt(2.0 / math.pi)
    square = gate * gate
    bend = jnp.tanh(root * gate * (1.0 + 0.044715 * square))
    value = 0.5 * gate * (1.0 + bend)
    slope = 0.5 * (1.0 + bend) + 0.5 * gate * (1.0 - bend * bend) * root * (1.0 + 3 * 0.044715 * square)
    return value, slope


def strips(count, size, body):
    def step(i, carry):
        body(pl.ds(pl.multiple_of(i * size, size), size))
        return carry

    lax.fori_loop(0, count, step, 0)


def ffn_forward_kernel(tiles, riders, *refs):
    b, wgu, gs, wd, cots, g3, ds = refs[:7]
    refs = refs[7:]
    rider_in, refs = refs[:riders], refs[riders:]
    gu_o, hid_o, hidy_o, down_o, gf_o, gft_o, sums_o, lev_o, levd_o = refs[:9]
    refs = refs[9:]
    rider_out, refs = refs[:riders], refs[riders:]
    (both, hid, unit, wbuf, wlev, dbuf, dlev, acc, downs, wsem, dsem, lsem, ldsem, osem, xs, xr, oks, hs, hr, ks,
     ys, yr, fs, fr, gxs, gxr, gcs, gcr, gfs, gfr, rs, rr, outs) = refs
    seq, me, x, c = place_now()
    y = seq % 2
    across = (seq, (1 - x) * 2 + c)
    beside = (seq, x * 2 + 1 - c)
    beyond = (seq + 1 - 2 * y, me)
    rows, tw = both.shape[2:]
    part = b.shape[2]
    deep = GROUP * part
    per = tiles // 4

    def load_up(t):
        return pltpu.make_async_copy(wgu.at[:, pl.ds(pl.multiple_of(t * tw, 128), tw)], wbuf.at[t % 2], wsem.at[t % 2])

    def load_down(t, half):
        start = ((c + half) % 2 * tiles + t) * tw
        return pltpu.make_async_copy(
            wd.at[:, pl.ds(pl.multiple_of(start, 128), tw)], dbuf.at[t % 2, half], dsem.at[t % 2, half]
        )

    load_up(0).start()
    load_up(1).start()
    for t in range(2):
        for half in range(2):
            load_down(t, half).start()
    greet([across, beside, beyond])
    travellers = []
    for i in range(riders):
        share = pl.ds(2 * c, 2)
        copy = remote(rider_in[i].at[share, 1 - y], rider_out[i].at[share], rs.at[i, 0], rr.at[i, 0], beyond)
        copy.start()
        got = rider_out[i].at[share]
        travellers.append((copy, remote(got, got, rs.at[i, 1], rr.at[i, 1], beside)))
    acc[...] = jnp.zeros_like(acc)
    fill_unit(unit)

    def to_x(t):
        return remote(both.at[t % 3, x], gu_o.at[x, t], xs.at[t], xr.at[t], across)

    def from_x(t):
        return remote(both.at[t % 3, x], gu_o.at[1 - x, t], xs.at[t], xr.at[t], across)

    def keep_own(t):
        return pltpu.make_async_copy(both.at[t % 3, x], gu_o.at[x, t], oks.at[t])

    def load_other(t):
        return pltpu.make_async_copy(gu_o.at[1 - x, t], both.at[t % 3, 1 - x], osem.at[t % 2])

    def keep_level(t):
        return pltpu.make_async_copy(wlev.at[t % 2], lev_o.at[t], lsem.at[t % 2])

    def keep_down(t, half):
        return pltpu.make_async_copy(dlev.at[t % 2, half], levd_o.at[half, t], ldsem.at[t % 2, half])

    def to_core(t):
        return remote(hid.at[c * tiles + t], hid.at[c * tiles + t], hs.at[t], hr.at[t], beside)

    def slot(t, core):
        return (2 * core + t // (2 * per)) * per + t % per

    def keep(t, core, i):
        return pltpu.make_async_copy(hid.at[core * tiles + t], hid_o.at[slot(t, core)], ks.at[i, t])

    def to_y(t):
        return remote(hid.at[c * tiles + t], hidy_o.at[slot(t, c)], ys.at[t], yr.at[t], beyond)

    def for_mine(t):
        return (t // per) % 2 == y

    def wide(t):
        load_up(t).wait()

        @pl.when(t >= 2)
        def _():
            keep_level(t - 2).wait()

        def level(span):
            wlev[t % 2, span, :] = levels(wbuf[t % 2, span, :], 16.0)

        strips(deep // 128, 128, level)
        keep_level(t).start()

        @pl.when(t + 2 < tiles)
        def _():
            load_up(t + 2).start()

        @pl.when(t >= 3)
        def _():
            to_x(t - 3).wait_send()
            keep_own(t - 3).wait()

        scale = gs[t]

        def product(span):
            total = dot(b[0, span, :], wlev[t % 2, 0:part, :])
            for j in range(1, GROUP):
                total = total + dot(b[j, span, :], wlev[t % 2, j * part : (j + 1) * part, :])
            both[t % 3, x, span, :] = (total * scale).astype(BF16)

        strips(rows // 256, 256, product)
        to_x(t).start()
        keep_own(t).start()

    def arrive(t):
        from_x(t).wait_recv()
        load_other(t).start()

    def middle(t):
        load_other(t).wait()

        def body(span):
            gate = both[t % 3, 0, span, :].astype(F32)
            up = both[t % 3, 1, span, :].astype(F32)
            hid[c * tiles + t, span, :] = (gelu_parts(gate)[0] * up).astype(BF16)

        strips(rows // 64, 64, body)
        to_core(t).start()

        @pl.when(for_mine(t))
        def _():
            keep(t, c, 0).start()

        @pl.when(jnp.logical_not(for_mine(t)))
        def _():
            to_y(t).start()

    def narrow(t):
        for half in range(2):
            load_down(t, half).wait()

            @pl.when(t >= 2)
            def _():
                keep_down(t - 2, half).wait()

            def level(span):
                dlev[t % 2, half, span, :] = levels(dbuf[t % 2, half, span, :], 64.0)

            strips(part // 64, 64, level)
            keep_down(t, half).start()

            @pl.when(t + 2 < tiles)
            def _():
                load_down(t + 2, half).start()

        to_core(t).wait_recv()

        def product(span):
            acc[span, :] += contract_last(hid[c * tiles + t, span, :], dlev[t % 2, 0]) + contract_last(
                hid[(1 - c) * tiles + t, span, :], dlev[t % 2, 1]
            )

        strips(rows // 256, 256, product)

        @pl.when(for_mine(t))
        def _():
            keep(t, 1 - c, 1).start()

    def step(i, carry):
        @pl.when(i < tiles)
        def _():
            wide(i)

        @pl.when((i >= 1) & (i < tiles + 1))
        def _():
            arrive(i - 1)

        @pl.when(i >= 2)
        def _():
            narrow(i - 2)

        @pl.when((i >= 1) & (i < tiles + 1))
        def _():
            middle(i - 1)

        return carry

    lax.fori_loop(0, tiles + 2, step, 0)

    for copy, forward in travellers:
        copy.wait_recv()
        forward.start()
    parts = 4
    size = rows // parts
    sends = []
    own_sends = []
    for k in range(parts):
        span = pl.ds(k * size, size)
        downs[me, span, :] = acc[span, :].astype(BF16)
        piece = downs.at[me, span]
        copy = remote(piece, piece, gxs.at[k], gxr.at[k], across)
        copy.start()
        sends.append(copy)
        copy = remote(piece, piece, gcs.at[k], gcr.at[k], beside)
        copy.start()
        own_sends.append(copy)

    def pass_on(t, carry):
        @pl.when(for_mine(t))
        def _():
            got = hidy_o.at[slot(t, c)]
            remote(hid.at[0], got, ys.at[t], yr.at[t], beyond).wait_recv()
            remote(got, got, fs.at[t], fr.at[t], beside).start()

        return carry

    lax.fori_loop(0, tiles, pass_on, 0)
    forwards = []
    for k in range(parts):
        sends[k].wait_recv()
        got = downs.at[(1 - x) * 2 + c, pl.ds(k * size, size)]
        copy = remote(got, got, gfs.at[k], gfr.at[k], beside)
        copy.start()
        forwards.append(copy)
    for copy in own_sends + forwards:
        copy.wait_recv()
    down_out = pltpu.make_async_copy(downs, down_o, outs)
    down_out.start()
    sums_o[...] = jnp.zeros_like(sums_o)
    width = GROUP * acc.shape[1]

    def last_norm(i, carry):
        pack = i // 2
        span = pl.ds(pl.multiple_of(i * 64, 64), 64)
        inner = (i % 2) * 64

        def cot_of(j):
            return cots[pack, pl.ds(pl.multiple_of(j * 128 + inner, 64), 64), :].astype(F32)

        square = jnp.zeros((64, 1), F32)
        cross = jnp.zeros((64, 1), F32)
        for j in range(GROUP):
            value = downs[j, span, :].astype(F32) * ds[j]
            square = square + jnp.sum(value * value, axis=1, keepdims=True)
            cross = cross + jnp.sum(value * (cot_of(j) * g3[j]), axis=1, keepdims=True)
        inverse = lax.rsqrt(square * (1.0 / width) + EPSILON)
        raw = downs[me, span, :].astype(F32)
        normed = raw * ds[me] * inverse
        cot = cot_of(me)
        grad = inverse * (cot * g3[me] - normed * (cross * inverse * (1.0 / width)))
        gf_o[span, :] = (grad * ds[me]).astype(BF16)
        sums_o[0:1, :] += jnp.sum(raw * grad, axis=0, keepdims=True)
        sums_o[1:2, :] += jnp.sum(cot * normed, axis=0, keepdims=True)
        return carry

    lax.fori_loop(0, rows // 64, last_norm, 0)
    gft_o[...] = contract_last(unit[...], gf_o[...]).astype(BF16)

    for t in range(tiles - 3, tiles):
        to_x(t).wait_send()
        keep_own(t).wait()
    for t in range(tiles - 2, tiles):
        keep_level(t).wait()
        for half in range(2):
            keep_down(t, half).wait()

    def drain(t, carry):
        to_core(t).wait_send()

        @pl.when(for_mine(t))
        def _():
            keep(t, c, 0).wait()
            keep(t, 1 - c, 1).wait()
            got = hidy_o.at[slot(t, c)]
            remote(got, got, fs.at[t], fr.at[t], beside).wait_send()
            got = hidy_o.at[slot(t, 1 - c)]
            remote(got, got, fs.at[t], fr.at[t], beside).wait_recv()

        @pl.when(jnp.logical_not(for_mine(t)))
        def _():
            to_y(t).wait_send()

        return carry

    lax.fori_loop(0, tiles, drain, 0)
    for copy in sends + own_sends + forwards:
        copy.wait_send()
    for copy, forward in travellers:
        copy.wait_send()
        forward.wait()
    down_out.wait()


def ffn_forward(cid, b, wgu, gs, wd, cots, g3, ds, riders):
    rows, part = b.shape[1:]
    deep = GROUP * part
    tiles, _, tw = gs.shape
    count = len(riders)
    lone = max(count, 1)
    each = DMA((tiles,))
    four = DMA((4,))
    return comm_call(
        functools.partial(ffn_forward_kernel, tiles, count),
        cid,
        [
            jax.ShapeDtypeStruct((2, tiles, rows, tw), BF16),
            jax.ShapeDtypeStruct((tiles, rows, tw), BF16),
            jax.ShapeDtypeStruct((tiles, rows, tw), BF16),
            jax.ShapeDtypeStruct((GROUP, rows, part), BF16),
            jax.ShapeDtypeStruct((rows, part), BF16),
            jax.ShapeDtypeStruct((part, rows), BF16),
            jax.ShapeDtypeStruct((8, part), F32),
            jax.ShapeDtypeStruct((tiles, deep, tw), BF16),
            jax.ShapeDtypeStruct((2, tiles, part, tw), BF16),
        ]
        + [jax.ShapeDtypeStruct(r.shape[:1] + r.shape[2:], r.dtype) for r in riders],
        [
            pltpu.VMEM((3, 2, rows, tw), BF16),
            pltpu.VMEM((2 * tiles, rows, tw), BF16),
            pltpu.VMEM((part, part), BF16),
            pltpu.VMEM((2, deep, tw), BF16),
            pltpu.VMEM((2, deep, tw), BF16),
            pltpu.VMEM((2, 2, part, tw), BF16),
            pltpu.VMEM((2, 2, part, tw), BF16),
            pltpu.VMEM((rows, part), F32),
            pltpu.VMEM((GROUP, rows, part), BF16),
            DMA((2,)), DMA((2, 2)), DMA((2,)), DMA((2, 2)), DMA((2,)), each, each, each, each, each, DMA((2, tiles)),
            each, each, each, each, four, four, four, four, four, four, DMA((lone, 2)), DMA((lone, 2)), DMA,
        ],
        [VMEM, ANY, VMEM, ANY, VMEM, VMEM, VMEM] + [ANY] * count,
        [ANY, ANY, ANY, ANY, VMEM, VMEM, VMEM, ANY, ANY] + [ANY] * count,
    )(b, wgu, gs, wd, cots, g3, ds, *riders)


def ffn_backward_kernel(tiles, nz, chained, gate_tiles, *refs):
    gf, gft, levd, lev, gs, gu, hid, hidy, bt, bty = refs[:10]
    dg_o, dgy_o, xg_o, gsum_o, out, ddown_o, gate_o = refs[10:17]
    landing = refs[17:21] if chained else []
    refs = refs[len(landing) + 1 :]
    (hh, hy, gfy, wbuf, dbuf, pair, co, cgot, near, sx, xgot, dg, acc, low, from_core, to_xb, from_x,
     hsem, wsem, dsem, psem, lsem, cs, cr, xs, xr, ys, yr, os, gys, gyr, ccs, ccr, cxs, cxr) = refs[16:51]
    rest = refs[51:]
    seq, me, x, c = place_now()
    y = seq % 2
    across = (seq, (1 - x) * 2 + c)
    beside = (seq, x * 2 + 1 - c)
    beyond = (seq + 1 - 2 * y, me)
    rows, tw = dg.shape[1:]
    part = acc.shape[2]
    per = hid.shape[0] // 4 if chained else 0
    ring = dg.shape[0]

    def load_up(t):
        return pltpu.make_async_copy(lev.at[t], wbuf.at[t % 2], wsem.at[t % 2])

    def load_down(t, half):
        return pltpu.make_async_copy(levd.at[half, t], dbuf.at[t % 2, half], dsem.at[t % 2, half])

    def load_pair(t):
        return pltpu.make_async_copy(gu.at[:, t], pair.at[t % 2], psem.at[t % 2])

    for t in range(2):
        for half in range(2):
            load_down(t, half).start()
        load_pair(t).start()
        load_up(t).start()
    if chained:
        load_hid = pltpu.make_async_copy(hid, hh, hsem.at[0])
        load_hidy = pltpu.make_async_copy(hidy, hy, hsem.at[1])
        load_hid.start()
        load_hidy.start()

        def partial(k, j):
            return dot(gft[...], hh[k * per + j]) + dot(gfy[...], hy[k * per + j])

        def keep_sum(j, stage, sem):
            return pltpu.make_async_copy(stage, ddown_o.at[:, pl.ds(pl.multiple_of(j * tw, 128), tw)], sem)

        downs = Chain(nz, per, seq, me, partial, keep_sum, landing[:2], rest[:11])
        gates, gate_loads = gate_chain(
            nz, 0, gate_tiles, seq, me, bt, bty, dg_o, dgy_o, gate_o, landing[2:], *rest[11:14], rest[14:]
        )
        gate_loads[0].start()
        gate_loads[1].start()
        greet_all(seq, me, nz, [across, beside])
        gf_swap = remote(gft, gfy, gys, gyr, beyond)
        gf_swap.start()
    else:
        greet([across, beside, beyond])
    acc[...] = jnp.zeros_like(acc)

    def to_core(t):
        return remote(co.at[t % 2], cgot.at[t % 4], cs.at[t], cr.at[t], beside)

    def to_x(t):
        return remote(sx.at[t % 4], xg_o.at[t], xs.at[t], xr.at[t], across)

    def load_got(t):
        return pltpu.make_async_copy(xg_o.at[t], xgot.at[t % 2], lsem.at[t % 2])

    def columns(ref, t):
        return ref.at[:, pl.ds(pl.multiple_of(t * tw, 128), tw)]

    def to_y(t):
        return remote(dg.at[t % ring], columns(dgy_o, t), ys.at[t], yr.at[t], beyond)

    def keep(t):
        return pltpu.make_async_copy(dg.at[t % ring], columns(dg_o, t), os.at[t])

    def hidden(t):
        for half in range(2):
            load_down(t, half).wait()

        @pl.when(t >= 2)
        def _():
            to_core(t - 2).wait_send()

        def product(span):
            co[t % 2, span, :] = dot(gf[span, :], dbuf[t % 2, 1]).astype(BF16)

        strips(rows // 256, 256, product)
        to_core(t).start()

        def product_near(span):
            near[t % 2, span, :] = dot(gf[span, :], dbuf[t % 2, 0])

        strips(rows // 256, 256, product_near)

        @pl.when(t + 2 < tiles)
        def _():
            for half in range(2):
                load_down(t + 2, half).start()

    def chip(t):
        @pl.when(t >= 4)
        def _():
            to_x(t - 4).wait_send()

        to_core(t).wait_recv()

        def body(span):
            sx[t % 4, span, :] = (near[t % 2, span, :] + cgot[t % 4, span, :].astype(F32)).astype(BF16)

        strips(rows // 64, 64, body)
        to_x(t).start()

    is_gate = jnp.where(x == 0, 1.0, 0.0).astype(F32)

    def arrive(t):
        to_x(t).wait_recv()
        load_got(t).start()

    def own(t):
        load_pair(t).wait()

        @pl.when(t >= ring)
        def _():
            to_y(t - ring).wait_send()
            keep(t - ring).wait()

        load_got(t).wait()
        scale = gs[t]
        gsum_o[t] = jnp.zeros((8, tw), F32)

        def body(span):
            grad = sx[t % 4, span, :].astype(F32) + xgot[t % 2, span, :].astype(F32)
            gate = pair[t % 2, 0, span, :].astype(F32)
            up = pair[t % 2, 1, span, :].astype(F32)
            value, slope = gelu_parts(gate)
            full = grad * (is_gate * (up * slope) + (1.0 - is_gate) * value)
            gsum_o[t, 0:1, :] += jnp.sum(pair[t % 2, x, span, :].astype(F32) * full, axis=0, keepdims=True)
            dg[t % ring, span, :] = (full * scale).astype(BF16)

        strips(rows // 64, 64, body)

        @pl.when(t + 2 < tiles)
        def _():
            load_pair(t + 2).start()

        to_y(t).start()
        keep(t).start()

    def back(t):
        load_up(t).wait()

        def product(span):
            for j in range(GROUP):
                acc[j, span, :] += contract_last(dg[t % ring, span, :], wbuf[t % 2, j * part : (j + 1) * part, :])

        strips(rows // 128, 128, product)

        @pl.when(t + 2 < tiles)
        def _():
            load_up(t + 2).start()

    def units(chain, i, table):
        unit = jnp.int32(0)
        hit = i < 0
        for when, u in table:
            unit = unit + jnp.where(i == when, u, 0)
            hit = hit | (i == when)

        @pl.when(hit)
        def _():
            chain.run(unit, unit + 1)

    def step(i, carry):
        @pl.when(i < tiles)
        def _():
            hidden(i)

        @pl.when((i >= 1) & (i < tiles + 1))
        def _():
            chip(i - 1)

        @pl.when((i >= 2) & (i < tiles + 2))
        def _():
            arrive(i - 2)

        if chained:

            @pl.when(i == 1)
            def _():
                gf_swap.wait_recv()
                load_hid.wait()
                load_hidy.wait()

            @pl.when(i == 9)
            def _():
                for t in range(gate_tiles):
                    to_y(t).wait_recv()
                gate_loads[2].start()
                gate_loads[3].start()

            @pl.when(i == 10)
            def _():
                for load in gate_loads:
                    load.wait()

            units(downs, i, ((1, 0), (2, 3), (3, 4), (4, 6), (5, 7), (6, 8), (7, 10), (8, 11), (10, 14), (12, 17)))
            units(gates, i, ((10, 0), (11, 3), (12, 4), (13, 7), (14, 8)))

        @pl.when(i >= 3)
        def _():
            back(i - 3)

        @pl.when((i >= 2) & (i < tiles + 2))
        def _():
            own(i - 2)

        return carry

    lax.fori_loop(0, tiles + 3, step, 0)

    parts = 4
    block = rows // GROUP
    size = block // parts
    order = [1 - x, x]
    js = range(GROUP)
    cores = []
    for i in range(2):
        for k in range(parts):
            owner = order[i] * 2 + 1 - c
            span = pl.ds(k * size, size)
            for j in js:
                low[i, j, span, :] = acc[j, pl.ds(pl.multiple_of(owner * block + k * size, 16), size), :].astype(BF16)
            copy = remote(low.at[i, :, span], from_core.at[i, :, span], ccs.at[i, k], ccr.at[i, k], beside)
            copy.start()
            cores.append(copy)
    sends = []
    for k in range(parts):
        span = pl.ds(k * size, size)
        here = pl.ds(pl.multiple_of((order[0] * 2 + c) * block + k * size, 16), size)
        cores[k].wait_recv()
        for j in js:
            to_xb[j, span, :] = (acc[j, here, :] + from_core[0, j, span, :].astype(F32)).astype(BF16)
        copy = remote(to_xb.at[:, span], from_x.at[:, span], cxs.at[k], cxr.at[k], across)
        copy.start()
        sends.append(copy)
    if chained:
        gates.run(9, gates.units())
        downs.finish()
        gates.finish()
    for k in range(parts):
        span = pl.ds(k * size, size)
        here = pl.ds(pl.multiple_of((order[1] * 2 + c) * block + k * size, 16), size)
        cores[parts + k].wait_recv()
        sends[k].wait_recv()
        for j in js:
            out[j, span, :] = acc[j, here, :] + from_core[1, j, span, :].astype(F32) + from_x[j, span, :].astype(F32)

    for copy in cores + sends:
        copy.wait_send()
    for t in range(tiles - 2, tiles):
        to_core(t).wait_send()
    for t in range(tiles - 4, tiles):
        to_x(t).wait_send()
    for t in range(tiles - ring, tiles):
        to_y(t).wait_send()
        keep(t).wait()

    def drain(t, carry):
        to_y(t).wait_recv()
        return carry

    lax.fori_loop(gate_tiles if chained else 0, tiles, drain, 0)
    if chained:
        gf_swap.wait_send()


def ffn_backward(cid, n, gate_tiles, gf, gft, levd, lev, gs, gu, hid, hidy, bt, bty):
    rows, part = gf.shape
    deep = lev.shape[1]
    tiles, _, tw = gs.shape
    nz = n // 2
    chained = nz == 4
    per = tiles // nz if chained else 1
    block = rows // GROUP
    half = (tiles, rows, tw) if chained else (1, 16, 128)
    message = (part, tw)
    ring = 4
    each = DMA((tiles,))
    wide = jax.ShapeDtypeStruct((rows, tiles * tw), BF16)
    return comm_call(
        functools.partial(ffn_backward_kernel, tiles, nz, chained, gate_tiles),
        cid,
        [
            wide,
            wide,
            jax.ShapeDtypeStruct((tiles, rows, tw), BF16),
            jax.ShapeDtypeStruct((tiles, 8, tw), F32),
            jax.ShapeDtypeStruct((GROUP, block, part), F32),
            jax.ShapeDtypeStruct((part, per * tw), F32),
            jax.ShapeDtypeStruct((bt.shape[2], max(gate_tiles, 1) * tw), F32),
        ]
        + (Chain.landing(nz, per, *message) + gate_landing(nz, gate_tiles, bt) if chained else []),
        [
            pltpu.VMEM(half, BF16),
            pltpu.VMEM(half, BF16),
            pltpu.VMEM((part, rows), BF16),
            pltpu.VMEM((2, deep, tw), BF16),
            pltpu.VMEM((2, 2, part, tw), BF16),
            pltpu.VMEM((2, 2, rows, tw), BF16),
            pltpu.VMEM((2, rows, tw), BF16),
            pltpu.VMEM((4, rows, tw), BF16),
            pltpu.VMEM((2, rows, tw), F32),
            pltpu.VMEM((4, rows, tw), BF16),
            pltpu.VMEM((2, rows, tw), BF16),
            pltpu.VMEM((ring, rows, tw), BF16),
            pltpu.VMEM((GROUP, rows, part), F32),
            pltpu.VMEM((2, GROUP, block, part), BF16),
            pltpu.VMEM((2, GROUP, block, part), BF16),
            pltpu.VMEM((GROUP, block, part), BF16),
            pltpu.VMEM((GROUP, block, part), BF16),
            DMA((2,)), DMA((2,)), DMA((2, 2)), DMA((2,)), DMA((2,)), each, each, each, each,
            each, each, each, DMA, DMA, DMA((2, 4)), DMA((2, 4)), DMA((4,)), DMA((4,)),
        ]
        + (Chain.scratch(nz, per, *message) + gate_scratch(nz, gate_tiles, bt) if chained else []),
        [VMEM, VMEM, ANY, ANY, VMEM, ANY, ANY, ANY, ANY, ANY],
        [ANY, ANY, ANY, VMEM, VMEM, ANY, ANY] + [ANY] * (4 if chained else 0),
    )(gf, gft, levd, lev, gs, gu, hid, hidy, bt, bty)


def branch_back_kernel(n, first, tiles, *refs):
    (gsi, mid, raw, cot, g2, g3, scale, wo, q, mixed, mass, own_meta, metas, kv, bt, bty, dg, dgy) = refs[:18]
    dmid, sums, gy, gyy, dq, dkv, gate_o = refs[18:25]
    landing = refs[25:27] if tiles else []
    refs = refs[len(landing) :]
    (unit, gyt, gys, gy_all, part, from_core, to_x, from_x, grad, kvs, dkvs, es, er, el, cs, cr, xs, xr, ks, ds, yss, ysr,
     ows) = refs[25:48]
    rest = refs[48:]
    seq, me, x, c = place_now()
    nz = n // 2
    across = (seq, (1 - x) * 2 + c)
    beside = (seq, x * 2 + 1 - c)
    beyond = (seq + 1 - 2 * (seq % 2), me)
    peers = [(seq, lax.rem(me + d, GROUP)) for d in range(1, GROUP)]
    chain = None
    if tiles:
        chain, loads = gate_chain(nz, first, tiles, seq, me, bt, bty, dg, dgy, gate_o, landing, *rest[:3], rest[3:])
        for load in loads:
            load.start()
        greet_all(seq, me, nz, peers)
    else:
        greet(peers + [beyond])
    width = GROUP * raw.shape[2]
    mean = 1.0 / width
    sums[...] = jnp.zeros_like(sums)
    js = range(GROUP)

    def rowsum(values):
        total = values[0]
        for value in values[1:]:
            total = total + value
        return jnp.sum(total, axis=1, keepdims=True) * mean

    def norms(span):
        middle = [mid[j, span, :] for j in js]
        up = [gsi[j, span, :] for j in js]
        inverse = lax.rsqrt(rowsum([v * v for v in middle]) + EPSILON)
        third = [v * inverse for v in middle]
        scaled = [up[j] * g3[j] for j in js]
        cross = rowsum([scaled[j] * third[j] for j in js])
        grad_middle = [
            cot[j, span, :].astype(F32) + inverse * (scaled[j] - third[j] * cross) for j in js
        ]
        plain = [raw[j, span, :].astype(F32) for j in js]
        branch = [plain[j] * scale[j] for j in js]
        inverse = lax.rsqrt(rowsum([v * v for v in branch]) + EPSILON)
        second = [v * inverse for v in branch]
        scaled = [grad_middle[j] * g2[j] for j in js]
        cross = rowsum([scaled[j] * second[j] for j in js])
        for j in js:
            full = inverse * (scaled[j] - second[j] * cross)
            gys[j, span, :] = (full * scale[j]).astype(BF16)
            dmid[j, span, :] = grad_middle[j]
            sums[j, 0:1, :] += jnp.sum(grad_middle[j] * second[j], axis=0, keepdims=True)
            sums[j, 1:2, :] += jnp.sum(up[j] * third[j], axis=0, keepdims=True)
            sums[j, 2:3, :] += jnp.sum(plain[j] * full, axis=0, keepdims=True)

    strips(raw.shape[1] // 16, 16, norms)

    copies = []
    for d in (2, 1, 3):
        peer = peers[d - 1]
        copy = remote(gys.at[peer[1]], gy_all.at[me], es.at[d - 1], er.at[d - 1], peer)
        copy.start()
        copies.append(copy)
    own = pltpu.make_async_copy(gys.at[me], gy_all.at[me], el)
    own.start()
    for p in range(2):
        pltpu.make_async_copy(kv.at[:, :, pl.ds(p * 128, 128)], kvs.at[p], ks.at[p]).start()
    units = chain.units() if chain else 0
    at = [0]

    def beside_work(count):
        if chain:
            last = min(units, at[0] + count)
            chain.run(at[0], last)
            at[0] = last

    if chain:
        for load in loads:
            load.wait()
    beside_work(3)
    for copy in copies:
        copy.wait_recv()
    own.wait()
    fill_unit(unit)
    gyt[...] = contract_last(unit[...], gy_all[...].reshape(gyt.shape[1], gyt.shape[0])).astype(BF16)
    gy_out = pltpu.make_async_copy(gyt, gy, ows)
    gy_out.start()
    swap = remote(gyt, gyy, yss, ysr, beyond)
    swap.start()

    heads = part.shape[3]
    rows = part.shape[2]
    order = [1 - x, x]

    def product(i, k, to):
        grad_branch = gy_all[...].reshape(rows, raw.shape[2])
        start = (order[i] * 2 + k) * heads
        to[...] = dot(grad_branch, wo[:, pl.ds(pl.multiple_of(start, 128), heads)]).astype(BF16)

    cores = []
    for i in range(2):
        product(i, 1 - c, part.at[i, 0])
        copy = remote(part.at[i, 0], from_core.at[i], cs.at[i], cr.at[i], beside)
        copy.start()
        cores.append(copy)
    for i in range(2):
        product(i, c, part.at[i, 1])
    cores[0].wait_recv()

    def add_core(span):
        to_x[span, :] = (part[0, 1, span, :].astype(F32) + from_core[0, span, :].astype(F32)).astype(BF16)

    strips(rows // 64, 64, add_core)
    over = remote(to_x, from_x, xs, xr, across)
    over.start()
    beside_work(4)
    cores[1].wait_recv()
    over.wait_recv()

    def add_all(span):
        grad[span, :] = (
            part[1, 1, span, :].astype(F32) + from_core[1, span, :].astype(F32) + from_x[span, :].astype(F32)
        ).astype(BF16)

    strips(rows // 64, 64, add_all)

    def load_pack(p):
        return pltpu.make_async_copy(
            kv.at[:, :, pl.ds(pl.multiple_of(p * 128, 128), 128)], kvs.at[p % 2], ks.at[p % 2]
        )

    def store_pack(p):
        return pltpu.make_async_copy(
            dkvs.at[p % 2], dkv.at[:, :, pl.ds(pl.multiple_of(p * 128, 128), 128)], ds.at[p % 2]
        )

    base = at[0]
    each = max(0, units - base) // GROUP

    def one_pack(p, carry):
        load_pack(p).wait()

        @pl.when(p >= 2)
        def _():
            store_pack(p - 2).wait()

        span = pl.ds(pl.multiple_of(p * 128, 128), 128)
        keys = kvs[p % 2, :, 0].reshape(n * 128, DH)
        values = kvs[p % 2, :, 1].reshape(n * 128, DH)
        allowed = masks(n, own_meta.at[pl.ds(p, 1)], metas.at[:, pl.ds(p, 1)])
        back_pack(
            n, keys, values, allowed, q.at[span], grad.at[span], mixed.at[span], mass.at[span], dq.at[span],
            dkvs.at[p % 2],
        )
        store_pack(p).start()

        @pl.when(p + 2 < GROUP)
        def _():
            load_pack(p + 2).start()

        if each:
            chain.run(base + p * each, base + (p + 1) * each)
        return carry

    lax.fori_loop(0, GROUP, one_pack, 0)
    at[0] = base + GROUP * each
    beside_work(units)
    if chain:
        chain.finish()
    for copy in copies + cores + [over]:
        copy.wait_send()
    store_pack(2).wait()
    store_pack(3).wait()
    swap.wait()
    gy_out.wait()


def branch_back(cid, n, first, tiles, gsi, mid, raw, cot, g2, g3, scale, wo, q, mixed, mass, own_meta, metas, kv, pairs):
    bt, bty, dg, dgy = pairs
    own, part = raw.shape[1:]
    rows = q.shape[0]
    heads = q.shape[1]
    block = lambda kind: jax.ShapeDtypeStruct((GROUP, own, part), kind)
    gate_rows = bt.shape[2]
    pack = (2, n, 2, own, DH)
    return comm_call(
        functools.partial(branch_back_kernel, n, first, tiles),
        cid,
        [
            block(F32),
            jax.ShapeDtypeStruct((GROUP, 8, part), F32),
            jax.ShapeDtypeStruct((part, rows), BF16),
            jax.ShapeDtypeStruct((part, rows), BF16),
            jax.ShapeDtypeStruct(q.shape, F32),
            jax.ShapeDtypeStruct(kv.shape, BF16),
            jax.ShapeDtypeStruct((gate_rows, max(tiles, 1) * TILE), F32),
        ]
        + (gate_landing(n // 2, tiles, bt) if tiles else []),
        [
            pltpu.VMEM((part, part), BF16),
            pltpu.VMEM((part, rows), BF16),
            pltpu.VMEM((GROUP, own, part), BF16),
            pltpu.VMEM((GROUP, own, part), BF16),
            pltpu.VMEM((2, 2, rows, heads), BF16),
            pltpu.VMEM((2, rows, heads), BF16),
            pltpu.VMEM((rows, heads), BF16),
            pltpu.VMEM((rows, heads), BF16),
            pltpu.VMEM((rows, heads), BF16),
            pltpu.VMEM(pack, BF16),
            pltpu.VMEM(pack, BF16),
            DMA((3,)), DMA((3,)), DMA, DMA((2,)), DMA((2,)), DMA, DMA, DMA((2,)), DMA((2,)), DMA, DMA, DMA,
        ]
        + (gate_scratch(n // 2, tiles, bt) if tiles else []),
        [VMEM] * 13 + [ANY] * 5,
        [VMEM, VMEM, ANY, ANY, VMEM, ANY, ANY] + [ANY] * (2 if tiles else 0),
    )(gsi, mid, raw, cot, g2, g3, scale, wo, q, mixed, mass, own_meta, metas, kv, bt, bty, dg, dgy)


def keys_back_kernel(n, first, tiles, *refs):
    (src, dq, q_raw, p_raw, cosine, sine, q_scale, p_scale, wq, wkv, bt, bty, dg, dgy) = refs[:14]
    joined, joined_y, out, sums, gate_o = refs[14:19]
    landing = refs[19:21]
    refs = refs[2:]
    (y_got, r_got, l_got, r_out, l_out, moved, back, acc, low, from_core, to_xb, from_x,
     ys, yr, rs, rr, ls, lr, hs, hr, local, jys, jyr, ccs, ccr, cxs, cxr) = refs[19:46]
    slabs, halves, slab_sem, *rest = refs[46:]
    seq, me, x, c = place_now()
    y = seq % 2
    z = seq // 2
    nz = n // 2
    right = (seq + 2, me)
    left = (seq - 2, me)
    beyond = (z * 2 + 1 - y, me)
    across = (seq, (1 - x) * 2 + c)
    beside = (seq, x * 2 + 1 - c)
    chain, loads = gate_chain(nz, first, tiles, seq, me, bt, bty, dg, dgy, gate_o, landing, slabs, halves, slab_sem, rest)
    for load in loads:
        load.start()
    greet_all(seq, me, nz, [(seq, lax.rem(me + d, GROUP)) for d in range(1, GROUP)])
    rows, width = dq.shape
    deep = acc.shape[1]
    half = DH // 2

    def swap(k):
        return remote(src.at[k * 2 + 1 - y], y_got.at[k], ys.at[k], yr.at[k], beyond)

    for t in range(1, nz):
        go_right = z + nz - t
        go_left = z - nz + t

        @pl.when(go_right < nz)
        def _():
            swap(go_right).start()

        @pl.when(go_left >= 0)
        def _():
            swap(go_left).start()

    swap(z).start()
    sums[...] = jnp.zeros_like(sums)

    def turn_queries(span):
        cos = cosine[span, :]
        sin = sine[span, :]
        for h in range(2):
            a = slice(h * DH, h * DH + half)
            b = slice(h * DH + half, (h + 1) * DH)
            one = dq[span, a]
            two = dq[span, b]
            for cols, full in ((a, one * cos + two * sin), (b, two * cos - one * sin)):
                sums[0:1, cols] += jnp.sum(q_raw[span, cols] * full, axis=0, keepdims=True)
                joined[span, cols] = (full * q_scale[:, cols]).astype(BF16)

    strips(rows // 64, 64, turn_queries)

    def query_part(span):
        acc[span, :] = contract_last(joined[span, :width], wq[...])

    strips(rows // 128, 128, query_part)

    def pair_sum(k, more, to):
        def body(i, carry):
            part = i // 4
            span = pl.ds(pl.multiple_of((i % 4) * 128, 128), 128)
            total = src[k * 2 + y, part, span, :].astype(F32) + y_got[k, part, span, :].astype(F32)
            for ref in more:
                total = total + ref[part, span, :].astype(F32)
            to[part, span, :] = total.astype(BF16)
            return carry

        lax.fori_loop(0, 8, body, 0)

    for load in loads:
        load.wait()
    units = chain.units()
    at = [0]

    def beside_work(count):
        last = min(units, at[0] + count)
        chain.run(at[0], last)
        at[0] = last

    for t in range(1, nz):
        go_right = z + nz - t
        go_left = z - nz + t

        def hop(go, at_end, got, send, ss, sr, to, source):
            swap(go).wait_recv()
            if t == 1:
                pair_sum(go, [], send.at[t - 1])
            else:

                @pl.when(jnp.logical_not(at_end))
                def _():
                    remote(send.at[t - 1], got.at[t - 2], ss.at[t - 2], sr.at[t - 2], source).wait_recv()
                    pair_sum(go, [got.at[t - 2]], send.at[t - 1])

                @pl.when(at_end)
                def _():
                    pair_sum(go, [], send.at[t - 1])

            remote(send.at[t - 1], got.at[t - 1], ss.at[t - 1], sr.at[t - 1], to).start()

        @pl.when(go_right < nz)
        def _():
            hop(go_right, z == 0, r_got, r_out, rs, rr, right, left)

        @pl.when(go_left >= 0)
        def _():
            hop(go_left, z == nz - 1, l_got, l_out, ls, lr, left, right)

        beside_work(1)

    swap(z).wait_recv()
    last = nz - 2

    def got_left():
        remote(r_out.at[last], r_got.at[last], rs.at[last], rr.at[last], left).wait_recv()

    def got_right():
        remote(l_out.at[last], l_got.at[last], ls.at[last], lr.at[last], right).wait_recv()

    @pl.when(z == 0)
    def _():
        got_right()
        pair_sum(z, [l_got.at[last]], moved)

    @pl.when(z == nz - 1)
    def _():
        got_left()
        pair_sum(z, [r_got.at[last]], moved)

    @pl.when((z > 0) & (z < nz - 1))
    def _():
        got_left()
        got_right()
        pair_sum(z, [r_got.at[last], l_got.at[last]], moved)

    for t in range(2):
        target = t * 2 + x

        @pl.when(target == me)
        def _():
            pltpu.make_async_copy(moved.at[t], back.at[c], local).start()

        @pl.when(target != me)
        def _():
            remote(moved.at[t], back.at[c], hs.at[t], hr.at[c], (seq, target)).start()

    beside_work(1)
    for j in range(2):
        source = c * 2 + j

        @pl.when(source == me)
        def _():
            pltpu.make_async_copy(moved.at[0], back.at[j], local).wait()

        @pl.when(source != me)
        def _():
            remote(moved.at[0], back.at[j], hs.at[0], hr.at[j], (seq, source)).wait_recv()

    is_key = jnp.where(x == 0, 1.0, 0.0).astype(F32)

    def turn_pairs(span):
        cos = is_key * cosine[span, :] + (1.0 - is_key)
        sin = is_key * sine[span, :]
        for h in range(2):
            a = slice(h * DH, h * DH + half)
            b = slice(h * DH + half, (h + 1) * DH)
            one = back[h, span, :half].astype(F32)
            two = back[h, span, half:].astype(F32)
            for cols, full in ((a, one * cos + two * sin), (b, two * cos - one * sin)):
                sums[1:2, cols] += jnp.sum(p_raw[span, cols] * full, axis=0, keepdims=True)
                joined[span, width + cols.start : width + cols.stop] = (full * p_scale[:, cols]).astype(BF16)

    strips(rows // 64, 64, turn_pairs)
    joined_swap = remote(joined, joined_y, jys, jyr, beyond)
    joined_swap.start()

    def pair_part(span):
        acc[span, :] += contract_last(joined[span, width:], wkv[...])

    strips(rows // 128, 128, pair_part)

    parts = 4
    block = rows // GROUP
    size = block // parts
    order = [1 - x, x]
    cores = []
    for i in range(2):
        for k in range(parts):
            owner = order[i] * 2 + 1 - c
            span = pl.ds(k * size, size)
            low[i, span, :] = acc[pl.ds(pl.multiple_of(owner * block + k * size, 16), size), :].astype(BF16)
            copy = remote(low.at[i, span], from_core.at[i, span], ccs.at[i, k], ccr.at[i, k], beside)
            copy.start()
            cores.append(copy)
    sends = []
    for k in range(parts):
        span = pl.ds(k * size, size)
        here = pl.ds(pl.multiple_of((order[0] * 2 + c) * block + k * size, 16), size)
        cores[k].wait_recv()
        to_xb[span, :] = (acc[here, :] + from_core[0, span, :].astype(F32)).astype(BF16)
        copy = remote(to_xb.at[span], from_x.at[span], cxs.at[k], cxr.at[k], across)
        copy.start()
        sends.append(copy)
    beside_work(units)
    chain.finish()
    for k in range(parts):
        span = pl.ds(k * size, size)
        here = pl.ds(pl.multiple_of((order[1] * 2 + c) * block + k * size, 16), size)
        cores[parts + k].wait_recv()
        sends[k].wait_recv()
        out[span, :] = acc[here, :] + from_core[1, span, :].astype(F32) + from_x[span, :].astype(F32)

    for t in range(2):

        @pl.when(t * 2 + x != me)
        def _():
            remote(moved.at[t], back.at[c], hs.at[t], hr.at[c], (seq, t * 2 + x)).wait_send()

    for k in range(nz):
        swap(k).wait_send()
    for t in range(1, nz):

        @pl.when(z + nz - t < nz)
        def _():
            remote(r_out.at[t - 1], r_got.at[t - 1], rs.at[t - 1], rr.at[t - 1], right).wait_send()

        @pl.when(z - nz + t >= 0)
        def _():
            remote(l_out.at[t - 1], l_got.at[t - 1], ls.at[t - 1], lr.at[t - 1], left).wait_send()

    for copy in cores + sends:
        copy.wait_send()
    joined_swap.wait()


def keys_back(cid, n, first, tiles, src, dq, q_raw, p_raw, cosine, sine, q_scale, p_scale, wq, wkv, pairs):
    bt, bty, dg, dgy = pairs
    nz = n // 2
    rows, width = dq.shape
    deep = wq.shape[0]
    block = rows // GROUP
    shape = src.shape[1:]
    chain = pltpu.VMEM((nz - 1,) + shape, BF16)
    joined = jax.ShapeDtypeStruct((rows, 2 * width), BF16)
    return comm_call(
        functools.partial(keys_back_kernel, n, first, tiles),
        cid,
        [
            joined,
            joined,
            jax.ShapeDtypeStruct((block, deep), F32),
            jax.ShapeDtypeStruct((8, width), F32),
            jax.ShapeDtypeStruct((bt.shape[2], tiles * TILE), F32),
        ]
        + gate_landing(nz, tiles, bt),
        [
            pltpu.VMEM((nz,) + shape, BF16), chain, chain, chain, chain, pltpu.VMEM(shape, BF16), pltpu.VMEM(shape, BF16),
            pltpu.VMEM((rows, deep), F32),
            pltpu.VMEM((2, block, deep), BF16),
            pltpu.VMEM((2, block, deep), BF16),
            pltpu.VMEM((block, deep), BF16),
            pltpu.VMEM((block, deep), BF16),
            DMA((nz,)), DMA((nz,)), DMA((nz - 1,)), DMA((nz - 1,)), DMA((nz - 1,)), DMA((nz - 1,)),
            DMA((2,)), DMA((2,)), DMA, DMA, DMA, DMA((2, 4)), DMA((2, 4)), DMA((4,)), DMA((4,)),
        ]
        + gate_scratch(nz, tiles, bt),
        [VMEM] * 10 + [ANY] * 4,
        [VMEM, ANY, VMEM, VMEM, ANY, ANY, ANY],
    )(src, dq, q_raw, p_raw, cosine, sine, q_scale, p_scale, wq, wkv, bt, bty, dg, dgy)


def finish_kernel(n, rounds, first, tiles, *refs):
    (whole, part, bt, bty, dg, dgy, ot, oty, gy, gyy, at, aty, joined, joined_y) = refs[:14]
    whole_out, part_out, gate_o, output_o, attention_o = refs[14:19]
    landing = refs[19:25]
    refs = refs[6:]
    bufs, gots, mine, theirs, ss, rs = refs[19:25]
    slabs, halves, slab_sem = refs[25:28]
    gate_refs, output_refs, attention_refs = refs[28:39], refs[39:50], refs[50:61]
    output_halves, attention_halves, half_sem = refs[61:]
    seq, me, x, c = place_now()
    nz = n // 2
    across = (seq, (1 - x) * 2 + c)
    beside = (seq, x * 2 + 1 - c)
    gates, loads = gate_chain(nz, first, tiles, seq, me, bt, bty, dg, dgy, gate_o, landing[:2], slabs, halves, slab_sem, gate_refs)
    for i, (ref, to) in enumerate(
        ((ot.at[:, seq % 2], output_halves.at[0]), (oty, output_halves.at[1]),
         (at.at[:, seq % 2], attention_halves.at[0]), (aty, attention_halves.at[1]))
    ):
        loads.append(pltpu.make_async_copy(ref, to, half_sem.at[i]))
    for load in loads:
        load.start()
    wide = joined.shape[1] // 2

    def output_partial(k, j):
        return dot(gy[...], output_halves[0, k]) + dot(gyy[...], output_halves[1, k])

    def attention_partial(k, j):
        cols = pl.ds(pl.multiple_of(j * wide, 128), wide)
        return dot(attention_halves[0, k], joined[:, cols]) + dot(attention_halves[1, k], joined_y[:, cols])

    def keep_output(j, stage, sem):
        return pltpu.make_async_copy(stage, output_o, sem)

    outputs = Chain(nz, 1, seq, me, output_partial, keep_output, landing[2:4], output_refs)
    attentions = Chain(
        nz,
        2,
        seq,
        me,
        attention_partial,
        lambda j, stage, sem: pltpu.make_async_copy(
            stage, attention_o.at[:, pl.ds(pl.multiple_of(j * wide, 128), wide)], sem
        ),
        landing[4:],
        attention_refs,
    )
    partners = []
    for r in range(rounds):
        bit = 1 << r
        partners.append((seq + bit - 2 * bit * ((seq // bit) % 2), me))
    greet([(lax.rem(seq + d, n), me) for d in range(1, n)] + [across, beside])
    for load in loads:
        load.wait()
    rows = whole.shape[0]
    bufs[0, :rows, :] = whole[...]
    bufs[0, rows:, :] = part[...]
    queues = [(chain, list(range(0, chain.units(), nz - 1))) for chain in (gates, outputs, attentions)]
    work = [(gates, u) for u in queues[0][1][:tiles]]
    rest = [queues[0][1][tiles:], queues[1][1], queues[2][1]]
    while any(rest):
        for (chain, _), left in zip(queues, rest):
            if left:
                work.append((chain, left.pop(0)))
    at_work = [0]

    def beside_work(count):
        todo = work[at_work[0] : at_work[0] + count]
        at_work[0] += count
        start = None
        for i, (chain, u) in enumerate(todo):
            if start is None:
                start = u
            if i + 1 == len(todo) or todo[i + 1][0] is not chain:
                chain.run(start, u + 3)
                start = None

    for r in range(rounds + 1):
        partner = partners[r] if r < rounds else across
        copy = remote(bufs.at[r], gots.at[r], ss.at[r], rs.at[r], partner)
        copy.start()
        beside_work(1)
        copy.wait()
        if r < rounds:
            bufs[r + 1] = bufs[r] + gots[r]
    mine[0, :rows, :] = bufs[rounds, :rows, :] + gots[rounds, :rows, :]
    mine[0, rows:, :] = bufs[rounds, rows:, :]
    mine[1, rows:, :] = gots[rounds, rows:, :]
    mine[1, :rows, :] = jnp.zeros((rows, 128), F32)
    copy = remote(mine, theirs, ss.at[rounds + 1], rs.at[rounds + 1], beside)
    copy.start()
    beside_work(len(work))
    copy.wait()
    whole_out[...] = mine[0, :rows, :] + theirs[0, :rows, :]
    part_out[x * 2 + c] = mine[0, rows:, :]
    part_out[(1 - x) * 2 + c] = mine[1, rows:, :]
    part_out[x * 2 + 1 - c] = theirs[0, rows:, :]
    part_out[(1 - x) * 2 + 1 - c] = theirs[1, rows:, :]
    gates.finish()
    outputs.finish()
    attentions.finish()


def finish(cid, n, first, tiles, whole, part, pairs, output_pairs, attention_pairs):
    bt, bty, dg, dgy = pairs
    ot, oty, gy, gyy = output_pairs
    at, aty, joined, joined_y = attention_pairs
    nz = n // 2
    rounds = int(math.log2(n))
    rows = whole.shape[0] + part.shape[0]
    output_shape = (gy.shape[0], ot.shape[3])
    attention_rows = at.shape[2]
    return comm_call(
        functools.partial(finish_kernel, n, rounds, first, tiles),
        cid,
        [
            jax.ShapeDtypeStruct(whole.shape, F32),
            jax.ShapeDtypeStruct((GROUP,) + part.shape, F32),
            jax.ShapeDtypeStruct((bt.shape[2], tiles * TILE), F32),
            jax.ShapeDtypeStruct(output_shape, F32),
            jax.ShapeDtypeStruct((attention_rows, joined.shape[1]), F32),
        ]
        + gate_landing(nz, tiles, bt)
        + Chain.landing(nz, 1, *output_shape)
        + Chain.landing(nz, 2, attention_rows, joined.shape[1] // 2),
        [
            pltpu.VMEM((rounds + 1, rows, 128), F32),
            pltpu.VMEM((rounds + 1, rows, 128), F32),
            pltpu.VMEM((2, rows, 128), F32),
            pltpu.VMEM((2, rows, 128), F32),
            DMA((rounds + 2,)),
            DMA((rounds + 2,)),
        ]
        + gate_scratch(nz, tiles, bt)
        + Chain.scratch(nz, 1, *output_shape)
        + Chain.scratch(nz, 2, attention_rows, joined.shape[1] // 2)
        + [
            pltpu.VMEM((2, nz) + ot.shape[2:], BF16),
            pltpu.VMEM((2, nz) + at.shape[2:], BF16),
            DMA((4,)),
        ],
        [VMEM] * 2 + [ANY] * 6 + [VMEM] * 2 + [ANY] * 2 + [VMEM] * 2,
        [VMEM, VMEM] + [ANY] * 9,
    )(whole, part, bt, bty, dg, dgy, ot, oty, gy, gyy, at, aty, joined, joined_y)


def rms_inverse(value):
    return lax.rsqrt(jnp.mean(value * value, axis=-1, keepdims=True) + EPSILON)


def norm_back(inverse, normed, upstream):
    return inverse * (upstream - normed * jnp.mean(upstream * normed, axis=-1, keepdims=True))


def rotate(value, cosine, sine):
    half = DH // 2
    first = value[..., :half]
    second = value[..., half:]
    return jnp.concatenate([first * cosine - second * sine, second * cosine + first * sine], axis=-1)


def core_swap(value):
    return lax.ppermute(value, "fsdp", [(f, f ^ 1) for f in range(GROUP)])


def lanes(value, rows):
    flat = value.reshape(-1)
    return jnp.pad(flat, (0, rows * 128 - flat.shape[0])).reshape(rows, 128)


def per_device(
    n,
    tokens,
    doc_ids,
    padding,
    token_order,
    query_code,
    key_value_code,
    output_code,
    gate_up_code,
    down_code,
    query_scale,
    key_value_scale,
    output_scale,
    gate_up_scale,
    down_scale,
    norm_gains,
    cotangent,
):
    me = lax.axis_index("fsdp")
    c = me % 2
    width = tokens.shape[2]
    part = width // GROUP
    rows = GROUP * tokens.shape[1]
    own = tokens.shape[1]

    def mine(vector):
        size = vector.shape[-1] // GROUP
        return lax.dynamic_slice_in_dim(vector, me * size, size, vector.ndim - 1)

    def blocks_to_rows(blocks):
        return jnp.concatenate([blocks[i] for i in range(GROUP)], axis=1)

    gain = 1.0 + norm_gains
    place = token_order[0].astype(F32)
    document = doc_ids[0].astype(F32)
    meta = jnp.stack([document, place, jnp.where(padding[0] == 1, document, -1.0)] + [document] * 5)

    def to_blocks(value):
        return value.reshape(own, GROUP, part).transpose(1, 0, 2)

    my_query_scale = mine(query_scale)
    my_pair_scale = mine(key_value_scale)
    token_cols = to_blocks(tokens[0])
    cot_cols = to_blocks(cotangent[0])
    rates = BASE ** (-2.0 * jnp.arange(DH // 2).astype(F32) / DH)
    (
        token_blocks, cot_blocks, own_meta, metas, pairs, query, query_raw, pair_raw, cosine, sine, first_turned
    ) = front(
        1,
        n,
        token_cols.reshape(rows, part),
        cot_cols.reshape(rows, part),
        meta,
        gain[0].reshape(GROUP, 1, part),
        rates[None],
        my_query_scale[None],
        my_pair_scale[None],
        query_code,
        key_value_code,
    )

    mixed_low, mixed, mass = attend(n, query, pairs, own_meta, metas)
    second_input, branch_own, my_middle, mixed_slices, second_turned = branch_forward(
        3,
        mixed_low,
        output_code.T,
        token_blocks,
        output_scale.reshape(GROUP, 1, part),
        gain[1].reshape(GROUP, 1, part),
        gain[2].reshape(GROUP, 1, part),
    )

    my_gate_scale = mine(gate_up_scale)
    columns = gate_up_code.shape[1]
    tiles = columns // TILE
    gate_scales = my_gate_scale.reshape(tiles, 1, TILE)
    (
        gate_up, hidden, hidden_y, down_blocks, grad_down, grad_down_turned, down_sums, gate_levels, down_levels, *riders
    ) = ffn_forward(
        5,
        second_input,
        gate_up_code,
        gate_scales,
        down_code.T,
        cot_blocks,
        gain[3].reshape(GROUP, 1, part),
        down_scale.reshape(GROUP, 1, part),
        [second_turned, mixed_slices, first_turned],
    )
    second_pair, mixed_pair, first_pair = zip((second_turned, mixed_slices, first_turned), riders)
    my_down = lax.dynamic_slice_in_dim(down_blocks, me * own, own, 1).astype(F32) * down_scale.reshape(GROUP, 1, part)
    down_inverse = lax.rsqrt(jnp.mean(my_down * my_down, axis=(0, 2), keepdims=True) + EPSILON)
    result = blocks_to_rows((my_middle + my_down * down_inverse * gain[3].reshape(GROUP, 1, part)).astype(BF16))
    tiles_zero, tiles_one, tiles_two = (2, 4, 4) if n == 8 else (0, 0, 0)
    tiles_three = tiles - tiles_zero - tiles_one - tiles_two
    grad_gate_up, grad_gate_up_y, _, gate_sums, grad_second_input, down_grad, gate_zero, *_ = ffn_backward(
        6,
        n,
        tiles_zero,
        grad_down,
        grad_down_turned,
        down_levels,
        gate_levels,
        gate_scales,
        gate_up,
        hidden,
        hidden_y,
        *second_pair,
    )
    if n == 8:
        down_grad = down_grad.T
    else:
        hidden_own = jnp.concatenate(
            [
                (jax.nn.gelu(gate_up[0, t].astype(F32)) * gate_up[1, t].astype(F32)).astype(BF16)
                for t in range(tiles)
            ],
            axis=1,
        )
        hidden_core = core_swap(hidden_own)
        hidden_rows = jnp.concatenate(
            [jnp.where(c == 0, hidden_own, hidden_core), jnp.where(c == 0, hidden_core, hidden_own)], axis=1
        )
        down_grad = lax.psum_scatter(
            contract_first(hidden_rows, grad_down), "seq", scatter_dimension=0, tiled=True
        )
    scale_down = down_sums[0]
    gain_four = down_sums[1]
    scale_gate = gate_sums[:, 0, :].reshape(columns) / my_gate_scale
    gate_pairs = second_pair + (grad_gate_up, grad_gate_up_y)
    grad_middle, branch_sums, grad_branch, grad_branch_y, grad_query, grad_pairs, gate_one, *_ = branch_back(
        7,
        n,
        tiles_zero,
        tiles_one,
        grad_second_input,
        my_middle,
        branch_own,
        cot_cols,
        gain[1].reshape(GROUP, 1, part),
        gain[2].reshape(GROUP, 1, part),
        output_scale.reshape(GROUP, 1, part),
        output_code.T,
        query,
        mixed,
        mass,
        own_meta,
        metas,
        pairs,
        gate_pairs,
    )
    grad_middle = blocks_to_rows(grad_middle)
    gain_two = branch_sums[:, 0].reshape(width)
    gain_three = branch_sums[:, 1].reshape(width)
    scale_output = branch_sums[:, 2].reshape(width)

    if n == 8:
        joined, joined_y, grad_first_input, key_sums, gate_two, *_ = keys_back(
            9,
            n,
            tiles_zero + tiles_one,
            tiles_two,
            grad_pairs,
            grad_query,
            query_raw,
            pair_raw,
            cosine,
            sine,
            my_query_scale[None],
            my_pair_scale[None],
            query_code,
            key_value_code,
            gate_pairs,
        )
        scale_query = key_sums[0]
        scale_pair = key_sums[1]
    else:
        is_key = me < 2
        pair_cosine = jnp.where(is_key, cosine, 1.0)
        pair_sine = jnp.where(is_key, sine, 0.0)
        grad_heads = keys_reduce(9, n, grad_pairs).astype(F32)
        grad_query_full = rotate(
            grad_query.reshape(rows, 2, DH), cosine[:, None], -sine[:, None]
        ).reshape(rows, 2 * DH)
        scale_query = jnp.sum(query_raw * grad_query_full, axis=0)
        grad_query_low = (grad_query_full * my_query_scale).astype(BF16)
        grad_pair_full = jnp.concatenate(
            [rotate(grad_heads[j], pair_cosine, -pair_sine) for j in range(2)], axis=1
        )
        scale_pair = jnp.sum(pair_raw * grad_pair_full, axis=0)
        grad_pair_low = (grad_pair_full * my_pair_scale).astype(BF16)
        joined = jnp.concatenate([grad_query_low, grad_pair_low], axis=1)
        grad_first_sum = contract_last(grad_query_low, query_code) + contract_last(grad_pair_low, key_value_code)
        grad_first_input = group_reduce(10, grad_first_sum.astype(BF16).reshape(GROUP, own, width), F32)
    my_inputs = tokens[0].astype(F32)
    my_inverse = rms_inverse(my_inputs)
    first = my_inputs * my_inverse
    gain_one = jnp.sum(grad_first_input * first, axis=0)
    grad_inputs = grad_middle + norm_back(my_inverse, first, grad_first_input * gain[0])

    wholes = lanes(jnp.concatenate([gain_one, gain_two, gain_three, scale_output]), 72)
    parts = [scale_query, scale_pair, scale_gate, scale_down, gain_four]
    part_rows = lanes(jnp.concatenate(parts), 56)
    if n == 8:
        whole_total, part_total, gate_three, output_grad, attention_grad, *_ = finish(
            11,
            n,
            tiles - tiles_three,
            tiles_three,
            wholes,
            part_rows,
            gate_pairs,
            mixed_pair + (grad_branch, grad_branch_y),
            first_pair + (joined, joined_y),
        )
        output_grad = output_grad.T
        gate_grad = jnp.concatenate([gate_zero, gate_one, gate_two, gate_three], axis=1)
    else:
        whole_total, part_total = totals(11, n, wholes, part_rows)

        def weight_sum(left, right):
            return lax.psum_scatter(dot(left.reshape(-1, rows), right), "seq", scatter_dimension=0, tiled=True)

        gate_grad = weight_sum(second_turned, grad_gate_up)
        output_grad = weight_sum(mixed_slices.transpose(0, 1, 3, 2), grad_branch.T)
        attention_grad = weight_sum(first_turned, joined)
    whole_total = whole_total.reshape(-1)
    part_total = part_total.reshape(GROUP, -1)
    pieces = []
    start = 0
    for vector in parts:
        pieces.append(part_total[:, start : start + vector.shape[0]].reshape(-1))
        start += vector.shape[0]
    q_width = query_code.shape[1]
    return (
        result[None],
        grad_inputs[None],
        attention_grad[:, :q_width],
        attention_grad[:, q_width:],
        output_grad,
        gate_grad,
        down_grad,
        pieces[0],
        pieces[1],
        whole_total[3 * width :],
        pieces[2],
        pieces[3],
        jnp.concatenate([whole_total[: 3 * width], pieces[4]]).reshape(4, width),
    )


def solution(mesh):
    return jax.shard_map(
        functools.partial(per_device, mesh.shape["seq"]),
        mesh=mesh,
        in_specs=(
            P("fsdp", "seq", None),
            P("fsdp", "seq"),
            P("fsdp", "seq"),
            P("fsdp", "seq"),
            P(None, "fsdp"),
            P(None, "fsdp"),
            P(None, "fsdp"),
            P(None, "fsdp"),
            P(None, "fsdp"),
            P(),
            P(),
            P(),
            P(),
            P(),
            P(),
            P("fsdp", "seq", None),
        ),
        out_specs=(
            P("fsdp", "seq", None),
            P("fsdp", "seq", None),
            P("seq", "fsdp"),
            P("seq", "fsdp"),
            P("seq", "fsdp"),
            P("seq", "fsdp"),
            P("seq", "fsdp"),
            P(),
            P(),
            P(),
            P(),
            P(),
            P(),
        ),
        check_vma=False,
    )
```

```python
import functools
import math

import jax
import jax.numpy as jnp
from jax import lax
from jax.experimental import pallas as pl
from jax.experimental.pallas import tpu as pltpu
from jax.sharding import PartitionSpec as P

HQ = 8
HK = 4
DH = 256
FF = 9216
GROUP = 4
TILE = 384
EPSILON = 1e-06
CAP = 50.0
BASE = 10000.0
VMEM_LIMIT = 60 * 1024 * 1024
MESH = pl.DeviceIdType.MESH
ANY = pl.BlockSpec(memory_space=pl.ANY)
VMEM = pl.BlockSpec(memory_space=pltpu.VMEM)
DMA = pltpu.SemaphoreType.DMA
F32 = jnp.float32
BF16 = jnp.bfloat16


def dot(left, right):
    return jnp.dot(left, right, preferred_element_type=F32)


def contract_last(left, right):
    return lax.dot_general(left, right, (((1,), (1,)), ((), ())), preferred_element_type=F32)


def contract_first(left, right):
    return lax.dot_general(left, right, (((0,), (0,)), ((), ())), preferred_element_type=F32)


def place_now():
    seq = lax.axis_index("seq")
    fsdp = lax.axis_index("fsdp")
    return seq, fsdp, fsdp // 2, fsdp % 2


def greet(peers):
    barrier = pltpu.get_barrier_semaphore()
    for peer in peers:
        pl.semaphore_signal(barrier, inc=1, device_id=peer, device_id_type=MESH)
    pl.semaphore_wait(barrier, len(peers))


def remote(src, dst, send, recv, peer):
    return pltpu.make_async_remote_copy(
        src_ref=src, dst_ref=dst, send_sem=send, recv_sem=recv, device_id=peer, device_id_type=MESH
    )


def comm_call(kernel, cid, out_shape, scratch, in_specs, out_specs):
    return pl.pallas_call(
        kernel,
        out_shape=out_shape,
        in_specs=in_specs,
        out_specs=out_specs,
        scratch_shapes=scratch,
        compiler_params=pltpu.CompilerParams(
            collective_id=cid, has_side_effects=True, vmem_limit_bytes=VMEM_LIMIT
        ),
    )


def group_reduce_kernel(parts, src, out, from_core, to_x, from_x, cs, cr, xs, xr):
    seq, me, x, c = place_now()
    across = (seq, (1 - x) * 2 + c)
    beside = (seq, x * 2 + 1 - c)
    greet([across, beside])
    rows = src.shape[1]
    step = rows // parts
    order = [1 - x, x]
    cores = []
    for i in range(2):
        for k in range(parts):
            span = pl.ds(k * step, step)
            copy = remote(
                src.at[order[i] * 2 + 1 - c, span], from_core.at[i, span], cs.at[i, k], cr.at[i, k], beside
            )
            copy.start()
            cores.append(copy)
    sends = []
    for k in range(parts):
        span = pl.ds(k * step, step)
        cores[k].wait_recv()
        to_x[span, :] = (
            src[order[0] * 2 + c, span, :].astype(F32) + from_core[0, span, :].astype(F32)
        ).astype(BF16)
        copy = remote(to_x.at[span], from_x.at[span], xs.at[k], xr.at[k], across)
        copy.start()
        sends.append(copy)
    for k in range(parts):
        span = pl.ds(k * step, step)
        cores[parts + k].wait_recv()
        sends[k].wait_recv()
        out[span, :] = (
            src[order[1] * 2 + c, span, :].astype(F32)
            + from_core[1, span, :].astype(F32)
            + from_x[span, :].astype(F32)
        ).astype(out.dtype)
    for copy in cores + sends:
        copy.wait_send()


def group_reduce(cid, value, dtype, parts=4):
    rows, width = value.shape[1:]
    return comm_call(
        functools.partial(group_reduce_kernel, parts),
        cid,
        jax.ShapeDtypeStruct((rows, width), dtype),
        [pltpu.VMEM((2, rows, width), BF16), pltpu.VMEM((rows, width), BF16), pltpu.VMEM((rows, width), BF16),
         DMA((2, parts)), DMA((2, parts)), DMA((parts,)), DMA((parts,))],
        [VMEM],
        VMEM,
    )(value)


def total_kernel(rounds, whole, part, whole_out, part_out, bufs, gots, mine, theirs, ss, rs):
    seq, me, x, c = place_now()
    across = (seq, (1 - x) * 2 + c)
    beside = (seq, x * 2 + 1 - c)
    partners = []
    for r in range(rounds):
        bit = 1 << r
        partners.append((seq + bit - 2 * bit * ((seq // bit) % 2), me))
    greet(partners + [across, beside])
    rows = whole.shape[0]
    bufs[0, :rows, :] = whole[...]
    bufs[0, rows:, :] = part[...]
    for r in range(rounds + 1):
        partner = partners[r] if r < rounds else across
        copy = remote(bufs.at[r], gots.at[r], ss.at[r], rs.at[r], partner)
        copy.start()
        copy.wait()
        if r < rounds:
            bufs[r + 1] = bufs[r] + gots[r]
    mine[0, :rows, :] = bufs[rounds, :rows, :] + gots[rounds, :rows, :]
    mine[0, rows:, :] = bufs[rounds, rows:, :]
    mine[1, rows:, :] = gots[rounds, rows:, :]
    mine[1, :rows, :] = jnp.zeros_like(whole)
    copy = remote(mine, theirs, ss.at[rounds + 1], rs.at[rounds + 1], beside)
    copy.start()
    copy.wait()
    whole_out[...] = mine[0, :rows, :] + theirs[0, :rows, :]
    part_out[x * 2 + c] = mine[0, rows:, :]
    part_out[(1 - x) * 2 + c] = mine[1, rows:, :]
    part_out[x * 2 + 1 - c] = theirs[0, rows:, :]
    part_out[(1 - x) * 2 + 1 - c] = theirs[1, rows:, :]


def totals(cid, n, whole, part):
    rounds = int(math.log2(n))
    rows = whole.shape[0] + part.shape[0]
    return comm_call(
        functools.partial(total_kernel, rounds),
        cid,
        [jax.ShapeDtypeStruct(whole.shape, F32), jax.ShapeDtypeStruct((GROUP,) + part.shape, F32)],
        [pltpu.VMEM((rounds + 1, rows, 128), F32), pltpu.VMEM((rounds + 1, rows, 128), F32),
         pltpu.VMEM((2, rows, 128), F32), pltpu.VMEM((2, rows, 128), F32),
         DMA((rounds + 2,)), DMA((rounds + 2,))],
        [VMEM, VMEM],
        [VMEM, VMEM],
    )(whole, part)


def turned(block, unit, to):
    half = to.shape[1]
    flat = contract_last(unit[...], block)
    to[0] = flat[:half].astype(BF16)
    to[1] = flat[half:].astype(BF16)


def fill_unit(unit):
    shape = unit.shape
    unit[...] = jnp.where(
        lax.broadcasted_iota(jnp.int32, shape, 0) == lax.broadcasted_iota(jnp.int32, shape, 1), 1.0, 0.0
    ).astype(BF16)


def front_kernel(n, *refs):
    tok, cot, meta, g1, rates, q_scale, p_scale, wq, wkv = refs[:9]
    toks, cots, own_meta, metas, out, q, q_raw, p_raw, cosine, sine, turned_o = refs[9:20]
    (tb, ab, wqs, wkvs, heads, om, unit, at,
     ws, txs, txr, tcs, tcr, tfs, tfr, gms, gmr, own_sem, hs, hr, ms, mr, rs, rr, ls, lr, ys, yr,
     xs, xr, cs, cr, fs, fr, os) = refs[20:]
    seq, me, x, c = place_now()
    y = seq % 2
    z = seq // 2
    nz = n // 2
    across = (seq, (1 - x) * 2 + c)
    beside = (seq, x * 2 + 1 - c)
    group = [(seq, lax.rem(me + d, GROUP)) for d in range(1, GROUP)]
    load_q = pltpu.make_async_copy(wq, wqs, ws.at[0])
    load_kv = pltpu.make_async_copy(wkv, wkvs, ws.at[1])
    load_q.start()
    load_kv.start()
    greet(group + [(lax.rem(seq + d, n), me) for d in range(1, n)])
    blk = tok.shape[0] // GROUP
    part = tok.shape[1]
    own = blk

    sends = []
    for k in range(GROUP):
        rows = pl.ds(k * blk, blk)
        copy = remote(tok.at[rows], tb.at[me, rows], txs.at[k], txr.at[k], across)
        copy.start()
        sends.append(copy)
    to_core = remote(tok, tb.at[me], tcs, tcr, beside)
    to_core.start()
    group_meta = []
    for d in range(1, GROUP):
        copy = remote(meta, om.at[me], gms.at[d - 1], gmr.at[d - 1], group[d - 1])
        copy.start()
        group_meta.append(copy)
    own_tok = pltpu.make_async_copy(tok, tb.at[me], own_sem.at[0])
    own_tok.start()
    own_row = pltpu.make_async_copy(meta, om.at[me], own_sem.at[1])
    own_row.start()
    fill_unit(unit)
    for copy in group_meta:
        copy.wait()
    own_row.wait()
    width = GROUP * part
    half = DH // 2
    js = range(GROUP)
    is_key = jnp.where(x == 0, 1.0, 0.0).astype(F32)

    def process(p):
        def norm(i, carry):
            span = lambda j: pl.ds(pl.multiple_of(j * blk + i * 32, 32), 32)
            values = [tb[p, span(j), :].astype(F32) for j in js]
            total = values[0] * values[0]
            for value in values[1:]:
                total = total + value * value
            inverse = lax.rsqrt(jnp.sum(total, axis=1, keepdims=True) * (1.0 / width) + EPSILON)
            to = pl.ds(pl.multiple_of(p * own + i * 32, 32), 32)
            for j in js:
                ab[j, to, :] = (values[j] * inverse * g1[j]).astype(BF16)
            return carry

        lax.fori_loop(0, blk // 32, norm, 0)
        rows = pl.ds(pl.multiple_of(p * own, 128), own)
        turn = jnp.broadcast_to(om[p, 1:2, :], (128, 128)).T * rates[...]
        cos = jnp.cos(turn)
        sin = jnp.sin(turn)
        cosine[rows, :] = cos
        sine[rows, :] = sin

        def product(weights):
            total = dot(ab[0, rows, :], weights[0:part, :])
            for j in range(1, GROUP):
                total = total + dot(ab[j, rows, :], weights[j * part : (j + 1) * part, :])
            return total

        plain = product(wqs)
        q_raw[rows, :] = plain
        plain = plain * q_scale[...]
        for h in range(2):
            one = plain[:, h * DH : h * DH + half]
            two = plain[:, h * DH + half : (h + 1) * DH]
            q[rows, h * DH : h * DH + half] = (one * cos - two * sin).astype(BF16)
            q[rows, h * DH + half : (h + 1) * DH] = (two * cos + one * sin).astype(BF16)
        cos = is_key * cos + (1.0 - is_key)
        sin = is_key * sin
        plain = product(wkvs)
        p_raw[rows, :] = plain
        plain = plain * p_scale[...]
        for h in range(2):
            one = plain[:, h * DH : h * DH + half]
            two = plain[:, h * DH + half : (h + 1) * DH]
            heads[h, rows, :half] = (one * cos - two * sin).astype(BF16)
            heads[h, rows, half:] = (two * cos + one * sin).astype(BF16)

    own_tok.wait()
    load_q.wait()
    load_kv.wait()
    process(me)
    to_core.wait_recv()
    process(x * 2 + 1 - c)
    forwards = []
    for k in range(GROUP):
        sends[k].wait_recv()
        got = tb.at[(1 - x) * 2 + c, pl.ds(k * blk, blk)]
        forward = remote(got, got, tfs.at[k], tfr.at[k], beside)
        forward.start()
        forwards.append(forward)
    process((1 - x) * 2 + c)
    for forward in forwards:
        forward.wait_recv()
    process((1 - x) * 2 + 1 - c)

    for j in range(2):
        target = c * 2 + j

        @pl.when(target == me)
        def _():
            pltpu.make_async_copy(heads.at[j], out.at[seq, x], own_sem.at[0]).start()

        @pl.when(target != me)
        def _():
            remote(heads.at[j], out.at[seq, x], hs.at[j], hr.at[x], (seq, target)).start()

    small = []
    for d in range(1, n):
        copy = remote(om, metas.at[seq], ms.at[d - 1], mr.at[d - 1], (lax.rem(seq + d, n), me))
        copy.start()
        small.append(copy)
    outs = [
        pltpu.make_async_copy(om, metas.at[seq], os.at[0]),
        pltpu.make_async_copy(om, own_meta, os.at[1]),
        pltpu.make_async_copy(tb, toks, os.at[2]),
    ]
    for copy in outs:
        copy.start()
    for t in range(2):
        source = t * 2 + x

        @pl.when(source == me)
        def _():
            pltpu.make_async_copy(heads.at[0], out.at[seq, t], own_sem.at[0]).wait()

        @pl.when(source != me)
        def _():
            remote(heads.at[0], out.at[seq, t], hs.at[0], hr.at[t], (seq, source)).wait_recv()

    def block(owner_z, owner_y):
        return out.at[owner_z * 2 + owner_y]

    right = (seq + 2, me)
    left = (seq - 2, me)
    beyond = (z * 2 + 1 - y, me)

    def to_y(owner_z):
        remote(block(owner_z, y), block(owner_z, y), ys.at[owner_z], yr.at[owner_z], beyond).start()

    parts = 2
    step = cot.shape[0] // parts
    for t in range(1, nz + 1):
        go_right = z - t + 1
        go_left = z + t - 1
        if t > 1:

            @pl.when(go_right >= 0)
            def _():
                remote(block(go_right, y), block(go_right, y), rs.at[t - 1], rr.at[t - 1], left).wait_recv()

            @pl.when(go_left < nz)
            def _():
                remote(block(go_left, y), block(go_left, y), ls.at[t - 1], lr.at[t - 1], right).wait_recv()

        if t < nz:

            @pl.when((go_right >= 0) & (z < nz - 1))
            def _():
                remote(block(go_right, y), block(go_right, y), rs.at[t], rr.at[t], right).start()

            @pl.when((go_left < nz) & (z > 0))
            def _():
                remote(block(go_left, y), block(go_left, y), ls.at[t], lr.at[t], left).start()

        @pl.when(go_right >= 0)
        def _():
            to_y(go_right)

        if t > 1:

            @pl.when(go_left < nz)
            def _():
                to_y(go_left)

        if t == 1:
            xcopies = []
            for k in range(parts):
                rows = pl.ds(k * step, step)
                copy = remote(cot.at[rows], cots.at[me, rows], xs.at[k], xr.at[k], across)
                copy.start()
                xcopies.append(copy)
            ccopy = remote(cot, cots.at[me], cs, cr, beside)
            ccopy.start()
            own_cot = pltpu.make_async_copy(cot, cots.at[me], os.at[3])
            own_cot.start()
            for j in js:
                turned(ab[j], unit, at.at[j])
            turned_out = pltpu.make_async_copy(at, turned_o, os.at[4])
            turned_out.start()
    later = []
    for k in range(parts):
        rows = pl.ds(k * step, step)
        xcopies[k].wait()
        got = cots.at[(1 - x) * 2 + c, rows]
        forward = remote(got, got, fs.at[k], fr.at[k], beside)
        forward.start()
        later.append(forward)
    for k in range(nz):
        remote(block(k, 1 - y), block(k, 1 - y), ys.at[k], yr.at[k], beyond).wait()
    for t in range(1, nz):

        @pl.when((z - t + 1 >= 0) & (z < nz - 1))
        def _():
            remote(block(z, y), block(z, y), rs.at[t], rr.at[t], right).wait_send()

        @pl.when((z + t - 1 < nz) & (z > 0))
        def _():
            remote(block(z, y), block(z, y), ls.at[t], lr.at[t], left).wait_send()

    for j in range(2):

        @pl.when(c * 2 + j != me)
        def _():
            remote(heads.at[j], out.at[seq, x], hs.at[j], hr.at[x], (seq, c * 2 + j)).wait_send()

    for copy in small + later + [ccopy]:
        copy.wait()
    for copy in sends + forwards + [to_core]:
        copy.wait_send()
    for copy in outs + [own_cot, turned_out]:
        copy.wait()


def front(cid, n, tok, cot, meta, g1, rates, q_scale, p_scale, wq, wkv):
    nz = n // 2
    rows, part = tok.shape
    own = rows // GROUP
    deep, wide = wq.shape
    blocks = jax.ShapeDtypeStruct((GROUP, rows, part), BF16)
    table = jax.ShapeDtypeStruct((rows, DH // 2), F32)
    raw = jax.ShapeDtypeStruct((rows, wide), F32)
    turned_shape = (GROUP, 2, part // 2, rows)
    return comm_call(
        functools.partial(front_kernel, n),
        cid,
        [
            blocks,
            blocks,
            jax.ShapeDtypeStruct((GROUP,) + meta.shape, F32),
            jax.ShapeDtypeStruct((n, GROUP) + meta.shape, F32),
            jax.ShapeDtypeStruct((n, 2, rows, DH), BF16),
            jax.ShapeDtypeStruct((rows, wide), BF16),
            raw,
            raw,
            table,
            table,
            jax.ShapeDtypeStruct(turned_shape, BF16),
        ],
        [
            pltpu.VMEM((GROUP, rows, part), BF16),
            pltpu.VMEM((GROUP, rows, part), BF16),
            pltpu.VMEM((deep, wide), BF16),
            pltpu.VMEM((deep, wide), BF16),
            pltpu.VMEM((2, rows, DH), BF16),
            pltpu.VMEM((GROUP,) + meta.shape, F32),
            pltpu.VMEM((part, part), BF16),
            pltpu.VMEM(turned_shape, BF16),
            DMA((2,)), DMA((GROUP,)), DMA((GROUP,)), DMA, DMA, DMA((GROUP,)), DMA((GROUP,)), DMA((GROUP - 1,)),
            DMA((GROUP - 1,)), DMA((2,)), DMA((2,)), DMA((2,)), DMA((n - 1,)), DMA((n - 1,)), DMA((nz,)), DMA((nz,)),
            DMA((nz,)), DMA((nz,)), DMA((nz,)), DMA((nz,)), DMA((2,)), DMA((2,)), DMA, DMA, DMA((2,)), DMA((2,)),
            DMA((5,)),
        ],
        [VMEM, ANY, VMEM, VMEM, VMEM, VMEM, VMEM, ANY, ANY],
        [ANY, ANY, ANY, ANY, ANY, VMEM, VMEM, VMEM, VMEM, VMEM, ANY],
    )(tok, cot, meta, g1, rates, q_scale, p_scale, wq, wkv)


def branch_kernel(low, wo, toks, scale, g2, g3, b_o, raw_o, mid_o, ot_o, bt_o, ob, pb, bb, acc, unit, bt,
                  xs, xr, cs, cr, fs, fr, gxs, gxr, gcs, gcr, gfs, gfr, local, os, hos):
    seq, me, x, c = place_now()
    across = (seq, (1 - x) * 2 + c)
    beside = (seq, x * 2 + 1 - c)
    greet([across, beside])
    rows, heads = low.shape
    part = pb.shape[2]
    parts = 4
    size = rows // parts
    own = rows // GROUP
    js = range(GROUP)

    def spot(owner, k):
        return ob.at[pl.ds(k * size, size), pl.ds(pl.multiple_of(owner * heads, 128), heads)]

    sends = []
    for k in range(parts):
        copy = remote(low.at[pl.ds(k * size, size)], spot(me, k), xs.at[k], xr.at[k], across)
        copy.start()
        sends.append(copy)
    mine = ob.at[:, pl.ds(pl.multiple_of(me * heads, 128), heads)]
    to_core = remote(low, mine, cs, cr, beside)
    to_core.start()
    own_copy = pltpu.make_async_copy(low, mine, local)
    own_copy.start()
    fill_unit(unit)

    def add(owner, start):
        cols = pl.ds(pl.multiple_of(owner * heads, 128), heads)
        more = contract_last(ob[:, cols], wo[:, cols])
        acc[...] = more if start else acc[...] + more

    own_copy.wait()
    add(me, True)
    to_core.wait_recv()
    add(x * 2 + 1 - c, False)
    forwards = []
    for k in range(parts):
        sends[k].wait_recv()
        got = spot((1 - x) * 2 + c, k)
        forward = remote(got, got, fs.at[k], fr.at[k], beside)
        forward.start()
        forwards.append(forward)
    add((1 - x) * 2 + c, False)
    for forward in forwards:
        forward.wait_recv()
    add((1 - x) * 2 + 1 - c, False)

    over = []
    core = []
    for k in range(parts):
        span = pl.ds(k * size, size)
        pb[me, span, :] = acc[span, :].astype(BF16)
        piece = pb.at[me, span]
        copy = remote(piece, piece, gxs.at[k], gxr.at[k], across)
        copy.start()
        over.append(copy)
        copy = remote(piece, piece, gcs.at[k], gcr.at[k], beside)
        copy.start()
        core.append(copy)
    head_outs = []
    for j in js:
        for i in range(2):
            cols = pl.ds(j * heads + i * (heads // 2), heads // 2)
            copy = pltpu.make_async_copy(ob.at[:, cols], ot_o.at[j, i], hos.at[j, i])
            copy.start()
            head_outs.append(copy)
    passed = []
    for k in range(parts):
        over[k].wait_recv()
        got = pb.at[(1 - x) * 2 + c, pl.ds(k * size, size)]
        forward = remote(got, got, gfs.at[k], gfr.at[k], beside)
        forward.start()
        passed.append(forward)
    for copy in core + passed:
        copy.wait_recv()
    mean = 1.0 / (GROUP * part)

    def rowsum(values):
        total = values[0] * values[0]
        for value in values[1:]:
            total = total + value * value
        return jnp.sum(total, axis=1, keepdims=True) * mean

    def norms(i, carry):
        pack = i // (own // 16)
        inner = i % (own // 16) * 16
        span = pl.ds(pl.multiple_of(i * 16, 16), 16)
        branch = [pb[j, span, :].astype(F32) * scale[j] for j in js]
        inverse = lax.rsqrt(rowsum(branch) + EPSILON)
        middle = [
            toks[pack, pl.ds(pl.multiple_of(j * own + inner, 16), 16), :].astype(F32) + branch[j] * inverse * g2[j]
            for j in js
        ]
        inverse = lax.rsqrt(rowsum(middle) + EPSILON)
        for j in js:
            bb[j, span, :] = (middle[j] * inverse * g3[j]).astype(BF16)

        @pl.when(pack == me)
        def _():
            for j in js:
                mid_o[j, pl.ds(pl.multiple_of(inner, 16), 16), :] = middle[j]

        return carry

    lax.fori_loop(0, rows // 16, norms, 0)
    b_out = pltpu.make_async_copy(bb, b_o, os.at[1])
    b_out.start()
    raw_out = pltpu.make_async_copy(pb.at[:, pl.ds(pl.multiple_of(me * own, 128), own)], raw_o, os.at[2])
    raw_out.start()
    for j in js:
        turned(bb[j], unit, bt.at[j])
    bt_out = pltpu.make_async_copy(bt, bt_o, os.at[3])
    bt_out.start()
    for copy in sends + forwards + over + core + passed + [to_core]:
        copy.wait_send()
    for copy in head_outs + [b_out, raw_out, bt_out]:
        copy.wait()


def branch_forward(cid, low, wo, toks, scale, g2, g3):
    rows, heads = low.shape
    part = wo.shape[0]
    own = rows // GROUP
    turned_b = (GROUP, 2, part // 2, rows)
    slices = (GROUP, 2, rows, heads // 2)
    four = DMA((4,))
    return comm_call(
        branch_kernel,
        cid,
        [
            jax.ShapeDtypeStruct((GROUP, rows, part), BF16),
            jax.ShapeDtypeStruct((GROUP, own, part), BF16),
            jax.ShapeDtypeStruct((GROUP, own, part), F32),
            jax.ShapeDtypeStruct(slices, BF16),
            jax.ShapeDtypeStruct(turned_b, BF16),
        ],
        [
            pltpu.VMEM((rows, GROUP * heads), BF16),
            pltpu.VMEM((GROUP, rows, part), BF16),
            pltpu.VMEM((GROUP, rows, part), BF16),
            pltpu.VMEM((rows, part), F32),
            pltpu.VMEM((part, part), BF16),
            pltpu.VMEM(turned_b, BF16),
            four, four, DMA, DMA, four, four, four, four, four, four, four, four, DMA, four, DMA((GROUP, 2)),
        ],
        [VMEM] * 6,
        [ANY, ANY, VMEM, ANY, ANY],
    )(low, wo, toks, scale, g2, g3)


def masks(n, own_ref, meta_ref):
    def column(row):
        return jnp.broadcast_to(own_ref[0, row : row + 1, :], (128, 128)).T

    row_document = column(0)
    row_place = column(1)
    out = []
    for j in range(n):
        key_place = meta_ref[j, 0, 1:2, :]
        key_document = meta_ref[j, 0, 2:3, :]
        allowed = (row_document == key_document) & (key_place <= row_place) | (key_place == row_place)
        out.append(allowed)
    return out


def attend_kernel(n, q_ref, kv_ref, own_ref, meta_ref, low_ref, mixed_ref, total_ref):
    keys = kv_ref[:, 0].reshape(n * 128, DH)
    values = kv_ref[:, 1].reshape(n * 128, DH)
    allowed = masks(n, own_ref, meta_ref)
    for h in range(2):
        cols = slice(h * DH, (h + 1) * DH)
        raw = contract_last(q_ref[:, cols], keys)
        pieces = []
        total = jnp.zeros((128, 128), F32)
        for j in range(n):
            squash = jnp.tanh(raw[:, j * 128 : (j + 1) * 128] * (DH ** (-0.5) / CAP))
            mass = jnp.where(allowed[j], jnp.exp(CAP * squash), 0.0)
            total = total + mass
            pieces.append(mass.astype(BF16))
        row = jnp.sum(total, axis=1, keepdims=True)
        mixed = dot(jnp.concatenate(pieces, axis=1), values) / row
        mixed_ref[:, cols] = mixed
        low_ref[:, cols] = mixed.astype(BF16)
        total_ref[:, h * 128 : (h + 1) * 128] = jnp.broadcast_to(row, (128, 128))


def attend(n, query, pairs, own_meta, metas):
    return pl.pallas_call(
        functools.partial(attend_kernel, n),
        grid=(GROUP,),
        out_shape=[
            jax.ShapeDtypeStruct(query.shape, BF16),
            jax.ShapeDtypeStruct(query.shape, F32),
            jax.ShapeDtypeStruct((query.shape[0], 256), F32),
        ],
        in_specs=[
            pl.BlockSpec((128, 2 * DH), lambda p: (p, 0)),
            pl.BlockSpec((n, 2, 128, DH), lambda p: (0, 0, p, 0)),
            pl.BlockSpec((1, 8, 128), lambda p: (p, 0, 0)),
            pl.BlockSpec((n, 1, 8, 128), lambda p: (0, p, 0, 0)),
        ],
        out_specs=[
            pl.BlockSpec((128, 2 * DH), lambda p: (p, 0)),
            pl.BlockSpec((128, 2 * DH), lambda p: (p, 0)),
            pl.BlockSpec((128, 256), lambda p: (p, 0)),
        ],
        compiler_params=pltpu.CompilerParams(vmem_limit_bytes=VMEM_LIMIT),
    )(query, pairs, own_meta, metas)


def back_pack(n, keys, values, allowed, q_ref, grad_ref, mixed_ref, total_ref, dq_ref, dkv_ref):
    grad_keys = None
    for h in range(2):
        cols = slice(h * DH, (h + 1) * DH)
        query = q_ref[:, cols]
        grad = grad_ref[:, cols]
        delta = jnp.sum(grad.astype(F32) * mixed_ref[:, cols], axis=1, keepdims=True)
        inverse = 1.0 / total_ref[:, h * 128 : (h + 1) * 128]
        raw = contract_last(query, keys)
        grad_share = contract_last(grad, values)
        shares = []
        grads = []
        for j in range(n):
            span = slice(j * 128, (j + 1) * 128)
            squash = jnp.tanh(raw[:, span] * (DH ** (-0.5) / CAP))
            share = jnp.where(allowed[j], jnp.exp(CAP * squash), 0.0) * inverse
            shares.append(share.astype(BF16))
            grads.append(
                (share * (grad_share[:, span] - delta) * ((1.0 - squash * squash) * DH ** (-0.5))).astype(BF16)
            )
        share = jnp.concatenate(shares, axis=1)
        grad_raw = jnp.concatenate(grads, axis=1)
        dq_ref[:, cols] = dot(grad_raw, keys)
        new_keys = contract_first(grad_raw, query)
        new_values = contract_first(share, grad)
        if grad_keys is None:
            grad_keys, grad_values = new_keys, new_values
        else:
            grad_keys, grad_values = grad_keys + new_keys, grad_values + new_values
    dkv_ref[:, :, 0] = grad_keys.astype(BF16).reshape(n // 2, 2, 128, DH)
    dkv_ref[:, :, 1] = grad_values.astype(BF16).reshape(n // 2, 2, 128, DH)


class Chain:
    def __init__(self, nz, count, seq, me, partial, keep, landing, scratch):
        self.nz, self.count, self.partial, self.keep = nz, count, partial, keep
        self.z = seq // 2
        self.right, self.left = (seq + 2, me), (seq - 2, me)
        self.got_r, self.got_l = landing
        (self.out_r, self.out_l, self.in_r, self.in_l, self.stage, self.ss_r, self.sr_r, self.ss_l, self.sr_l,
         self.keep_sem, self.load_sem) = scratch

    @staticmethod
    def landing(nz, count, rows, width):
        return [jax.ShapeDtypeStruct((count, nz - 1, rows, width), BF16)] * 2

    @staticmethod
    def scratch(nz, count, rows, width):
        hops = nz - 1
        message = (rows, width)
        sems = DMA((count, hops))
        return [
            pltpu.VMEM((hops,) + message, BF16), pltpu.VMEM((hops,) + message, BF16),
            pltpu.VMEM(message, BF16), pltpu.VMEM(message, BF16),
            pltpu.VMEM((2,) + message, F32), sems, sems, sems, sems, DMA((2,)), DMA((2,)),
        ]

    def copy_right(self, j, s, peer):
        return remote(
            self.out_r.at[s - 1], self.got_r.at[j, s - 1], self.ss_r.at[j, s - 1], self.sr_r.at[j, s - 1], peer
        )

    def copy_left(self, j, s, peer):
        return remote(
            self.out_l.at[s - 1], self.got_l.at[j, s - 1], self.ss_l.at[j, s - 1], self.sr_l.at[j, s - 1], peer
        )

    def load_right(self, j, s):
        return pltpu.make_async_copy(self.got_r.at[j, s - 1], self.in_r, self.load_sem.at[0])

    def load_left(self, j, s):
        return pltpu.make_async_copy(self.got_l.at[j, s - 1], self.in_l, self.load_sem.at[1])

    def step(self, j, s):
        z, nz = self.z, self.nz

        def one(go, copy, load, out, into, to, source, first):
            more = (s > 1) & jnp.logical_not(first)

            @pl.when(more)
            def _():
                copy(j, s - 1, source).wait_recv()
                load(j, s - 1).start()

            @pl.when(j > 0)
            def _():
                copy(j - 1, s, to).wait_send()

            total = self.partial(go, j)

            @pl.when(more)
            def _():
                load(j, s - 1).wait()
                out[s - 1] = (total + into[...].astype(F32)).astype(BF16)

            @pl.when(jnp.logical_not(more))
            def _():
                out[s - 1] = total.astype(BF16)

            copy(j, s, to).start()

        go_right = z + nz - s
        go_left = z - nz + s

        @pl.when(go_right < nz)
        def _():
            one(go_right, self.copy_right, self.load_right, self.out_r, self.in_r, self.right, self.left, z == 0)

        @pl.when(go_left >= 0)
        def _():
            one(go_left, self.copy_left, self.load_left, self.out_l, self.in_l, self.left, self.right, z == nz - 1)

    def end(self, j):
        z, nz = self.z, self.nz
        k = j % 2

        @pl.when(j >= 2)
        def _():
            self.keep(j - 2, self.stage.at[k], self.keep_sem.at[k]).wait()

        @pl.when(z > 0)
        def _():
            self.copy_right(j, nz - 1, self.left).wait_recv()
            self.load_right(j, nz - 1).start()

        @pl.when(z < nz - 1)
        def _():
            self.copy_left(j, nz - 1, self.right).wait_recv()
            self.load_left(j, nz - 1).start()

        self.stage[k] = self.partial(z, j)

        @pl.when(z > 0)
        def _():
            self.load_right(j, nz - 1).wait()
            self.stage[k] += self.in_r[...].astype(F32)

        @pl.when(z < nz - 1)
        def _():
            self.load_left(j, nz - 1).wait()
            self.stage[k] += self.in_l[...].astype(F32)

        self.keep(j, self.stage.at[k], self.keep_sem.at[k]).start()

    def run(self, first, last):
        hops = self.nz - 1

        def unit(u, carry):
            slot = u // hops
            s = u % hops + 1
            j = slot - (s - 1)

            @pl.when((j >= 0) & (j < self.count))
            def _():
                self.step(j, s)

            @pl.when((s == hops) & (slot >= hops))
            def _():
                self.end(slot - hops)

            return carry

        lax.fori_loop(first, last, unit, 0)

    def units(self):
        return (self.count + self.nz - 1) * (self.nz - 1)

    def finish(self):
        z, nz = self.z, self.nz
        last = self.count - 1
        for j in range(max(0, last - 1), last + 1):
            self.keep(j, self.stage.at[j % 2], self.keep_sem.at[j % 2]).wait()
        for s in range(1, nz):

            @pl.when(z + nz - s < nz)
            def _():
                self.copy_right(last, s, self.right).wait_send()

            @pl.when(z - nz + s >= 0)
            def _():
                self.copy_left(last, s, self.left).wait_send()


def greet_all(seq, me, nz, others):
    z = seq // 2
    barrier = pltpu.get_barrier_semaphore()
    for peer in others + [(seq + 1 - 2 * (seq % 2), me)]:
        pl.semaphore_signal(barrier, inc=1, device_id=peer, device_id_type=MESH)

    @pl.when(z > 0)
    def _():
        pl.semaphore_signal(barrier, inc=1, device_id=(seq - 2, me), device_id_type=MESH)

    @pl.when(z < nz - 1)
    def _():
        pl.semaphore_signal(barrier, inc=1, device_id=(seq + 2, me), device_id_type=MESH)

    pl.semaphore_wait(barrier, len(others) + 1 + jnp.where(z > 0, 1, 0) + jnp.where(z < nz - 1, 1, 0))


def gate_chain(nz, first, count, seq, me, bt, bty, dg, dgy, out, landing, slabs, halves, slab_sem, scratch):
    loads = [pltpu.make_async_copy(bt.at[:, seq % 2], halves.at[0], slab_sem.at[2])]
    loads.append(pltpu.make_async_copy(bty, halves.at[1], slab_sem.at[3]))
    for i, ref in enumerate((dg, dgy)):
        loads.append(
            pltpu.make_async_copy(ref.at[:, pl.ds(first * TILE, count * TILE)], slabs.at[i], slab_sem.at[i])
        )

    def partial(k, j):
        cols = pl.ds(pl.multiple_of(j * TILE, 128), TILE)
        return dot(halves[0, k], slabs[0, :, cols]) + dot(halves[1, k], slabs[1, :, cols])

    def keep(j, stage, sem):
        return pltpu.make_async_copy(stage, out.at[:, pl.ds(pl.multiple_of(j * TILE, 128), TILE)], sem)

    return Chain(nz, count, seq, me, partial, keep, landing, scratch), loads


def gate_landing(nz, count, bt):
    return Chain.landing(nz, count, bt.shape[2], TILE)


def gate_scratch(nz, count, bt):
    rows = bt.shape[3]
    return [
        pltpu.VMEM((2, rows, count * TILE), BF16), pltpu.VMEM((2, nz) + bt.shape[2:], BF16), DMA((4,))
    ] + Chain.scratch(nz, count, bt.shape[2], TILE)


def levels(code, step):
    return (jnp.floor(code.astype(F32) * (1.0 / step)) * step + step / 2.0).astype(BF16)


def gelu_parts(gate):
    root = math.sqrt(2.0 / math.pi)
    square = gate * gate
    bend = jnp.tanh(root * gate * (1.0 + 0.044715 * square))
    value = 0.5 * gate * (1.0 + bend)
    slope = 0.5 * (1.0 + bend) + 0.5 * gate * (1.0 - bend * bend) * root * (1.0 + 3 * 0.044715 * square)
    return value, slope


def strips(count, size, body):
    def step(i, carry):
        body(pl.ds(pl.multiple_of(i * size, size), size))
        return carry

    lax.fori_loop(0, count, step, 0)


def ffn_forward_kernel(tiles, riders, *refs):
    b, wgu, gs, wd, cots, g3, ds = refs[:7]
    refs = refs[7:]
    rider_in, refs = refs[:riders], refs[riders:]
    gu_o, hid_o, hidy_o, down_o, gf_o, gft_o, sums_o, lev_o, levd_o = refs[:9]
    refs = refs[9:]
    rider_out, refs = refs[:riders], refs[riders:]
    (both, hid, unit, wbuf, wlev, dbuf, dlev, acc, downs, wsem, dsem, lsem, ldsem, osem, xs, xr, oks, hs, hr, ks,
     ys, yr, fs, fr, gxs, gxr, gcs, gcr, gfs, gfr, rs, rr, outs) = refs
    seq, me, x, c = place_now()
    y = seq % 2
    across = (seq, (1 - x) * 2 + c)
    beside = (seq, x * 2 + 1 - c)
    beyond = (seq + 1 - 2 * y, me)
    rows, tw = both.shape[2:]
    part = b.shape[2]
    deep = GROUP * part
    per = tiles // 4

    def load_up(t):
        return pltpu.make_async_copy(wgu.at[:, pl.ds(pl.multiple_of(t * tw, 128), tw)], wbuf.at[t % 2], wsem.at[t % 2])

    def load_down(t, half):
        start = ((c + half) % 2 * tiles + t) * tw
        return pltpu.make_async_copy(
            wd.at[:, pl.ds(pl.multiple_of(start, 128), tw)], dbuf.at[t % 2, half], dsem.at[t % 2, half]
        )

    load_up(0).start()
    load_up(1).start()
    for t in range(2):
        for half in range(2):
            load_down(t, half).start()
    greet([across, beside, beyond])
    travellers = []
    for i in range(riders):
        share = pl.ds(2 * c, 2)
        copy = remote(rider_in[i].at[share, 1 - y], rider_out[i].at[share], rs.at[i, 0], rr.at[i, 0], beyond)
        copy.start()
        got = rider_out[i].at[share]
        travellers.append((copy, remote(got, got, rs.at[i, 1], rr.at[i, 1], beside)))
    acc[...] = jnp.zeros_like(acc)
    fill_unit(unit)

    def to_x(t):
        return remote(both.at[t % 3, x], gu_o.at[x, t], xs.at[t], xr.at[t], across)

    def from_x(t):
        return remote(both.at[t % 3, x], gu_o.at[1 - x, t], xs.at[t], xr.at[t], across)

    def keep_own(t):
        return pltpu.make_async_copy(both.at[t % 3, x], gu_o.at[x, t], oks.at[t])

    def load_other(t):
        return pltpu.make_async_copy(gu_o.at[1 - x, t], both.at[t % 3, 1 - x], osem.at[t % 2])

    def keep_level(t):
        return pltpu.make_async_copy(wlev.at[t % 2], lev_o.at[t], lsem.at[t % 2])

    def keep_down(t, half):
        return pltpu.make_async_copy(dlev.at[t % 2, half], levd_o.at[half, t], ldsem.at[t % 2, half])

    def to_core(t):
        return remote(hid.at[c * tiles + t], hid.at[c * tiles + t], hs.at[t], hr.at[t], beside)

    def slot(t, core):
        return (2 * core + t // (2 * per)) * per + t % per

    def keep(t, core, i):
        return pltpu.make_async_copy(hid.at[core * tiles + t], hid_o.at[slot(t, core)], ks.at[i, t])

    def to_y(t):
        return remote(hid.at[c * tiles + t], hidy_o.at[slot(t, c)], ys.at[t], yr.at[t], beyond)

    def for_mine(t):
        return (t // per) % 2 == y

    def wide(t):
        load_up(t).wait()

        @pl.when(t >= 2)
        def _():
            keep_level(t - 2).wait()

        def level(span):
            wlev[t % 2, span, :] = levels(wbuf[t % 2, span, :], 16.0)

        strips(deep // 128, 128, level)
        keep_level(t).start()

        @pl.when(t + 2 < tiles)
        def _():
            load_up(t + 2).start()

        @pl.when(t >= 3)
        def _():
            to_x(t - 3).wait_send()
            keep_own(t - 3).wait()

        scale = gs[t]

        def product(span):
            total = dot(b[0, span, :], wlev[t % 2, 0:part, :])
            for j in range(1, GROUP):
                total = total + dot(b[j, span, :], wlev[t % 2, j * part : (j + 1) * part, :])
            both[t % 3, x, span, :] = (total * scale).astype(BF16)

        strips(rows // 256, 256, product)
        to_x(t).start()
        keep_own(t).start()

    def arrive(t):
        from_x(t).wait_recv()
        load_other(t).start()

    def middle(t):
        load_other(t).wait()

        def body(span):
            gate = both[t % 3, 0, span, :].astype(F32)
            up = both[t % 3, 1, span, :].astype(F32)
            hid[c * tiles + t, span, :] = (gelu_parts(gate)[0] * up).astype(BF16)

        strips(rows // 64, 64, body)
        to_core(t).start()

        @pl.when(for_mine(t))
        def _():
            keep(t, c, 0).start()

        @pl.when(jnp.logical_not(for_mine(t)))
        def _():
            to_y(t).start()

    def narrow(t):
        for half in range(2):
            load_down(t, half).wait()

            @pl.when(t >= 2)
            def _():
                keep_down(t - 2, half).wait()

            def level(span):
                dlev[t % 2, half, span, :] = levels(dbuf[t % 2, half, span, :], 64.0)

            strips(part // 64, 64, level)
            keep_down(t, half).start()

            @pl.when(t + 2 < tiles)
            def _():
                load_down(t + 2, half).start()

        to_core(t).wait_recv()

        def product(span):
            acc[span, :] += contract_last(hid[c * tiles + t, span, :], dlev[t % 2, 0]) + contract_last(
                hid[(1 - c) * tiles + t, span, :], dlev[t % 2, 1]
            )

        strips(rows // 256, 256, product)

        @pl.when(for_mine(t))
        def _():
            keep(t, 1 - c, 1).start()

    def step(i, carry):
        @pl.when(i < tiles)
        def _():
            wide(i)

        @pl.when((i >= 1) & (i < tiles + 1))
        def _():
            arrive(i - 1)

        @pl.when(i >= 2)
        def _():
            narrow(i - 2)

        @pl.when((i >= 1) & (i < tiles + 1))
        def _():
            middle(i - 1)

        return carry

    lax.fori_loop(0, tiles + 2, step, 0)

    for copy, forward in travellers:
        copy.wait_recv()
        forward.start()
    parts = 4
    size = rows // parts
    sends = []
    own_sends = []
    for k in range(parts):
        span = pl.ds(k * size, size)
        downs[me, span, :] = acc[span, :].astype(BF16)
        piece = downs.at[me, span]
        copy = remote(piece, piece, gxs.at[k], gxr.at[k], across)
        copy.start()
        sends.append(copy)
        copy = remote(piece, piece, gcs.at[k], gcr.at[k], beside)
        copy.start()
        own_sends.append(copy)

    def pass_on(t, carry):
        @pl.when(for_mine(t))
        def _():
            got = hidy_o.at[slot(t, c)]
            remote(hid.at[0], got, ys.at[t], yr.at[t], beyond).wait_recv()
            remote(got, got, fs.at[t], fr.at[t], beside).start()

        return carry

    lax.fori_loop(0, tiles, pass_on, 0)
    forwards = []
    for k in range(parts):
        sends[k].wait_recv()
        got = downs.at[(1 - x) * 2 + c, pl.ds(k * size, size)]
        copy = remote(got, got, gfs.at[k], gfr.at[k], beside)
        copy.start()
        forwards.append(copy)
    for copy in own_sends + forwards:
        copy.wait_recv()
    down_out = pltpu.make_async_copy(downs, down_o, outs)
    down_out.start()
    sums_o[...] = jnp.zeros_like(sums_o)
    width = GROUP * acc.shape[1]

    def last_norm(i, carry):
        pack = i // 2
        span = pl.ds(pl.multiple_of(i * 64, 64), 64)
        inner = (i % 2) * 64

        def cot_of(j):
            return cots[pack, pl.ds(pl.multiple_of(j * 128 + inner, 64), 64), :].astype(F32)

        square = jnp.zeros((64, 1), F32)
        cross = jnp.zeros((64, 1), F32)
        for j in range(GROUP):
            value = downs[j, span, :].astype(F32) * ds[j]
            square = square + jnp.sum(value * value, axis=1, keepdims=True)
            cross = cross + jnp.sum(value * (cot_of(j) * g3[j]), axis=1, keepdims=True)
        inverse = lax.rsqrt(square * (1.0 / width) + EPSILON)
        raw = downs[me, span, :].astype(F32)
        normed = raw * ds[me] * inverse
        cot = cot_of(me)
        grad = inverse * (cot * g3[me] - normed * (cross * inverse * (1.0 / width)))
        gf_o[span, :] = (grad * ds[me]).astype(BF16)
        sums_o[0:1, :] += jnp.sum(raw * grad, axis=0, keepdims=True)
        sums_o[1:2, :] += jnp.sum(cot * normed, axis=0, keepdims=True)
        return carry

    lax.fori_loop(0, rows // 64, last_norm, 0)
    gft_o[...] = contract_last(unit[...], gf_o[...]).astype(BF16)

    for t in range(tiles - 3, tiles):
        to_x(t).wait_send()
        keep_own(t).wait()
    for t in range(tiles - 2, tiles):
        keep_level(t).wait()
        for half in range(2):
            keep_down(t, half).wait()

    def drain(t, carry):
        to_core(t).wait_send()

        @pl.when(for_mine(t))
        def _():
            keep(t, c, 0).wait()
            keep(t, 1 - c, 1).wait()
            got = hidy_o.at[slot(t, c)]
            remote(got, got, fs.at[t], fr.at[t], beside).wait_send()
            got = hidy_o.at[slot(t, 1 - c)]
            remote(got, got, fs.at[t], fr.at[t], beside).wait_recv()

        @pl.when(jnp.logical_not(for_mine(t)))
        def _():
            to_y(t).wait_send()

        return carry

    lax.fori_loop(0, tiles, drain, 0)
    for copy in sends + own_sends + forwards:
        copy.wait_send()
    for copy, forward in travellers:
        copy.wait_send()
        forward.wait()
    down_out.wait()


def ffn_forward(cid, b, wgu, gs, wd, cots, g3, ds, riders):
    rows, part = b.shape[1:]
    deep = GROUP * part
    tiles, _, tw = gs.shape
    count = len(riders)
    lone = max(count, 1)
    each = DMA((tiles,))
    four = DMA((4,))
    return comm_call(
        functools.partial(ffn_forward_kernel, tiles, count),
        cid,
        [
            jax.ShapeDtypeStruct((2, tiles, rows, tw), BF16),
            jax.ShapeDtypeStruct((tiles, rows, tw), BF16),
            jax.ShapeDtypeStruct((tiles, rows, tw), BF16),
            jax.ShapeDtypeStruct((GROUP, rows, part), BF16),
            jax.ShapeDtypeStruct((rows, part), BF16),
            jax.ShapeDtypeStruct((part, rows), BF16),
            jax.ShapeDtypeStruct((8, part), F32),
            jax.ShapeDtypeStruct((tiles, deep, tw), BF16),
            jax.ShapeDtypeStruct((2, tiles, part, tw), BF16),
        ]
        + [jax.ShapeDtypeStruct(r.shape[:1] + r.shape[2:], r.dtype) for r in riders],
        [
            pltpu.VMEM((3, 2, rows, tw), BF16),
            pltpu.VMEM((2 * tiles, rows, tw), BF16),
            pltpu.VMEM((part, part), BF16),
            pltpu.VMEM((2, deep, tw), BF16),
            pltpu.VMEM((2, deep, tw), BF16),
            pltpu.VMEM((2, 2, part, tw), BF16),
            pltpu.VMEM((2, 2, part, tw), BF16),
            pltpu.VMEM((rows, part), F32),
            pltpu.VMEM((GROUP, rows, part), BF16),
            DMA((2,)), DMA((2, 2)), DMA((2,)), DMA((2, 2)), DMA((2,)), each, each, each, each, each, DMA((2, tiles)),
            each, each, each, each, four, four, four, four, four, four, DMA((lone, 2)), DMA((lone, 2)), DMA,
        ],
        [VMEM, ANY, VMEM, ANY, VMEM, VMEM, VMEM] + [ANY] * count,
        [ANY, ANY, ANY, ANY, VMEM, VMEM, VMEM, ANY, ANY] + [ANY] * count,
    )(b, wgu, gs, wd, cots, g3, ds, *riders)


def ffn_backward_kernel(tiles, nz, chained, gate_tiles, *refs):
    gf, gft, levd, lev, gs, gu, hid, hidy, bt, bty = refs[:10]
    dg_o, dgy_o, gsum_o, out, ddown_o, gate_o = refs[10:16]
    landing = refs[16:20] if chained else []
    refs = refs[len(landing) :]
    (hh, hy, gfy, wbuf, dbuf, pair, co, cgot, near, sx, xgot, dg, acc, low, from_core, to_xb, from_x,
     hsem, wsem, dsem, psem, cs, cr, xs, xr, ys, yr, os, gys, gyr, ccs, ccr, cxs, cxr) = refs[16:50]
    rest = refs[50:]
    seq, me, x, c = place_now()
    y = seq % 2
    across = (seq, (1 - x) * 2 + c)
    beside = (seq, x * 2 + 1 - c)
    beyond = (seq + 1 - 2 * y, me)
    rows, tw = dg.shape[1:]
    part = acc.shape[2]
    per = hid.shape[0] // 4 if chained else 0
    ring = dg.shape[0]

    def load_up(t):
        return pltpu.make_async_copy(lev.at[t], wbuf.at[t % 2], wsem.at[t % 2])

    def load_down(t, half):
        return pltpu.make_async_copy(levd.at[half, t], dbuf.at[t % 2, half], dsem.at[t % 2, half])

    def load_pair(t):
        return pltpu.make_async_copy(gu.at[:, t], pair.at[t % 2], psem.at[t % 2])

    for t in range(2):
        for half in range(2):
            load_down(t, half).start()
        load_pair(t).start()
        load_up(t).start()
    if chained:
        load_hid = pltpu.make_async_copy(hid, hh, hsem.at[0])
        load_hidy = pltpu.make_async_copy(hidy, hy, hsem.at[1])
        load_hid.start()
        load_hidy.start()

        def partial(k, j):
            return dot(gft[...], hh[k * per + j]) + dot(gfy[...], hy[k * per + j])

        def keep_sum(j, stage, sem):
            return pltpu.make_async_copy(stage, ddown_o.at[:, pl.ds(pl.multiple_of(j * tw, 128), tw)], sem)

        downs = Chain(nz, per, seq, me, partial, keep_sum, landing[:2], rest[:11])
        gates, gate_loads = gate_chain(
            nz, 0, gate_tiles, seq, me, bt, bty, dg_o, dgy_o, gate_o, landing[2:], *rest[11:14], rest[14:]
        )
        gate_loads[0].start()
        gate_loads[1].start()
        greet_all(seq, me, nz, [across, beside])
        gf_swap = remote(gft, gfy, gys, gyr, beyond)
        gf_swap.start()
    else:
        greet([across, beside, beyond])
    acc[...] = jnp.zeros_like(acc)

    def to_core(t):
        return remote(co.at[t % 2], cgot.at[t % 4], cs.at[t], cr.at[t], beside)

    def to_x(t):
        return remote(sx.at[t % 4], xgot.at[t], xs.at[t], xr.at[t], across)

    def columns(ref, t):
        return ref.at[:, pl.ds(pl.multiple_of(t * tw, 128), tw)]

    def to_y(t):
        return remote(dg.at[t % ring], columns(dgy_o, t), ys.at[t], yr.at[t], beyond)

    def keep(t):
        return pltpu.make_async_copy(dg.at[t % ring], columns(dg_o, t), os.at[t])

    def hidden(t):
        for half in range(2):
            load_down(t, half).wait()

        @pl.when(t >= 2)
        def _():
            to_core(t - 2).wait_send()

        def product(span):
            co[t % 2, span, :] = dot(gf[span, :], dbuf[t % 2, 1]).astype(BF16)

        strips(rows // 256, 256, product)
        to_core(t).start()

        def product_near(span):
            near[t % 2, span, :] = dot(gf[span, :], dbuf[t % 2, 0])

        strips(rows // 256, 256, product_near)

        @pl.when(t + 2 < tiles)
        def _():
            for half in range(2):
                load_down(t + 2, half).start()

    def chip(t):
        @pl.when(t >= 4)
        def _():
            to_x(t - 4).wait_send()

        to_core(t).wait_recv()

        def body(span):
            sx[t % 4, span, :] = (near[t % 2, span, :] + cgot[t % 4, span, :].astype(F32)).astype(BF16)

        strips(rows // 64, 64, body)
        to_x(t).start()

    is_gate = jnp.where(x == 0, 1.0, 0.0).astype(F32)

    def own(t):
        load_pair(t).wait()

        @pl.when(t >= ring)
        def _():
            to_y(t - ring).wait_send()
            keep(t - ring).wait()

        to_x(t).wait_recv()
        scale = gs[t]
        gsum_o[t] = jnp.zeros((8, tw), F32)

        def body(span):
            grad = sx[t % 4, span, :].astype(F32) + xgot[t, span, :].astype(F32)
            gate = pair[t % 2, 0, span, :].astype(F32)
            up = pair[t % 2, 1, span, :].astype(F32)
            value, slope = gelu_parts(gate)
            full = grad * (is_gate * (up * slope) + (1.0 - is_gate) * value)
            gsum_o[t, 0:1, :] += jnp.sum(pair[t % 2, x, span, :].astype(F32) * full, axis=0, keepdims=True)
            dg[t % ring, span, :] = (full * scale).astype(BF16)

        strips(rows // 64, 64, body)

        @pl.when(t + 2 < tiles)
        def _():
            load_pair(t + 2).start()

        to_y(t).start()
        keep(t).start()

    def back(t):
        load_up(t).wait()

        def product(span):
            for j in range(GROUP):
                acc[j, span, :] += contract_last(dg[t % ring, span, :], wbuf[t % 2, j * part : (j + 1) * part, :])

        strips(rows // 128, 128, product)

        @pl.when(t + 2 < tiles)
        def _():
            load_up(t + 2).start()

    def units(chain, i, table):
        unit = jnp.int32(0)
        hit = i < 0
        for when, u in table:
            unit = unit + jnp.where(i == when, u, 0)
            hit = hit | (i == when)

        @pl.when(hit)
        def _():
            chain.run(unit, unit + 1)

    def step(i, carry):
        @pl.when(i < tiles)
        def _():
            hidden(i)

        @pl.when((i >= 1) & (i < tiles + 1))
        def _():
            chip(i - 1)

        if chained:

            @pl.when(i == 1)
            def _():
                gf_swap.wait_recv()
                load_hid.wait()
                load_hidy.wait()

            @pl.when(i == 9)
            def _():
                for t in range(gate_tiles):
                    to_y(t).wait_recv()
                gate_loads[2].start()
                gate_loads[3].start()

            @pl.when(i == 10)
            def _():
                for load in gate_loads:
                    load.wait()

            units(downs, i, ((1, 0), (2, 3), (3, 4), (4, 6), (5, 7), (6, 8), (7, 10), (8, 11), (10, 14), (12, 17)))
            units(gates, i, ((10, 0), (11, 3), (12, 4), (13, 7), (14, 8)))

        @pl.when(i >= 3)
        def _():
            back(i - 3)

        @pl.when((i >= 2) & (i < tiles + 2))
        def _():
            own(i - 2)

        return carry

    lax.fori_loop(0, tiles + 3, step, 0)

    parts = 4
    block = rows // GROUP
    size = block // parts
    order = [1 - x, x]
    js = range(GROUP)
    cores = []
    for i in range(2):
        for k in range(parts):
            owner = order[i] * 2 + 1 - c
            span = pl.ds(k * size, size)
            for j in js:
                low[i, j, span, :] = acc[j, pl.ds(pl.multiple_of(owner * block + k * size, 16), size), :].astype(BF16)
            copy = remote(low.at[i, :, span], from_core.at[i, :, span], ccs.at[i, k], ccr.at[i, k], beside)
            copy.start()
            cores.append(copy)
    sends = []
    for k in range(parts):
        span = pl.ds(k * size, size)
        here = pl.ds(pl.multiple_of((order[0] * 2 + c) * block + k * size, 16), size)
        cores[k].wait_recv()
        for j in js:
            to_xb[j, span, :] = (acc[j, here, :] + from_core[0, j, span, :].astype(F32)).astype(BF16)
        copy = remote(to_xb.at[:, span], from_x.at[:, span], cxs.at[k], cxr.at[k], across)
        copy.start()
        sends.append(copy)
    if chained:
        gates.run(9, gates.units())
        downs.finish()
        gates.finish()
    for k in range(parts):
        span = pl.ds(k * size, size)
        here = pl.ds(pl.multiple_of((order[1] * 2 + c) * block + k * size, 16), size)
        cores[parts + k].wait_recv()
        sends[k].wait_recv()
        for j in js:
            out[j, span, :] = acc[j, here, :] + from_core[1, j, span, :].astype(F32) + from_x[j, span, :].astype(F32)

    for copy in cores + sends:
        copy.wait_send()
    for t in range(tiles - 2, tiles):
        to_core(t).wait_send()
    for t in range(tiles - 4, tiles):
        to_x(t).wait_send()
    for t in range(tiles - ring, tiles):
        to_y(t).wait_send()
        keep(t).wait()

    def drain(t, carry):
        to_y(t).wait_recv()
        return carry

    lax.fori_loop(gate_tiles if chained else 0, tiles, drain, 0)
    if chained:
        gf_swap.wait_send()


def ffn_backward(cid, n, gate_tiles, gf, gft, levd, lev, gs, gu, hid, hidy, bt, bty):
    rows, part = gf.shape
    deep = lev.shape[1]
    tiles, _, tw = gs.shape
    nz = n // 2
    chained = nz == 4
    per = tiles // nz if chained else 1
    block = rows // GROUP
    half = (tiles, rows, tw) if chained else (1, 16, 128)
    message = (part, tw)
    ring = 4
    each = DMA((tiles,))
    wide = jax.ShapeDtypeStruct((rows, tiles * tw), BF16)
    return comm_call(
        functools.partial(ffn_backward_kernel, tiles, nz, chained, gate_tiles),
        cid,
        [
            wide,
            wide,
            jax.ShapeDtypeStruct((tiles, 8, tw), F32),
            jax.ShapeDtypeStruct((GROUP, block, part), F32),
            jax.ShapeDtypeStruct((part, per * tw), F32),
            jax.ShapeDtypeStruct((bt.shape[2], max(gate_tiles, 1) * tw), F32),
        ]
        + (Chain.landing(nz, per, *message) + gate_landing(nz, gate_tiles, bt) if chained else []),
        [
            pltpu.VMEM(half, BF16),
            pltpu.VMEM(half, BF16),
            pltpu.VMEM((part, rows), BF16),
            pltpu.VMEM((2, deep, tw), BF16),
            pltpu.VMEM((2, 2, part, tw), BF16),
            pltpu.VMEM((2, 2, rows, tw), BF16),
            pltpu.VMEM((2, rows, tw), BF16),
            pltpu.VMEM((4, rows, tw), BF16),
            pltpu.VMEM((2, rows, tw), F32),
            pltpu.VMEM((4, rows, tw), BF16),
            pltpu.VMEM((tiles, rows, tw), BF16),
            pltpu.VMEM((ring, rows, tw), BF16),
            pltpu.VMEM((GROUP, rows, part), F32),
            pltpu.VMEM((2, GROUP, block, part), BF16),
            pltpu.VMEM((2, GROUP, block, part), BF16),
            pltpu.VMEM((GROUP, block, part), BF16),
            pltpu.VMEM((GROUP, block, part), BF16),
            DMA((2,)), DMA((2,)), DMA((2, 2)), DMA((2,)), each, each, each, each,
            each, each, each, DMA, DMA, DMA((2, 4)), DMA((2, 4)), DMA((4,)), DMA((4,)),
        ]
        + (Chain.scratch(nz, per, *message) + gate_scratch(nz, gate_tiles, bt) if chained else []),
        [VMEM, VMEM, ANY, ANY, VMEM, ANY, ANY, ANY, ANY, ANY],
        [ANY, ANY, VMEM, VMEM, ANY, ANY] + [ANY] * (4 if chained else 0),
    )(gf, gft, levd, lev, gs, gu, hid, hidy, bt, bty)


def branch_back_kernel(n, first, tiles, *refs):
    (gsi, mid, raw, cot, g2, g3, scale, wo, q, mixed, mass, own_meta, metas, kv, bt, bty, dg, dgy) = refs[:18]
    dmid, sums, gy, gyy, dq, dkv, gate_o, dkv_y = refs[18:26]
    refs = refs[1:]
    landing = refs[25:27] if tiles else []
    refs = refs[len(landing) :]
    (unit, gyt, gys, gy_all, part, from_core, to_x, from_x, grad, kvs, dkvs, es, er, el, cs, cr, xs, xr, ks, ds, yss, ysr,
     ows, pys, pyr) = refs[25:50]
    rest = refs[50:]
    seq, me, x, c = place_now()
    nz = n // 2
    across = (seq, (1 - x) * 2 + c)
    beside = (seq, x * 2 + 1 - c)
    beyond = (seq + 1 - 2 * (seq % 2), me)
    peers = [(seq, lax.rem(me + d, GROUP)) for d in range(1, GROUP)]
    chain = None
    if tiles:
        chain, loads = gate_chain(nz, first, tiles, seq, me, bt, bty, dg, dgy, gate_o, landing, *rest[:3], rest[3:])
        for load in loads:
            load.start()
        greet_all(seq, me, nz, peers)
    else:
        greet(peers + [beyond])
    width = GROUP * raw.shape[2]
    mean = 1.0 / width
    sums[...] = jnp.zeros_like(sums)
    js = range(GROUP)

    def rowsum(values):
        total = values[0]
        for value in values[1:]:
            total = total + value
        return jnp.sum(total, axis=1, keepdims=True) * mean

    def norms(span):
        middle = [mid[j, span, :] for j in js]
        up = [gsi[j, span, :] for j in js]
        inverse = lax.rsqrt(rowsum([v * v for v in middle]) + EPSILON)
        third = [v * inverse for v in middle]
        scaled = [up[j] * g3[j] for j in js]
        cross = rowsum([scaled[j] * third[j] for j in js])
        grad_middle = [
            cot[j, span, :].astype(F32) + inverse * (scaled[j] - third[j] * cross) for j in js
        ]
        plain = [raw[j, span, :].astype(F32) for j in js]
        branch = [plain[j] * scale[j] for j in js]
        inverse = lax.rsqrt(rowsum([v * v for v in branch]) + EPSILON)
        second = [v * inverse for v in branch]
        scaled = [grad_middle[j] * g2[j] for j in js]
        cross = rowsum([scaled[j] * second[j] for j in js])
        for j in js:
            full = inverse * (scaled[j] - second[j] * cross)
            gys[j, span, :] = (full * scale[j]).astype(BF16)
            dmid[j, span, :] = grad_middle[j]
            sums[j, 0:1, :] += jnp.sum(grad_middle[j] * second[j], axis=0, keepdims=True)
            sums[j, 1:2, :] += jnp.sum(up[j] * third[j], axis=0, keepdims=True)
            sums[j, 2:3, :] += jnp.sum(plain[j] * full, axis=0, keepdims=True)

    strips(raw.shape[1] // 16, 16, norms)

    copies = []
    for d in (2, 1, 3):
        peer = peers[d - 1]
        copy = remote(gys.at[peer[1]], gy_all.at[me], es.at[d - 1], er.at[d - 1], peer)
        copy.start()
        copies.append(copy)
    own = pltpu.make_async_copy(gys.at[me], gy_all.at[me], el)
    own.start()
    for p in range(2):
        pltpu.make_async_copy(kv.at[:, :, pl.ds(p * 128, 128)], kvs.at[p], ks.at[p]).start()
    units = chain.units() if chain else 0
    at = [0]

    def beside_work(count):
        if chain:
            last = min(units, at[0] + count)
            chain.run(at[0], last)
            at[0] = last

    if chain:
        for load in loads:
            load.wait()
    beside_work(3)
    for copy in copies:
        copy.wait_recv()
    own.wait()
    fill_unit(unit)
    gyt[...] = contract_last(unit[...], gy_all[...].reshape(gyt.shape[1], gyt.shape[0])).astype(BF16)
    gy_out = pltpu.make_async_copy(gyt, gy, ows)
    gy_out.start()
    swap = remote(gyt, gyy, yss, ysr, beyond)
    swap.start()

    heads = part.shape[3]
    rows = part.shape[2]
    order = [1 - x, x]

    def product(i, k, to):
        grad_branch = gy_all[...].reshape(rows, raw.shape[2])
        start = (order[i] * 2 + k) * heads
        to[...] = dot(grad_branch, wo[:, pl.ds(pl.multiple_of(start, 128), heads)]).astype(BF16)

    cores = []
    for i in range(2):
        product(i, 1 - c, part.at[i, 0])
        copy = remote(part.at[i, 0], from_core.at[i], cs.at[i], cr.at[i], beside)
        copy.start()
        cores.append(copy)
    for i in range(2):
        product(i, c, part.at[i, 1])
    cores[0].wait_recv()

    def add_core(span):
        to_x[span, :] = (part[0, 1, span, :].astype(F32) + from_core[0, span, :].astype(F32)).astype(BF16)

    strips(rows // 64, 64, add_core)
    over = remote(to_x, from_x, xs, xr, across)
    over.start()
    beside_work(4)
    cores[1].wait_recv()
    over.wait_recv()

    def add_all(span):
        grad[span, :] = (
            part[1, 1, span, :].astype(F32) + from_core[1, span, :].astype(F32) + from_x[span, :].astype(F32)
        ).astype(BF16)

    strips(rows // 64, 64, add_all)

    def load_pack(p):
        return pltpu.make_async_copy(
            kv.at[:, :, pl.ds(pl.multiple_of(p * 128, 128), 128)], kvs.at[p % 2], ks.at[p % 2]
        )

    y = seq % 2

    def store_pack(p):
        return pltpu.make_async_copy(
            dkvs.at[p, :, y], dkv.at[:, :, pl.ds(pl.multiple_of(p * 128, 128), 128)], ds.at[p]
        )

    def pack_to_y(p):
        return remote(
            dkvs.at[p, :, 1 - y], dkv_y.at[:, :, pl.ds(pl.multiple_of(p * 128, 128), 128)], pys.at[p], pyr.at[p], beyond
        )

    base = at[0]
    each = 1 if units - base >= GROUP else 0

    def one_pack(p, carry):
        load_pack(p).wait()
        span = pl.ds(pl.multiple_of(p * 128, 128), 128)
        keys = kvs[p % 2, :, 0].reshape(n * 128, DH)
        values = kvs[p % 2, :, 1].reshape(n * 128, DH)
        allowed = masks(n, own_meta.at[pl.ds(p, 1)], metas.at[:, pl.ds(p, 1)])
        back_pack(
            n, keys, values, allowed, q.at[span], grad.at[span], mixed.at[span], mass.at[span], dq.at[span],
            dkvs.at[p],
        )
        pack_to_y(p).start()
        store_pack(p).start()

        @pl.when(p + 2 < GROUP)
        def _():
            load_pack(p + 2).start()

        if each:
            chain.run(base + p * each, base + (p + 1) * each)
        return carry

    lax.fori_loop(0, GROUP, one_pack, 0)
    at[0] = base + GROUP * each
    beside_work(units)
    if chain:
        chain.finish()
    for copy in copies + cores + [over]:
        copy.wait_send()
    for p in js:
        store_pack(p).wait()
        pack_to_y(p).wait()
    swap.wait()
    gy_out.wait()


def branch_back(cid, n, first, tiles, gsi, mid, raw, cot, g2, g3, scale, wo, q, mixed, mass, own_meta, metas, kv, pairs):
    bt, bty, dg, dgy = pairs
    own, part = raw.shape[1:]
    rows = q.shape[0]
    heads = q.shape[1]
    block = lambda kind: jax.ShapeDtypeStruct((GROUP, own, part), kind)
    gate_rows = bt.shape[2]
    pack = (2, n, 2, own, DH)
    return comm_call(
        functools.partial(branch_back_kernel, n, first, tiles),
        cid,
        [
            block(F32),
            jax.ShapeDtypeStruct((GROUP, 8, part), F32),
            jax.ShapeDtypeStruct((part, rows), BF16),
            jax.ShapeDtypeStruct((part, rows), BF16),
            jax.ShapeDtypeStruct(q.shape, F32),
            jax.ShapeDtypeStruct((n // 2,) + kv.shape[1:], BF16),
            jax.ShapeDtypeStruct((gate_rows, max(tiles, 1) * TILE), F32),
            jax.ShapeDtypeStruct((n // 2,) + kv.shape[1:], BF16),
        ]
        + (gate_landing(n // 2, tiles, bt) if tiles else []),
        [
            pltpu.VMEM((part, part), BF16),
            pltpu.VMEM((part, rows), BF16),
            pltpu.VMEM((GROUP, own, part), BF16),
            pltpu.VMEM((GROUP, own, part), BF16),
            pltpu.VMEM((2, 2, rows, heads), BF16),
            pltpu.VMEM((2, rows, heads), BF16),
            pltpu.VMEM((rows, heads), BF16),
            pltpu.VMEM((rows, heads), BF16),
            pltpu.VMEM((rows, heads), BF16),
            pltpu.VMEM(pack, BF16),
            pltpu.VMEM((GROUP, n // 2, 2) + pack[2:], BF16),
            DMA((3,)), DMA((3,)), DMA, DMA((2,)), DMA((2,)), DMA, DMA, DMA((2,)), DMA((GROUP,)), DMA, DMA, DMA,
            DMA((GROUP,)), DMA((GROUP,)),
        ]
        + (gate_scratch(n // 2, tiles, bt) if tiles else []),
        [VMEM] * 13 + [ANY] * 5,
        [VMEM, VMEM, ANY, ANY, VMEM, ANY, ANY, ANY] + [ANY] * (2 if tiles else 0),
    )(gsi, mid, raw, cot, g2, g3, scale, wo, q, mixed, mass, own_meta, metas, kv, bt, bty, dg, dgy)


def keys_back_kernel(n, first, tiles, *refs):
    (src, y_got, dq, q_raw, p_raw, cosine, sine, q_scale, p_scale, wq, wkv, tok, dmid, gain, bt, bty, dg, dgy) = refs[:18]
    refs = refs[4:]
    joined, joined_y, out, sums, gain_o, gate_o = refs[14:20]
    refs = refs[1:]
    landing = refs[19:21]
    refs = refs[2:]
    (r_got, l_got, r_out, l_out, moved, back, acc, low, from_core, to_xb, from_x,
     rs, rr, ls, lr, hs, hr, local, jys, jyr, ccs, ccr, cxs, cxr) = refs[19:43]
    slabs, halves, slab_sem, *rest = refs[43:]
    seq, me, x, c = place_now()
    z = seq // 2
    nz = n // 2
    right = (seq + 2, me)
    left = (seq - 2, me)
    beyond = (seq + 1 - 2 * (seq % 2), me)
    across = (seq, (1 - x) * 2 + c)
    beside = (seq, x * 2 + 1 - c)
    chain, loads = gate_chain(nz, first, tiles, seq, me, bt, bty, dg, dgy, gate_o, landing, slabs, halves, slab_sem, rest)
    for load in loads:
        load.start()
    greet_all(seq, me, nz, [(seq, lax.rem(me + d, GROUP)) for d in range(1, GROUP)])
    rows, width = dq.shape
    deep = acc.shape[1]
    half = DH // 2

    sums[...] = jnp.zeros_like(sums)
    gain_o[...] = jnp.zeros_like(gain_o)

    def pair_sum(k, more, to):
        def body(i, carry):
            part = i // 4
            span = pl.ds(pl.multiple_of((i % 4) * 128, 128), 128)
            total = src[k, part, span, :].astype(F32) + y_got[k, part, span, :].astype(F32)
            for ref in more:
                total = total + ref[part, span, :].astype(F32)
            to[part, span, :] = total.astype(BF16)
            return carry

        lax.fori_loop(0, 8, body, 0)

    def queries():
        def turn_queries(span):
            cos = cosine[span, :]
            sin = sine[span, :]
            for h in range(2):
                a = slice(h * DH, h * DH + half)
                b = slice(h * DH + half, (h + 1) * DH)
                one = dq[span, a]
                two = dq[span, b]
                for cols, full in ((a, one * cos + two * sin), (b, two * cos - one * sin)):
                    sums[0:1, cols] += jnp.sum(q_raw[span, cols] * full, axis=0, keepdims=True)
                    joined[span, cols] = (full * q_scale[:, cols]).astype(BF16)

        strips(rows // 64, 64, turn_queries)

        def query_part(span):
            acc[span, :] = contract_last(joined[span, :width], wq[...])

        strips(rows // 128, 128, query_part)

    for load in loads:
        load.wait()
    units = chain.units()
    at = [0]

    def beside_work(count):
        last = min(units, at[0] + count)
        chain.run(at[0], last)
        at[0] = last

    for t in range(1, nz):
        go_right = z + nz - t
        go_left = z - nz + t

        def hop(go, at_end, got, send, ss, sr, to, source):
            if t == 1:
                pair_sum(go, [], send.at[t - 1])
            else:

                @pl.when(jnp.logical_not(at_end))
                def _():
                    remote(send.at[t - 1], got.at[t - 2], ss.at[t - 2], sr.at[t - 2], source).wait_recv()
                    pair_sum(go, [got.at[t - 2]], send.at[t - 1])

                @pl.when(at_end)
                def _():
                    pair_sum(go, [], send.at[t - 1])

            remote(send.at[t - 1], got.at[t - 1], ss.at[t - 1], sr.at[t - 1], to).start()

        @pl.when(go_right < nz)
        def _():
            hop(go_right, z == 0, r_got, r_out, rs, rr, right, left)

        @pl.when(go_left >= 0)
        def _():
            hop(go_left, z == nz - 1, l_got, l_out, ls, lr, left, right)

        beside_work(3)
        if t == 1:
            queries()

    last = nz - 2

    def got_left():
        remote(r_out.at[last], r_got.at[last], rs.at[last], rr.at[last], left).wait_recv()

    def got_right():
        remote(l_out.at[last], l_got.at[last], ls.at[last], lr.at[last], right).wait_recv()

    @pl.when(z == 0)
    def _():
        got_right()
        pair_sum(z, [l_got.at[last]], moved)

    @pl.when(z == nz - 1)
    def _():
        got_left()
        pair_sum(z, [r_got.at[last]], moved)

    @pl.when((z > 0) & (z < nz - 1))
    def _():
        got_left()
        got_right()
        pair_sum(z, [r_got.at[last], l_got.at[last]], moved)

    for t in range(2):
        target = t * 2 + x

        @pl.when(target == me)
        def _():
            pltpu.make_async_copy(moved.at[t], back.at[c], local).start()

        @pl.when(target != me)
        def _():
            remote(moved.at[t], back.at[c], hs.at[t], hr.at[c], (seq, target)).start()

    beside_work(3)
    for j in range(2):
        source = c * 2 + j

        @pl.when(source == me)
        def _():
            pltpu.make_async_copy(moved.at[0], back.at[j], local).wait()

        @pl.when(source != me)
        def _():
            remote(moved.at[0], back.at[j], hs.at[0], hr.at[j], (seq, source)).wait_recv()

    is_key = jnp.where(x == 0, 1.0, 0.0).astype(F32)

    def turn_pairs(span):
        cos = is_key * cosine[span, :] + (1.0 - is_key)
        sin = is_key * sine[span, :]
        for h in range(2):
            a = slice(h * DH, h * DH + half)
            b = slice(h * DH + half, (h + 1) * DH)
            one = back[h, span, :half].astype(F32)
            two = back[h, span, half:].astype(F32)
            for cols, full in ((a, one * cos + two * sin), (b, two * cos - one * sin)):
                sums[1:2, cols] += jnp.sum(p_raw[span, cols] * full, axis=0, keepdims=True)
                joined[span, width + cols.start : width + cols.stop] = (full * p_scale[:, cols]).astype(BF16)

    strips(rows // 64, 64, turn_pairs)
    joined_swap = remote(joined, joined_y, jys, jyr, beyond)
    joined_swap.start()

    def pair_part(span):
        acc[span, :] += contract_last(joined[span, width:], wkv[...])

    strips(rows // 128, 128, pair_part)

    parts = 4
    block = rows // GROUP
    size = block // parts
    order = [1 - x, x]
    cores = []
    for i in range(2):
        for k in range(parts):
            owner = order[i] * 2 + 1 - c
            span = pl.ds(k * size, size)
            low[i, span, :] = acc[pl.ds(pl.multiple_of(owner * block + k * size, 16), size), :].astype(BF16)
            copy = remote(low.at[i, span], from_core.at[i, span], ccs.at[i, k], ccr.at[i, k], beside)
            copy.start()
            cores.append(copy)
    sends = []
    for k in range(parts):
        span = pl.ds(k * size, size)
        here = pl.ds(pl.multiple_of((order[0] * 2 + c) * block + k * size, 16), size)
        cores[k].wait_recv()
        to_xb[span, :] = (acc[here, :] + from_core[0, span, :].astype(F32)).astype(BF16)
        copy = remote(to_xb.at[span], from_x.at[span], cxs.at[k], cxr.at[k], across)
        copy.start()
        sends.append(copy)
    beside_work(units)
    chain.finish()
    for k in range(parts):
        span = pl.ds(k * size, size)
        here = pl.ds(pl.multiple_of((order[1] * 2 + c) * block + k * size, 16), size)
        cores[parts + k].wait_recv()
        sends[k].wait_recv()
        grad = acc[here, :] + from_core[1, span, :].astype(F32) + from_x[span, :].astype(F32)
        value = tok[span, :].astype(F32)
        inverse = lax.rsqrt(jnp.mean(value * value, axis=1, keepdims=True) + EPSILON)
        normed = value * inverse
        scaled = grad * gain[...]
        out[span, :] = dmid[span, :] + inverse * (
            scaled - normed * jnp.mean(scaled * normed, axis=1, keepdims=True)
        )
        gain_o[0:1, :] += jnp.sum(grad * normed, axis=0, keepdims=True)

    for t in range(2):

        @pl.when(t * 2 + x != me)
        def _():
            remote(moved.at[t], back.at[c], hs.at[t], hr.at[c], (seq, t * 2 + x)).wait_send()

    for t in range(1, nz):

        @pl.when(z + nz - t < nz)
        def _():
            remote(r_out.at[t - 1], r_got.at[t - 1], rs.at[t - 1], rr.at[t - 1], right).wait_send()

        @pl.when(z - nz + t >= 0)
        def _():
            remote(l_out.at[t - 1], l_got.at[t - 1], ls.at[t - 1], lr.at[t - 1], left).wait_send()

    for copy in cores + sends:
        copy.wait_send()
    joined_swap.wait()


def keys_back(cid, n, first, tiles, src, src_y, dq, q_raw, p_raw, cosine, sine, q_scale, p_scale, wq, wkv, tok, dmid, gain, pairs):
    bt, bty, dg, dgy = pairs
    nz = n // 2
    rows, width = dq.shape
    deep = wq.shape[0]
    block = rows // GROUP
    shape = src.shape[1:]
    chain = pltpu.VMEM((nz - 1,) + shape, BF16)
    joined = jax.ShapeDtypeStruct((rows, 2 * width), BF16)
    return comm_call(
        functools.partial(keys_back_kernel, n, first, tiles),
        cid,
        [
            joined,
            joined,
            jax.ShapeDtypeStruct((block, deep), F32),
            jax.ShapeDtypeStruct((8, width), F32),
            jax.ShapeDtypeStruct((8, deep), F32),
            jax.ShapeDtypeStruct((bt.shape[2], tiles * TILE), F32),
        ]
        + gate_landing(nz, tiles, bt),
        [
            chain, chain, chain, chain, pltpu.VMEM(shape, BF16), pltpu.VMEM(shape, BF16),
            pltpu.VMEM((rows, deep), F32),
            pltpu.VMEM((2, block, deep), BF16),
            pltpu.VMEM((2, block, deep), BF16),
            pltpu.VMEM((block, deep), BF16),
            pltpu.VMEM((block, deep), BF16),
            DMA((nz - 1,)), DMA((nz - 1,)), DMA((nz - 1,)), DMA((nz - 1,)),
            DMA((2,)), DMA((2,)), DMA, DMA, DMA, DMA((2, 4)), DMA((2, 4)), DMA((4,)), DMA((4,)),
        ]
        + gate_scratch(nz, tiles, bt),
        [VMEM] * 14 + [ANY] * 4,
        [VMEM, ANY, VMEM, VMEM, VMEM, ANY, ANY, ANY],
    )(src, src_y, dq, q_raw, p_raw, cosine, sine, q_scale, p_scale, wq, wkv, tok, dmid, gain, bt, bty, dg, dgy)


def finish_kernel(n, rounds, first, tiles, *refs):
    (whole, part, bt, bty, dg, dgy, ot, oty, gy, gyy, at, aty, joined, joined_y) = refs[:14]
    whole_out, part_out, gate_o, output_o, attention_o = refs[14:19]
    landing = refs[19:25]
    refs = refs[6:]
    bufs, gots, mine, theirs, ss, rs = refs[19:25]
    slabs, halves, slab_sem = refs[25:28]
    gate_refs, output_refs, attention_refs = refs[28:39], refs[39:50], refs[50:61]
    output_halves, attention_halves, half_sem = refs[61:]
    seq, me, x, c = place_now()
    nz = n // 2
    across = (seq, (1 - x) * 2 + c)
    beside = (seq, x * 2 + 1 - c)
    gates, loads = gate_chain(nz, first, tiles, seq, me, bt, bty, dg, dgy, gate_o, landing[:2], slabs, halves, slab_sem, gate_refs)
    for i, (ref, to) in enumerate(
        ((ot.at[:, seq % 2], output_halves.at[0]), (oty, output_halves.at[1]),
         (at.at[:, seq % 2], attention_halves.at[0]), (aty, attention_halves.at[1]))
    ):
        loads.append(pltpu.make_async_copy(ref, to, half_sem.at[i]))
    for load in loads:
        load.start()
    wide = joined.shape[1] // 2

    def output_partial(k, j):
        return dot(gy[...], output_halves[0, k]) + dot(gyy[...], output_halves[1, k])

    def attention_partial(k, j):
        cols = pl.ds(pl.multiple_of(j * wide, 128), wide)
        return dot(attention_halves[0, k], joined[:, cols]) + dot(attention_halves[1, k], joined_y[:, cols])

    def keep_output(j, stage, sem):
        return pltpu.make_async_copy(stage, output_o, sem)

    outputs = Chain(nz, 1, seq, me, output_partial, keep_output, landing[2:4], output_refs)
    attentions = Chain(
        nz,
        2,
        seq,
        me,
        attention_partial,
        lambda j, stage, sem: pltpu.make_async_copy(
            stage, attention_o.at[:, pl.ds(pl.multiple_of(j * wide, 128), wide)], sem
        ),
        landing[4:],
        attention_refs,
    )
    partners = []
    for r in range(rounds):
        bit = 1 << r
        partners.append((seq + bit - 2 * bit * ((seq // bit) % 2), me))
    greet([(lax.rem(seq + d, n), me) for d in range(1, n)] + [across, beside])
    for load in loads:
        load.wait()
    rows = whole.shape[0]
    bufs[0, :rows, :] = whole[...]
    bufs[0, rows:, :] = part[...]
    queues = [(chain, list(range(0, chain.units(), nz - 1))) for chain in (gates, outputs, attentions)]
    work = [(gates, u) for u in queues[0][1][:tiles]]
    rest = [queues[0][1][tiles:], queues[1][1], queues[2][1]]
    while any(rest):
        for (chain, _), left in zip(queues, rest):
            if left:
                work.append((chain, left.pop(0)))
    at_work = [0]

    def beside_work(count):
        todo = work[at_work[0] : at_work[0] + count]
        at_work[0] += count
        start = None
        for i, (chain, u) in enumerate(todo):
            if start is None:
                start = u
            if i + 1 == len(todo) or todo[i + 1][0] is not chain:
                chain.run(start, u + 3)
                start = None

    for r in range(rounds + 1):
        partner = partners[r] if r < rounds else across
        copy = remote(bufs.at[r], gots.at[r], ss.at[r], rs.at[r], partner)
        copy.start()
        beside_work(1)
        copy.wait()
        if r < rounds:
            bufs[r + 1] = bufs[r] + gots[r]
    mine[0, :rows, :] = bufs[rounds, :rows, :] + gots[rounds, :rows, :]
    mine[0, rows:, :] = bufs[rounds, rows:, :]
    mine[1, rows:, :] = gots[rounds, rows:, :]
    mine[1, :rows, :] = jnp.zeros((rows, 128), F32)
    copy = remote(mine, theirs, ss.at[rounds + 1], rs.at[rounds + 1], beside)
    copy.start()
    beside_work(len(work))
    copy.wait()
    whole_out[...] = mine[0, :rows, :] + theirs[0, :rows, :]
    part_out[x * 2 + c] = mine[0, rows:, :]
    part_out[(1 - x) * 2 + c] = mine[1, rows:, :]
    part_out[x * 2 + 1 - c] = theirs[0, rows:, :]
    part_out[(1 - x) * 2 + 1 - c] = theirs[1, rows:, :]
    gates.finish()
    outputs.finish()
    attentions.finish()


def finish(cid, n, first, tiles, whole, part, pairs, output_pairs, attention_pairs):
    bt, bty, dg, dgy = pairs
    ot, oty, gy, gyy = output_pairs
    at, aty, joined, joined_y = attention_pairs
    nz = n // 2
    rounds = int(math.log2(n))
    rows = whole.shape[0] + part.shape[0]
    output_shape = (gy.shape[0], ot.shape[3])
    attention_rows = at.shape[2]
    return comm_call(
        functools.partial(finish_kernel, n, rounds, first, tiles),
        cid,
        [
            jax.ShapeDtypeStruct(whole.shape, F32),
            jax.ShapeDtypeStruct((GROUP,) + part.shape, F32),
            jax.ShapeDtypeStruct((bt.shape[2], tiles * TILE), F32),
            jax.ShapeDtypeStruct(output_shape, F32),
            jax.ShapeDtypeStruct((attention_rows, joined.shape[1]), F32),
        ]
        + gate_landing(nz, tiles, bt)
        + Chain.landing(nz, 1, *output_shape)
        + Chain.landing(nz, 2, attention_rows, joined.shape[1] // 2),
        [
            pltpu.VMEM((rounds + 1, rows, 128), F32),
            pltpu.VMEM((rounds + 1, rows, 128), F32),
            pltpu.VMEM((2, rows, 128), F32),
            pltpu.VMEM((2, rows, 128), F32),
            DMA((rounds + 2,)),
            DMA((rounds + 2,)),
        ]
        + gate_scratch(nz, tiles, bt)
        + Chain.scratch(nz, 1, *output_shape)
        + Chain.scratch(nz, 2, attention_rows, joined.shape[1] // 2)
        + [
            pltpu.VMEM((2, nz) + ot.shape[2:], BF16),
            pltpu.VMEM((2, nz) + at.shape[2:], BF16),
            DMA((4,)),
        ],
        [VMEM] * 2 + [ANY] * 6 + [VMEM] * 2 + [ANY] * 2 + [VMEM] * 2,
        [VMEM, VMEM] + [ANY] * 9,
    )(whole, part, bt, bty, dg, dgy, ot, oty, gy, gyy, at, aty, joined, joined_y)


def rms_inverse(value):
    return lax.rsqrt(jnp.mean(value * value, axis=-1, keepdims=True) + EPSILON)


def norm_back(inverse, normed, upstream):
    return inverse * (upstream - normed * jnp.mean(upstream * normed, axis=-1, keepdims=True))


def rotate(value, cosine, sine):
    half = DH // 2
    first = value[..., :half]
    second = value[..., half:]
    return jnp.concatenate([first * cosine - second * sine, second * cosine + first * sine], axis=-1)


def core_swap(value):
    return lax.ppermute(value, "fsdp", [(f, f ^ 1) for f in range(GROUP)])


def lanes(value, rows):
    flat = value.reshape(-1)
    return jnp.pad(flat, (0, rows * 128 - flat.shape[0])).reshape(rows, 128)


def per_device(
    n,
    tokens,
    doc_ids,
    padding,
    token_order,
    query_code,
    key_value_code,
    output_code,
    gate_up_code,
    down_code,
    query_scale,
    key_value_scale,
    output_scale,
    gate_up_scale,
    down_scale,
    norm_gains,
    cotangent,
):
    me = lax.axis_index("fsdp")
    c = me % 2
    width = tokens.shape[2]
    part = width // GROUP
    rows = GROUP * tokens.shape[1]
    own = tokens.shape[1]

    def mine(vector):
        size = vector.shape[-1] // GROUP
        return lax.dynamic_slice_in_dim(vector, me * size, size, vector.ndim - 1)

    def blocks_to_rows(blocks):
        return jnp.concatenate([blocks[i] for i in range(GROUP)], axis=1)

    gain = 1.0 + norm_gains
    place = token_order[0].astype(F32)
    document = doc_ids[0].astype(F32)
    meta = jnp.stack([document, place, jnp.where(padding[0] == 1, document, -1.0)] + [document] * 5)

    def to_blocks(value):
        return value.reshape(own, GROUP, part).transpose(1, 0, 2)

    my_query_scale = mine(query_scale)
    my_pair_scale = mine(key_value_scale)
    token_cols = to_blocks(tokens[0])
    cot_cols = to_blocks(cotangent[0])
    rates = BASE ** (-2.0 * jnp.arange(DH // 2).astype(F32) / DH)
    (
        token_blocks, cot_blocks, own_meta, metas, pairs, query, query_raw, pair_raw, cosine, sine, first_turned
    ) = front(
        1,
        n,
        token_cols.reshape(rows, part),
        cot_cols.reshape(rows, part),
        meta,
        gain[0].reshape(GROUP, 1, part),
        rates[None],
        my_query_scale[None],
        my_pair_scale[None],
        query_code,
        key_value_code,
    )

    mixed_low, mixed, mass = attend(n, query, pairs, own_meta, metas)
    second_input, branch_own, my_middle, mixed_slices, second_turned = branch_forward(
        3,
        mixed_low,
        output_code.T,
        token_blocks,
        output_scale.reshape(GROUP, 1, part),
        gain[1].reshape(GROUP, 1, part),
        gain[2].reshape(GROUP, 1, part),
    )

    my_gate_scale = mine(gate_up_scale)
    columns = gate_up_code.shape[1]
    tiles = columns // TILE
    gate_scales = my_gate_scale.reshape(tiles, 1, TILE)
    (
        gate_up, hidden, hidden_y, down_blocks, grad_down, grad_down_turned, down_sums, gate_levels, down_levels, *riders
    ) = ffn_forward(
        5,
        second_input,
        gate_up_code,
        gate_scales,
        down_code.T,
        cot_blocks,
        gain[3].reshape(GROUP, 1, part),
        down_scale.reshape(GROUP, 1, part),
        [second_turned, mixed_slices, first_turned],
    )
    second_pair, mixed_pair, first_pair = zip((second_turned, mixed_slices, first_turned), riders)
    my_down = lax.dynamic_slice_in_dim(down_blocks, me * own, own, 1).astype(F32) * down_scale.reshape(GROUP, 1, part)
    down_inverse = lax.rsqrt(jnp.mean(my_down * my_down, axis=(0, 2), keepdims=True) + EPSILON)
    result = blocks_to_rows((my_middle + my_down * down_inverse * gain[3].reshape(GROUP, 1, part)).astype(BF16))
    tiles_zero, tiles_one, tiles_two = (2, 5, 4) if n == 8 else (0, 0, 0)
    tiles_three = tiles - tiles_zero - tiles_one - tiles_two
    grad_gate_up, grad_gate_up_y, gate_sums, grad_second_input, down_grad, gate_zero, *_ = ffn_backward(
        6,
        n,
        tiles_zero,
        grad_down,
        grad_down_turned,
        down_levels,
        gate_levels,
        gate_scales,
        gate_up,
        hidden,
        hidden_y,
        *second_pair,
    )
    if n == 8:
        down_grad = down_grad.T
    else:
        hidden_own = jnp.concatenate(
            [
                (jax.nn.gelu(gate_up[0, t].astype(F32)) * gate_up[1, t].astype(F32)).astype(BF16)
                for t in range(tiles)
            ],
            axis=1,
        )
        hidden_core = core_swap(hidden_own)
        hidden_rows = jnp.concatenate(
            [jnp.where(c == 0, hidden_own, hidden_core), jnp.where(c == 0, hidden_core, hidden_own)], axis=1
        )
        down_grad = lax.psum_scatter(
            contract_first(hidden_rows, grad_down), "seq", scatter_dimension=0, tiled=True
        )
    scale_down = down_sums[0]
    gain_four = down_sums[1]
    scale_gate = gate_sums[:, 0, :].reshape(columns) / my_gate_scale
    gate_pairs = second_pair + (grad_gate_up, grad_gate_up_y)
    grad_middle, branch_sums, grad_branch, grad_branch_y, grad_query, grad_pairs, gate_one, grad_pairs_y, *_ = branch_back(
        7,
        n,
        tiles_zero,
        tiles_one,
        grad_second_input,
        my_middle,
        branch_own,
        cot_cols,
        gain[1].reshape(GROUP, 1, part),
        gain[2].reshape(GROUP, 1, part),
        output_scale.reshape(GROUP, 1, part),
        output_code.T,
        query,
        mixed,
        mass,
        own_meta,
        metas,
        pairs,
        gate_pairs,
    )
    grad_middle = blocks_to_rows(grad_middle)
    gain_two = branch_sums[:, 0].reshape(width)
    gain_three = branch_sums[:, 1].reshape(width)
    scale_output = branch_sums[:, 2].reshape(width)

    if n == 8:
        joined, joined_y, grad_inputs, key_sums, gain_one, gate_two, *_ = keys_back(
            9,
            n,
            tiles_zero + tiles_one,
            tiles_two,
            grad_pairs,
            grad_pairs_y,
            grad_query,
            query_raw,
            pair_raw,
            cosine,
            sine,
            my_query_scale[None],
            my_pair_scale[None],
            query_code,
            key_value_code,
            tokens[0],
            grad_middle,
            gain[0][None],
            gate_pairs,
        )
        gain_one = gain_one[0]
        scale_query = key_sums[0]
        scale_pair = key_sums[1]
    else:
        is_key = me < 2
        pair_cosine = jnp.where(is_key, cosine, 1.0)
        pair_sine = jnp.where(is_key, sine, 0.0)
        y = lax.axis_index("seq") % 2
        both = (grad_pairs.astype(F32) + grad_pairs_y.astype(F32))[:, None]
        spread = jnp.concatenate([jnp.where(y == 0, both, 0.0), jnp.where(y == 1, both, 0.0)], axis=1)
        summed = lax.psum_scatter(spread.reshape((n,) + grad_pairs.shape[1:]), "seq", scatter_dimension=0)
        heads = lax.all_gather(summed, "fsdp")
        grad_heads = lax.dynamic_index_in_dim(
            lax.dynamic_slice_in_dim(heads, c * 2, 2, 0), me // 2, 1, keepdims=False
        )
        grad_query_full = rotate(
            grad_query.reshape(rows, 2, DH), cosine[:, None], -sine[:, None]
        ).reshape(rows, 2 * DH)
        scale_query = jnp.sum(query_raw * grad_query_full, axis=0)
        grad_query_low = (grad_query_full * my_query_scale).astype(BF16)
        grad_pair_full = jnp.concatenate(
            [rotate(grad_heads[j], pair_cosine, -pair_sine) for j in range(2)], axis=1
        )
        scale_pair = jnp.sum(pair_raw * grad_pair_full, axis=0)
        grad_pair_low = (grad_pair_full * my_pair_scale).astype(BF16)
        joined = jnp.concatenate([grad_query_low, grad_pair_low], axis=1)
        grad_first_sum = contract_last(grad_query_low, query_code) + contract_last(grad_pair_low, key_value_code)
        grad_first_input = group_reduce(10, grad_first_sum.astype(BF16).reshape(GROUP, own, width), F32)
        my_inputs = tokens[0].astype(F32)
        my_inverse = rms_inverse(my_inputs)
        first = my_inputs * my_inverse
        gain_one = jnp.sum(grad_first_input * first, axis=0)
        grad_inputs = grad_middle + norm_back(my_inverse, first, grad_first_input * gain[0])

    wholes = lanes(jnp.concatenate([gain_one, gain_two, gain_three, scale_output]), 72)
    parts = [scale_query, scale_pair, scale_gate, scale_down, gain_four]
    part_rows = lanes(jnp.concatenate(parts), 56)
    if n == 8:
        whole_total, part_total, gate_three, output_grad, attention_grad, *_ = finish(
            11,
            n,
            tiles - tiles_three,
            tiles_three,
            wholes,
            part_rows,
            gate_pairs,
            mixed_pair + (grad_branch, grad_branch_y),
            first_pair + (joined, joined_y),
        )
        output_grad = output_grad.T
        gate_grad = jnp.concatenate([gate_zero, gate_one, gate_two, gate_three], axis=1)
    else:
        whole_total, part_total = totals(11, n, wholes, part_rows)

        def weight_sum(left, right):
            return lax.psum_scatter(dot(left.reshape(-1, rows), right), "seq", scatter_dimension=0, tiled=True)

        gate_grad = weight_sum(second_turned, grad_gate_up)
        output_grad = weight_sum(mixed_slices.transpose(0, 1, 3, 2), grad_branch.T)
        attention_grad = weight_sum(first_turned, joined)
    whole_total = whole_total.reshape(-1)
    part_total = part_total.reshape(GROUP, -1)
    pieces = []
    start = 0
    for vector in parts:
        pieces.append(part_total[:, start : start + vector.shape[0]].reshape(-1))
        start += vector.shape[0]
    q_width = query_code.shape[1]
    return (
        result[None],
        grad_inputs[None],
        attention_grad[:, :q_width],
        attention_grad[:, q_width:],
        output_grad,
        gate_grad,
        down_grad,
        pieces[0],
        pieces[1],
        whole_total[3 * width :],
        pieces[2],
        pieces[3],
        jnp.concatenate([whole_total[: 3 * width], pieces[4]]).reshape(4, width),
    )


def solution(mesh):
    return jax.shard_map(
        functools.partial(per_device, mesh.shape["seq"]),
        mesh=mesh,
        in_specs=(
            P("fsdp", "seq", None),
            P("fsdp", "seq"),
            P("fsdp", "seq"),
            P("fsdp", "seq"),
            P(None, "fsdp"),
            P(None, "fsdp"),
            P(None, "fsdp"),
            P(None, "fsdp"),
            P(None, "fsdp"),
            P(),
            P(),
            P(),
            P(),
            P(),
            P(),
            P("fsdp", "seq", None),
        ),
        out_specs=(
            P("fsdp", "seq", None),
            P("fsdp", "seq", None),
            P("seq", "fsdp"),
            P("seq", "fsdp"),
            P("seq", "fsdp"),
            P("seq", "fsdp"),
            P("seq", "fsdp"),
            P(),
            P(),
            P(),
            P(),
            P(),
            P(),
        ),
        check_vma=False,
    )
```

```python
import functools
import math

import jax
import jax.numpy as jnp
from jax import lax
from jax.experimental import pallas as pl
from jax.experimental.pallas import tpu as pltpu
from jax.sharding import PartitionSpec as P

HQ = 8
HK = 4
DH = 256
FF = 9216
GROUP = 4
TILE = 384
EPSILON = 1e-06
CAP = 50.0
BASE = 10000.0
VMEM_LIMIT = 60 * 1024 * 1024
MESH = pl.DeviceIdType.MESH
ANY = pl.BlockSpec(memory_space=pl.ANY)
VMEM = pl.BlockSpec(memory_space=pltpu.VMEM)
DMA = pltpu.SemaphoreType.DMA
F32 = jnp.float32
BF16 = jnp.bfloat16


def dot(left, right):
    return jnp.dot(left, right, preferred_element_type=F32)


def contract_last(left, right):
    return lax.dot_general(left, right, (((1,), (1,)), ((), ())), preferred_element_type=F32)


def contract_first(left, right):
    return lax.dot_general(left, right, (((0,), (0,)), ((), ())), preferred_element_type=F32)


def place_now():
    seq = lax.axis_index("seq")
    fsdp = lax.axis_index("fsdp")
    return seq, fsdp, fsdp // 2, fsdp % 2


def greet(peers):
    barrier = pltpu.get_barrier_semaphore()
    for peer in peers:
        pl.semaphore_signal(barrier, inc=1, device_id=peer, device_id_type=MESH)
    pl.semaphore_wait(barrier, len(peers))


def remote(src, dst, send, recv, peer):
    return pltpu.make_async_remote_copy(
        src_ref=src, dst_ref=dst, send_sem=send, recv_sem=recv, device_id=peer, device_id_type=MESH
    )


def comm_call(kernel, cid, out_shape, scratch, in_specs, out_specs):
    return pl.pallas_call(
        kernel,
        out_shape=out_shape,
        in_specs=in_specs,
        out_specs=out_specs,
        scratch_shapes=scratch,
        compiler_params=pltpu.CompilerParams(
            collective_id=cid, has_side_effects=True, vmem_limit_bytes=VMEM_LIMIT
        ),
    )


def group_reduce_kernel(parts, src, out, from_core, to_x, from_x, cs, cr, xs, xr):
    seq, me, x, c = place_now()
    across = (seq, (1 - x) * 2 + c)
    beside = (seq, x * 2 + 1 - c)
    greet([across, beside])
    rows = src.shape[1]
    step = rows // parts
    order = [1 - x, x]
    cores = []
    for i in range(2):
        for k in range(parts):
            span = pl.ds(k * step, step)
            copy = remote(
                src.at[order[i] * 2 + 1 - c, span], from_core.at[i, span], cs.at[i, k], cr.at[i, k], beside
            )
            copy.start()
            cores.append(copy)
    sends = []
    for k in range(parts):
        span = pl.ds(k * step, step)
        cores[k].wait_recv()
        to_x[span, :] = (
            src[order[0] * 2 + c, span, :].astype(F32) + from_core[0, span, :].astype(F32)
        ).astype(BF16)
        copy = remote(to_x.at[span], from_x.at[span], xs.at[k], xr.at[k], across)
        copy.start()
        sends.append(copy)
    for k in range(parts):
        span = pl.ds(k * step, step)
        cores[parts + k].wait_recv()
        sends[k].wait_recv()
        out[span, :] = (
            src[order[1] * 2 + c, span, :].astype(F32)
            + from_core[1, span, :].astype(F32)
            + from_x[span, :].astype(F32)
        ).astype(out.dtype)
    for copy in cores + sends:
        copy.wait_send()


def group_reduce(cid, value, dtype, parts=4):
    rows, width = value.shape[1:]
    return comm_call(
        functools.partial(group_reduce_kernel, parts),
        cid,
        jax.ShapeDtypeStruct((rows, width), dtype),
        [pltpu.VMEM((2, rows, width), BF16), pltpu.VMEM((rows, width), BF16), pltpu.VMEM((rows, width), BF16),
         DMA((2, parts)), DMA((2, parts)), DMA((parts,)), DMA((parts,))],
        [VMEM],
        VMEM,
    )(value)


def total_kernel(rounds, whole, part, whole_out, part_out, bufs, gots, mine, theirs, ss, rs):
    seq, me, x, c = place_now()
    across = (seq, (1 - x) * 2 + c)
    beside = (seq, x * 2 + 1 - c)
    partners = []
    for r in range(rounds):
        bit = 1 << r
        partners.append((seq + bit - 2 * bit * ((seq // bit) % 2), me))
    greet(partners + [across, beside])
    rows = whole.shape[0]
    bufs[0, :rows, :] = whole[...]
    bufs[0, rows:, :] = part[...]
    for r in range(rounds + 1):
        partner = partners[r] if r < rounds else across
        copy = remote(bufs.at[r], gots.at[r], ss.at[r], rs.at[r], partner)
        copy.start()
        copy.wait()
        if r < rounds:
            bufs[r + 1] = bufs[r] + gots[r]
    mine[0, :rows, :] = bufs[rounds, :rows, :] + gots[rounds, :rows, :]
    mine[0, rows:, :] = bufs[rounds, rows:, :]
    mine[1, rows:, :] = gots[rounds, rows:, :]
    mine[1, :rows, :] = jnp.zeros_like(whole)
    copy = remote(mine, theirs, ss.at[rounds + 1], rs.at[rounds + 1], beside)
    copy.start()
    copy.wait()
    whole_out[...] = mine[0, :rows, :] + theirs[0, :rows, :]
    part_out[x * 2 + c] = mine[0, rows:, :]
    part_out[(1 - x) * 2 + c] = mine[1, rows:, :]
    part_out[x * 2 + 1 - c] = theirs[0, rows:, :]
    part_out[(1 - x) * 2 + 1 - c] = theirs[1, rows:, :]


def totals(cid, n, whole, part):
    rounds = int(math.log2(n))
    rows = whole.shape[0] + part.shape[0]
    return comm_call(
        functools.partial(total_kernel, rounds),
        cid,
        [jax.ShapeDtypeStruct(whole.shape, F32), jax.ShapeDtypeStruct((GROUP,) + part.shape, F32)],
        [pltpu.VMEM((rounds + 1, rows, 128), F32), pltpu.VMEM((rounds + 1, rows, 128), F32),
         pltpu.VMEM((2, rows, 128), F32), pltpu.VMEM((2, rows, 128), F32),
         DMA((rounds + 2,)), DMA((rounds + 2,))],
        [VMEM, VMEM],
        [VMEM, VMEM],
    )(whole, part)


def turned(block, unit, to):
    half = to.shape[1]
    flat = contract_last(unit[...], block)
    to[0] = flat[:half].astype(BF16)
    to[1] = flat[half:].astype(BF16)


def fill_unit(unit):
    shape = unit.shape
    unit[...] = jnp.where(
        lax.broadcasted_iota(jnp.int32, shape, 0) == lax.broadcasted_iota(jnp.int32, shape, 1), 1.0, 0.0
    ).astype(BF16)


def front_kernel(n, *refs):
    tok, cot, meta, g1, rates, q_scale, p_scale, wq, wkv = refs[:9]
    toks, cots, own_meta, metas, out, q, q_raw, p_raw, cosine, sine, turned_o = refs[9:20]
    (tb, ab, wqs, wkvs, heads, om, unit, at,
     ws, txs, txr, tcs, tcr, tfs, tfr, gms, gmr, own_sem, hs, hr, ms, mr, rs, rr, ls, lr, ys, yr,
     xs, xr, cs, cr, fs, fr, os) = refs[20:]
    seq, me, x, c = place_now()
    y = seq % 2
    z = seq // 2
    nz = n // 2
    across = (seq, (1 - x) * 2 + c)
    beside = (seq, x * 2 + 1 - c)
    group = [(seq, lax.rem(me + d, GROUP)) for d in range(1, GROUP)]
    load_q = pltpu.make_async_copy(wq, wqs, ws.at[0])
    load_kv = pltpu.make_async_copy(wkv, wkvs, ws.at[1])
    load_q.start()
    load_kv.start()
    greet(group + [(lax.rem(seq + d, n), me) for d in range(1, n)])
    blk = tok.shape[0] // GROUP
    part = tok.shape[1]
    own = blk

    sends = []
    for k in range(GROUP):
        rows = pl.ds(k * blk, blk)
        copy = remote(tok.at[rows], tb.at[me, rows], txs.at[k], txr.at[k], across)
        copy.start()
        sends.append(copy)
    to_core = remote(tok, tb.at[me], tcs, tcr, beside)
    to_core.start()
    group_meta = []
    for d in range(1, GROUP):
        copy = remote(meta, om.at[me], gms.at[d - 1], gmr.at[d - 1], group[d - 1])
        copy.start()
        group_meta.append(copy)
    own_tok = pltpu.make_async_copy(tok, tb.at[me], own_sem.at[0])
    own_tok.start()
    own_row = pltpu.make_async_copy(meta, om.at[me], own_sem.at[1])
    own_row.start()
    fill_unit(unit)
    for copy in group_meta:
        copy.wait()
    own_row.wait()
    width = GROUP * part
    half = DH // 2
    js = range(GROUP)
    is_key = jnp.where(x == 0, 1.0, 0.0).astype(F32)

    def process(p):
        def norm(i, carry):
            span = lambda j: pl.ds(pl.multiple_of(j * blk + i * 32, 32), 32)
            values = [tb[p, span(j), :].astype(F32) for j in js]
            total = values[0] * values[0]
            for value in values[1:]:
                total = total + value * value
            inverse = lax.rsqrt(jnp.sum(total, axis=1, keepdims=True) * (1.0 / width) + EPSILON)
            to = pl.ds(pl.multiple_of(p * own + i * 32, 32), 32)
            for j in js:
                ab[j, to, :] = (values[j] * inverse * g1[j]).astype(BF16)
            return carry

        lax.fori_loop(0, blk // 32, norm, 0)
        rows = pl.ds(pl.multiple_of(p * own, 128), own)
        turn = jnp.broadcast_to(om[p, 1:2, :], (128, 128)).T * rates[...]
        cos = jnp.cos(turn)
        sin = jnp.sin(turn)
        cosine[rows, :] = cos
        sine[rows, :] = sin

        def product(weights):
            total = dot(ab[0, rows, :], weights[0:part, :])
            for j in range(1, GROUP):
                total = total + dot(ab[j, rows, :], weights[j * part : (j + 1) * part, :])
            return total

        plain = product(wqs)
        q_raw[rows, :] = plain
        plain = plain * q_scale[...]
        for h in range(2):
            one = plain[:, h * DH : h * DH + half]
            two = plain[:, h * DH + half : (h + 1) * DH]
            q[rows, h * DH : h * DH + half] = (one * cos - two * sin).astype(BF16)
            q[rows, h * DH + half : (h + 1) * DH] = (two * cos + one * sin).astype(BF16)
        cos = is_key * cos + (1.0 - is_key)
        sin = is_key * sin
        plain = product(wkvs)
        p_raw[rows, :] = plain
        plain = plain * p_scale[...]
        for h in range(2):
            one = plain[:, h * DH : h * DH + half]
            two = plain[:, h * DH + half : (h + 1) * DH]
            heads[h, rows, :half] = (one * cos - two * sin).astype(BF16)
            heads[h, rows, half:] = (two * cos + one * sin).astype(BF16)

    own_tok.wait()
    load_q.wait()
    load_kv.wait()
    process(me)
    to_core.wait_recv()
    process(x * 2 + 1 - c)
    forwards = []
    for k in range(GROUP):
        sends[k].wait_recv()
        got = tb.at[(1 - x) * 2 + c, pl.ds(k * blk, blk)]
        forward = remote(got, got, tfs.at[k], tfr.at[k], beside)
        forward.start()
        forwards.append(forward)
    process((1 - x) * 2 + c)
    for forward in forwards:
        forward.wait_recv()
    process((1 - x) * 2 + 1 - c)

    for j in range(2):
        target = c * 2 + j

        @pl.when(target == me)
        def _():
            pltpu.make_async_copy(heads.at[j], out.at[seq, x], own_sem.at[0]).start()

        @pl.when(target != me)
        def _():
            remote(heads.at[j], out.at[seq, x], hs.at[j], hr.at[x], (seq, target)).start()

    small = []
    for d in range(1, n):
        copy = remote(om, metas.at[seq], ms.at[d - 1], mr.at[d - 1], (lax.rem(seq + d, n), me))
        copy.start()
        small.append(copy)
    outs = [
        pltpu.make_async_copy(om, metas.at[seq], os.at[0]),
        pltpu.make_async_copy(om, own_meta, os.at[1]),
        pltpu.make_async_copy(tb, toks, os.at[2]),
    ]
    for copy in outs:
        copy.start()
    for t in range(2):
        source = t * 2 + x

        @pl.when(source == me)
        def _():
            pltpu.make_async_copy(heads.at[0], out.at[seq, t], own_sem.at[0]).wait()

        @pl.when(source != me)
        def _():
            remote(heads.at[0], out.at[seq, t], hs.at[0], hr.at[t], (seq, source)).wait_recv()

    def block(owner_z, owner_y):
        return out.at[owner_z * 2 + owner_y]

    right = (seq + 2, me)
    left = (seq - 2, me)
    beyond = (z * 2 + 1 - y, me)

    def to_y(owner_z):
        remote(block(owner_z, y), block(owner_z, y), ys.at[owner_z], yr.at[owner_z], beyond).start()

    parts = 2
    step = cot.shape[0] // parts
    for t in range(1, nz + 1):
        go_right = z - t + 1
        go_left = z + t - 1
        if t > 1:

            @pl.when(go_right >= 0)
            def _():
                remote(block(go_right, y), block(go_right, y), rs.at[t - 1], rr.at[t - 1], left).wait_recv()

            @pl.when(go_left < nz)
            def _():
                remote(block(go_left, y), block(go_left, y), ls.at[t - 1], lr.at[t - 1], right).wait_recv()

        if t < nz:

            @pl.when((go_right >= 0) & (z < nz - 1))
            def _():
                remote(block(go_right, y), block(go_right, y), rs.at[t], rr.at[t], right).start()

            @pl.when((go_left < nz) & (z > 0))
            def _():
                remote(block(go_left, y), block(go_left, y), ls.at[t], lr.at[t], left).start()

        @pl.when(go_right >= 0)
        def _():
            to_y(go_right)

        if t > 1:

            @pl.when(go_left < nz)
            def _():
                to_y(go_left)

        if t == 1:
            xcopies = []
            for k in range(parts):
                rows = pl.ds(k * step, step)
                copy = remote(cot.at[rows], cots.at[me, rows], xs.at[k], xr.at[k], across)
                copy.start()
                xcopies.append(copy)
            ccopy = remote(cot, cots.at[me], cs, cr, beside)
            ccopy.start()
            own_cot = pltpu.make_async_copy(cot, cots.at[me], os.at[3])
            own_cot.start()
            for j in js:
                turned(ab[j], unit, at.at[j])
            turned_out = pltpu.make_async_copy(at, turned_o, os.at[4])
            turned_out.start()
    later = []
    for k in range(parts):
        rows = pl.ds(k * step, step)
        xcopies[k].wait()
        got = cots.at[(1 - x) * 2 + c, rows]
        forward = remote(got, got, fs.at[k], fr.at[k], beside)
        forward.start()
        later.append(forward)
    for k in range(nz):
        remote(block(k, 1 - y), block(k, 1 - y), ys.at[k], yr.at[k], beyond).wait()
    for t in range(1, nz):

        @pl.when((z - t + 1 >= 0) & (z < nz - 1))
        def _():
            remote(block(z, y), block(z, y), rs.at[t], rr.at[t], right).wait_send()

        @pl.when((z + t - 1 < nz) & (z > 0))
        def _():
            remote(block(z, y), block(z, y), ls.at[t], lr.at[t], left).wait_send()

    for j in range(2):

        @pl.when(c * 2 + j != me)
        def _():
            remote(heads.at[j], out.at[seq, x], hs.at[j], hr.at[x], (seq, c * 2 + j)).wait_send()

    for copy in small + later + [ccopy]:
        copy.wait()
    for copy in sends + forwards + [to_core]:
        copy.wait_send()
    for copy in outs + [own_cot, turned_out]:
        copy.wait()


def front(cid, n, tok, cot, meta, g1, rates, q_scale, p_scale, wq, wkv):
    nz = n // 2
    rows, part = tok.shape
    own = rows // GROUP
    deep, wide = wq.shape
    blocks = jax.ShapeDtypeStruct((GROUP, rows, part), BF16)
    table = jax.ShapeDtypeStruct((rows, DH // 2), F32)
    raw = jax.ShapeDtypeStruct((rows, wide), F32)
    turned_shape = (GROUP, 2, part // 2, rows)
    return comm_call(
        functools.partial(front_kernel, n),
        cid,
        [
            blocks,
            blocks,
            jax.ShapeDtypeStruct((GROUP,) + meta.shape, F32),
            jax.ShapeDtypeStruct((n, GROUP) + meta.shape, F32),
            jax.ShapeDtypeStruct((n, 2, rows, DH), BF16),
            jax.ShapeDtypeStruct((rows, wide), BF16),
            raw,
            raw,
            table,
            table,
            jax.ShapeDtypeStruct(turned_shape, BF16),
        ],
        [
            pltpu.VMEM((GROUP, rows, part), BF16),
            pltpu.VMEM((GROUP, rows, part), BF16),
            pltpu.VMEM((deep, wide), BF16),
            pltpu.VMEM((deep, wide), BF16),
            pltpu.VMEM((2, rows, DH), BF16),
            pltpu.VMEM((GROUP,) + meta.shape, F32),
            pltpu.VMEM((part, part), BF16),
            pltpu.VMEM(turned_shape, BF16),
            DMA((2,)), DMA((GROUP,)), DMA((GROUP,)), DMA, DMA, DMA((GROUP,)), DMA((GROUP,)), DMA((GROUP - 1,)),
            DMA((GROUP - 1,)), DMA((2,)), DMA((2,)), DMA((2,)), DMA((n - 1,)), DMA((n - 1,)), DMA((nz,)), DMA((nz,)),
            DMA((nz,)), DMA((nz,)), DMA((nz,)), DMA((nz,)), DMA((2,)), DMA((2,)), DMA, DMA, DMA((2,)), DMA((2,)),
            DMA((5,)),
        ],
        [VMEM, ANY, VMEM, VMEM, VMEM, VMEM, VMEM, ANY, ANY],
        [ANY, ANY, ANY, ANY, ANY, VMEM, VMEM, VMEM, VMEM, VMEM, ANY],
    )(tok, cot, meta, g1, rates, q_scale, p_scale, wq, wkv)


def branch_kernel(low, wo, toks, scale, g2, g3, b_o, raw_o, mid_o, ot_o, bt_o, ob, pb, bb, acc, unit, bt,
                  xs, xr, cs, cr, fs, fr, gxs, gxr, gcs, gcr, gfs, gfr, local, os, hos):
    seq, me, x, c = place_now()
    across = (seq, (1 - x) * 2 + c)
    beside = (seq, x * 2 + 1 - c)
    greet([across, beside])
    rows, heads = low.shape
    part = pb.shape[2]
    parts = 4
    size = rows // parts
    own = rows // GROUP
    js = range(GROUP)

    def spot(owner, k):
        return ob.at[pl.ds(k * size, size), pl.ds(pl.multiple_of(owner * heads, 128), heads)]

    sends = []
    for k in range(parts):
        copy = remote(low.at[pl.ds(k * size, size)], spot(me, k), xs.at[k], xr.at[k], across)
        copy.start()
        sends.append(copy)
    mine = ob.at[:, pl.ds(pl.multiple_of(me * heads, 128), heads)]
    to_core = remote(low, mine, cs, cr, beside)
    to_core.start()
    own_copy = pltpu.make_async_copy(low, mine, local)
    own_copy.start()
    fill_unit(unit)

    def add(owner, start):
        cols = pl.ds(pl.multiple_of(owner * heads, 128), heads)
        more = contract_last(ob[:, cols], wo[:, cols])
        acc[...] = more if start else acc[...] + more

    own_copy.wait()
    add(me, True)
    to_core.wait_recv()
    add(x * 2 + 1 - c, False)
    forwards = []
    for k in range(parts):
        sends[k].wait_recv()
        got = spot((1 - x) * 2 + c, k)
        forward = remote(got, got, fs.at[k], fr.at[k], beside)
        forward.start()
        forwards.append(forward)
    add((1 - x) * 2 + c, False)
    for forward in forwards:
        forward.wait_recv()
    add((1 - x) * 2 + 1 - c, False)

    over = []
    core = []
    for k in range(parts):
        span = pl.ds(k * size, size)
        pb[me, span, :] = acc[span, :].astype(BF16)
        piece = pb.at[me, span]
        copy = remote(piece, piece, gxs.at[k], gxr.at[k], across)
        copy.start()
        over.append(copy)
        copy = remote(piece, piece, gcs.at[k], gcr.at[k], beside)
        copy.start()
        core.append(copy)
    head_outs = []
    for j in js:
        for i in range(2):
            cols = pl.ds(j * heads + i * (heads // 2), heads // 2)
            copy = pltpu.make_async_copy(ob.at[:, cols], ot_o.at[j, i], hos.at[j, i])
            copy.start()
            head_outs.append(copy)
    passed = []
    for k in range(parts):
        over[k].wait_recv()
        got = pb.at[(1 - x) * 2 + c, pl.ds(k * size, size)]
        forward = remote(got, got, gfs.at[k], gfr.at[k], beside)
        forward.start()
        passed.append(forward)
    for copy in core + passed:
        copy.wait_recv()
    mean = 1.0 / (GROUP * part)

    def rowsum(values):
        total = values[0] * values[0]
        for value in values[1:]:
            total = total + value * value
        return jnp.sum(total, axis=1, keepdims=True) * mean

    def norms(i, carry):
        pack = i // (own // 16)
        inner = i % (own // 16) * 16
        span = pl.ds(pl.multiple_of(i * 16, 16), 16)
        branch = [pb[j, span, :].astype(F32) * scale[j] for j in js]
        inverse = lax.rsqrt(rowsum(branch) + EPSILON)
        middle = [
            toks[pack, pl.ds(pl.multiple_of(j * own + inner, 16), 16), :].astype(F32) + branch[j] * inverse * g2[j]
            for j in js
        ]
        inverse = lax.rsqrt(rowsum(middle) + EPSILON)
        for j in js:
            bb[j, span, :] = (middle[j] * inverse * g3[j]).astype(BF16)

        @pl.when(pack == me)
        def _():
            for j in js:
                mid_o[j, pl.ds(pl.multiple_of(inner, 16), 16), :] = middle[j]

        return carry

    lax.fori_loop(0, rows // 16, norms, 0)
    b_out = pltpu.make_async_copy(bb, b_o, os.at[1])
    b_out.start()
    raw_out = pltpu.make_async_copy(pb.at[:, pl.ds(pl.multiple_of(me * own, 128), own)], raw_o, os.at[2])
    raw_out.start()
    for j in js:
        turned(bb[j], unit, bt.at[j])
    bt_out = pltpu.make_async_copy(bt, bt_o, os.at[3])
    bt_out.start()
    for copy in sends + forwards + over + core + passed + [to_core]:
        copy.wait_send()
    for copy in head_outs + [b_out, raw_out, bt_out]:
        copy.wait()


def branch_forward(cid, low, wo, toks, scale, g2, g3):
    rows, heads = low.shape
    part = wo.shape[0]
    own = rows // GROUP
    turned_b = (GROUP, 2, part // 2, rows)
    slices = (GROUP, 2, rows, heads // 2)
    four = DMA((4,))
    return comm_call(
        branch_kernel,
        cid,
        [
            jax.ShapeDtypeStruct((GROUP, rows, part), BF16),
            jax.ShapeDtypeStruct((GROUP, own, part), BF16),
            jax.ShapeDtypeStruct((GROUP, own, part), F32),
            jax.ShapeDtypeStruct(slices, BF16),
            jax.ShapeDtypeStruct(turned_b, BF16),
        ],
        [
            pltpu.VMEM((rows, GROUP * heads), BF16),
            pltpu.VMEM((GROUP, rows, part), BF16),
            pltpu.VMEM((GROUP, rows, part), BF16),
            pltpu.VMEM((rows, part), F32),
            pltpu.VMEM((part, part), BF16),
            pltpu.VMEM(turned_b, BF16),
            four, four, DMA, DMA, four, four, four, four, four, four, four, four, DMA, four, DMA((GROUP, 2)),
        ],
        [VMEM] * 6,
        [ANY, ANY, VMEM, ANY, ANY],
    )(low, wo, toks, scale, g2, g3)


def masks(n, own_ref, meta_ref):
    def column(row):
        return jnp.broadcast_to(own_ref[0, row : row + 1, :], (128, 128)).T

    row_document = column(0)
    row_place = column(1)
    out = []
    for j in range(n):
        key_place = meta_ref[j, 0, 1:2, :]
        key_document = meta_ref[j, 0, 2:3, :]
        allowed = (row_document == key_document) & (key_place <= row_place) | (key_place == row_place)
        out.append(allowed)
    return out


def attend_kernel(n, q_ref, kv_ref, own_ref, meta_ref, low_ref, mixed_ref, total_ref):
    keys = kv_ref[:, 0].reshape(n * 128, DH)
    values = kv_ref[:, 1].reshape(n * 128, DH)
    allowed = masks(n, own_ref, meta_ref)
    for h in range(2):
        cols = slice(h * DH, (h + 1) * DH)
        raw = contract_last(q_ref[:, cols], keys)
        pieces = []
        total = jnp.zeros((128, 128), F32)
        for j in range(n):
            squash = jnp.tanh(raw[:, j * 128 : (j + 1) * 128] * (DH ** (-0.5) / CAP))
            mass = jnp.where(allowed[j], jnp.exp(CAP * squash), 0.0)
            total = total + mass
            pieces.append(mass.astype(BF16))
        row = jnp.sum(total, axis=1, keepdims=True)
        mixed = dot(jnp.concatenate(pieces, axis=1), values) / row
        mixed_ref[:, cols] = mixed
        low_ref[:, cols] = mixed.astype(BF16)
        total_ref[:, h * 128 : (h + 1) * 128] = jnp.broadcast_to(row, (128, 128))


def attend(n, query, pairs, own_meta, metas):
    return pl.pallas_call(
        functools.partial(attend_kernel, n),
        grid=(GROUP,),
        out_shape=[
            jax.ShapeDtypeStruct(query.shape, BF16),
            jax.ShapeDtypeStruct(query.shape, F32),
            jax.ShapeDtypeStruct((query.shape[0], 256), F32),
        ],
        in_specs=[
            pl.BlockSpec((128, 2 * DH), lambda p: (p, 0)),
            pl.BlockSpec((n, 2, 128, DH), lambda p: (0, 0, p, 0)),
            pl.BlockSpec((1, 8, 128), lambda p: (p, 0, 0)),
            pl.BlockSpec((n, 1, 8, 128), lambda p: (0, p, 0, 0)),
        ],
        out_specs=[
            pl.BlockSpec((128, 2 * DH), lambda p: (p, 0)),
            pl.BlockSpec((128, 2 * DH), lambda p: (p, 0)),
            pl.BlockSpec((128, 256), lambda p: (p, 0)),
        ],
        compiler_params=pltpu.CompilerParams(vmem_limit_bytes=VMEM_LIMIT),
    )(query, pairs, own_meta, metas)


def back_pack(n, keys, values, allowed, q_ref, grad_ref, mixed_ref, total_ref, dq_ref, dkv_ref):
    grad_keys = None
    for h in range(2):
        cols = slice(h * DH, (h + 1) * DH)
        query = q_ref[:, cols]
        grad = grad_ref[:, cols]
        delta = jnp.sum(grad.astype(F32) * mixed_ref[:, cols], axis=1, keepdims=True)
        inverse = 1.0 / total_ref[:, h * 128 : (h + 1) * 128]
        raw = contract_last(query, keys)
        grad_share = contract_last(grad, values)
        shares = []
        grads = []
        for j in range(n):
            span = slice(j * 128, (j + 1) * 128)
            squash = jnp.tanh(raw[:, span] * (DH ** (-0.5) / CAP))
            share = jnp.where(allowed[j], jnp.exp(CAP * squash), 0.0) * inverse
            shares.append(share.astype(BF16))
            grads.append(
                (share * (grad_share[:, span] - delta) * ((1.0 - squash * squash) * DH ** (-0.5))).astype(BF16)
            )
        share = jnp.concatenate(shares, axis=1)
        grad_raw = jnp.concatenate(grads, axis=1)
        dq_ref[:, cols] = dot(grad_raw, keys)
        new_keys = contract_first(grad_raw, query)
        new_values = contract_first(share, grad)
        if grad_keys is None:
            grad_keys, grad_values = new_keys, new_values
        else:
            grad_keys, grad_values = grad_keys + new_keys, grad_values + new_values
    dkv_ref[:, :, 0] = grad_keys.astype(BF16).reshape(n // 2, 2, 128, DH)
    dkv_ref[:, :, 1] = grad_values.astype(BF16).reshape(n // 2, 2, 128, DH)


class Chain:
    def __init__(self, nz, count, seq, me, partial, keep, landing, scratch):
        self.nz, self.count, self.partial, self.keep = nz, count, partial, keep
        self.z = seq // 2
        self.right, self.left = (seq + 2, me), (seq - 2, me)
        self.got_r, self.got_l = landing
        (self.out_r, self.out_l, self.in_r, self.in_l, self.stage, self.ss_r, self.sr_r, self.ss_l, self.sr_l,
         self.keep_sem, self.load_sem) = scratch

    @staticmethod
    def landing(nz, count, rows, width):
        return [jax.ShapeDtypeStruct((count, nz - 1, rows, width), BF16)] * 2

    @staticmethod
    def scratch(nz, count, rows, width):
        hops = nz - 1
        message = (rows, width)
        sems = DMA((count, hops))
        return [
            pltpu.VMEM((hops,) + message, BF16), pltpu.VMEM((hops,) + message, BF16),
            pltpu.VMEM(message, BF16), pltpu.VMEM(message, BF16),
            pltpu.VMEM((2,) + message, F32), sems, sems, sems, sems, DMA((2,)), DMA((2,)),
        ]

    def copy_right(self, j, s, peer):
        return remote(
            self.out_r.at[s - 1], self.got_r.at[j, s - 1], self.ss_r.at[j, s - 1], self.sr_r.at[j, s - 1], peer
        )

    def copy_left(self, j, s, peer):
        return remote(
            self.out_l.at[s - 1], self.got_l.at[j, s - 1], self.ss_l.at[j, s - 1], self.sr_l.at[j, s - 1], peer
        )

    def load_right(self, j, s):
        return pltpu.make_async_copy(self.got_r.at[j, s - 1], self.in_r, self.load_sem.at[0])

    def load_left(self, j, s):
        return pltpu.make_async_copy(self.got_l.at[j, s - 1], self.in_l, self.load_sem.at[1])

    def step(self, j, s):
        z, nz = self.z, self.nz

        def one(go, copy, load, out, into, to, source, first):
            more = (s > 1) & jnp.logical_not(first)

            @pl.when(more)
            def _():
                copy(j, s - 1, source).wait_recv()
                load(j, s - 1).start()

            @pl.when(j > 0)
            def _():
                copy(j - 1, s, to).wait_send()

            total = self.partial(go, j)

            @pl.when(more)
            def _():
                load(j, s - 1).wait()
                out[s - 1] = (total + into[...].astype(F32)).astype(BF16)

            @pl.when(jnp.logical_not(more))
            def _():
                out[s - 1] = total.astype(BF16)

            copy(j, s, to).start()

        go_right = z + nz - s
        go_left = z - nz + s

        @pl.when(go_right < nz)
        def _():
            one(go_right, self.copy_right, self.load_right, self.out_r, self.in_r, self.right, self.left, z == 0)

        @pl.when(go_left >= 0)
        def _():
            one(go_left, self.copy_left, self.load_left, self.out_l, self.in_l, self.left, self.right, z == nz - 1)

    def end(self, j):
        z, nz = self.z, self.nz
        k = j % 2

        @pl.when(j >= 2)
        def _():
            self.keep(j - 2, self.stage.at[k], self.keep_sem.at[k]).wait()

        @pl.when(z > 0)
        def _():
            self.copy_right(j, nz - 1, self.left).wait_recv()
            self.load_right(j, nz - 1).start()

        @pl.when(z < nz - 1)
        def _():
            self.copy_left(j, nz - 1, self.right).wait_recv()
            self.load_left(j, nz - 1).start()

        self.stage[k] = self.partial(z, j)

        @pl.when(z > 0)
        def _():
            self.load_right(j, nz - 1).wait()
            self.stage[k] += self.in_r[...].astype(F32)

        @pl.when(z < nz - 1)
        def _():
            self.load_left(j, nz - 1).wait()
            self.stage[k] += self.in_l[...].astype(F32)

        self.keep(j, self.stage.at[k], self.keep_sem.at[k]).start()

    def run(self, first, last):
        hops = self.nz - 1

        def unit(u, carry):
            slot = u // hops
            s = u % hops + 1
            j = slot - (s - 1)

            @pl.when((j >= 0) & (j < self.count))
            def _():
                self.step(j, s)

            @pl.when((s == hops) & (slot >= hops))
            def _():
                self.end(slot - hops)

            return carry

        lax.fori_loop(first, last, unit, 0)

    def units(self):
        return (self.count + self.nz - 1) * (self.nz - 1)

    def finish(self):
        z, nz = self.z, self.nz
        last = self.count - 1
        for j in range(max(0, last - 1), last + 1):
            self.keep(j, self.stage.at[j % 2], self.keep_sem.at[j % 2]).wait()
        for s in range(1, nz):

            @pl.when(z + nz - s < nz)
            def _():
                self.copy_right(last, s, self.right).wait_send()

            @pl.when(z - nz + s >= 0)
            def _():
                self.copy_left(last, s, self.left).wait_send()


def greet_all(seq, me, nz, others):
    z = seq // 2
    barrier = pltpu.get_barrier_semaphore()
    for peer in others + [(seq + 1 - 2 * (seq % 2), me)]:
        pl.semaphore_signal(barrier, inc=1, device_id=peer, device_id_type=MESH)

    @pl.when(z > 0)
    def _():
        pl.semaphore_signal(barrier, inc=1, device_id=(seq - 2, me), device_id_type=MESH)

    @pl.when(z < nz - 1)
    def _():
        pl.semaphore_signal(barrier, inc=1, device_id=(seq + 2, me), device_id_type=MESH)

    pl.semaphore_wait(barrier, len(others) + 1 + jnp.where(z > 0, 1, 0) + jnp.where(z < nz - 1, 1, 0))


def gate_chain(nz, first, count, seq, me, bt, bty, dg, dgy, out, landing, slabs, halves, slab_sem, scratch):
    loads = [pltpu.make_async_copy(bt.at[:, seq % 2], halves.at[0], slab_sem.at[2])]
    loads.append(pltpu.make_async_copy(bty, halves.at[1], slab_sem.at[3]))
    for i, ref in enumerate((dg, dgy)):
        loads.append(
            pltpu.make_async_copy(ref.at[:, pl.ds(first * TILE, count * TILE)], slabs.at[i], slab_sem.at[i])
        )

    def partial(k, j):
        cols = pl.ds(pl.multiple_of(j * TILE, 128), TILE)
        return dot(halves[0, k], slabs[0, :, cols]) + dot(halves[1, k], slabs[1, :, cols])

    def keep(j, stage, sem):
        return pltpu.make_async_copy(stage, out.at[:, pl.ds(pl.multiple_of(j * TILE, 128), TILE)], sem)

    return Chain(nz, count, seq, me, partial, keep, landing, scratch), loads


def gate_landing(nz, count, bt):
    return Chain.landing(nz, count, bt.shape[2], TILE)


def gate_scratch(nz, count, bt):
    rows = bt.shape[3]
    return [
        pltpu.VMEM((2, rows, count * TILE), BF16), pltpu.VMEM((2, nz) + bt.shape[2:], BF16), DMA((4,))
    ] + Chain.scratch(nz, count, bt.shape[2], TILE)


def levels(code, step):
    return (jnp.floor(code.astype(F32) * (1.0 / step)) * step + step / 2.0).astype(BF16)


def gelu_parts(gate):
    root = math.sqrt(2.0 / math.pi)
    square = gate * gate
    bend = jnp.tanh(root * gate * (1.0 + 0.044715 * square))
    value = 0.5 * gate * (1.0 + bend)
    slope = 0.5 * (1.0 + bend) + 0.5 * gate * (1.0 - bend * bend) * root * (1.0 + 3 * 0.044715 * square)
    return value, slope


def strips(count, size, body):
    def step(i, carry):
        body(pl.ds(pl.multiple_of(i * size, size), size))
        return carry

    lax.fori_loop(0, count, step, 0)


def ffn_forward_kernel(tiles, riders, *refs):
    b, wgu, gs, wd, cots, g3, ds = refs[:7]
    refs = refs[7:]
    rider_in, refs = refs[:riders], refs[riders:]
    gu_o, hid_o, hidy_o, down_o, gf_o, gft_o, sums_o, lev_o, levd_o = refs[:9]
    refs = refs[9:]
    rider_out, refs = refs[:riders], refs[riders:]
    (both, other, hid, unit, wbuf, wlev, dbuf, dlev, acc, downs, wsem, dsem, lsem, ldsem, osem, xs, xr, oks, hs, hr, ks,
     ys, yr, fs, fr, gxs, gxr, gcs, gcr, gfs, gfr, rs, rr, outs) = refs
    seq, me, x, c = place_now()
    y = seq % 2
    across = (seq, (1 - x) * 2 + c)
    beside = (seq, x * 2 + 1 - c)
    beyond = (seq + 1 - 2 * y, me)
    rows, tw = both.shape[1:]
    part = b.shape[2]
    deep = GROUP * part
    per = tiles // 4

    def load_up(t):
        return pltpu.make_async_copy(wgu.at[:, pl.ds(pl.multiple_of(t * tw, 128), tw)], wbuf.at[t % 2], wsem.at[t % 2])

    def load_down(t, half):
        start = ((c + half) % 2 * tiles + t) * tw
        return pltpu.make_async_copy(
            wd.at[:, pl.ds(pl.multiple_of(start, 128), tw)], dbuf.at[t % 2, half], dsem.at[t % 2, half]
        )

    load_up(0).start()
    load_up(1).start()
    for t in range(2):
        for half in range(2):
            load_down(t, half).start()
    greet([across, beside, beyond])
    travellers = []
    for i in range(riders):
        share = pl.ds(2 * c, 2)
        copy = remote(rider_in[i].at[share, 1 - y], rider_out[i].at[share], rs.at[i, 0], rr.at[i, 0], beyond)
        copy.start()
        got = rider_out[i].at[share]
        travellers.append((copy, remote(got, got, rs.at[i, 1], rr.at[i, 1], beside)))
    acc[...] = jnp.zeros_like(acc)
    fill_unit(unit)

    def to_x(t):
        return remote(both.at[t % 3], other.at[t], xs.at[t], xr.at[t], across)

    def keep_own(t):
        return pltpu.make_async_copy(both.at[t % 3], gu_o.at[x, t], oks.at[t])

    def keep_other(t):
        return pltpu.make_async_copy(other.at[t], gu_o.at[1 - x, t], osem.at[t])

    def keep_level(t):
        return pltpu.make_async_copy(wlev.at[t % 2], lev_o.at[t], lsem.at[t % 2])

    def keep_down(t, half):
        return pltpu.make_async_copy(dlev.at[t % 2, half], levd_o.at[half, t], ldsem.at[t % 2, half])

    def to_core(t):
        return remote(hid.at[c * tiles + t], hid.at[c * tiles + t], hs.at[t], hr.at[t], beside)

    def slot(t, core):
        return (2 * core + t // (2 * per)) * per + t % per

    def keep(t, core, i):
        return pltpu.make_async_copy(hid.at[core * tiles + t], hid_o.at[slot(t, core)], ks.at[i, t])

    def to_y(t):
        return remote(hid.at[c * tiles + t], hidy_o.at[slot(t, c)], ys.at[t], yr.at[t], beyond)

    def for_mine(t):
        return (t // per) % 2 == y

    def wide(t):
        load_up(t).wait()

        @pl.when(t >= 2)
        def _():
            keep_level(t - 2).wait()

        def level(span):
            wlev[t % 2, span, :] = levels(wbuf[t % 2, span, :], 16.0)

        strips(deep // 128, 128, level)
        keep_level(t).start()

        @pl.when(t + 2 < tiles)
        def _():
            load_up(t + 2).start()

        @pl.when(t >= 3)
        def _():
            to_x(t - 3).wait_send()
            keep_own(t - 3).wait()

        scale = gs[t]

        def product(span):
            total = dot(b[0, span, :], wlev[t % 2, 0:part, :])
            for j in range(1, GROUP):
                total = total + dot(b[j, span, :], wlev[t % 2, j * part : (j + 1) * part, :])
            both[t % 3, span, :] = (total * scale).astype(BF16)

        strips(rows // 256, 256, product)
        to_x(t).start()
        keep_own(t).start()

    is_gate = jnp.where(x == 0, 1.0, 0.0).astype(F32)

    def middle(t):
        to_x(t).wait_recv()
        keep_other(t).start()

        def body(span):
            mine = both[t % 3, span, :].astype(F32)
            theirs = other[t, span, :].astype(F32)
            gate = is_gate * mine + (1.0 - is_gate) * theirs
            up = is_gate * theirs + (1.0 - is_gate) * mine
            hid[c * tiles + t, span, :] = (gelu_parts(gate)[0] * up).astype(BF16)

        strips(rows // 64, 64, body)
        to_core(t).start()

        @pl.when(for_mine(t))
        def _():
            keep(t, c, 0).start()

        @pl.when(jnp.logical_not(for_mine(t)))
        def _():
            to_y(t).start()

    def narrow(t):
        for half in range(2):
            load_down(t, half).wait()

            @pl.when(t >= 2)
            def _():
                keep_down(t - 2, half).wait()

            def level(span):
                dlev[t % 2, half, span, :] = levels(dbuf[t % 2, half, span, :], 64.0)

            strips(part // 64, 64, level)
            keep_down(t, half).start()

            @pl.when(t + 2 < tiles)
            def _():
                load_down(t + 2, half).start()

        to_core(t).wait_recv()

        def product(span):
            acc[span, :] += contract_last(hid[c * tiles + t, span, :], dlev[t % 2, 0]) + contract_last(
                hid[(1 - c) * tiles + t, span, :], dlev[t % 2, 1]
            )

        strips(rows // 256, 256, product)

        @pl.when(for_mine(t))
        def _():
            keep(t, 1 - c, 1).start()

    def step(i, carry):
        @pl.when(i < tiles)
        def _():
            wide(i)

        @pl.when(i >= 2)
        def _():
            narrow(i - 2)

        @pl.when((i >= 1) & (i < tiles + 1))
        def _():
            middle(i - 1)

        return carry

    lax.fori_loop(0, tiles + 2, step, 0)

    for copy, forward in travellers:
        copy.wait_recv()
        forward.start()
    parts = 4
    size = rows // parts
    sends = []
    own_sends = []
    for k in range(parts):
        span = pl.ds(k * size, size)
        downs[me, span, :] = acc[span, :].astype(BF16)
        piece = downs.at[me, span]
        copy = remote(piece, piece, gxs.at[k], gxr.at[k], across)
        copy.start()
        sends.append(copy)
        copy = remote(piece, piece, gcs.at[k], gcr.at[k], beside)
        copy.start()
        own_sends.append(copy)

    def pass_on(t, carry):
        @pl.when(for_mine(t))
        def _():
            got = hidy_o.at[slot(t, c)]
            remote(hid.at[0], got, ys.at[t], yr.at[t], beyond).wait_recv()
            remote(got, got, fs.at[t], fr.at[t], beside).start()

        return carry

    lax.fori_loop(0, tiles, pass_on, 0)
    forwards = []
    for k in range(parts):
        sends[k].wait_recv()
        got = downs.at[(1 - x) * 2 + c, pl.ds(k * size, size)]
        copy = remote(got, got, gfs.at[k], gfr.at[k], beside)
        copy.start()
        forwards.append(copy)
    for copy in own_sends + forwards:
        copy.wait_recv()
    down_out = pltpu.make_async_copy(downs, down_o, outs)
    down_out.start()
    sums_o[...] = jnp.zeros_like(sums_o)
    width = GROUP * acc.shape[1]

    def last_norm(i, carry):
        pack = i // 2
        span = pl.ds(pl.multiple_of(i * 64, 64), 64)
        inner = (i % 2) * 64

        def cot_of(j):
            return cots[pack, pl.ds(pl.multiple_of(j * 128 + inner, 64), 64), :].astype(F32)

        square = jnp.zeros((64, 1), F32)
        cross = jnp.zeros((64, 1), F32)
        for j in range(GROUP):
            value = downs[j, span, :].astype(F32) * ds[j]
            square = square + jnp.sum(value * value, axis=1, keepdims=True)
            cross = cross + jnp.sum(value * (cot_of(j) * g3[j]), axis=1, keepdims=True)
        inverse = lax.rsqrt(square * (1.0 / width) + EPSILON)
        raw = downs[me, span, :].astype(F32)
        normed = raw * ds[me] * inverse
        cot = cot_of(me)
        grad = inverse * (cot * g3[me] - normed * (cross * inverse * (1.0 / width)))
        gf_o[span, :] = (grad * ds[me]).astype(BF16)
        sums_o[0:1, :] += jnp.sum(raw * grad, axis=0, keepdims=True)
        sums_o[1:2, :] += jnp.sum(cot * normed, axis=0, keepdims=True)
        return carry

    lax.fori_loop(0, rows // 64, last_norm, 0)
    gft_o[...] = contract_last(unit[...], gf_o[...]).astype(BF16)

    for t in range(tiles - 3, tiles):
        to_x(t).wait_send()
        keep_own(t).wait()
    for t in range(tiles - 2, tiles):
        keep_level(t).wait()
        for half in range(2):
            keep_down(t, half).wait()

    def drain(t, carry):
        to_core(t).wait_send()
        keep_other(t).wait()

        @pl.when(for_mine(t))
        def _():
            keep(t, c, 0).wait()
            keep(t, 1 - c, 1).wait()
            got = hidy_o.at[slot(t, c)]
            remote(got, got, fs.at[t], fr.at[t], beside).wait_send()
            got = hidy_o.at[slot(t, 1 - c)]
            remote(got, got, fs.at[t], fr.at[t], beside).wait_recv()

        @pl.when(jnp.logical_not(for_mine(t)))
        def _():
            to_y(t).wait_send()

        return carry

    lax.fori_loop(0, tiles, drain, 0)
    for copy in sends + own_sends + forwards:
        copy.wait_send()
    for copy, forward in travellers:
        copy.wait_send()
        forward.wait()
    down_out.wait()


def ffn_forward(cid, b, wgu, gs, wd, cots, g3, ds, riders):
    rows, part = b.shape[1:]
    deep = GROUP * part
    tiles, _, tw = gs.shape
    count = len(riders)
    lone = max(count, 1)
    each = DMA((tiles,))
    four = DMA((4,))
    return comm_call(
        functools.partial(ffn_forward_kernel, tiles, count),
        cid,
        [
            jax.ShapeDtypeStruct((2, tiles, rows, tw), BF16),
            jax.ShapeDtypeStruct((tiles, rows, tw), BF16),
            jax.ShapeDtypeStruct((tiles, rows, tw), BF16),
            jax.ShapeDtypeStruct((GROUP, rows, part), BF16),
            jax.ShapeDtypeStruct((rows, part), BF16),
            jax.ShapeDtypeStruct((part, rows), BF16),
            jax.ShapeDtypeStruct((8, part), F32),
            jax.ShapeDtypeStruct((tiles, deep, tw), BF16),
            jax.ShapeDtypeStruct((2, tiles, part, tw), BF16),
        ]
        + [jax.ShapeDtypeStruct(r.shape[:1] + r.shape[2:], r.dtype) for r in riders],
        [
            pltpu.VMEM((3, rows, tw), BF16),
            pltpu.VMEM((tiles, rows, tw), BF16),
            pltpu.VMEM((2 * tiles, rows, tw), BF16),
            pltpu.VMEM((part, part), BF16),
            pltpu.VMEM((2, deep, tw), BF16),
            pltpu.VMEM((2, deep, tw), BF16),
            pltpu.VMEM((2, 2, part, tw), BF16),
            pltpu.VMEM((2, 2, part, tw), BF16),
            pltpu.VMEM((rows, part), F32),
            pltpu.VMEM((GROUP, rows, part), BF16),
            DMA((2,)), DMA((2, 2)), DMA((2,)), DMA((2, 2)), each, each, each, each, each, each, DMA((2, tiles)),
            each, each, each, each, four, four, four, four, four, four, DMA((lone, 2)), DMA((lone, 2)), DMA,
        ],
        [VMEM, ANY, VMEM, ANY, VMEM, VMEM, VMEM] + [ANY] * count,
        [ANY, ANY, ANY, ANY, VMEM, VMEM, VMEM, ANY, ANY] + [ANY] * count,
    )(b, wgu, gs, wd, cots, g3, ds, *riders)


def ffn_backward_kernel(tiles, nz, chained, gate_tiles, *refs):
    gf, gft, levd, lev, gs, gu, hid, hidy, bt, bty = refs[:10]
    dg_o, dgy_o, gsum_o, out, ddown_o, gate_o = refs[10:16]
    landing = refs[16:20] if chained else []
    refs = refs[len(landing) :]
    (hh, hy, gfy, wbuf, dbuf, pair, co, cgot, near, sx, xgot, dg, acc, low, from_core, to_xb, from_x,
     hsem, wsem, dsem, psem, cs, cr, xs, xr, ys, yr, os, gys, gyr, ccs, ccr, cxs, cxr) = refs[16:50]
    rest = refs[50:]
    seq, me, x, c = place_now()
    y = seq % 2
    across = (seq, (1 - x) * 2 + c)
    beside = (seq, x * 2 + 1 - c)
    beyond = (seq + 1 - 2 * y, me)
    rows, tw = dg.shape[1:]
    part = acc.shape[2]
    per = hid.shape[0] // 4 if chained else 0
    ring = dg.shape[0]

    def load_up(t):
        return pltpu.make_async_copy(lev.at[t], wbuf.at[t % 2], wsem.at[t % 2])

    def load_down(t, half):
        return pltpu.make_async_copy(levd.at[half, t], dbuf.at[t % 2, half], dsem.at[t % 2, half])

    def load_pair(t):
        return pltpu.make_async_copy(gu.at[:, t], pair.at[t % 2], psem.at[t % 2])

    for t in range(2):
        for half in range(2):
            load_down(t, half).start()
        load_pair(t).start()
        load_up(t).start()
    if chained:
        load_hid = pltpu.make_async_copy(hid, hh, hsem.at[0])
        load_hidy = pltpu.make_async_copy(hidy, hy, hsem.at[1])
        load_hid.start()
        load_hidy.start()

        def partial(k, j):
            return dot(gft[...], hh[k * per + j]) + dot(gfy[...], hy[k * per + j])

        def keep_sum(j, stage, sem):
            return pltpu.make_async_copy(stage, ddown_o.at[:, pl.ds(pl.multiple_of(j * tw, 128), tw)], sem)

        downs = Chain(nz, per, seq, me, partial, keep_sum, landing[:2], rest[:11])
        gates, gate_loads = gate_chain(
            nz, 0, gate_tiles, seq, me, bt, bty, dg_o, dgy_o, gate_o, landing[2:], *rest[11:14], rest[14:]
        )
        gate_loads[0].start()
        gate_loads[1].start()
        greet_all(seq, me, nz, [across, beside])
        gf_swap = remote(gft, gfy, gys, gyr, beyond)
        gf_swap.start()
    else:
        greet([across, beside, beyond])
    acc[...] = jnp.zeros_like(acc)

    def to_core(t):
        return remote(co.at[t % 2], cgot.at[t % 4], cs.at[t], cr.at[t], beside)

    def to_x(t):
        return remote(sx.at[t % 4], xgot.at[t], xs.at[t], xr.at[t], across)

    def columns(ref, t):
        return ref.at[:, pl.ds(pl.multiple_of(t * tw, 128), tw)]

    def to_y(t):
        return remote(dg.at[t % ring], columns(dgy_o, t), ys.at[t], yr.at[t], beyond)

    def keep(t):
        return pltpu.make_async_copy(dg.at[t % ring], columns(dg_o, t), os.at[t])

    def hidden(t):
        for half in range(2):
            load_down(t, half).wait()

        @pl.when(t >= 2)
        def _():
            to_core(t - 2).wait_send()

        def product(span):
            co[t % 2, span, :] = dot(gf[span, :], dbuf[t % 2, 1]).astype(BF16)

        strips(rows // 256, 256, product)
        to_core(t).start()

        def product_near(span):
            near[t % 2, span, :] = dot(gf[span, :], dbuf[t % 2, 0])

        strips(rows // 256, 256, product_near)

        @pl.when(t + 2 < tiles)
        def _():
            for half in range(2):
                load_down(t + 2, half).start()

    def chip(t):
        @pl.when(t >= 4)
        def _():
            to_x(t - 4).wait_send()

        to_core(t).wait_recv()

        def body(span):
            sx[t % 4, span, :] = (near[t % 2, span, :] + cgot[t % 4, span, :].astype(F32)).astype(BF16)

        strips(rows // 64, 64, body)
        to_x(t).start()

    is_gate = jnp.where(x == 0, 1.0, 0.0).astype(F32)

    def own(t):
        load_pair(t).wait()

        @pl.when(t >= ring)
        def _():
            to_y(t - ring).wait_send()
            keep(t - ring).wait()

        to_x(t).wait_recv()
        scale = gs[t]
        gsum_o[t] = jnp.zeros((8, tw), F32)

        def body(span):
            grad = sx[t % 4, span, :].astype(F32) + xgot[t, span, :].astype(F32)
            gate = pair[t % 2, 0, span, :].astype(F32)
            up = pair[t % 2, 1, span, :].astype(F32)
            value, slope = gelu_parts(gate)
            full = grad * (is_gate * (up * slope) + (1.0 - is_gate) * value)
            gsum_o[t, 0:1, :] += jnp.sum(pair[t % 2, x, span, :].astype(F32) * full, axis=0, keepdims=True)
            dg[t % ring, span, :] = (full * scale).astype(BF16)

        strips(rows // 64, 64, body)

        @pl.when(t + 2 < tiles)
        def _():
            load_pair(t + 2).start()

        to_y(t).start()
        keep(t).start()

    def back(t):
        load_up(t).wait()

        def product(span):
            for j in range(GROUP):
                acc[j, span, :] += contract_last(dg[t % ring, span, :], wbuf[t % 2, j * part : (j + 1) * part, :])

        strips(rows // 128, 128, product)

        @pl.when(t + 2 < tiles)
        def _():
            load_up(t + 2).start()

    def units(chain, i, table):
        unit = jnp.int32(0)
        hit = i < 0
        for when, u in table:
            unit = unit + jnp.where(i == when, u, 0)
            hit = hit | (i == when)

        @pl.when(hit)
        def _():
            chain.run(unit, unit + 1)

    def step(i, carry):
        @pl.when(i < tiles)
        def _():
            hidden(i)

        @pl.when((i >= 1) & (i < tiles + 1))
        def _():
            chip(i - 1)

        if chained:

            @pl.when(i == 1)
            def _():
                gf_swap.wait_recv()
                load_hid.wait()
                load_hidy.wait()

            @pl.when(i == 9)
            def _():
                for t in range(gate_tiles):
                    to_y(t).wait_recv()
                gate_loads[2].start()
                gate_loads[3].start()

            @pl.when(i == 10)
            def _():
                for load in gate_loads:
                    load.wait()

            units(downs, i, ((1, 0), (2, 3), (3, 4), (4, 6), (5, 7), (6, 8), (7, 10), (8, 11), (10, 14), (12, 17)))
            units(gates, i, ((10, 0), (11, 3), (12, 4), (13, 7), (14, 8)))

        @pl.when(i >= 3)
        def _():
            back(i - 3)

        @pl.when((i >= 2) & (i < tiles + 2))
        def _():
            own(i - 2)

        return carry

    lax.fori_loop(0, tiles + 3, step, 0)

    parts = 4
    block = rows // GROUP
    size = block // parts
    order = [1 - x, x]
    js = range(GROUP)
    cores = []
    for i in range(2):
        for k in range(parts):
            owner = order[i] * 2 + 1 - c
            span = pl.ds(k * size, size)
            for j in js:
                low[i, j, span, :] = acc[j, pl.ds(pl.multiple_of(owner * block + k * size, 16), size), :].astype(BF16)
            copy = remote(low.at[i, :, span], from_core.at[i, :, span], ccs.at[i, k], ccr.at[i, k], beside)
            copy.start()
            cores.append(copy)
    sends = []
    for k in range(parts):
        span = pl.ds(k * size, size)
        here = pl.ds(pl.multiple_of((order[0] * 2 + c) * block + k * size, 16), size)
        cores[k].wait_recv()
        for j in js:
            to_xb[j, span, :] = (acc[j, here, :] + from_core[0, j, span, :].astype(F32)).astype(BF16)
        copy = remote(to_xb.at[:, span], from_x.at[:, span], cxs.at[k], cxr.at[k], across)
        copy.start()
        sends.append(copy)
    if chained:
        gates.run(9, gates.units())
        downs.finish()
        gates.finish()
    for k in range(parts):
        span = pl.ds(k * size, size)
        here = pl.ds(pl.multiple_of((order[1] * 2 + c) * block + k * size, 16), size)
        cores[parts + k].wait_recv()
        sends[k].wait_recv()
        for j in js:
            out[j, span, :] = acc[j, here, :] + from_core[1, j, span, :].astype(F32) + from_x[j, span, :].astype(F32)

    for copy in cores + sends:
        copy.wait_send()
    for t in range(tiles - 2, tiles):
        to_core(t).wait_send()
    for t in range(tiles - 4, tiles):
        to_x(t).wait_send()
    for t in range(tiles - ring, tiles):
        to_y(t).wait_send()
        keep(t).wait()

    def drain(t, carry):
        to_y(t).wait_recv()
        return carry

    lax.fori_loop(gate_tiles if chained else 0, tiles, drain, 0)
    if chained:
        gf_swap.wait_send()


def ffn_backward(cid, n, gate_tiles, gf, gft, levd, lev, gs, gu, hid, hidy, bt, bty):
    rows, part = gf.shape
    deep = lev.shape[1]
    tiles, _, tw = gs.shape
    nz = n // 2
    chained = nz == 4
    per = tiles // nz if chained else 1
    block = rows // GROUP
    half = (tiles, rows, tw) if chained else (1, 16, 128)
    message = (part, tw)
    ring = 4
    each = DMA((tiles,))
    wide = jax.ShapeDtypeStruct((rows, tiles * tw), BF16)
    return comm_call(
        functools.partial(ffn_backward_kernel, tiles, nz, chained, gate_tiles),
        cid,
        [
            wide,
            wide,
            jax.ShapeDtypeStruct((tiles, 8, tw), F32),
            jax.ShapeDtypeStruct((GROUP, block, part), F32),
            jax.ShapeDtypeStruct((part, per * tw), F32),
            jax.ShapeDtypeStruct((bt.shape[2], max(gate_tiles, 1) * tw), F32),
        ]
        + (Chain.landing(nz, per, *message) + gate_landing(nz, gate_tiles, bt) if chained else []),
        [
            pltpu.VMEM(half, BF16),
            pltpu.VMEM(half, BF16),
            pltpu.VMEM((part, rows), BF16),
            pltpu.VMEM((2, deep, tw), BF16),
            pltpu.VMEM((2, 2, part, tw), BF16),
            pltpu.VMEM((2, 2, rows, tw), BF16),
            pltpu.VMEM((2, rows, tw), BF16),
            pltpu.VMEM((4, rows, tw), BF16),
            pltpu.VMEM((2, rows, tw), F32),
            pltpu.VMEM((4, rows, tw), BF16),
            pltpu.VMEM((tiles, rows, tw), BF16),
            pltpu.VMEM((ring, rows, tw), BF16),
            pltpu.VMEM((GROUP, rows, part), F32),
            pltpu.VMEM((2, GROUP, block, part), BF16),
            pltpu.VMEM((2, GROUP, block, part), BF16),
            pltpu.VMEM((GROUP, block, part), BF16),
            pltpu.VMEM((GROUP, block, part), BF16),
            DMA((2,)), DMA((2,)), DMA((2, 2)), DMA((2,)), each, each, each, each,
            each, each, each, DMA, DMA, DMA((2, 4)), DMA((2, 4)), DMA((4,)), DMA((4,)),
        ]
        + (Chain.scratch(nz, per, *message) + gate_scratch(nz, gate_tiles, bt) if chained else []),
        [VMEM, VMEM, ANY, ANY, VMEM, ANY, ANY, ANY, ANY, ANY],
        [ANY, ANY, VMEM, VMEM, ANY, ANY] + [ANY] * (4 if chained else 0),
    )(gf, gft, levd, lev, gs, gu, hid, hidy, bt, bty)


def branch_back_kernel(n, first, tiles, *refs):
    (gsi, mid, raw, cot, g2, g3, scale, wo, q, mixed, mass, own_meta, metas, kv, bt, bty, dg, dgy) = refs[:18]
    dmid, sums, gy, gyy, dq, dkv, gate_o, dkv_y = refs[18:26]
    refs = refs[1:]
    landing = refs[25:27] if tiles else []
    refs = refs[len(landing) :]
    (unit, gyt, gys, gy_all, part, from_core, to_x, from_x, grad, kvs, dkvs, es, er, el, cs, cr, xs, xr, ks, ds, yss, ysr,
     ows, pys, pyr) = refs[25:50]
    rest = refs[50:]
    seq, me, x, c = place_now()
    nz = n // 2
    across = (seq, (1 - x) * 2 + c)
    beside = (seq, x * 2 + 1 - c)
    beyond = (seq + 1 - 2 * (seq % 2), me)
    peers = [(seq, lax.rem(me + d, GROUP)) for d in range(1, GROUP)]
    chain = None
    if tiles:
        chain, loads = gate_chain(nz, first, tiles, seq, me, bt, bty, dg, dgy, gate_o, landing, *rest[:3], rest[3:])
        for load in loads:
            load.start()
        greet_all(seq, me, nz, peers)
    else:
        greet(peers + [beyond])
    width = GROUP * raw.shape[2]
    mean = 1.0 / width
    sums[...] = jnp.zeros_like(sums)
    js = range(GROUP)

    def rowsum(values):
        total = values[0]
        for value in values[1:]:
            total = total + value
        return jnp.sum(total, axis=1, keepdims=True) * mean

    def norms(span):
        middle = [mid[j, span, :] for j in js]
        up = [gsi[j, span, :] for j in js]
        inverse = lax.rsqrt(rowsum([v * v for v in middle]) + EPSILON)
        third = [v * inverse for v in middle]
        scaled = [up[j] * g3[j] for j in js]
        cross = rowsum([scaled[j] * third[j] for j in js])
        grad_middle = [
            cot[j, span, :].astype(F32) + inverse * (scaled[j] - third[j] * cross) for j in js
        ]
        plain = [raw[j, span, :].astype(F32) for j in js]
        branch = [plain[j] * scale[j] for j in js]
        inverse = lax.rsqrt(rowsum([v * v for v in branch]) + EPSILON)
        second = [v * inverse for v in branch]
        scaled = [grad_middle[j] * g2[j] for j in js]
        cross = rowsum([scaled[j] * second[j] for j in js])
        for j in js:
            full = inverse * (scaled[j] - second[j] * cross)
            gys[j, span, :] = (full * scale[j]).astype(BF16)
            dmid[j, span, :] = grad_middle[j]
            sums[j, 0:1, :] += jnp.sum(grad_middle[j] * second[j], axis=0, keepdims=True)
            sums[j, 1:2, :] += jnp.sum(up[j] * third[j], axis=0, keepdims=True)
            sums[j, 2:3, :] += jnp.sum(plain[j] * full, axis=0, keepdims=True)

    strips(raw.shape[1] // 16, 16, norms)

    copies = []
    for d in (2, 1, 3):
        peer = peers[d - 1]
        copy = remote(gys.at[peer[1]], gy_all.at[me], es.at[d - 1], er.at[d - 1], peer)
        copy.start()
        copies.append(copy)
    own = pltpu.make_async_copy(gys.at[me], gy_all.at[me], el)
    own.start()
    for p in range(2):
        pltpu.make_async_copy(kv.at[:, :, pl.ds(p * 128, 128)], kvs.at[p], ks.at[p]).start()
    units = chain.units() if chain else 0
    at = [0]

    def beside_work(count):
        if chain:
            last = min(units, at[0] + count)
            chain.run(at[0], last)
            at[0] = last

    if chain:
        for load in loads:
            load.wait()
    beside_work(3)
    for copy in copies:
        copy.wait_recv()
    own.wait()
    fill_unit(unit)
    gyt[...] = contract_last(unit[...], gy_all[...].reshape(gyt.shape[1], gyt.shape[0])).astype(BF16)
    gy_out = pltpu.make_async_copy(gyt, gy, ows)
    gy_out.start()
    swap = remote(gyt, gyy, yss, ysr, beyond)
    swap.start()

    heads = part.shape[3]
    rows = part.shape[2]
    order = [1 - x, x]

    def product(i, k, to):
        grad_branch = gy_all[...].reshape(rows, raw.shape[2])
        start = (order[i] * 2 + k) * heads
        to[...] = dot(grad_branch, wo[:, pl.ds(pl.multiple_of(start, 128), heads)]).astype(BF16)

    cores = []
    for i in range(2):
        product(i, 1 - c, part.at[i, 0])
        copy = remote(part.at[i, 0], from_core.at[i], cs.at[i], cr.at[i], beside)
        copy.start()
        cores.append(copy)
    for i in range(2):
        product(i, c, part.at[i, 1])
    cores[0].wait_recv()

    def add_core(span):
        to_x[span, :] = (part[0, 1, span, :].astype(F32) + from_core[0, span, :].astype(F32)).astype(BF16)

    strips(rows // 64, 64, add_core)
    over = remote(to_x, from_x, xs, xr, across)
    over.start()
    beside_work(4)
    cores[1].wait_recv()
    over.wait_recv()

    def add_all(span):
        grad[span, :] = (
            part[1, 1, span, :].astype(F32) + from_core[1, span, :].astype(F32) + from_x[span, :].astype(F32)
        ).astype(BF16)

    strips(rows // 64, 64, add_all)

    def load_pack(p):
        return pltpu.make_async_copy(
            kv.at[:, :, pl.ds(pl.multiple_of(p * 128, 128), 128)], kvs.at[p % 2], ks.at[p % 2]
        )

    y = seq % 2

    def store_pack(p):
        return pltpu.make_async_copy(
            dkvs.at[p, :, y], dkv.at[:, :, pl.ds(pl.multiple_of(p * 128, 128), 128)], ds.at[p]
        )

    def pack_to_y(p):
        return remote(
            dkvs.at[p, :, 1 - y], dkv_y.at[:, :, pl.ds(pl.multiple_of(p * 128, 128), 128)], pys.at[p], pyr.at[p], beyond
        )

    base = at[0]
    each = 1 if units - base >= GROUP else 0

    def one_pack(p, carry):
        load_pack(p).wait()
        span = pl.ds(pl.multiple_of(p * 128, 128), 128)
        keys = kvs[p % 2, :, 0].reshape(n * 128, DH)
        values = kvs[p % 2, :, 1].reshape(n * 128, DH)
        allowed = masks(n, own_meta.at[pl.ds(p, 1)], metas.at[:, pl.ds(p, 1)])
        back_pack(
            n, keys, values, allowed, q.at[span], grad.at[span], mixed.at[span], mass.at[span], dq.at[span],
            dkvs.at[p],
        )
        pack_to_y(p).start()
        store_pack(p).start()

        @pl.when(p + 2 < GROUP)
        def _():
            load_pack(p + 2).start()

        if each:
            chain.run(base + p * each, base + (p + 1) * each)
        return carry

    lax.fori_loop(0, GROUP, one_pack, 0)
    at[0] = base + GROUP * each
    beside_work(units)
    if chain:
        chain.finish()
    for copy in copies + cores + [over]:
        copy.wait_send()
    for p in js:
        store_pack(p).wait()
        pack_to_y(p).wait()
    swap.wait()
    gy_out.wait()


def branch_back(cid, n, first, tiles, gsi, mid, raw, cot, g2, g3, scale, wo, q, mixed, mass, own_meta, metas, kv, pairs):
    bt, bty, dg, dgy = pairs
    own, part = raw.shape[1:]
    rows = q.shape[0]
    heads = q.shape[1]
    block = lambda kind: jax.ShapeDtypeStruct((GROUP, own, part), kind)
    gate_rows = bt.shape[2]
    pack = (2, n, 2, own, DH)
    return comm_call(
        functools.partial(branch_back_kernel, n, first, tiles),
        cid,
        [
            block(F32),
            jax.ShapeDtypeStruct((GROUP, 8, part), F32),
            jax.ShapeDtypeStruct((part, rows), BF16),
            jax.ShapeDtypeStruct((part, rows), BF16),
            jax.ShapeDtypeStruct(q.shape, F32),
            jax.ShapeDtypeStruct((n // 2,) + kv.shape[1:], BF16),
            jax.ShapeDtypeStruct((gate_rows, max(tiles, 1) * TILE), F32),
            jax.ShapeDtypeStruct((n // 2,) + kv.shape[1:], BF16),
        ]
        + (gate_landing(n // 2, tiles, bt) if tiles else []),
        [
            pltpu.VMEM((part, part), BF16),
            pltpu.VMEM((part, rows), BF16),
            pltpu.VMEM((GROUP, own, part), BF16),
            pltpu.VMEM((GROUP, own, part), BF16),
            pltpu.VMEM((2, 2, rows, heads), BF16),
            pltpu.VMEM((2, rows, heads), BF16),
            pltpu.VMEM((rows, heads), BF16),
            pltpu.VMEM((rows, heads), BF16),
            pltpu.VMEM((rows, heads), BF16),
            pltpu.VMEM(pack, BF16),
            pltpu.VMEM((GROUP, n // 2, 2) + pack[2:], BF16),
            DMA((3,)), DMA((3,)), DMA, DMA((2,)), DMA((2,)), DMA, DMA, DMA((2,)), DMA((GROUP,)), DMA, DMA, DMA,
            DMA((GROUP,)), DMA((GROUP,)),
        ]
        + (gate_scratch(n // 2, tiles, bt) if tiles else []),
        [VMEM] * 13 + [ANY] * 5,
        [VMEM, VMEM, ANY, ANY, VMEM, ANY, ANY, ANY] + [ANY] * (2 if tiles else 0),
    )(gsi, mid, raw, cot, g2, g3, scale, wo, q, mixed, mass, own_meta, metas, kv, bt, bty, dg, dgy)


def keys_back_kernel(n, first, tiles, *refs):
    (src, y_got, dq, q_raw, p_raw, cosine, sine, q_scale, p_scale, wq, wkv, tok, dmid, gain, bt, bty, dg, dgy) = refs[:18]
    refs = refs[4:]
    joined, joined_y, out, sums, gain_o, gate_o = refs[14:20]
    refs = refs[1:]
    landing = refs[19:21]
    refs = refs[2:]
    (r_got, l_got, r_out, l_out, moved, back, acc, low, from_core, to_xb, from_x,
     rs, rr, ls, lr, hs, hr, local, jys, jyr, ccs, ccr, cxs, cxr) = refs[19:43]
    slabs, halves, slab_sem, *rest = refs[43:]
    seq, me, x, c = place_now()
    z = seq // 2
    nz = n // 2
    right = (seq + 2, me)
    left = (seq - 2, me)
    beyond = (seq + 1 - 2 * (seq % 2), me)
    across = (seq, (1 - x) * 2 + c)
    beside = (seq, x * 2 + 1 - c)
    chain, loads = gate_chain(nz, first, tiles, seq, me, bt, bty, dg, dgy, gate_o, landing, slabs, halves, slab_sem, rest)
    for load in loads:
        load.start()
    greet_all(seq, me, nz, [(seq, lax.rem(me + d, GROUP)) for d in range(1, GROUP)])
    rows, width = dq.shape
    deep = acc.shape[1]
    half = DH // 2

    sums[...] = jnp.zeros_like(sums)
    gain_o[...] = jnp.zeros_like(gain_o)

    def pair_sum(k, more, to):
        def body(i, carry):
            part = i // 4
            span = pl.ds(pl.multiple_of((i % 4) * 128, 128), 128)
            total = src[k, part, span, :].astype(F32) + y_got[k, part, span, :].astype(F32)
            for ref in more:
                total = total + ref[part, span, :].astype(F32)
            to[part, span, :] = total.astype(BF16)
            return carry

        lax.fori_loop(0, 8, body, 0)

    def queries():
        def turn_queries(span):
            cos = cosine[span, :]
            sin = sine[span, :]
            for h in range(2):
                a = slice(h * DH, h * DH + half)
                b = slice(h * DH + half, (h + 1) * DH)
                one = dq[span, a]
                two = dq[span, b]
                for cols, full in ((a, one * cos + two * sin), (b, two * cos - one * sin)):
                    sums[0:1, cols] += jnp.sum(q_raw[span, cols] * full, axis=0, keepdims=True)
                    joined[span, cols] = (full * q_scale[:, cols]).astype(BF16)

        strips(rows // 64, 64, turn_queries)

        def query_part(span):
            acc[span, :] = contract_last(joined[span, :width], wq[...])

        strips(rows // 128, 128, query_part)

    for load in loads:
        load.wait()
    units = chain.units()
    at = [0]

    def beside_work(count):
        last = min(units, at[0] + count)
        chain.run(at[0], last)
        at[0] = last

    for t in range(1, nz):
        go_right = z + nz - t
        go_left = z - nz + t

        def hop(go, at_end, got, send, ss, sr, to, source):
            if t == 1:
                pair_sum(go, [], send.at[t - 1])
            else:

                @pl.when(jnp.logical_not(at_end))
                def _():
                    remote(send.at[t - 1], got.at[t - 2], ss.at[t - 2], sr.at[t - 2], source).wait_recv()
                    pair_sum(go, [got.at[t - 2]], send.at[t - 1])

                @pl.when(at_end)
                def _():
                    pair_sum(go, [], send.at[t - 1])

            remote(send.at[t - 1], got.at[t - 1], ss.at[t - 1], sr.at[t - 1], to).start()

        @pl.when(go_right < nz)
        def _():
            hop(go_right, z == 0, r_got, r_out, rs, rr, right, left)

        @pl.when(go_left >= 0)
        def _():
            hop(go_left, z == nz - 1, l_got, l_out, ls, lr, left, right)

        beside_work(3)
        if t == 1:
            queries()

    last = nz - 2

    def got_left():
        remote(r_out.at[last], r_got.at[last], rs.at[last], rr.at[last], left).wait_recv()

    def got_right():
        remote(l_out.at[last], l_got.at[last], ls.at[last], lr.at[last], right).wait_recv()

    @pl.when(z == 0)
    def _():
        got_right()
        pair_sum(z, [l_got.at[last]], moved)

    @pl.when(z == nz - 1)
    def _():
        got_left()
        pair_sum(z, [r_got.at[last]], moved)

    @pl.when((z > 0) & (z < nz - 1))
    def _():
        got_left()
        got_right()
        pair_sum(z, [r_got.at[last], l_got.at[last]], moved)

    for t in range(2):
        target = t * 2 + x

        @pl.when(target == me)
        def _():
            pltpu.make_async_copy(moved.at[t], back.at[c], local).start()

        @pl.when(target != me)
        def _():
            remote(moved.at[t], back.at[c], hs.at[t], hr.at[c], (seq, target)).start()

    beside_work(3)
    for j in range(2):
        source = c * 2 + j

        @pl.when(source == me)
        def _():
            pltpu.make_async_copy(moved.at[0], back.at[j], local).wait()

        @pl.when(source != me)
        def _():
            remote(moved.at[0], back.at[j], hs.at[0], hr.at[j], (seq, source)).wait_recv()

    is_key = jnp.where(x == 0, 1.0, 0.0).astype(F32)

    def turn_pairs(span):
        cos = is_key * cosine[span, :] + (1.0 - is_key)
        sin = is_key * sine[span, :]
        for h in range(2):
            a = slice(h * DH, h * DH + half)
            b = slice(h * DH + half, (h + 1) * DH)
            one = back[h, span, :half].astype(F32)
            two = back[h, span, half:].astype(F32)
            for cols, full in ((a, one * cos + two * sin), (b, two * cos - one * sin)):
                sums[1:2, cols] += jnp.sum(p_raw[span, cols] * full, axis=0, keepdims=True)
                joined[span, width + cols.start : width + cols.stop] = (full * p_scale[:, cols]).astype(BF16)

    strips(rows // 64, 64, turn_pairs)
    joined_swap = remote(joined, joined_y, jys, jyr, beyond)
    joined_swap.start()

    def pair_part(span):
        acc[span, :] += contract_last(joined[span, width:], wkv[...])

    strips(rows // 128, 128, pair_part)

    parts = 4
    block = rows // GROUP
    size = block // parts
    order = [1 - x, x]
    cores = []
    for i in range(2):
        for k in range(parts):
            owner = order[i] * 2 + 1 - c
            span = pl.ds(k * size, size)
            low[i, span, :] = acc[pl.ds(pl.multiple_of(owner * block + k * size, 16), size), :].astype(BF16)
            copy = remote(low.at[i, span], from_core.at[i, span], ccs.at[i, k], ccr.at[i, k], beside)
            copy.start()
            cores.append(copy)
    sends = []
    for k in range(parts):
        span = pl.ds(k * size, size)
        here = pl.ds(pl.multiple_of((order[0] * 2 + c) * block + k * size, 16), size)
        cores[k].wait_recv()
        to_xb[span, :] = (acc[here, :] + from_core[0, span, :].astype(F32)).astype(BF16)
        copy = remote(to_xb.at[span], from_x.at[span], cxs.at[k], cxr.at[k], across)
        copy.start()
        sends.append(copy)
    beside_work(units)
    chain.finish()
    for k in range(parts):
        span = pl.ds(k * size, size)
        here = pl.ds(pl.multiple_of((order[1] * 2 + c) * block + k * size, 16), size)
        cores[parts + k].wait_recv()
        sends[k].wait_recv()
        grad = acc[here, :] + from_core[1, span, :].astype(F32) + from_x[span, :].astype(F32)
        value = tok[span, :].astype(F32)
        inverse = lax.rsqrt(jnp.mean(value * value, axis=1, keepdims=True) + EPSILON)
        normed = value * inverse
        scaled = grad * gain[...]
        out[span, :] = dmid[span, :] + inverse * (
            scaled - normed * jnp.mean(scaled * normed, axis=1, keepdims=True)
        )
        gain_o[0:1, :] += jnp.sum(grad * normed, axis=0, keepdims=True)

    for t in range(2):

        @pl.when(t * 2 + x != me)
        def _():
            remote(moved.at[t], back.at[c], hs.at[t], hr.at[c], (seq, t * 2 + x)).wait_send()

    for t in range(1, nz):

        @pl.when(z + nz - t < nz)
        def _():
            remote(r_out.at[t - 1], r_got.at[t - 1], rs.at[t - 1], rr.at[t - 1], right).wait_send()

        @pl.when(z - nz + t >= 0)
        def _():
            remote(l_out.at[t - 1], l_got.at[t - 1], ls.at[t - 1], lr.at[t - 1], left).wait_send()

    for copy in cores + sends:
        copy.wait_send()
    joined_swap.wait()


def keys_back(cid, n, first, tiles, src, src_y, dq, q_raw, p_raw, cosine, sine, q_scale, p_scale, wq, wkv, tok, dmid, gain, pairs):
    bt, bty, dg, dgy = pairs
    nz = n // 2
    rows, width = dq.shape
    deep = wq.shape[0]
    block = rows // GROUP
    shape = src.shape[1:]
    chain = pltpu.VMEM((nz - 1,) + shape, BF16)
    joined = jax.ShapeDtypeStruct((rows, 2 * width), BF16)
    return comm_call(
        functools.partial(keys_back_kernel, n, first, tiles),
        cid,
        [
            joined,
            joined,
            jax.ShapeDtypeStruct((block, deep), F32),
            jax.ShapeDtypeStruct((8, width), F32),
            jax.ShapeDtypeStruct((8, deep), F32),
            jax.ShapeDtypeStruct((bt.shape[2], tiles * TILE), F32),
        ]
        + gate_landing(nz, tiles, bt),
        [
            chain, chain, chain, chain, pltpu.VMEM(shape, BF16), pltpu.VMEM(shape, BF16),
            pltpu.VMEM((rows, deep), F32),
            pltpu.VMEM((2, block, deep), BF16),
            pltpu.VMEM((2, block, deep), BF16),
            pltpu.VMEM((block, deep), BF16),
            pltpu.VMEM((block, deep), BF16),
            DMA((nz - 1,)), DMA((nz - 1,)), DMA((nz - 1,)), DMA((nz - 1,)),
            DMA((2,)), DMA((2,)), DMA, DMA, DMA, DMA((2, 4)), DMA((2, 4)), DMA((4,)), DMA((4,)),
        ]
        + gate_scratch(nz, tiles, bt),
        [VMEM] * 14 + [ANY] * 4,
        [VMEM, ANY, VMEM, VMEM, VMEM, ANY, ANY, ANY],
    )(src, src_y, dq, q_raw, p_raw, cosine, sine, q_scale, p_scale, wq, wkv, tok, dmid, gain, bt, bty, dg, dgy)


def finish_kernel(n, rounds, first, tiles, *refs):
    (whole, part, bt, bty, dg, dgy, ot, oty, gy, gyy, at, aty, joined, joined_y) = refs[:14]
    whole_out, part_out, gate_o, output_o, attention_o = refs[14:19]
    landing = refs[19:25]
    refs = refs[6:]
    bufs, gots, mine, theirs, ss, rs = refs[19:25]
    slabs, halves, slab_sem = refs[25:28]
    gate_refs, output_refs, attention_refs = refs[28:39], refs[39:50], refs[50:61]
    output_halves, attention_halves, half_sem = refs[61:]
    seq, me, x, c = place_now()
    nz = n // 2
    across = (seq, (1 - x) * 2 + c)
    beside = (seq, x * 2 + 1 - c)
    gates, loads = gate_chain(nz, first, tiles, seq, me, bt, bty, dg, dgy, gate_o, landing[:2], slabs, halves, slab_sem, gate_refs)
    for i, (ref, to) in enumerate(
        ((ot.at[:, seq % 2], output_halves.at[0]), (oty, output_halves.at[1]),
         (at.at[:, seq % 2], attention_halves.at[0]), (aty, attention_halves.at[1]))
    ):
        loads.append(pltpu.make_async_copy(ref, to, half_sem.at[i]))
    for load in loads:
        load.start()
    wide = joined.shape[1] // 2

    def output_partial(k, j):
        return dot(gy[...], output_halves[0, k]) + dot(gyy[...], output_halves[1, k])

    def attention_partial(k, j):
        cols = pl.ds(pl.multiple_of(j * wide, 128), wide)
        return dot(attention_halves[0, k], joined[:, cols]) + dot(attention_halves[1, k], joined_y[:, cols])

    def keep_output(j, stage, sem):
        return pltpu.make_async_copy(stage, output_o, sem)

    outputs = Chain(nz, 1, seq, me, output_partial, keep_output, landing[2:4], output_refs)
    attentions = Chain(
        nz,
        2,
        seq,
        me,
        attention_partial,
        lambda j, stage, sem: pltpu.make_async_copy(
            stage, attention_o.at[:, pl.ds(pl.multiple_of(j * wide, 128), wide)], sem
        ),
        landing[4:],
        attention_refs,
    )
    partners = []
    for r in range(rounds):
        bit = 1 << r
        partners.append((seq + bit - 2 * bit * ((seq // bit) % 2), me))
    greet([(lax.rem(seq + d, n), me) for d in range(1, n)] + [across, beside])
    for load in loads:
        load.wait()
    rows = whole.shape[0]
    bufs[0, :rows, :] = whole[...]
    bufs[0, rows:, :] = part[...]
    queues = [(chain, list(range(0, chain.units(), nz - 1))) for chain in (gates, outputs, attentions)]
    work = [(gates, u) for u in queues[0][1][:tiles]]
    rest = [queues[0][1][tiles:], queues[1][1], queues[2][1]]
    while any(rest):
        for (chain, _), left in zip(queues, rest):
            if left:
                work.append((chain, left.pop(0)))
    at_work = [0]

    def beside_work(count):
        todo = work[at_work[0] : at_work[0] + count]
        at_work[0] += count
        start = None
        for i, (chain, u) in enumerate(todo):
            if start is None:
                start = u
            if i + 1 == len(todo) or todo[i + 1][0] is not chain:
                chain.run(start, u + 3)
                start = None

    for r in range(rounds + 1):
        partner = partners[r] if r < rounds else across
        copy = remote(bufs.at[r], gots.at[r], ss.at[r], rs.at[r], partner)
        copy.start()
        beside_work(1)
        copy.wait()
        if r < rounds:
            bufs[r + 1] = bufs[r] + gots[r]
    mine[0, :rows, :] = bufs[rounds, :rows, :] + gots[rounds, :rows, :]
    mine[0, rows:, :] = bufs[rounds, rows:, :]
    mine[1, rows:, :] = gots[rounds, rows:, :]
    mine[1, :rows, :] = jnp.zeros((rows, 128), F32)
    copy = remote(mine, theirs, ss.at[rounds + 1], rs.at[rounds + 1], beside)
    copy.start()
    beside_work(len(work))
    copy.wait()
    whole_out[...] = mine[0, :rows, :] + theirs[0, :rows, :]
    part_out[x * 2 + c] = mine[0, rows:, :]
    part_out[(1 - x) * 2 + c] = mine[1, rows:, :]
    part_out[x * 2 + 1 - c] = theirs[0, rows:, :]
    part_out[(1 - x) * 2 + 1 - c] = theirs[1, rows:, :]
    gates.finish()
    outputs.finish()
    attentions.finish()


def finish(cid, n, first, tiles, whole, part, pairs, output_pairs, attention_pairs):
    bt, bty, dg, dgy = pairs
    ot, oty, gy, gyy = output_pairs
    at, aty, joined, joined_y = attention_pairs
    nz = n // 2
    rounds = int(math.log2(n))
    rows = whole.shape[0] + part.shape[0]
    output_shape = (gy.shape[0], ot.shape[3])
    attention_rows = at.shape[2]
    return comm_call(
        functools.partial(finish_kernel, n, rounds, first, tiles),
        cid,
        [
            jax.ShapeDtypeStruct(whole.shape, F32),
            jax.ShapeDtypeStruct((GROUP,) + part.shape, F32),
            jax.ShapeDtypeStruct((bt.shape[2], tiles * TILE), F32),
            jax.ShapeDtypeStruct(output_shape, F32),
            jax.ShapeDtypeStruct((attention_rows, joined.shape[1]), F32),
        ]
        + gate_landing(nz, tiles, bt)
        + Chain.landing(nz, 1, *output_shape)
        + Chain.landing(nz, 2, attention_rows, joined.shape[1] // 2),
        [
            pltpu.VMEM((rounds + 1, rows, 128), F32),
            pltpu.VMEM((rounds + 1, rows, 128), F32),
            pltpu.VMEM((2, rows, 128), F32),
            pltpu.VMEM((2, rows, 128), F32),
            DMA((rounds + 2,)),
            DMA((rounds + 2,)),
        ]
        + gate_scratch(nz, tiles, bt)
        + Chain.scratch(nz, 1, *output_shape)
        + Chain.scratch(nz, 2, attention_rows, joined.shape[1] // 2)
        + [
            pltpu.VMEM((2, nz) + ot.shape[2:], BF16),
            pltpu.VMEM((2, nz) + at.shape[2:], BF16),
            DMA((4,)),
        ],
        [VMEM] * 2 + [ANY] * 6 + [VMEM] * 2 + [ANY] * 2 + [VMEM] * 2,
        [VMEM, VMEM] + [ANY] * 9,
    )(whole, part, bt, bty, dg, dgy, ot, oty, gy, gyy, at, aty, joined, joined_y)


def rms_inverse(value):
    return lax.rsqrt(jnp.mean(value * value, axis=-1, keepdims=True) + EPSILON)


def norm_back(inverse, normed, upstream):
    return inverse * (upstream - normed * jnp.mean(upstream * normed, axis=-1, keepdims=True))


def rotate(value, cosine, sine):
    half = DH // 2
    first = value[..., :half]
    second = value[..., half:]
    return jnp.concatenate([first * cosine - second * sine, second * cosine + first * sine], axis=-1)


def core_swap(value):
    return lax.ppermute(value, "fsdp", [(f, f ^ 1) for f in range(GROUP)])


def lanes(value, rows):
    flat = value.reshape(-1)
    return jnp.pad(flat, (0, rows * 128 - flat.shape[0])).reshape(rows, 128)


def per_device(
    n,
    tokens,
    doc_ids,
    padding,
    token_order,
    query_code,
    key_value_code,
    output_code,
    gate_up_code,
    down_code,
    query_scale,
    key_value_scale,
    output_scale,
    gate_up_scale,
    down_scale,
    norm_gains,
    cotangent,
):
    me = lax.axis_index("fsdp")
    c = me % 2
    width = tokens.shape[2]
    part = width // GROUP
    rows = GROUP * tokens.shape[1]
    own = tokens.shape[1]

    def mine(vector):
        size = vector.shape[-1] // GROUP
        return lax.dynamic_slice_in_dim(vector, me * size, size, vector.ndim - 1)

    def blocks_to_rows(blocks):
        return jnp.concatenate([blocks[i] for i in range(GROUP)], axis=1)

    gain = 1.0 + norm_gains
    place = token_order[0].astype(F32)
    document = doc_ids[0].astype(F32)
    meta = jnp.stack([document, place, jnp.where(padding[0] == 1, document, -1.0)] + [document] * 5)

    def to_blocks(value):
        return value.reshape(own, GROUP, part).transpose(1, 0, 2)

    my_query_scale = mine(query_scale)
    my_pair_scale = mine(key_value_scale)
    token_cols = to_blocks(tokens[0])
    cot_cols = to_blocks(cotangent[0])
    rates = BASE ** (-2.0 * jnp.arange(DH // 2).astype(F32) / DH)
    (
        token_blocks, cot_blocks, own_meta, metas, pairs, query, query_raw, pair_raw, cosine, sine, first_turned
    ) = front(
        1,
        n,
        token_cols.reshape(rows, part),
        cot_cols.reshape(rows, part),
        meta,
        gain[0].reshape(GROUP, 1, part),
        rates[None],
        my_query_scale[None],
        my_pair_scale[None],
        query_code,
        key_value_code,
    )

    mixed_low, mixed, mass = attend(n, query, pairs, own_meta, metas)
    second_input, branch_own, my_middle, mixed_slices, second_turned = branch_forward(
        3,
        mixed_low,
        output_code.T,
        token_blocks,
        output_scale.reshape(GROUP, 1, part),
        gain[1].reshape(GROUP, 1, part),
        gain[2].reshape(GROUP, 1, part),
    )

    my_gate_scale = mine(gate_up_scale)
    columns = gate_up_code.shape[1]
    tiles = columns // TILE
    gate_scales = my_gate_scale.reshape(tiles, 1, TILE)
    (
        gate_up, hidden, hidden_y, down_blocks, grad_down, grad_down_turned, down_sums, gate_levels, down_levels, *riders
    ) = ffn_forward(
        5,
        second_input,
        gate_up_code,
        gate_scales,
        down_code.T,
        cot_blocks,
        gain[3].reshape(GROUP, 1, part),
        down_scale.reshape(GROUP, 1, part),
        [second_turned, mixed_slices, first_turned],
    )
    second_pair, mixed_pair, first_pair = zip((second_turned, mixed_slices, first_turned), riders)
    my_down = lax.dynamic_slice_in_dim(down_blocks, me * own, own, 1).astype(F32) * down_scale.reshape(GROUP, 1, part)
    down_inverse = lax.rsqrt(jnp.mean(my_down * my_down, axis=(0, 2), keepdims=True) + EPSILON)
    result = blocks_to_rows((my_middle + my_down * down_inverse * gain[3].reshape(GROUP, 1, part)).astype(BF16))
    tiles_zero, tiles_one, tiles_two = (2, 5, 4) if n == 8 else (0, 0, 0)
    tiles_three = tiles - tiles_zero - tiles_one - tiles_two
    grad_gate_up, grad_gate_up_y, gate_sums, grad_second_input, down_grad, gate_zero, *_ = ffn_backward(
        6,
        n,
        tiles_zero,
        grad_down,
        grad_down_turned,
        down_levels,
        gate_levels,
        gate_scales,
        gate_up,
        hidden,
        hidden_y,
        *second_pair,
    )
    if n == 8:
        down_grad = down_grad.T
    else:
        hidden_own = jnp.concatenate(
            [
                (jax.nn.gelu(gate_up[0, t].astype(F32)) * gate_up[1, t].astype(F32)).astype(BF16)
                for t in range(tiles)
            ],
            axis=1,
        )
        hidden_core = core_swap(hidden_own)
        hidden_rows = jnp.concatenate(
            [jnp.where(c == 0, hidden_own, hidden_core), jnp.where(c == 0, hidden_core, hidden_own)], axis=1
        )
        down_grad = lax.psum_scatter(
            contract_first(hidden_rows, grad_down), "seq", scatter_dimension=0, tiled=True
        )
    scale_down = down_sums[0]
    gain_four = down_sums[1]
    scale_gate = gate_sums[:, 0, :].reshape(columns) / my_gate_scale
    gate_pairs = second_pair + (grad_gate_up, grad_gate_up_y)
    grad_middle, branch_sums, grad_branch, grad_branch_y, grad_query, grad_pairs, gate_one, grad_pairs_y, *_ = branch_back(
        7,
        n,
        tiles_zero,
        tiles_one,
        grad_second_input,
        my_middle,
        branch_own,
        cot_cols,
        gain[1].reshape(GROUP, 1, part),
        gain[2].reshape(GROUP, 1, part),
        output_scale.reshape(GROUP, 1, part),
        output_code.T,
        query,
        mixed,
        mass,
        own_meta,
        metas,
        pairs,
        gate_pairs,
    )
    grad_middle = blocks_to_rows(grad_middle)
    gain_two = branch_sums[:, 0].reshape(width)
    gain_three = branch_sums[:, 1].reshape(width)
    scale_output = branch_sums[:, 2].reshape(width)

    if n == 8:
        joined, joined_y, grad_inputs, key_sums, gain_one, gate_two, *_ = keys_back(
            9,
            n,
            tiles_zero + tiles_one,
            tiles_two,
            grad_pairs,
            grad_pairs_y,
            grad_query,
            query_raw,
            pair_raw,
            cosine,
            sine,
            my_query_scale[None],
            my_pair_scale[None],
            query_code,
            key_value_code,
            tokens[0],
            grad_middle,
            gain[0][None],
            gate_pairs,
        )
        gain_one = gain_one[0]
        scale_query = key_sums[0]
        scale_pair = key_sums[1]
    else:
        is_key = me < 2
        pair_cosine = jnp.where(is_key, cosine, 1.0)
        pair_sine = jnp.where(is_key, sine, 0.0)
        y = lax.axis_index("seq") % 2
        both = (grad_pairs.astype(F32) + grad_pairs_y.astype(F32))[:, None]
        spread = jnp.concatenate([jnp.where(y == 0, both, 0.0), jnp.where(y == 1, both, 0.0)], axis=1)
        summed = lax.psum_scatter(spread.reshape((n,) + grad_pairs.shape[1:]), "seq", scatter_dimension=0)
        heads = lax.all_gather(summed, "fsdp")
        grad_heads = lax.dynamic_index_in_dim(
            lax.dynamic_slice_in_dim(heads, c * 2, 2, 0), me // 2, 1, keepdims=False
        )
        grad_query_full = rotate(
            grad_query.reshape(rows, 2, DH), cosine[:, None], -sine[:, None]
        ).reshape(rows, 2 * DH)
        scale_query = jnp.sum(query_raw * grad_query_full, axis=0)
        grad_query_low = (grad_query_full * my_query_scale).astype(BF16)
        grad_pair_full = jnp.concatenate(
            [rotate(grad_heads[j], pair_cosine, -pair_sine) for j in range(2)], axis=1
        )
        scale_pair = jnp.sum(pair_raw * grad_pair_full, axis=0)
        grad_pair_low = (grad_pair_full * my_pair_scale).astype(BF16)
        joined = jnp.concatenate([grad_query_low, grad_pair_low], axis=1)
        grad_first_sum = contract_last(grad_query_low, query_code) + contract_last(grad_pair_low, key_value_code)
        grad_first_input = group_reduce(10, grad_first_sum.astype(BF16).reshape(GROUP, own, width), F32)
        my_inputs = tokens[0].astype(F32)
        my_inverse = rms_inverse(my_inputs)
        first = my_inputs * my_inverse
        gain_one = jnp.sum(grad_first_input * first, axis=0)
        grad_inputs = grad_middle + norm_back(my_inverse, first, grad_first_input * gain[0])

    wholes = lanes(jnp.concatenate([gain_one, gain_two, gain_three, scale_output]), 72)
    parts = [scale_query, scale_pair, scale_gate, scale_down, gain_four]
    part_rows = lanes(jnp.concatenate(parts), 56)
    if n == 8:
        whole_total, part_total, gate_three, output_grad, attention_grad, *_ = finish(
            11,
            n,
            tiles - tiles_three,
            tiles_three,
            wholes,
            part_rows,
            gate_pairs,
            mixed_pair + (grad_branch, grad_branch_y),
            first_pair + (joined, joined_y),
        )
        output_grad = output_grad.T
        gate_grad = jnp.concatenate([gate_zero, gate_one, gate_two, gate_three], axis=1)
    else:
        whole_total, part_total = totals(11, n, wholes, part_rows)

        def weight_sum(left, right):
            return lax.psum_scatter(dot(left.reshape(-1, rows), right), "seq", scatter_dimension=0, tiled=True)

        gate_grad = weight_sum(second_turned, grad_gate_up)
        output_grad = weight_sum(mixed_slices.transpose(0, 1, 3, 2), grad_branch.T)
        attention_grad = weight_sum(first_turned, joined)
    whole_total = whole_total.reshape(-1)
    part_total = part_total.reshape(GROUP, -1)
    pieces = []
    start = 0
    for vector in parts:
        pieces.append(part_total[:, start : start + vector.shape[0]].reshape(-1))
        start += vector.shape[0]
    q_width = query_code.shape[1]
    return (
        result[None],
        grad_inputs[None],
        attention_grad[:, :q_width],
        attention_grad[:, q_width:],
        output_grad,
        gate_grad,
        down_grad,
        pieces[0],
        pieces[1],
        whole_total[3 * width :],
        pieces[2],
        pieces[3],
        jnp.concatenate([whole_total[: 3 * width], pieces[4]]).reshape(4, width),
    )


def solution(mesh):
    return jax.shard_map(
        functools.partial(per_device, mesh.shape["seq"]),
        mesh=mesh,
        in_specs=(
            P("fsdp", "seq", None),
            P("fsdp", "seq"),
            P("fsdp", "seq"),
            P("fsdp", "seq"),
            P(None, "fsdp"),
            P(None, "fsdp"),
            P(None, "fsdp"),
            P(None, "fsdp"),
            P(None, "fsdp"),
            P(),
            P(),
            P(),
            P(),
            P(),
            P(),
            P("fsdp", "seq", None),
        ),
        out_specs=(
            P("fsdp", "seq", None),
            P("fsdp", "seq", None),
            P("seq", "fsdp"),
            P("seq", "fsdp"),
            P("seq", "fsdp"),
            P("seq", "fsdp"),
            P("seq", "fsdp"),
            P(),
            P(),
            P(),
            P(),
            P(),
            P(),
        ),
        check_vma=False,
    )
```
